32 devices in a mesh: wide: 8 (over y, x, core), narrow: 4 (over z).
Axes of the slice: x: 2, y: 2, z: 4, core: 2. Of those that a mesh axis runs over, the one named last changes fastest.
Arguments:
- tokens: bfloat16 [8, 2048, 768], P('wide', 'narrow'), may hold values from -6 to 6
- segment: int32 [8, 2048], P('wide'), may hold values from 0 to 10, as said below
- padding: int32 [8, 2048], P('wide'), may hold values from 0 to 1, as said below
- coords: int32 [2, 8, 2048], P(None, 'wide'), may hold values from 0 to 23, as said below
- ln1_gain: float32 [768], replicated, may hold values from 0.5 to 1.5
- ln1_shift: float32 [768], replicated, may hold values from -1 to 1
- query_key_value_weight: bfloat16 [768, 2304], replicated, may hold values from -0.21875 to 0.21875
- b_qkv: float32 [2304], replicated, may hold values from -3 to 3
- output_weight: bfloat16 [768, 768], replicated, may hold values from -0.875 to 0.875
- b_out: float32 [768], replicated, may hold values from -3 to 3
- rope_freqs: float32 [2, 12, 32], replicated, may hold values from -3 to 3
- ln2_gain: float32 [768], replicated, may hold values from 0.5 to 1.5
- ln2_shift: float32 [768], replicated, may hold values from -1 to 1
- w_up: bfloat16 [768, 3072], P(None, 'narrow'), may hold values from -0.21875 to 0.21875
- b_up: float32 [3072], P('narrow'), may hold values from -3 to 3
- w_down: bfloat16 [3072, 768], P('narrow')
- b_down: float32 [768], replicated, may hold values from -3 to 3
- cotangent: bfloat16 [8, 2048, 768], P('wide', 'narrow'), may hold values from -6 to 6
Outputs:
- activations: bfloat16 [8, 2048, 768], P('wide', 'narrow')
- input_grad: float32 [8, 2048, 768], P('wide', 'narrow')
- grad_ln1_gain: float32 [768], replicated
- grad_ln1_shift: float32 [768], replicated
- grad_w_qkv: float32 [768, 2304], replicated
- grad_b_qkv: float32 [2304], replicated
- grad_w_out: float32 [768, 768], replicated
- grad_b_out: float32 [768], replicated
- grad_freqs: float32 [2, 12, 32], replicated
- grad_ln2_gain: float32 [768], replicated
- grad_ln2_shift: float32 [768], replicated
- grad_w_up: float32 [768, 3072], P(None, 'narrow')
- grad_b_up: float32 [3072], P('narrow')
- grad_w_down: float32 [3072, 768], P('narrow')
- grad_b_down: float32 [768], replicated
- rot_sq: float32 [], replicated
- other_sq: float32 [], replicated
The draws below stay inside these ranges and needn't reach their ends.
Inputs may be any that keep to these rules, and one draw needn't show every extreme that they name: `segment`: each sequence packs whole images of 14, 20 or 24 patches on a side in order while they fit; slots of one image carry its number, counted from 0; padding slots at the end carry the number after the last image. One sequence holds only 14-side images. `padding`: 1 exactly on the slots after the last image of a sequence. `coords`: row and column of a patch in its image, row by row; 0 on padding.
All inputs are finite; a program needn't handle non-finite values.
Results may differ from the reference program's by a relative error of at most 0.009.
The reference program's roundings to bfloat16 on the way count: a program that leaves them out, or rounds other values in their place, can miss the bound.
Values may be sent and summed in bfloat16 or wider, within the bound.
No kernel may reach another device: no remote copies, remote signals or barrier semaphores. Data moves between devices by JAX's collectives and lax.ppermute only.
A program may use at most 384 MiB of HBM per device.

```python
import jax
import jax.numpy as jnp
from jax import lax

D = 768
HEADS = 12
HEAD = 64
FF = 3072
HALF = 32
LEN = 2048
SIDE_S = 14
SIDE_M = 20
SIDE_L = 24
SEQS = 8


def packing(key):
    side_table = jnp.array([SIDE_S, SIDE_M, SIDE_L], jnp.int32)
    most_images = LEN // (SIDE_S * SIDE_S) + 1
    image_kind = jax.random.randint(jax.random.fold_in(key, 11), (SEQS, most_images), 0, 3)
    special = jax.random.randint(jax.random.fold_in(key, 12), (), 0, SEQS)
    seq_ids = jnp.arange(SEQS)
    image_kind = jnp.where((seq_ids == special)[:, None], 0, image_kind)
    first_large = (seq_ids == (special + 1) % SEQS)[:, None] & (jnp.arange(most_images) == 0)[None, :]
    image_kind = jnp.where(first_large, 2, image_kind)
    image_side = jnp.sum(jnp.where(image_kind[..., None] == jnp.arange(3), side_table, 0), -1)
    image_size = image_side * image_side
    image_end = jnp.cumsum(image_size, 1)
    fitted = image_end <= LEN
    image_first_token = image_end - image_size
    position = jnp.arange(LEN)
    passed = (image_end[:, None, :] <= position[None, :, None]) & fitted[:, None, :]
    segment_id = jnp.sum(passed.astype(jnp.int32), -1)
    image_count = jnp.sum(fitted.astype(jnp.int32), 1)
    padded = segment_id == image_count[:, None]
    chosen = segment_id[..., None] == jnp.arange(most_images)
    start_of = jnp.sum(jnp.where(chosen, image_first_token[:, None, :], 0), -1)
    side_of = jnp.sum(jnp.where(chosen, image_side[:, None, :], 0), -1)
    local_pos = position[None, :] - start_of
    grid_row = jnp.where(padded, 0, local_pos // side_of)
    grid_col = jnp.where(padded, 0, local_pos % side_of)
    return (segment_id.astype(jnp.int32), padded.astype(jnp.int32), grid_row.astype(jnp.int32), grid_col.astype(jnp.int32))


def draw_segment(key, part):
    return packing(key)[0]


def draw_padding(key, part):
    return packing(key)[1]


def draw_coords(key, part):
    packed = packing(key)
    return jnp.stack([packed[2], packed[3]])


def row_scaled(key, lowest, highest, entries):
    fraction = jnp.arange(FF).astype(jnp.float32) / (FF - 1)
    row_scale = jnp.exp(jnp.log(lowest) + (jnp.log(highest) - jnp.log(lowest)) * fraction)
    return (entries * row_scale[:, None] * FF ** (-0.5)).astype(jnp.bfloat16)


def draw_w_down(key, part):
    key = jax.random.fold_in(key, 5)
    entries = jnp.clip(jax.random.normal(key, (FF, D), jnp.float32), -4.0, 4.0)
    return row_scaled(key, 0.5, 2.0, entries)


def level_of(stream_key, shape, shards, smallest, high):
    def one(dim, blocks):
        steps = jax.random.uniform(jax.random.fold_in(jax.random.fold_in(stream_key, 6), dim), (blocks,), jnp.float32, smallest / len(shards), high / len(shards))
        return jnp.repeat(jnp.exp(steps), shape[dim] // blocks).reshape((-1,) + (1,) * (len(shape) - dim - 1))

    loudness = one(*shards[0])
    for cut in shards[1:]:
        loudness = loudness * one(*cut)
    return loudness


def bell_draw(stream_key, dims, deviation, reach, shards=(), held_as=jnp.bfloat16):
    values = deviation * jax.random.normal(stream_key, dims, jnp.float32)
    if shards:
        values = values * level_of(stream_key, dims, shards, -0.22, 0.18)
    return jnp.clip(values, -reach, reach).astype(held_as)


def setup_inputs(seed: int = 0) -> dict:
    key_list = jax.random.split(jax.random.key(seed), 19)
    tokens = bell_draw(key_list[0], (SEQS, LEN, D), 1.0, 6.0, ((0, 8), (1, 4)))
    segment = draw_segment(jax.random.fold_in(key_list[18], 71), 0)
    padding = draw_padding(jax.random.fold_in(key_list[18], 71), 0)
    coords = draw_coords(jax.random.fold_in(key_list[18], 71), 0)
    ln1_gain = jnp.clip(1.0 + 0.1 * jax.random.normal(key_list[4], (D,), jnp.float32), 0.5, 1.5)
    ln1_shift = bell_draw(key_list[5], (D,), 0.2, 1.0, (), jnp.float32)
    query_key_value_weight = bell_draw(key_list[6], (D, 3 * D), D ** -0.5, 0.21875)
    b_qkv = bell_draw(key_list[7], (3 * D,), 0.5, 3.0, (), jnp.float32)
    output_weight = bell_draw(key_list[8], (D, D), (D // 16) ** -0.5, 0.875)
    b_out = bell_draw(key_list[9], (D,), 0.5, 3.0, (), jnp.float32)
    rope_freqs = bell_draw(key_list[10], (2, HEADS, HALF), 0.5, 3.0, (), jnp.float32)
    ln2_gain = jnp.clip(1.0 + 0.1 * jax.random.normal(key_list[11], (D,), jnp.float32), 0.5, 1.5)
    ln2_shift = bell_draw(key_list[12], (D,), 0.2, 1.0, (), jnp.float32)
    w_up = bell_draw(key_list[13], (D, FF), D ** -0.5, 0.21875, ((1, 4),))
    b_up = bell_draw(key_list[14], (FF,), 0.5, 3.0, ((0, 4),), jnp.float32)
    w_down = draw_w_down(jax.random.fold_in(key_list[18], 71), 0)
    b_down = bell_draw(key_list[16], (D,), 0.5, 3.0, (), jnp.float32)
    cotangent = bell_draw(key_list[17], (SEQS, LEN, D), 1.0, 6.0, ((0, 8), (1, 4)))
    return {"tokens": tokens, "segment": segment, "padding": padding, "coords": coords, "ln1_gain": ln1_gain, "ln1_shift": ln1_shift, "query_key_value_weight": query_key_value_weight, "b_qkv": b_qkv, "output_weight": output_weight, "b_out": b_out, "rope_freqs": rope_freqs, "ln2_gain": ln2_gain, "ln2_shift": ln2_shift, "w_up": w_up, "b_up": b_up, "w_down": w_down, "b_down": b_down, "cotangent": cotangent}


EPS = 1e-06
MASKED = -1e+30
HIGH = lax.Precision.HIGHEST

@jax.custom_vjp
def low(v):
    return lax.optimization_barrier(v.astype(jnp.bfloat16)).astype(jnp.float32)

@jax.custom_vjp
def low_back(v):
    return v

def low_keep(v):
    return (low(v), None)

def low_pass(kept, grad):
    return (grad,)

def back_keep(v):
    return (v, None)

def back_low(kept, grad):
    return (low(grad),)
low.defvjp(low_keep, low_pass)
low_back.defvjp(back_keep, back_low)

def matmul(left, right):
    return jnp.dot(left, right, precision=HIGH, preferred_element_type=jnp.float32)

def layer_norm(inputs, scales, token_shift):
    mean = lax.optimization_barrier(jnp.mean(inputs, -1, keepdims=True))
    centred = inputs - mean
    variance = lax.optimization_barrier(jnp.mean(centred * centred, -1, keepdims=True))
    return centred * lax.rsqrt(variance + EPS) * scales + token_shift

def rotate(tensor, angle):
    half_size = tensor.shape[-1] // 2
    first = tensor[..., :half_size]
    second = tensor[..., half_size:]
    cosine = jnp.cos(angle)
    sine_val = jnp.sin(angle)
    return jnp.concatenate([first * cosine - second * sine_val, first * sine_val + second * cosine], -1)

def sequence(inputs, segment, padding, grid, params):
    ln1_gain, ln1_shift, query_key_value_weight, b_qkv, output_weight, b_out, rope_freqs, ln2_gain, ln2_shift, w_up, b_up, w_down, b_down = params
    norm1 = low(layer_norm(inputs, ln1_gain, ln1_shift))
    proj_qkv = low_back(matmul(norm1, query_key_value_weight) + b_qkv)
    queries = proj_qkv[:, :D].reshape(LEN, HEADS, HEAD)
    keys_pre = proj_qkv[:, D:2 * D].reshape(LEN, HEADS, HEAD)
    values_low = low(proj_qkv[:, 2 * D:].reshape(LEN, HEADS, HEAD))
    grid_rows = grid[0].astype(jnp.float32)[:, None, None]
    grid_cols = grid[1].astype(jnp.float32)[:, None, None]
    angle = grid_rows * rope_freqs[0][None] + grid_cols * rope_freqs[1][None]
    rot_q = low(rotate(queries, angle))
    rot_k = low(rotate(keys_pre, angle))
    scores = low_back(jnp.einsum('qhd,khd->hqk', rot_q, rot_k, precision=HIGH) * HEAD ** (-0.5))
    position = jnp.arange(LEN)
    allowed = (segment[:, None] == segment[None, :]) & (padding[None, :] == 0) | (position[:, None] == position[None, :])
    scores = jnp.where(allowed[None], scores, MASKED)
    attn_prob = low(jax.nn.softmax(scores, axis=-1))
    mixed_heads = jnp.einsum('hqk,khd->qhd', attn_prob, values_low, precision=HIGH).reshape(LEN, D)
    mixed_heads = low_back(low(mixed_heads))
    attended = low_back(matmul(mixed_heads, output_weight) + b_out)
    hidden = inputs + attended
    norm2 = low(layer_norm(hidden, ln2_gain, ln2_shift))
    pre_act = low_back(matmul(norm2, w_up) + b_up)
    activated = low(jax.nn.gelu(pre_act, approximate=False))
    return hidden + matmul(activated, w_down) + b_down

def reference(tokens, segment, padding, coords, ln1_gain, ln1_shift, query_key_value_weight, b_qkv, output_weight, b_out, rope_freqs, ln2_gain, ln2_shift, w_up, b_up, w_down, b_down, cotangent):
    unpacked_parameters = (ln1_gain, ln1_shift, query_key_value_weight, b_qkv, output_weight, b_out, rope_freqs, ln2_gain, ln2_shift, w_up, b_up, w_down, b_down)
    params = tuple((member.astype(jnp.float32) for member in unpacked_parameters))
    inputs = tokens.astype(jnp.float32)
    grid = jnp.moveaxis(coords, 0, 1)

    def forward(layer_in, layer_params):

        def one_sequence(items):
            return sequence(items[0], items[1], items[2], items[3], layer_params)
        return lax.map(jax.checkpoint(one_sequence), (layer_in, segment, padding, grid))
    outputs, pull = jax.vjp(forward, inputs, params)
    input_grad, grads = pull(cotangent.astype(jnp.float32))
    rot_sq = jnp.sum(grads[6] * grads[6])
    other_sq = jnp.zeros((), jnp.float32)
    for number in range(len(grads)):
        if number != 6:
            other_sq = other_sq + jnp.sum(grads[number] * grads[number])
    return (outputs.astype(jnp.bfloat16), input_grad, grads[0], grads[1], grads[2], grads[3], grads[4], grads[5], grads[6], grads[7], grads[8], grads[9], grads[10], grads[11], grads[12], rot_sq, other_sq)
```

```python
import functools

import jax
import jax.numpy as jnp
import numpy as np
from jax import lax
from jax.experimental import pallas as pl
from jax.experimental.pallas import tpu as pltpu
from jax.sharding import Mesh, PartitionSpec as P

EPS = 1e-06
MASKED = -1e30
BLK = 128
CHUNK = 256
GROUP = 4
REACH = 64
STAT_ROWS = 6
STAT_PAD = 16
SIDE = 32
LN1_GAIN, LN1_SHIFT, B_OUT, LN2_GAIN, LN2_SHIFT, B_DOWN = (slice(n, n + 1) for n in range(6))
BF = jnp.bfloat16
F32 = jnp.float32
PLANE = ("a", "b", "c")
SWAP = [(0, 1), (1, 0)]
VMEM_LIMIT = 56 * 1024 * 1024


def dot(left, right):
    return lax.dot_general(left, right, (((1,), (0,)), ((), ())), preferred_element_type=F32)


def dot_nt(left, right):
    return lax.dot_general(left, right, (((1,), (1,)), ((), ())), preferred_element_type=F32)


def dot_tn(left, right):
    return lax.dot_general(left, right, (((0,), (0,)), ((), ())), preferred_element_type=F32)


def params(**kw):
    return pltpu.CompilerParams(vmem_limit_bytes=VMEM_LIMIT, **kw)


def cost(us):
    return pl.CostEstimate(
        flops=int(us * 1.15e9), bytes_accessed=int(us * 3.0e6), transcendentals=0
    )


def whole(shape):
    return pl.BlockSpec(shape, lambda *_: (0,) * len(shape))


ANY = pl.BlockSpec(memory_space=pl.ANY)
SMEM = pl.BlockSpec(memory_space=pltpu.SMEM)


def rounded(x):
    return lax.reduce_precision(x, exponent_bits=8, mantissa_bits=7)


def turn_table(rope_freqs):
    lanes = rope_freqs.shape[1] * rope_freqs.shape[2]
    freq = rope_freqs.reshape(2, 1, lanes)
    angle = jnp.arange(SIDE, dtype=F32)[None, :, None] * freq
    cosine, sine = jnp.cos(angle), jnp.sin(angle)

    def halves(x):
        return jnp.concatenate([x.astype(BF), (x - rounded(x)).astype(BF)], 0)

    zero = jnp.zeros((2 * SIDE, 2 * lanes), BF)
    rows = jnp.concatenate([halves(cosine[0]), halves(sine[0]), zero], 1)
    cols = jnp.concatenate([zero, halves(cosine[1]), halves(sine[1])], 1)
    return jnp.concatenate([rows, cols], 0)


def cos_sin(onehot, table, lanes):
    parts = dot(onehot, table)
    cr, sr = parts[:, :lanes], parts[:, lanes : 2 * lanes]
    cc, sc = parts[:, 2 * lanes : 3 * lanes], parts[:, 3 * lanes :]
    return cr * cc - sr * sc, sr * cc + cr * sc


def layer_norm_low(x, gain, shift):
    centred = x - jnp.mean(x, -1, keepdims=True)
    var = jnp.mean(centred * centred, -1, keepdims=True)
    return (centred * lax.rsqrt(var + EPS) * gain + shift).astype(BF)


def project(norm, cosine, sine, weights, b_ref, q_out, k_out, v_ref, exact):
    width = norm.shape[1]
    for n, out in enumerate((q_out, k_out)):
        for g in range(width // 256):
            lo = n * width + 256 * g
            proj = dot(norm, weights[:, lo : lo + 256]) + b_ref[:, lo : lo + 256]
            c, s = cosine[:, 128 * g : 128 * g + 128], sine[:, 128 * g : 128 * g + 128]
            for half, turned in enumerate(
                (proj[:, :128] * c - proj[:, 128:] * s, proj[:, :128] * s + proj[:, 128:] * c)
            ):
                at = slice(256 * g + 128 * half, 256 * g + 128 * half + 128)
                out[:, at] = turned.astype(BF)
                if exact:
                    exact[n][:, at] = turned
    for g in range(width // 256):
        lo = 2 * width + 256 * g
        v_ref[:, 256 * g : 256 * g + 256] = (
            dot(norm, weights[:, lo : lo + 256]) + b_ref[:, lo : lo + 256]
        ).astype(BF)


def qkv_own_kernel(
    x_ref, hot_ref, vec_ref, w_ref, b_ref, order_ref, table_ref,
    q_ref, k_ref, v_ref, pq_ref, pk_ref, w_turned,
):
    width = x_ref.shape[1]

    @pl.when(pl.program_id(0) == 0)
    def _():
        for g in range(2 * width // 256):
            at = slice(256 * g, 256 * g + 256)
            w_turned[:, at] = dot(w_ref[:, at], order_ref[...]).astype(BF)
        w_turned[:, 2 * width :] = w_ref[:, 2 * width :]

    norm = layer_norm_low(x_ref[...].astype(F32), vec_ref[LN1_GAIN], vec_ref[LN1_SHIFT])
    cosine, sine = cos_sin(hot_ref[...], table_ref[...], width // 2)
    project(norm, cosine, sine, w_turned, b_ref, q_ref, k_ref, v_ref, (pq_ref, pk_ref))


def qkv_own_call(x, onehot, vectors, weight, bias, order, table, first):
    own, width = x.shape
    rows = onehot.shape[0]
    tile = 256
    shape = jax.ShapeDtypeStruct((rows, width), BF)
    exact = jax.ShapeDtypeStruct((own, width), F32)
    row = lambda w: pl.BlockSpec((tile, w), lambda i: (i, 0))
    inside = lambda w: pl.BlockSpec(
        (pl.Element(tile), pl.Element(w)), lambda i: (pl.multiple_of(first + tile * i, BLK), 0)
    )
    return pl.pallas_call(
        qkv_own_kernel,
        grid=(own // tile,),
        in_specs=[
            row(width),
            inside(onehot.shape[1]),
            whole(vectors.shape),
            whole(weight.shape),
            whole((1, 3 * width)),
            whole(order.shape),
            whole(table.shape),
        ],
        out_specs=[inside(width)] * 3 + [row(width)] * 2 + [whole(weight.shape)],
        out_shape=[shape] * 3 + [exact] * 2 + [jax.ShapeDtypeStruct(weight.shape, BF)],
        compiler_params=params(),
        cost_estimate=cost(8),
        name="qkv_own",
    )(x, onehot, vectors, weight, bias[None], order, table)


def qkv_halo_kernel(
    far_l, near_l, near_r, far_r, hot_ref, vec_ref, w_ref, b_ref, table_ref,
    q_in, k_in, v_in, q_ref, k_ref, v_ref, x_all, sem,
):
    width = x_all.shape[1]
    step = pl.program_id(0)
    tile = q_ref.shape[0]

    @pl.when(step == 0)
    def _():
        own, reach = near_l.shape[0], far_l.shape[0]
        total = x_all.shape[0]
        blank = total // 2 - own - reach
        copies = []
        at = blank
        for n, ref in enumerate((far_l, near_l, near_r, far_r)):
            copies.append(
                pltpu.make_async_copy(ref, x_all.at[at : at + ref.shape[0], :], sem.at[n])
            )
            copies[-1].start()
            at += ref.shape[0]
        x_all[:blank, :] = jnp.zeros((blank, width), BF)
        x_all[total - blank :, :] = jnp.zeros((blank, width), BF)
        for copy in copies:
            copy.wait()

    x = x_all[pl.ds(pl.multiple_of(step * tile, tile), tile), :].astype(F32)
    norm = layer_norm_low(x, vec_ref[LN1_GAIN], vec_ref[LN1_SHIFT])
    cosine, sine = cos_sin(hot_ref[...], table_ref[...], width // 2)
    project(norm, cosine, sine, w_ref, b_ref, q_ref, k_ref, v_ref, ())


def qkv_halo_call(pieces, onehot, vectors, weight, bias, table, q, k, v, first):
    rows, width = q.shape
    own = pieces[1].shape[0]
    tile = first // 2
    shape = jax.ShapeDtypeStruct((rows, width), BF)
    at = lambda w: pl.BlockSpec(
        (pl.Element(tile), pl.Element(w)), lambda i: (pl.multiple_of(tile * i + jnp.where(i >= 2, own, 0), 64), 0)
    )
    return pl.pallas_call(
        qkv_halo_kernel,
        grid=(4,),
        in_specs=[ANY] * 4
        + [
            at(onehot.shape[1]),
            whole(vectors.shape),
            whole(weight.shape),
            whole((1, 3 * width)),
            whole(table.shape),
        ]
        + [ANY] * 3,
        out_specs=[at(width)] * 3,
        out_shape=[shape] * 3,
        input_output_aliases={9: 0, 10: 1, 11: 2},
        scratch_shapes=[pltpu.VMEM((2 * first, width), BF), pltpu.SemaphoreType.DMA((4,))],
        compiler_params=params(),
        cost_estimate=cost(11.5),
        name="qkv_halo",
    )(*pieces, onehot, vectors, weight, bias[None], table, q, k, v)


def head_stack(block, turned, scale=None):
    lane = lax.broadcasted_iota(jnp.int32, block.shape, 1)
    head = (lane % 128) // 32 if turned else lane // 64
    if scale is not None:
        block = block * scale
    zero = jnp.zeros_like(block)
    return jnp.concatenate([jnp.where(head == h, block, zero) for h in range(GROUP)], 0)


def fold8(x, op):
    return op(x.reshape(x.shape[0] // 8, 8, x.shape[1]), axis=0)


def forward_kernel(
    bound_ref, q_ref, k_ref, v_ref, bias_ref, o_ref, low_ref, lse_ref, s_ref
):
    blocks = q_ref.shape[0] // BLK
    lanes = GROUP * BLK

    def one_block(i, _):
        rows = pl.ds(pl.multiple_of(i * BLK, BLK), BLK)
        q4 = head_stack(q_ref[rows, :], True, jnp.asarray(0.125, BF))
        start, count = bound_ref[i, 0], bound_ref[i, 1]

        def scores(c, top):
            at = pl.ds(pl.multiple_of((start + 2 * c) * BLK, BLK), CHUNK)
            s = dot_nt(k_ref[at, :], q4)
            here = pl.ds(pl.multiple_of(c * CHUNK, CHUNK), CHUNK)
            tops = []
            for h in range(GROUP):
                lo = h * BLK
                masked = s[:, lo : lo + BLK] + bias_ref[at, rows_lane(i)]
                s_ref[here, lo : lo + BLK] = masked
                tops.append(fold8(masked, jnp.max))
            return jnp.maximum(top, jnp.concatenate(tops, 1))

        top = lax.fori_loop(0, count, scores, jnp.full((8, lanes), -3e38, F32))
        top = jnp.max(top, 0, keepdims=True)

        def mix(c, state):
            total, acc = state
            at = pl.ds(pl.multiple_of((start + 2 * c) * BLK, BLK), CHUNK)
            here = pl.ds(pl.multiple_of(c * CHUNK, CHUNK), CHUNK)
            e = jnp.exp(s_ref[here, :] - top)
            return total + fold8(e, jnp.sum), acc + dot_tn(v_ref[at, :], e.astype(BF))

        total, acc = lax.fori_loop(
            0, count, mix, (jnp.zeros((8, lanes), F32), jnp.zeros((256, lanes), F32))
        )
        total = jnp.sum(total, 0, keepdims=True)
        lse_ref[0, pl.ds(i, 1), :] = top + jnp.log(total)
        acc = acc / total
        out = jnp.concatenate(
            [acc[64 * h : 64 * h + 64, BLK * h : BLK * h + BLK] for h in range(GROUP)], 0
        )
        out = out.T
        o_ref[rows, :] = out
        low_ref[rows, :] = out.astype(BF)
        return 0

    def rows_lane(i):
        return pl.ds(pl.multiple_of(i * BLK, BLK), BLK)

    lax.fori_loop(0, blocks, one_block, 0)


def own_rows(own, first, base=0):
    return pl.BlockSpec((pl.Element(own), pl.Element(256)), lambda g: (first, 256 * (base + g)))


def forward_call(bounds, q_win, k_win, v_win, bias, first):
    win, width = k_win.shape
    own = bias.shape[1]
    groups = width // 256
    blocks = own // BLK
    tile = lambda n: pl.BlockSpec((n, 256), lambda g: (0, g))
    return pl.pallas_call(
        forward_kernel,
        grid=(groups,),
        in_specs=[SMEM, own_rows(own, first), tile(win), tile(win), whole(bias.shape)],
        out_specs=[tile(own), tile(own), pl.BlockSpec((1, blocks, GROUP * BLK), lambda g: (g, 0, 0))],
        out_shape=[
            jax.ShapeDtypeStruct((own, width), F32),
            jax.ShapeDtypeStruct((own, width), BF),
            jax.ShapeDtypeStruct((groups, blocks, GROUP * BLK), F32),
        ],
        scratch_shapes=[pltpu.VMEM((win, GROUP * BLK), F32)],
        compiler_params=params(),
        cost_estimate=cost(17.5),
        name="attention_forward",
    )(bounds, q_win, k_win, v_win, bias)


def backward_own_kernel(
    bound_ref, q_ref, do_ref, k_ref, v_ref, bias_ref, lse_ref, delta_ref,
    dq_ref, dk_ref, dv_ref, dk_acc, dv_acc, *, first,
):
    blocks = q_ref.shape[0] // BLK
    lanes = GROUP * BLK
    dk_acc[...] = jnp.zeros_like(dk_acc)
    dv_acc[...] = jnp.zeros_like(dv_acc)

    def one_block(i, _):
        rows = pl.ds(pl.multiple_of(i * BLK, BLK), BLK)
        q4 = head_stack(q_ref[rows, :], True, jnp.asarray(0.125, BF))
        do4 = head_stack(do_ref[rows, :], False)
        lse = lse_ref[0, pl.ds(i, 1), :]
        delta = delta_ref[0, pl.ds(i, 1), :]
        start, count = bound_ref[i, 0], bound_ref[i, 1]

        def step(c, acc):
            block = start + 2 * c
            at = pl.ds(pl.multiple_of(block * BLK, BLK), CHUNK)
            keys = k_ref[at, :]
            s = dot_nt(keys, q4)
            dp = dot_nt(v_ref[at, :], do4)
            bias = bias_ref[at, rows]
            low_p, low_ds = [], []
            for h in range(GROUP):
                lo = h * BLK
                p = jnp.exp(s[:, lo : lo + BLK] + bias - lse[:, lo : lo + BLK])
                low_p.append(p.astype(BF))
                low_ds.append((p * (dp[:, lo : lo + BLK] - delta[:, lo : lo + BLK])).astype(BF))
            low_p, low_ds = jnp.concatenate(low_p, 1), jnp.concatenate(low_ds, 1)

            @pl.when((block + 1 >= first) & (block < first + blocks))
            def _():
                dk_acc[at, :] += dot(low_ds, q4)
                dv_acc[at, :] += dot(low_p, do4)

            return acc + dot_tn(keys, low_ds)

        acc = lax.fori_loop(0, count, step, jnp.zeros((256, lanes), F32))
        parts = [acc[32 * h : 32 * h + 32, BLK * h : BLK * h + BLK] for h in range(GROUP)]
        parts += [acc[128 + 32 * h : 160 + 32 * h, BLK * h : BLK * h + BLK] for h in range(GROUP)]
        dq_ref[rows, :] = (jnp.concatenate(parts, 0) * 0.125).T
        return 0

    lax.fori_loop(0, blocks, one_block, 0)
    dk_ref[...] = dk_acc[first * BLK : (first + blocks) * BLK, :]
    dv_ref[...] = dv_acc[first * BLK : (first + blocks) * BLK, :]


def backward_own_call(bounds, q_win, do_own, k_win, v_win, bias, lse, delta, first, base, groups):
    own, width = bias.shape[1], 256 * groups
    win = k_win.shape[0]
    blocks = own // BLK
    tile = lambda n: pl.BlockSpec((n, 256), lambda g: (0, base + g))
    out = pl.BlockSpec((own, 256), lambda g: (0, g))
    stat = pl.BlockSpec((1, blocks, GROUP * BLK), lambda g: (base + g, 0, 0))
    return pl.pallas_call(
        functools.partial(backward_own_kernel, first=first // BLK),
        grid=(groups,),
        in_specs=[SMEM, own_rows(own, first, base), tile(own), tile(win), tile(win)]
        + [whole(bias.shape), stat, stat],
        out_specs=[out] * 3,
        out_shape=[jax.ShapeDtypeStruct((own, width), F32)] * 3,
        scratch_shapes=[pltpu.VMEM((win, 256), F32)] * 2,
        compiler_params=params(),
        cost_estimate=cost(9.5 * groups),
        name="attention_backward_own",
    )(bounds, q_win, do_own, k_win, v_win, bias, lse, delta)


def backward_halo_kernel(
    bound_ref, q_ref, far_l, near_l, near_r, far_r, k_ref, v_ref, bias_ref, *refs, first, splits
):
    d_in = refs[: 2 * splits]
    dk_ref, dv_ref, stat_ref = refs[2 * splits :]
    own, reach = k_ref.shape[0], far_l.shape[0] - STAT_PAD
    group = pl.program_id(0)
    base = 0
    for n in range(splits):
        size = (1, 2)[n]

        @pl.when((group >= base) & (group < base + size))
        def _():
            dk_ref[...] = d_in[n][...]
            dv_ref[...] = d_in[splits + n][...]

        base += size

    def stats(ref, row):
        parts = ref[row : row + 2 * STAT_ROWS, :].astype(F32)
        whole_row = parts[0:4] + parts[4:8] + parts[8:12]
        return [
            jnp.concatenate([whole_row[2 * n : 2 * n + 1], whole_row[2 * n + 1 : 2 * n + 2]], 1)
            for n in range(2)
        ]

    def one_block(j, block, ref, row, low, high):
        start, count = bound_ref[j, 0], bound_ref[j, 1]

        @pl.when(count > 0)
        def _():
            q4 = head_stack(q_ref[j * BLK : (j + 1) * BLK, :], True, jnp.asarray(0.125, BF))
            gone = jnp.zeros((BLK - (high - low), 256), BF)
            here = ref[row : row + high - low, :]
            if low:
                here = jnp.concatenate([gone, here], 0)
            elif high < BLK:
                here = jnp.concatenate([here, gone], 0)
            do4 = head_stack(here, False)
            size = ref.shape[0] - (STAT_PAD if high - low < BLK else own // BLK * 2 * STAT_ROWS)
            lse, delta = stats(ref, size + (block * 2 * STAT_ROWS))

            def step(c, _):
                at = pl.ds(pl.multiple_of((start + 2 * c) * BLK, BLK), CHUNK)
                s = dot_nt(k_ref[at, :], q4)
                dp = dot_nt(v_ref[at, :], do4)
                bias = bias_ref[at, j * BLK : (j + 1) * BLK]
                low_p, low_ds = [], []
                for h in range(GROUP):
                    lo = h * BLK
                    p = jnp.exp(s[:, lo : lo + BLK] + bias - lse[:, lo : lo + BLK])
                    low_p.append(p.astype(BF))
                    low_ds.append((p * (dp[:, lo : lo + BLK] - delta[:, lo : lo + BLK])).astype(BF))
                dk_ref[at, :] += dot(jnp.concatenate(low_ds, 1), q4)
                dv_ref[at, :] += dot(jnp.concatenate(low_p, 1), do4)
                return 0

            lax.fori_loop(0, count, step, 0)

    blocks = own // BLK
    one_block(0, 0, far_l, 0, BLK - reach, BLK)
    for i in range(blocks):
        one_block(1 + i, i, near_l, i * BLK, 0, BLK)
        one_block(first + blocks + i, i, near_r, i * BLK, 0, BLK)
    one_block(first + 2 * blocks, 0, far_r, 0, 0, reach)


def backward_halo_call(bounds, q_win, pieces, k_win, v_win, bias, dks, dvs, first):
    own = dks[0].shape[0]
    win, width = q_win.shape
    groups = width // 256
    tile = lambda n: pl.BlockSpec((n, 256), lambda g: (0, g))
    splits = len(dks)
    d_spec = [
        pl.BlockSpec((own, 256), lambda g: (0, 0)),
        pl.BlockSpec((own, 256), lambda g: (0, jnp.maximum(g - 1, 0))),
    ]
    return pl.pallas_call(
        functools.partial(backward_halo_kernel, first=first // BLK, splits=splits),
        grid=(groups,),
        in_specs=[SMEM, tile(win)]
        + [tile(p.shape[0]) for p in pieces]
        + [own_rows(own, first)] * 2
        + [whole(bias.shape)]
        + d_spec * 2,
        out_specs=[tile(own)] * 2,
        out_shape=[jax.ShapeDtypeStruct((own, width), F32)] * 2,
        scratch_shapes=[pltpu.VMEM((8, 128), F32)],
        compiler_params=params(),
        cost_estimate=cost(9),
        name="attention_backward_halo",
    )(bounds, q_win, *pieces, k_win, v_win, bias, *dks, *dvs)


def norm_parts(x):
    centred = x - jnp.mean(x, -1, keepdims=True)
    inverse = lax.rsqrt(jnp.mean(centred * centred, -1, keepdims=True) + EPS)
    return centred * inverse, inverse


def norm_back(grad, xhat, inverse, gain):
    scaled = grad * gain
    return inverse * (
        scaled
        - jnp.mean(scaled, -1, keepdims=True)
        - xhat * jnp.mean(scaled * xhat, -1, keepdims=True)
    )


def columns_sum(x):
    return jnp.sum(x, 0, keepdims=True)


def slices_out(place, source, keep, away, lead, sem, slices, rows):
    for n in range(slices):
        rel = place ^ n
        for target, odd in ((keep, 0), (away, 1)):

            @pl.when(rel % 2 == odd)
            def _():
                pltpu.make_async_copy(
                    source.at[n * rows : (n + 1) * rows, :],
                    target.at[rel // 2, pl.ds(lead, rows), :],
                    sem.at[n],
                ).start()


def slices_wait(source, keep, sem, slices, rows):
    for n in range(slices):
        pltpu.make_async_copy(
            source.at[n * rows : (n + 1) * rows, :], keep.at[0, 0:rows, :], sem.at[n]
        ).wait()


def one_quarter(q, w_all, norm_ref, dy_ref, bu_ref, dbu_ref, out_acc, dn_acc, g_all, fresh):
    own, width = norm_ref.shape
    tile = 256
    for t in range((w_all.shape[1] - width) // tile):
        cols = slice(tile * t, tile * t + tile)
        down = slice(width + tile * t, width + tile * t + tile)
        norm, dy = norm_ref[...], dy_ref[...]
        up_w = w_all[q, :width, cols]
        down_w = w_all[q, down, :]
        pre = dot(norm, up_w) + bu_ref[pl.ds(q, 1), cols]
        cdf = 0.5 * (1.0 + lax.erf(pre * np.float32(0.7071067811865476)))
        density = jnp.exp(-0.5 * pre * pre) * np.float32(0.3989422804014327)
        act = (pre * cdf).astype(BF)
        d_pre = (dot_nt(dy, down_w) * (cdf + pre * density)).astype(BF)
        dbu_ref[pl.ds(q, 1), cols] = columns_sum(d_pre.astype(F32))
        if fresh and t == 0:
            out_acc[...] = dot(act, down_w)
            dn_acc[...] = dot_nt(d_pre, up_w)
        else:
            out_acc[...] += dot(act, down_w)
            dn_acc[...] += dot_nt(d_pre, up_w)
        g_all[q, :width, cols] = dot_tn(norm, d_pre).astype(BF)
        g_all[q, down, :] = dot_tn(act, dy).astype(BF)


def middle_own_kernel(
    place_ref, x_ref, low_ref, wo_ref, vec_ref, dy_ref, bu_ref, up_ref, down_ref,
    hid_ref, norm_ref, out_ref, dn_ref, dbu_ref, keep_ref, send_ref, w_all, g_all, w_sem, g_sem,
    *, slices,
):
    width = x_ref.shape[1]
    rows = w_all.shape[1] // slices
    copies = [
        pltpu.make_async_copy(up_ref, w_all.at[0, :width, :], w_sem.at[0]),
        pltpu.make_async_copy(down_ref, w_all.at[0, width:, :], w_sem.at[1]),
    ]
    for copy in copies:
        copy.start()
    hidden_in = x_ref[...].astype(F32) + dot(low_ref[...], wo_ref[...]) + vec_ref[B_OUT]
    hid_ref[...] = hidden_in
    norm_ref[...] = layer_norm_low(hidden_in, vec_ref[LN2_GAIN], vec_ref[LN2_SHIFT])
    for copy in copies:
        copy.wait()
    one_quarter(0, w_all, norm_ref, dy_ref, bu_ref, dbu_ref, out_ref, dn_ref, g_all, True)
    slices_out(place_ref[0], g_all.at[0], keep_ref, send_ref, 0, g_sem, slices, rows)
    slices_wait(g_all.at[0], keep_ref, g_sem, slices, rows)


def middle_own_call(place, x, low, w_out, vectors, dy, b_up, w_up, w_down, slices):
    own, width = x.shape
    hidden = b_up.shape[1]
    rows = width + hidden
    vmem = pl.BlockSpec(memory_space=pltpu.VMEM)
    sds = jax.ShapeDtypeStruct
    return pl.pallas_call(
        functools.partial(middle_own_kernel, slices=slices),
        in_specs=[SMEM] + [vmem] * 6 + [ANY] * 2,
        out_specs=[vmem] * 5 + [ANY] * 2,
        out_shape=[
            sds((own, width), F32),
            sds((own, width), BF),
            sds((own, width), F32),
            sds((own, width), F32),
            sds((1, hidden), F32),
        ]
        + [sds((slices // 2, rows // slices, width), BF)] * 2,
        scratch_shapes=[
            pltpu.VMEM((1, rows, width), BF),
            pltpu.VMEM((1, rows, width), BF),
            pltpu.SemaphoreType.DMA((2,)),
            pltpu.SemaphoreType.DMA((slices,)),
        ],
        compiler_params=params(),
        cost_estimate=cost(12),
        name="middle_own",
    )(place, x, low, w_out, vectors, dy, b_up, w_up, w_down)


def middle_kernel(
    place_ref, hid_ref, norm_ref, out_in, dn_in, low_ref, mixed_ref, wo_ref, vec_ref, dy_ref,
    bu_ref, lse_ref, *refs, slices,
):
    piece_refs = refs[:10]
    (
        act_ref, dh_ref, dheads_ref, head_ref, tail_ref, delta_ref, small_ref, dbu_ref,
        keep_ref, send_ref, w_all, g_all, go_all, out_acc, dn_acc, w_sem, g_sem,
    ) = refs[10:]
    place = place_ref[0]
    own, width = norm_ref.shape
    quarters = w_all.shape[0]
    rows = w_all.shape[1] // slices
    part = rows // 2

    def fetches(q):
        copies = []
        for n in range(slices):
            for half in range(2):
                at = pl.multiple_of((place ^ n) * rows + half * part, part)
                copies.append(
                    pltpu.make_async_copy(
                        pieces_of(piece_refs, n, half).at[q],
                        w_all.at[q, pl.ds(at, part), :],
                        w_sem.at[q, 2 * n + half],
                    )
                )
        return copies

    for q in range(quarters):
        for copy in fetches(q):
            copy.start()
    out_acc[...] = out_in[...]
    dn_acc[...] = dn_in[...]

    def quarter(q, _):
        for copy in fetches(q):
            copy.wait()
        one_quarter(q, w_all, norm_ref, dy_ref, bu_ref, dbu_ref, out_acc, dn_acc, g_all, False)
        slices_out(
            place, g_all.at[q], keep_ref, send_ref, pl.multiple_of(q * rows, rows), g_sem.at[q],
            slices, rows,
        )
        return 0

    lax.fori_loop(0, quarters, quarter, 0)

    hidden_in = hid_ref[...]
    act_ref[...] = (hidden_in + out_acc[...] + vec_ref[B_DOWN]).astype(BF)
    xhat, inverse = norm_parts(hidden_in)
    dn = dn_acc[...]
    dy = dy_ref[...].astype(F32)
    d_hidden = dy + norm_back(dn, xhat, inverse, vec_ref[LN2_GAIN])
    dh_ref[...] = d_hidden
    d_att = d_hidden.astype(BF)
    small_ref[0:1, :] = columns_sum(dn * xhat)
    small_ref[1:2, :] = columns_sum(dn)
    small_ref[2:3, :] = columns_sum(dy)
    small_ref[3:4, :] = columns_sum(d_att.astype(F32))
    d_heads = dot_nt(d_att, wo_ref[...]).astype(BF)
    dheads_ref[:own, :] = d_heads
    spread = d_heads.astype(F32) * mixed_ref[...]
    pick = lax.broadcasted_iota(jnp.int32, (8, 256), 0)
    pick = (pick == lax.broadcasted_iota(jnp.int32, (8, 256), 1) // 64).astype(F32)
    for g in range(width // 256):
        for i in range(own // BLK):
            block = spread[BLK * i : BLK * i + BLK, 256 * g : 256 * g + 256]
            sums = lax.dot_general(
                pick, block, (((1,), (1,)), ((), ())),
                preferred_element_type=F32, precision=lax.Precision.HIGHEST,
            )
            delta = jnp.concatenate([sums[h : h + 1, :] for h in range(GROUP)], 1)
            delta_ref[g, i : i + 1, :] = delta
            lse = lse_ref[g, i : i + 1, :]
            left = jnp.concatenate(
                [lse[:, :256], lse[:, 256:], delta[:, :256], delta[:, 256:]], 0
            )
            parts = []
            for _ in range(3):
                parts.append(left.astype(BF))
                left = left - parts[-1].astype(F32)
            parts = jnp.concatenate(parts, 0)
            at = slice(256 * g, 256 * g + 256)
            lo = own + 2 * STAT_ROWS * i
            dheads_ref[lo : lo + 2 * STAT_ROWS, at] = parts
            for target, row in ((head_ref, 0), (tail_ref, own // BLK - 1)):
                if i == row:
                    target[REACH : REACH + 2 * STAT_ROWS, at] = parts
    blank = jnp.zeros((STAT_PAD - 2 * STAT_ROWS, width), BF)
    head_ref[REACH + 2 * STAT_ROWS :, :] = blank
    tail_ref[REACH + 2 * STAT_ROWS :, :] = blank
    head_ref[:REACH, :] = d_heads[:REACH, :]
    tail_ref[:REACH, :] = d_heads[own - REACH :, :]
    go_all[...] = dot_tn(low_ref[...], d_att).astype(BF)
    few = width // slices
    slices_out(place, go_all, keep_ref, send_ref, quarters * rows, g_sem.at[quarters], slices, few)
    for q in range(quarters):
        slices_wait(g_all.at[q], keep_ref, g_sem.at[q], slices, rows)
    slices_wait(go_all, keep_ref, g_sem.at[quarters], slices, few)


def middle_call(
    place, hidden_in, norm, out, dn, low, mixed, w_out, vectors, dy, b_up, lse, pieces, slices
):
    own, width = norm.shape
    quarters, hidden = b_up.shape
    rows = width + hidden
    vmem = pl.BlockSpec(memory_space=pltpu.VMEM)
    sds = jax.ShapeDtypeStruct
    grads = sds((slices // 2, (quarters * rows + width) // slices, width), BF)
    return pl.pallas_call(
        functools.partial(middle_kernel, slices=slices),
        in_specs=[SMEM] + [vmem] * 11 + [ANY] * len(pieces),
        out_specs=[vmem] * 8 + [ANY] * 2,
        out_shape=[
            sds((own, width), BF),
            sds((own, width), F32),
            sds((own + own // BLK * 2 * STAT_ROWS, width), BF),
            sds((REACH + STAT_PAD, width), BF),
            sds((REACH + STAT_PAD, width), BF),
            sds((width // 256, own // BLK, GROUP * BLK), F32),
            sds((4, width), F32),
            sds((quarters, hidden), F32),
            grads,
            grads,
        ],
        scratch_shapes=[
            pltpu.VMEM((quarters, rows, width), BF),
            pltpu.VMEM((quarters, rows, width), BF),
            pltpu.VMEM((width, width), BF),
            pltpu.VMEM((own, width), F32),
            pltpu.VMEM((own, width), F32),
            pltpu.SemaphoreType.DMA((quarters, 2 * slices)),
            pltpu.SemaphoreType.DMA((quarters + 1, slices)),
        ],
        compiler_params=params(),
        cost_estimate=cost(26),
        name="middle",
    )(place, hidden_in, norm, out, dn, low, mixed, w_out, vectors, dy, b_up, lse, *pieces)


def turn_back_kernel(
    place_ref, x_ref, vec_ref, dq0_ref, dq1_ref, dk_ref, dv_ref, q_ref, k_ref, hot_ref,
    table_ref, grid_ref, back_ref,
    d_ref, db_ref, freq_ref, keep_ref, send_ref, g_all, sem, *, slices,
):
    rows, width = dk_ref.shape
    norm = layer_norm_low(x_ref[...].astype(F32), vec_ref[LN1_GAIN], vec_ref[LN1_SHIFT])
    cosine, sine = cos_sin(hot_ref[...], table_ref[...], width // 2)

    def gradient(at, low):
        d_ref[:, at] = low
        db_ref[:, at] = columns_sum(low.astype(F32))
        g_all[:, at] = dot_tn(norm, low).astype(BF)

    for g in range(width // 256):
        c, s = cosine[:, 128 * g : 128 * g + 128], sine[:, 128 * g : 128 * g + 128]
        d_angle = jnp.zeros((rows, 128), F32)
        for n, (grad, turned_ref) in enumerate(((dq1_ref if g else dq0_ref, q_ref), (dk_ref, k_ref))):
            lo = 256 * (g - 1) if g and n == 0 else 256 * g
            g1, g2 = grad[:, lo : lo + 128], grad[:, lo + 128 : lo + 256]
            p1 = turned_ref[:, 256 * g : 256 * g + 128]
            p2 = turned_ref[:, 256 * g + 128 : 256 * g + 256]
            d_angle = d_angle + (g2 * p1 - g1 * p2)
            back = jnp.concatenate([g1 * c + g2 * s, g2 * c - g1 * s], 1).astype(BF)
            at = slice(n * width + 256 * g, n * width + 256 * g + 256)
            gradient(at, dot(back, back_ref[...]).astype(BF))
        freq_ref[:, 128 * g : 128 * g + 128] = lax.dot_general(
            grid_ref[...], d_angle, (((1,), (0,)), ((), ())),
            preferred_element_type=F32, precision=lax.Precision.HIGHEST,
        )
        at = slice(256 * g, 256 * g + 256)
        gradient(slice(2 * width + 256 * g, 2 * width + 256 * g + 256), dv_ref[:, at].astype(BF))
    slices_out(place_ref[0], g_all, keep_ref, send_ref, 0, sem, slices, width // slices)
    slices_wait(g_all, keep_ref, sem, slices, width // slices)


def turn_back_call(
    place, x, vectors, dqs, dk, dv, q_exact, k_exact, onehot, table, grid8, back, first, slices
):
    rows, width = dk.shape
    vmem = pl.BlockSpec(memory_space=pltpu.VMEM)
    sds = jax.ShapeDtypeStruct
    return pl.pallas_call(
        functools.partial(turn_back_kernel, slices=slices),
        in_specs=[SMEM] + [vmem] * 12,
        out_specs=[vmem] * 3 + [ANY] * 2,
        out_shape=[
            sds((rows, 3 * width), BF),
            sds((1, 3 * width), F32),
            sds((8, width // 2), F32),
        ]
        + [sds((slices // 2, width // slices, 3 * width), BF)] * 2,
        scratch_shapes=[
            pltpu.VMEM((width, 3 * width), BF),
            pltpu.SemaphoreType.DMA((slices,)),
        ],
        compiler_params=params(),
        cost_estimate=cost(11),
        name="turn_back",
    )(
        place, x, vectors, *dqs, dk, dv, q_exact, k_exact,
        onehot[first : first + rows], table, grid8, back,
    )


def input_grad_kernel(x_ref, vec_ref, d_ref, w_ref, dh_ref, out_ref, small_ref):
    d_norm = dot_nt(d_ref[...], w_ref[...])
    xhat, inverse = norm_parts(x_ref[...].astype(F32))
    small_ref[0:1, :] = columns_sum(d_norm * xhat)
    small_ref[1:2, :] = columns_sum(d_norm)
    out_ref[...] = dh_ref[...] + norm_back(d_norm, xhat, inverse, vec_ref[LN1_GAIN])


def input_grad_call(x, vectors, d_qkv, weight, d_hidden):
    rows, width = x.shape
    return pl.pallas_call(
        input_grad_kernel,
        out_shape=[
            jax.ShapeDtypeStruct((rows, width), F32),
            jax.ShapeDtypeStruct((2, width), F32),
        ],
        compiler_params=params(),
        cost_estimate=cost(7),
        name="input_grad",
    )(x, vectors, d_qkv, weight, d_hidden)


def assemble_kernel(place_ref, *refs, split, outs):
    piece_refs, out_refs = refs[:10], refs[10 : 10 + len(outs)]
    held, sem = refs[10 + len(outs) :]
    place, depth = place_ref[0], place_ref[1]
    pieces = held.shape[0]
    slot = pl.program_id(0)

    def copy(n, half, target):
        return pltpu.make_async_copy(
            pieces_of(piece_refs, n, half), held.at[target, half], sem.at[target, half]
        )

    @pl.when(slot == 0)
    def _():
        for n in range(pieces):
            for half in range(2):
                copy(n, half, place ^ n).start()

    for half in range(2):
        copy(0, half, slot).wait()
    rows = held.shape[-2]
    if split:
        for rel in range(split):
            block = held[slot, rel // (split // 2), rel % (split // 2)].astype(F32)
            at = ((depth - rel + split) % split) * rows
            lo = 0
            for ref in out_refs:
                ref[pl.ds(pl.multiple_of(at, 8), rows), :] = block[:, lo : lo + ref.shape[1]]
                lo += ref.shape[1]
    else:
        each = pieces // len(out_refs)
        for n, ref in enumerate(out_refs):

            @pl.when(slot // each == n)
            def _():
                for half in range(2):
                    ref[half * rows : half * rows + rows, :] = held[slot, half].astype(F32)


def assemble_call(place, arrays, shapes, split):
    pieces = 8
    rows = arrays[0].shape[-2] * max(split, 2)
    each = pieces if split else pieces // len(shapes)

    def spec(n, shape):
        lead = 0 if split else n * each
        return pl.BlockSpec((rows, shape[1]), lambda i: (jnp.clip(i - lead, 0, each - 1), 0))

    return pl.pallas_call(
        functools.partial(assemble_kernel, split=split, outs=shapes),
        grid=(pieces,),
        in_specs=[SMEM] + [ANY] * len(arrays),
        out_specs=[spec(n, shape) for n, shape in enumerate(shapes)],
        out_shape=[jax.ShapeDtypeStruct(s, F32) for s in shapes],
        scratch_shapes=[
            pltpu.VMEM((pieces,) + arrays[0].shape, BF),
            pltpu.SemaphoreType.DMA((pieces, 2)),
        ],
        compiler_params=params(),
        cost_estimate=cost(6),
        name="assemble",
    )(place, *arrays)


def send(x, axis, pairs):
    return lax.ppermute(x, axis, pairs)


def plane_gather(halves):
    over_b = send(halves, "b", SWAP)
    over_a = send(halves, "a", SWAP)
    near = [halves, over_b, over_a, send(over_b[0], "a", SWAP), send(over_a[1], "b", SWAP)]
    return near + [send(x, "c", SWAP) for x in near]


def pieces_of(refs, rel, half):
    refs = refs[5 * (rel % 2) : 5 * (rel % 2) + 5]
    return refs[3 + half] if rel // 2 == 3 else refs[rel // 2].at[half]


def wide_sum(x, extra):
    return lax.psum(x, "e") if extra > 1 else x


def sum_low(*terms):
    return functools.reduce(lambda x, y: x + y, [t.astype(F32) for t in terms])


def plane_scatter(kept, far, extra):
    chip = [sum_low(kept[n], far[n]).astype(BF) for n in range(4)]
    over_b = send(chip[1], "b", SWAP)
    over_a = send(chip[2], "a", SWAP)
    diagonal = send(chip[3], ("a", "b"), [(0, 3), (1, 2), (2, 1), (3, 0)])
    return chip, (chip[0], over_b, over_a, diagonal)


def split_scatter(kept, far):
    mid = kept.shape[1] // 2
    part = lambda n, half: sum_low(*(x[n, half * mid : half * mid + mid] for x in (kept, far)))
    over_b = jnp.stack([part(1, 0), part(3, 0)]).astype(BF)
    over_a = jnp.stack([part(2, 1), part(3, 1)]).astype(BF)
    rest = [part(0, 0), part(2, 0), part(0, 1), part(1, 1)]
    rest = [x.astype(BF) for x in rest]
    return (over_b, over_a, rest), (send(over_b, "b", SWAP), send(over_a, "a", SWAP))


def split_scatter_on(rest, got_b, got_a):
    on_a = sum_low(rest[1], got_b[1]).astype(BF)
    on_b = sum_low(rest[3], got_a[1]).astype(BF)
    return (on_a, on_b), (send(on_a, "a", SWAP), send(on_b, "b", SWAP))


def split_scatter_end(rest, got_b, got_a, got2_a, got2_b):
    return jnp.concatenate(
        [sum_low(rest[0], got_b[0], got2_a), sum_low(rest[2], got_a[0], got2_b)], 0
    )


def after(x, *others):
    return lax.optimization_barrier((x, others))[0]


def ring(size, step):
    return [(i, (i + step) % size) for i in range(size)]


def sum_all(vector, depth, extra):
    for axis in ("c", "b", "a"):
        vector = vector + send(vector, axis, SWAP)
    if extra > 1:
        vector = lax.psum(vector, "e")
    reach = 1
    while reach < depth:
        vector = vector + send(vector, "n", [(i, i ^ reach) for i in range(depth)])
        reach *= 2
    return vector


def on_device(
    tokens,
    segment,
    padding,
    coords,
    ln1_gain,
    ln1_shift,
    query_key_value_weight,
    b_qkv,
    output_weight,
    b_out,
    rope_freqs,
    ln2_gain,
    ln2_shift,
    w_up,
    b_up,
    w_down,
    b_down,
    cotangent,
    *,
    extra,
    depth,
):
    tokens, cotangent = tokens[0], cotangent[0]
    own, width = tokens.shape
    length = own * depth
    heads = rope_freqs.shape[1]
    half = width // heads // 2
    groups = heads // GROUP
    slices = 8
    outer = BLK
    side = own + outer
    win = own + 2 * side
    blocks = own // BLK
    z = lax.axis_index("n")
    plane = lax.axis_index("a") * 4 + lax.axis_index("b") * 2 + lax.axis_index("c")
    place = jnp.stack([plane, z]).astype(jnp.int32)
    up = [(i, i + 1) for i in range(depth - 1)]
    down = [(i + 1, i) for i in range(depth - 1)]
    up2 = [(i, i + 2) for i in range(depth - 2)]
    down2 = [(i + 2, i) for i in range(depth - 2)]

    def around(x, head, tail):
        before2 = send(tail, "n", up2)
        before = send(x, "n", up)
        after_ = send(x, "n", down)
        after2 = send(head, "n", down2)
        return [before2, before, after_, after2]

    position = jnp.arange(length, dtype=jnp.int32)
    ident = jnp.where(padding[0] == 0, segment[0], 1000 + position)
    ident = jnp.pad(ident, (side, side), constant_values=-1)
    ident_win = lax.dynamic_slice_in_dim(ident, z * own, win, 0)
    near = lax.broadcasted_iota(jnp.int32, (win,), 0)
    ident_win = jnp.where((near < outer - REACH) | (near >= win - outer + REACH), -1, ident_win)
    ident_own = lax.dynamic_slice_in_dim(ident, z * own + side, own, 0)
    seen = ident_win[:, None] == ident_own[None, :]
    bias_fwd = jnp.where(seen, 0.0, MASKED).astype(F32)
    bias_bwd = jnp.where(ident_own[:, None] == ident_win[None, :], 0.0, MASKED).astype(F32)
    touch = jnp.any(seen.reshape(win // BLK, BLK, blocks, BLK), (1, 3))

    def bounds(hit):
        size = hit.shape[1]
        lo = jnp.argmax(hit, 1).astype(jnp.int32)
        hi = size - jnp.argmax(hit[:, ::-1], 1).astype(jnp.int32)
        count = jnp.where(jnp.any(hit, 1), (hi - lo + 1) // 2, 0)
        return jnp.stack([jnp.minimum(lo, size - 2 * count), count], 1).astype(jnp.int32)

    bounds_fwd = bounds(touch.T)
    outside = (jnp.arange(win // BLK) < side // BLK) | (jnp.arange(win // BLK) >= side // BLK + blocks)
    bounds_bwd = bounds(touch) * outside[:, None].astype(jnp.int32)

    grid = jnp.pad(coords[:, 0], ((0, 0), (side, side)))
    grid_win = lax.dynamic_slice_in_dim(grid, z * own, win, 1)
    grid_own = lax.dynamic_slice_in_dim(grid, z * own + side, own, 1)
    lane = jnp.arange(4 * SIDE)
    picked = jnp.where(lane[None, :] < 2 * SIDE, grid_win[0][:, None], grid_win[1][:, None])
    onehot = (picked == (lane % SIDE)[None, :]).astype(BF)
    table = turn_table(rope_freqs)

    local = np.arange(256)
    order = np.zeros((256, 256), np.float32)
    order[(local % 128) // 32 * 64 + local // 128 * 32 + local % 32, local] = 1.0
    order = jnp.asarray(order, BF)
    qk_bias = b_qkv[: 2 * width].reshape(2 * groups, GROUP, 2, half).swapaxes(1, 2)
    bias_turned = jnp.concatenate([qk_bias.reshape(-1), b_qkv[2 * width :]])

    x_parts = around(tokens, tokens[:REACH], tokens[own - REACH :])
    vectors = jnp.stack([ln1_gain, ln1_shift, b_out, ln2_gain, ln2_shift, b_down])
    rot_q, rot_k, values, q_exact, k_exact, weight_turned = qkv_own_call(
        tokens, onehot, vectors, query_key_value_weight, bias_turned, order, table, side
    )

    rows = (width + w_down.shape[0]) // slices
    eighth = jnp.where(
        plane < width // rows,
        lax.dynamic_slice_in_dim(w_up, jnp.minimum(plane * rows, width - rows), rows, 0),
        lax.dynamic_slice_in_dim(w_down, jnp.maximum(plane * rows - width, 0), rows, 0),
    )
    left, bias_rows = b_up, []
    for _ in range(3):
        bias_rows.append(left.astype(BF))
        left = left - rounded(left)
    bias_rows = jnp.pad(jnp.stack(bias_rows), ((0, 13), (0, 0)))
    eighth = jnp.concatenate([eighth, bias_rows], 0)
    others = [send(eighth, "n", ring(depth, k)) for k in range(1, depth)]
    ready = (bias_fwd, bias_bwd, bounds_fwd, bounds_bwd, rot_q)
    x_parts, ready = lax.optimization_barrier((x_parts, ready))
    bias_fwd, bias_bwd, bounds_fwd, bounds_bwd, rot_q = ready
    rot_q, rot_k, values = qkv_halo_call(
        x_parts, onehot, vectors, weight_turned, bias_turned, table, rot_q, rot_k, values, side
    )
    others, rot_q = lax.optimization_barrier((others, rot_q))
    up_biases = jnp.concatenate(
        [jnp.sum(x[rows : rows + 3].astype(F32), 0, keepdims=True) for x in others]
    )
    part = rows // 2
    own_w = jnp.stack([x[half * part : half * part + part] for half in range(2) for x in others])
    own_w = own_w.reshape(2, depth - 1, part, width)
    over_b = send(own_w, "b", SWAP)
    over_a = send(own_w, "a", SWAP)
    mixed, mixed_low, lse = forward_call(bounds_fwd, rot_q, rot_k, values, bias_fwd, side)
    over_b, over_a, mixed_low = lax.optimization_barrier((over_b, over_a, mixed_low))
    diagonal = (send(over_b[0], "a", SWAP), send(over_a[1], "b", SWAP))
    hidden_in, norm2, out0, dn0, up_sum0, kept_own, sent_own = middle_own_call(
        place, tokens, mixed_low, output_weight, vectors, cotangent, b_up[None], w_up, w_down,
        slices,
    )
    far_own = send(sent_own, "c", SWAP)
    diagonal, norm2 = lax.optimization_barrier((diagonal, norm2))
    near = [own_w, over_b, over_a, *diagonal]
    pieces = near + [send(x, "c", SWAP) for x in near]
    chip_own, parts_own = plane_scatter(kept_own, far_own, extra)
    norm2 = after(norm2, chip_own)
    (
        activations, d_hidden, d_heads, d_head, d_tail, delta, small_mid, up_sums, kept_mid,
        sent_mid,
    ) = middle_call(
        place, hidden_in, norm2, out0, dn0, mixed_low, mixed, output_weight, vectors, cotangent,
        up_biases, lse, pieces, slices,
    )
    far_mid = send(sent_mid, "c", SWAP)
    do_parts = around(d_heads, d_head, d_tail)

    own_args = (bounds_fwd, rot_q, d_heads, rot_k, values, bias_fwd, lse, delta, side)
    dq0, dk0, dv0 = backward_own_call(*own_args, 0, 1)
    far_mid, dq0 = lax.optimization_barrier((far_mid, dq0))
    (sent_b, sent_a, rest), round_1 = split_scatter(kept_mid, far_mid)
    own_args = own_args[:-2] + (after(delta, dq0, sent_b, sent_a, rest), side)
    dq1, dk1, dv1 = backward_own_call(*own_args, 1, groups - 1)
    do_parts, dq1 = lax.optimization_barrier((do_parts, dq1))
    dk, dv = backward_halo_call(
        bounds_bwd, rot_q, do_parts, rot_k, values, bias_bwd, [dk0, dk1], [dv0, dv1], side
    )
    round_1, dk = lax.optimization_barrier((round_1, dk))
    crossing, round_2 = split_scatter_on(rest, *round_1)
    dk = after(dk, crossing)

    grid8 = jnp.pad(grid_own.astype(F32), ((0, 6), (0, 0)))
    d_qkv, grad_b_qkv, freqs8, kept_qkv, sent_qkv = turn_back_call(
        place, tokens, vectors, (dq0, dq1), dk, dv, q_exact, k_exact, onehot, table, grid8,
        order.T, side, slices,
    )
    far_qkv = send(sent_qkv, "c", SWAP)
    round_2, d_qkv = lax.optimization_barrier((round_2, d_qkv))
    plane_mid = wide_sum(split_scatter_end(rest, *round_1, *round_2), extra)
    ff_sent = [plane_mid[k * rows - rows : k * rows].astype(BF) for k in range(1, depth)]
    ff_got = [send(ff_sent[k - 1], "n", ring(depth, -k)) for k in range(1, depth)]
    input_grad, small_in = input_grad_call(
        tokens, vectors, after(d_qkv, ff_sent), query_key_value_weight, d_hidden
    )
    far_qkv, small_in = lax.optimization_barrier((far_qkv, small_in))
    (_, _, rest_qkv), round_1 = split_scatter(kept_qkv, far_qkv)
    _, round_2 = split_scatter_on(rest_qkv, *round_1)
    plane_qkv = wide_sum(split_scatter_end(rest_qkv, *round_1, *round_2), extra)

    ff_total = wide_sum(sum_low(*parts_own), extra) + sum_low(*ff_got)
    ff_square = jnp.sum(ff_total * ff_total)
    gathered = plane_gather(ff_total.astype(BF).reshape(2, rows // 2, width))
    total_w_up, total_w_down = assemble_call(place, gathered, [w_up.shape, w_down.shape], 0)

    part = jnp.concatenate([plane_qkv, plane_mid[(depth - 1) * rows :]], 1).astype(BF)
    thin = part.shape[0] // depth
    cut = lambda k: lax.dynamic_slice_in_dim(part, ((z + k) % depth) * thin, thin, 0)
    total = cut(0).astype(F32)
    for k in range(1, depth):
        total = total + send(cut(k), "n", ring(depth, k)).astype(F32)
    proj_square = jnp.sum(total * total)
    low = total.astype(BF)
    strip = jnp.stack([low] + [send(low, "n", ring(depth, k)) for k in range(1, depth)])
    gathered = plane_gather(strip.reshape((2, depth // 2) + low.shape))
    total_w_qkv, total_w_out = assemble_call(
        place, gathered, [query_key_value_weight.shape, output_weight.shape], depth
    )

    slot = (z - jnp.arange(depth)) % depth
    quarter_sums = jnp.take(jnp.concatenate([up_sum0, up_sums]), slot, axis=0)
    named = [
        small_in[0], small_in[1], grad_b_qkv[0], small_mid[3], freqs8[:2].reshape(-1),
        small_mid[0], small_mid[1], small_mid[2], quarter_sums.reshape(-1),
    ]
    large = jnp.full((128,), ff_square + proj_square)
    if extra > 1:
        large = large / extra
    small = jnp.concatenate(named + [large])
    small = sum_all(small.reshape(-1, 128), depth, extra).reshape(-1)
    out, at = [], 0
    for vector in named:
        out.append(small[at : at + vector.size])
        at += vector.size
    t_gain1, t_shift1, t_b_qkv, t_b_out, t_freqs, t_gain2, t_shift2, t_b_down, t_up = out
    t_freqs = t_freqs.reshape(rope_freqs.shape)
    rot_sq = jnp.sum(t_freqs * t_freqs)
    skip = sum(v.size for v in named[:4])
    lane = jnp.arange(small.size)
    others = (lane < skip) | (lane >= skip + freqs8.shape[1] * 2) & (lane < at)
    other_sq = small[at] + jnp.sum(jnp.where(others, small * small, 0.0))
    t_b_up = lax.dynamic_slice_in_dim(t_up, z * b_up.shape[0], b_up.shape[0], 0)
    return (
        activations[None],
        input_grad[None],
        t_gain1,
        t_shift1,
        total_w_qkv,
        t_b_qkv,
        total_w_out,
        t_b_out,
        t_freqs,
        t_gain2,
        t_shift2,
        total_w_up,
        t_b_up,
        total_w_down,
        t_b_down,
        rot_sq,
        other_sq,
    )


def solution(mesh):
    wide, depth = mesh.shape["wide"], mesh.shape["narrow"]
    extra = wide // 8
    fine = Mesh(mesh.devices.reshape(extra, 2, 2, 2, depth), ("e", "a", "b", "c", "n"))
    w, n = ("e", "a", "b", "c"), "n"
    return jax.shard_map(
        functools.partial(on_device, extra=extra, depth=depth),
        mesh=fine,
        in_specs=(
            P(w, n, None), P(w, None), P(w, None), P(None, w, None),
            P(), P(), P(), P(), P(), P(), P(), P(), P(),
            P(None, n), P(n), P(n, None), P(), P(w, n, None),
        ),
        out_specs=(
            P(w, n, None), P(w, n, None),
            P(), P(), P(), P(), P(), P(), P(), P(), P(),
            P(None, n), P(n), P(n, None), P(), P(), P(),
        ),
        check_vma=False,
    )
```

```python
import functools

import jax
import jax.numpy as jnp
import numpy as np
from jax import lax
from jax.experimental import pallas as pl
from jax.experimental.pallas import tpu as pltpu
from jax.sharding import Mesh, PartitionSpec as P

EPS = 1e-06
MASKED = -1e30
BLK = 128
SPAN = 6
SPAN_SIDE = 3
SPAN_BACK = 2
GROUP = 4
REACH = 64
STAT_ROWS = 6
STAT_PAD = 16
SIDE = 32
LN1_GAIN, LN1_SHIFT, B_OUT, LN2_GAIN, LN2_SHIFT, B_DOWN = (slice(n, n + 1) for n in range(6))
LOG2E = np.float32(1.4426950408889634)
BF = jnp.bfloat16
F32 = jnp.float32
PLANE = ("a", "b", "c")
SWAP = [(0, 1), (1, 0)]
FIRST = [(i, i ^ (4 if i % 2 else 2)) for i in range(8)]
SECOND = [(i, i ^ (2 if i % 2 else 4)) for i in range(8)]
VMEM_LIMIT = 56 * 1024 * 1024


def dot(left, right):
    return lax.dot_general(left, right, (((1,), (0,)), ((), ())), preferred_element_type=F32)


def dot_nt(left, right):
    return lax.dot_general(left, right, (((1,), (1,)), ((), ())), preferred_element_type=F32)


def dot_tn(left, right):
    return lax.dot_general(left, right, (((0,), (0,)), ((), ())), preferred_element_type=F32)


def params(**kw):
    return pltpu.CompilerParams(vmem_limit_bytes=VMEM_LIMIT, **kw)


def cost(us):
    return pl.CostEstimate(
        flops=int(us * 1.15e9), bytes_accessed=int(us * 3.0e6), transcendentals=0
    )


def whole(shape):
    return pl.BlockSpec(shape, lambda *_: (0,) * len(shape))


ANY = pl.BlockSpec(memory_space=pl.ANY)
SMEM = pl.BlockSpec(memory_space=pltpu.SMEM)


def rounded(x):
    return lax.reduce_precision(x, exponent_bits=8, mantissa_bits=7)


def turn_table(rope_freqs):
    lanes = rope_freqs.shape[1] * rope_freqs.shape[2]
    freq = rope_freqs.reshape(2, 1, lanes)
    angle = jnp.arange(SIDE, dtype=F32)[None, :, None] * freq
    cosine, sine = jnp.cos(angle), jnp.sin(angle)

    def halves(x):
        return jnp.concatenate([x.astype(BF), (x - rounded(x)).astype(BF)], 0)

    def grouped(x):
        return x.reshape(2 * SIDE, lanes // 128, 1, 128)

    zero = jnp.zeros((2 * SIDE, lanes // 128, 2, 128), BF)
    rows = jnp.concatenate([grouped(halves(cosine[0])), grouped(halves(sine[0])), zero], 2)
    cols = jnp.concatenate([zero, grouped(halves(cosine[1])), grouped(halves(sine[1]))], 2)
    return jnp.concatenate([rows, cols], 0).reshape(4 * SIDE, 4 * lanes)


def cos_sin(onehot, table):
    parts = dot(onehot, table)
    cr, sr, cc, sc = (parts[:, lanes_of(n, 128)] for n in range(4))
    return cr * cc - sr * sc, sr * cc + cr * sc


def layer_norm_low(x, gain, shift):
    centred = x - jnp.mean(x, -1, keepdims=True)
    var = jnp.mean(centred * centred, -1, keepdims=True)
    return (centred * lax.rsqrt(var + EPS) * gain + shift).astype(BF)


def project(norm, hot_ref, table_ref, weights, b_ref, q_out, k_out, v_ref, exact):
    width = norm.shape[1]
    for g in range(width // 256):
        c, s = cos_sin(hot_ref[...], table_ref[:, lanes_of(g, 512)])
        for n, out in enumerate((q_out, k_out)):
            lo = n * width + 256 * g
            proj = dot(norm, weights[:, lo : lo + 256]) + b_ref[:, lo : lo + 256]
            for half, turned in enumerate(
                (proj[:, :128] * c - proj[:, 128:] * s, proj[:, :128] * s + proj[:, 128:] * c)
            ):
                at = slice(256 * g + 128 * half, 256 * g + 128 * half + 128)
                out[:, at] = turned.astype(BF)
                if exact:
                    exact[n][:, at] = turned
    for g in range(width // 256):
        lo = 2 * width + 256 * g
        v_ref[:, 256 * g : 256 * g + 256] = (
            dot(norm, weights[:, lo : lo + 256]) + b_ref[:, lo : lo + 256]
        ).astype(BF)


def qkv_own_kernel(
    x_ref, hot_ref, vec_ref, w_ref, b_ref, order_ref, table_ref,
    q_ref, k_ref, v_ref, pq_ref, pk_ref, w_turned,
):
    width = x_ref.shape[1]

    @pl.when(pl.program_id(0) == 0)
    def _():
        for g in range(2 * width // 256):
            at = slice(256 * g, 256 * g + 256)
            w_turned[:, at] = dot(w_ref[:, at], order_ref[...]).astype(BF)
        w_turned[:, 2 * width :] = w_ref[:, 2 * width :]

    norm = layer_norm_low(x_ref[...].astype(F32), vec_ref[LN1_GAIN], vec_ref[LN1_SHIFT])
    project(norm, hot_ref, table_ref, w_turned, b_ref, q_ref, k_ref, v_ref, (pq_ref, pk_ref))


def qkv_own_call(x, onehot, vectors, weight, bias, order, table, first):
    own, width = x.shape
    rows = onehot.shape[0]
    tile = 256
    shape = jax.ShapeDtypeStruct((rows, width), BF)
    exact = jax.ShapeDtypeStruct((own, width), F32)
    row = lambda w: pl.BlockSpec((tile, w), lambda i: (i, 0))
    inside = lambda w: pl.BlockSpec(
        (pl.Element(tile), pl.Element(w)), lambda i: (pl.multiple_of(first + tile * i, BLK), 0)
    )
    return pl.pallas_call(
        qkv_own_kernel,
        grid=(own // tile,),
        in_specs=[
            row(width),
            inside(onehot.shape[1]),
            whole(vectors.shape),
            whole(weight.shape),
            whole((1, 3 * width)),
            whole(order.shape),
            whole(table.shape),
        ],
        out_specs=[inside(width)] * 3 + [row(width)] * 2 + [whole(weight.shape)],
        out_shape=[shape] * 3 + [exact] * 2 + [jax.ShapeDtypeStruct(weight.shape, BF)],
        compiler_params=params(),
        cost_estimate=cost(8),
        name="qkv_own",
    )(x, onehot, vectors, weight, bias[None], order, table)


def qkv_halo_kernel(
    far_l, near_l, near_r, far_r, hot_ref, vec_ref, w_ref, b_ref, table_ref,
    q_in, k_in, v_in, q_ref, k_ref, v_ref, x_all, sem,
):
    width = x_all.shape[1]
    step = pl.program_id(0)
    tile = q_ref.shape[0]

    @pl.when(step == 0)
    def _():
        own, reach = near_l.shape[0], far_l.shape[0]
        total = x_all.shape[0]
        blank = total // 2 - own - reach
        copies = []
        at = blank
        for n, ref in enumerate((far_l, near_l, near_r, far_r)):
            copies.append(
                pltpu.make_async_copy(ref, x_all.at[at : at + ref.shape[0], :], sem.at[n])
            )
            copies[-1].start()
            at += ref.shape[0]
        x_all[:blank, :] = jnp.zeros((blank, width), BF)
        x_all[total - blank :, :] = jnp.zeros((blank, width), BF)
        for copy in copies:
            copy.wait()

    x = x_all[pl.ds(pl.multiple_of(step * tile, tile), tile), :].astype(F32)
    norm = layer_norm_low(x, vec_ref[LN1_GAIN], vec_ref[LN1_SHIFT])
    project(norm, hot_ref, table_ref, w_ref, b_ref, q_ref, k_ref, v_ref, ())


def qkv_halo_call(pieces, onehot, vectors, weight, bias, table, q, k, v, first):
    rows, width = q.shape
    own = pieces[1].shape[0]
    tile = first // 2
    shape = jax.ShapeDtypeStruct((rows, width), BF)
    at = lambda w: pl.BlockSpec(
        (pl.Element(tile), pl.Element(w)), lambda i: (pl.multiple_of(tile * i + jnp.where(i >= 2, own, 0), 64), 0)
    )
    return pl.pallas_call(
        qkv_halo_kernel,
        grid=(4,),
        in_specs=[ANY] * 4
        + [
            at(onehot.shape[1]),
            whole(vectors.shape),
            whole(weight.shape),
            whole((1, 3 * width)),
            whole(table.shape),
        ]
        + [ANY] * 3,
        out_specs=[at(width)] * 3,
        out_shape=[shape] * 3,
        input_output_aliases={9: 0, 10: 1, 11: 2},
        scratch_shapes=[pltpu.VMEM((2 * first, width), BF), pltpu.SemaphoreType.DMA((4,))],
        compiler_params=params(),
        cost_estimate=cost(11.5),
        name="qkv_halo",
    )(*pieces, onehot, vectors, weight, bias[None], table, q, k, v)


def head_stack(block, turned, scale=None):
    lane = lax.broadcasted_iota(jnp.int32, block.shape, 1)
    head = (lane % 128) // 32 if turned else lane // 64
    if scale is not None:
        block = block * scale
    zero = jnp.zeros_like(block)
    return jnp.concatenate([jnp.where(head == h, block, zero) for h in range(GROUP)], 0)


def fold8(x, op):
    return op(x.reshape(x.shape[0] // 8, 8, x.shape[1]), axis=0)


def key_span(ident_ref, ident_q, start, c, span, end):
    block = jnp.minimum(start + c * span, end - span)
    lower = (start + c * span - block) * BLK
    at = pl.ds(pl.multiple_of(block * BLK, BLK), span * BLK)
    row = lax.broadcasted_iota(jnp.int32, (span * BLK, BLK), 0)
    return at, (ident_ref[at, :] == ident_q) & (row >= lower)


def lanes_of(g, size=256):
    return slice(size * g, size * g + size)


def forward_kernel(
    bound_ref, q_ref, k_ref, v_ref, idk_ref, idq_ref, *refs, first, base
):
    o_ref, low_ref, lse_ref, s_ref, acc_ref, q4_ref = refs[-6:]
    i = pl.program_id(0) + base
    groups = k_ref.shape[1] // 256
    lanes = GROUP * BLK
    window = k_ref.shape[0] // BLK
    start, count = bound_ref[i, 0], bound_ref[i, 1]
    for g in range(groups):
        q4_ref[g] = head_stack(q_ref[:, lanes_of(g)], True, jnp.asarray(0.125, BF))
    ident_q = idq_ref[pl.ds(first // BLK + i, 1), :]

    def scores(c, top):
        at, seen = key_span(idk_ref, ident_q, start, c, SPAN, window)
        here = pl.ds(pl.multiple_of(c * SPAN * BLK, BLK), SPAN * BLK)
        tops = []
        for g in range(groups):
            s = dot_nt(k_ref[at, lanes_of(g)], q4_ref[g]) * LOG2E
            for h in range(GROUP):
                masked = jnp.where(seen, s[:, lanes_of(h, BLK)], MASKED)
                s_ref[g, here, lanes_of(h, BLK)] = masked
                tops.append(fold8(masked, jnp.max))
        return jnp.maximum(top, jnp.concatenate(tops, 1))

    top = lax.fori_loop(0, count, scores, jnp.full((8, groups * lanes), -3e38, F32))
    top = jnp.max(top, 0, keepdims=True)
    acc_ref[...] = jnp.zeros_like(acc_ref)

    def mix(c, total):
        at, _ = key_span(idk_ref, ident_q, start, c, SPAN, window)
        here = pl.ds(pl.multiple_of(c * SPAN * BLK, BLK), SPAN * BLK)
        sums = []
        for g in range(groups):
            e = jnp.exp2(s_ref[g, here, :] - top[:, lanes_of(g, lanes)])
            sums.append(fold8(e, jnp.sum))
            acc_ref[g] += dot_tn(v_ref[at, lanes_of(g)], e.astype(BF))
        return total + jnp.concatenate(sums, 1)

    total = lax.fori_loop(0, count, mix, jnp.zeros((8, groups * lanes), F32))
    total = jnp.sum(total, 0, keepdims=True)
    lse = top + jnp.log(total) * LOG2E
    inverse = 1.0 / total
    for g in range(groups):
        lse_ref[g] = lse[:, lanes_of(g, lanes)]
        acc = acc_ref[g] * inverse[:, lanes_of(g, lanes)]
        out = jnp.concatenate(
            [acc[64 * h : 64 * h + 64, lanes_of(h, BLK)] for h in range(GROUP)], 0
        ).T
        o_ref[:, lanes_of(g)] = out
        low_ref[:, lanes_of(g)] = out.astype(BF)


def stat_spec(groups, base=0):
    return pl.BlockSpec((groups, None, 1, GROUP * BLK), lambda i: (0, i + base, 0, 0))


def query_rows(first, width):
    return pl.BlockSpec(
        (pl.Element(BLK), pl.Element(width)), lambda i: (pl.multiple_of(first + BLK * i, BLK), 0)
    )


def forward_call(bounds, q_win, k_win, v_win, idk, idq, first, own, base, count, earlier=()):
    win, width = k_win.shape
    groups, blocks = width // 256, own // BLK
    row = pl.BlockSpec((BLK, width), lambda i: (i + base, 0))
    steps = -(-win // (SPAN * BLK))
    return pl.pallas_call(
        functools.partial(forward_kernel, first=first, base=base),
        grid=(count,),
        in_specs=[SMEM, query_rows(first + base * BLK, width)]
        + [whole((win, width))] * 2
        + [whole(idk.shape), whole(idq.shape)]
        + [ANY] * len(earlier),
        out_specs=[row, row, stat_spec(groups, base)],
        input_output_aliases={6 + n: n for n in range(len(earlier))},
        out_shape=[
            jax.ShapeDtypeStruct((own, width), F32),
            jax.ShapeDtypeStruct((own, width), BF),
            jax.ShapeDtypeStruct((groups, blocks, 1, GROUP * BLK), F32),
        ],
        scratch_shapes=[
            pltpu.VMEM((groups, steps * SPAN * BLK, GROUP * BLK), F32),
            pltpu.VMEM((groups, 256, GROUP * BLK), F32),
            pltpu.VMEM((groups, GROUP * BLK, 256), BF),
        ],
        compiler_params=params(),
        cost_estimate=cost(4 * count),
        name="attention_forward",
    )(bounds, q_win, k_win, v_win, idk, idq, *earlier)


def score_gradients(s, dp, lse, delta, seen):
    low_p, low_ds = [], []
    for h in range(GROUP):
        at = lanes_of(h, BLK)
        p = jnp.exp2(jnp.where(seen, s[:, at] * LOG2E - lse[:, at], MASKED))
        low_p.append(p.astype(BF))
        low_ds.append((p * (dp[:, at] - delta[:, at])).astype(BF))
    return jnp.concatenate(low_p, 1), jnp.concatenate(low_ds, 1)


def backward_own_kernel(
    bound_ref, q_ref, do_ref, k_ref, v_ref, idk_ref, idq_ref, lse_ref, delta_ref,
    dq_ref, dk_ref, dv_ref, acc_ref, q4_ref, do4_ref, *, first,
):
    i = pl.program_id(0)
    groups = k_ref.shape[1] // 256
    own = dk_ref.shape[0]

    @pl.when(i == 0)
    def _():
        dk_ref[...] = jnp.zeros_like(dk_ref)
        dv_ref[...] = jnp.zeros_like(dv_ref)

    for g in range(groups):
        q4_ref[g] = head_stack(q_ref[:, lanes_of(g)], True, jnp.asarray(0.125, BF))
        do4_ref[g] = head_stack(do_ref[:, lanes_of(g)], False)
    ident_q = idq_ref[pl.ds(first // BLK + i, 1), :]

    def attend(at, seen, inside):
        for g in range(groups):
            keys = k_ref[at, lanes_of(g)]
            s = dot_nt(keys, q4_ref[g])
            dp = dot_nt(v_ref[at, lanes_of(g)], do4_ref[g])
            low_p, low_ds = score_gradients(s, dp, lse_ref[g], delta_ref[g], seen)
            if inside:
                acc_ref[g] = dot_tn(keys, low_ds)
                dk_ref[:, lanes_of(g)] += dot(low_ds, q4_ref[g])
                dv_ref[:, lanes_of(g)] += dot(low_p, do4_ref[g])
            else:
                acc_ref[g] += dot_tn(keys, low_ds)

    attend(slice(first, first + own), idk_ref[first : first + own, :] == ident_q, True)
    for start, count, end in (
        (bound_ref[i, 2], bound_ref[i, 3], first // BLK),
        ((first + own) // BLK, bound_ref[i, 4], k_ref.shape[0] // BLK),
    ):

        def step(c, _):
            attend(*key_span(idk_ref, ident_q, start, c, SPAN_SIDE, end), False)
            return 0

        lax.fori_loop(0, count, step, 0)
    for g in range(groups):
        acc = acc_ref[g]
        parts = [acc[32 * h : 32 * h + 32, lanes_of(h, BLK)] for h in range(GROUP)]
        parts += [acc[128 + 32 * h : 160 + 32 * h, lanes_of(h, BLK)] for h in range(GROUP)]
        dq_ref[:, lanes_of(g)] = (jnp.concatenate(parts, 0) * 0.125).T


def backward_own_call(bounds, q_win, do_own, k_win, v_win, idk, idq, lse, delta, first, own):
    win, width = k_win.shape
    groups = width // 256
    row = pl.BlockSpec((BLK, width), lambda i: (i, 0))
    return pl.pallas_call(
        functools.partial(backward_own_kernel, first=first),
        grid=(own // BLK,),
        in_specs=[SMEM, query_rows(first, width), row]
        + [whole((win, width))] * 2
        + [whole(idk.shape), whole(idq.shape), stat_spec(groups), stat_spec(groups)],
        out_specs=[row] + [whole((own, width))] * 2,
        out_shape=[jax.ShapeDtypeStruct((own, width), F32)] * 3,
        scratch_shapes=[pltpu.VMEM((groups, 256, GROUP * BLK), F32)]
        + [pltpu.VMEM((groups, GROUP * BLK, 256), BF)] * 2,
        compiler_params=params(),
        cost_estimate=cost(20),
        name="attention_backward_own",
    )(bounds, q_win, do_own, k_win, v_win, idk, idq, lse, delta)


def backward_halo_kernel(
    bound_ref, q_ref, far_l, near_l, near_r, far_r, k_ref, v_ref, idk_ref, idq_ref, dk_in, dv_in,
    dk_ref, dv_ref, q4_ref, do_all, do4_ref, stat_ref, *, first,
):
    groups = k_ref.shape[1] // 256
    own, reach = k_ref.shape[0], far_l.shape[0] - STAT_PAD
    blocks = own // BLK
    side = first // BLK
    step_id = pl.program_id(0)
    j = jnp.where(step_id < side, step_id, step_id + blocks)
    lanes = GROUP * BLK

    def stats(ref, row, slot):
        parts = ref[row : row + 2 * STAT_ROWS, :].astype(F32)
        sums = parts[0:4] + parts[4:8] + parts[8:12]
        for g in range(groups):
            for n in range(2):
                stat_ref[n, g, slot : slot + 1, :] = jnp.concatenate(
                    [sums[2 * n : 2 * n + 1, lanes_of(g)], sums[2 * n + 1 : 2 * n + 2, lanes_of(g)]],
                    1,
                )

    @pl.when(step_id == 0)
    def _():
        dk_ref[...] = dk_in[...]
        dv_ref[...] = dv_in[...]
        blank = jnp.zeros((BLK - reach, do_all.shape[1]), BF)
        do_all[0 : BLK - reach, :] = blank
        do_all[BLK - reach : BLK, :] = far_l[:reach, :]
        do_all[BLK : BLK + own, :] = near_l[:own, :]
        do_all[BLK + own : BLK + 2 * own, :] = near_r[:own, :]
        do_all[BLK + 2 * own : BLK + 2 * own + reach, :] = far_r[:reach, :]
        do_all[BLK + 2 * own + reach :, :] = blank
        stats(far_l, reach, 0)
        for i in range(blocks):
            stats(near_l, own + 2 * STAT_ROWS * i, 1 + i)
            stats(near_r, own + 2 * STAT_ROWS * i, 1 + blocks + i)
        stats(far_r, reach, 1 + 2 * blocks)

    start, count = bound_ref[j, 0], bound_ref[j, 1]

    @pl.when(count > 0)
    def _():
        here = pl.ds(pl.multiple_of(step_id * BLK, BLK), BLK)
        for g in range(groups):
            q4_ref[g] = head_stack(q_ref[:, lanes_of(g)], True, jnp.asarray(0.125, BF))
            do4_ref[g] = head_stack(do_all[here, lanes_of(g)], False)
        ident_q = idq_ref[pl.ds(j, 1), :]

        def step(c, _):
            at, seen = key_span(idk_ref, ident_q, start, c, SPAN_BACK, blocks)
            for g in range(groups):
                s = dot_nt(k_ref[at, lanes_of(g)], q4_ref[g])
                dp = dot_nt(v_ref[at, lanes_of(g)], do4_ref[g])
                lse = stat_ref[0, g, pl.ds(step_id, 1), :]
                delta = stat_ref[1, g, pl.ds(step_id, 1), :]
                low_p, low_ds = score_gradients(s, dp, lse, delta, seen)
                dk_ref[at, lanes_of(g)] += dot(low_ds, q4_ref[g])
                dv_ref[at, lanes_of(g)] += dot(low_p, do4_ref[g])
            return 0

        lax.fori_loop(0, count, step, 0)


def backward_halo_call(bounds, q_win, pieces, k_win, v_win, idk, idq, dk, dv, first):
    own, width = dk.shape
    groups = width // 256
    side, blocks = first // BLK, own // BLK
    inside = lambda w: pl.BlockSpec(
        (pl.Element(own), pl.Element(w)), lambda i: (pl.multiple_of(first + 0 * i, BLK), 0)
    )
    outside = pl.BlockSpec((BLK, width), lambda i: (jnp.where(i < side, i, i + blocks), 0))
    return pl.pallas_call(
        functools.partial(backward_halo_kernel, first=first),
        grid=(2 * side,),
        in_specs=[SMEM, outside]
        + [whole(p.shape) for p in pieces]
        + [inside(width)] * 2
        + [inside(idk.shape[1]), whole(idq.shape)]
        + [whole((own, width))] * 2,
        out_specs=[whole((own, width))] * 2,
        out_shape=[jax.ShapeDtypeStruct((own, width), F32)] * 2,
        scratch_shapes=[
            pltpu.VMEM((groups, GROUP * BLK, 256), BF),
            pltpu.VMEM((2 * first, width), BF),
            pltpu.VMEM((groups, GROUP * BLK, 256), BF),
            pltpu.VMEM((2, groups, 16, GROUP * BLK), F32),
        ],
        compiler_params=params(),
        cost_estimate=cost(11),
        name="attention_backward_halo",
    )(bounds, q_win, *pieces, k_win, v_win, idk, idq, dk, dv)


def norm_parts(x):
    centred = x - jnp.mean(x, -1, keepdims=True)
    inverse = lax.rsqrt(jnp.mean(centred * centred, -1, keepdims=True) + EPS)
    return centred * inverse, inverse


def norm_back(grad, xhat, inverse, gain):
    scaled = grad * gain
    return inverse * (
        scaled
        - jnp.mean(scaled, -1, keepdims=True)
        - xhat * jnp.mean(scaled * xhat, -1, keepdims=True)
    )


def columns_sum(x):
    return jnp.sum(x, 0, keepdims=True)


def chip_order(ab, core):
    return jnp.where(core == 0, ab, ab % 2 * 2 + ab // 2)


def slices_out(place, source, keep, away, lead, sem, slices, rows):
    for n in range(slices):
        rel = place ^ n
        for target, odd in ((keep, 0), (away, 1)):
            core = place % 2 ^ odd

            @pl.when(rel % 2 == odd)
            def _():
                pltpu.make_async_copy(
                    source.at[n * rows : (n + 1) * rows, :],
                    target.at[chip_order(rel // 2, core), pl.ds(lead, rows), :],
                    sem.at[n],
                ).start()


def gathered(place, refs):
    for far in range(2):
        for n in range(4):
            rel = 2 * chip_order(jnp.int32(n), place % 2 ^ far) + far
            yield refs[4 * far + n], place ^ rel


def slices_wait(source, keep, sem, slices, rows):
    for n in range(slices):
        pltpu.make_async_copy(
            source.at[n * rows : (n + 1) * rows, :], keep.at[0, 0:rows, :], sem.at[n]
        ).wait()


def one_quarter(q, w_all, norm_ref, dy_ref, bu_ref, dbu_ref, out_acc, dn_acc, g_all, fresh):
    own, width = norm_ref.shape
    tile = 256
    for t in range((w_all.shape[1] - width) // tile):
        cols = slice(tile * t, tile * t + tile)
        down = slice(width + tile * t, width + tile * t + tile)
        norm, dy = norm_ref[...], dy_ref[...]
        up_w = w_all[q, :width, cols]
        down_w = w_all[q, down, :]
        pre = dot(norm, up_w) + bu_ref[pl.ds(q, 1), cols]
        cdf = 0.5 * (1.0 + lax.erf(pre * np.float32(0.7071067811865476)))
        density = jnp.exp(-0.5 * pre * pre) * np.float32(0.3989422804014327)
        act = (pre * cdf).astype(BF)
        d_pre = (dot_nt(dy, down_w) * (cdf + pre * density)).astype(BF)
        dbu_ref[pl.ds(q, 1), cols] = columns_sum(d_pre.astype(F32))
        if fresh and t == 0:
            out_acc[...] = dot(act, down_w)
            dn_acc[...] = dot_nt(d_pre, up_w)
        else:
            out_acc[...] += dot(act, down_w)
            dn_acc[...] += dot_nt(d_pre, up_w)
        g_all[q, :width, cols] = dot_tn(norm, d_pre).astype(BF)
        g_all[q, down, :] = dot_tn(act, dy).astype(BF)


def middle_own_kernel(
    place_ref, x_ref, low_ref, wo_ref, vec_ref, dy_ref, bu_ref, up_ref, down_ref,
    hid_ref, norm_ref, out_ref, dn_ref, dbu_ref, keep_ref, send_ref, w_all, g_all, w_sem, g_sem,
    *, slices,
):
    width = x_ref.shape[1]
    rows = w_all.shape[1] // slices
    copies = [
        pltpu.make_async_copy(up_ref, w_all.at[0, :width, :], w_sem.at[0]),
        pltpu.make_async_copy(down_ref, w_all.at[0, width:, :], w_sem.at[1]),
    ]
    for copy in copies:
        copy.start()
    hidden_in = x_ref[...].astype(F32) + dot(low_ref[...], wo_ref[...]) + vec_ref[B_OUT]
    hid_ref[...] = hidden_in
    norm_ref[...] = layer_norm_low(hidden_in, vec_ref[LN2_GAIN], vec_ref[LN2_SHIFT])
    for copy in copies:
        copy.wait()
    one_quarter(0, w_all, norm_ref, dy_ref, bu_ref, dbu_ref, out_ref, dn_ref, g_all, True)
    slices_out(place_ref[0], g_all.at[0], keep_ref, send_ref, 0, g_sem, slices, rows)
    slices_wait(g_all.at[0], keep_ref, g_sem, slices, rows)


def middle_own_call(place, x, low, w_out, vectors, dy, b_up, w_up, w_down, slices):
    own, width = x.shape
    hidden = b_up.shape[1]
    rows = width + hidden
    vmem = pl.BlockSpec(memory_space=pltpu.VMEM)
    sds = jax.ShapeDtypeStruct
    return pl.pallas_call(
        functools.partial(middle_own_kernel, slices=slices),
        in_specs=[SMEM] + [vmem] * 6 + [ANY] * 2,
        out_specs=[vmem] * 5 + [ANY] * 2,
        out_shape=[
            sds((own, width), F32),
            sds((own, width), BF),
            sds((own, width), F32),
            sds((own, width), F32),
            sds((1, hidden), F32),
        ]
        + [sds((slices // 2, rows // slices, width), BF)] * 2,
        scratch_shapes=[
            pltpu.VMEM((1, rows, width), BF),
            pltpu.VMEM((1, rows, width), BF),
            pltpu.SemaphoreType.DMA((2,)),
            pltpu.SemaphoreType.DMA((slices,)),
        ],
        compiler_params=params(),
        cost_estimate=cost(12),
        name="middle_own",
    )(place, x, low, w_out, vectors, dy, b_up, w_up, w_down)


def other_quarters(
    place, piece_refs, base, w_all, w_sem, norm_ref, dy_ref, bu_ref, dbu_ref, out_acc, dn_acc,
    g_all, g_sem, keep_ref, send_ref, slices,
):
    rows = w_all.shape[1] // slices

    def fetches(q):
        return [
            pltpu.make_async_copy(
                ref.at[base + q],
                w_all.at[q, pl.ds(pl.multiple_of(source * rows, rows), rows), :],
                w_sem.at[q, n],
            )
            for n, (ref, source) in enumerate(gathered(place, piece_refs))
        ]

    for q in range(w_all.shape[0]):
        for copy in fetches(q):
            copy.start()

    def quarter(q, _):
        for copy in fetches(q):
            copy.wait()
        one_quarter(q, w_all, norm_ref, dy_ref, bu_ref, dbu_ref, out_acc, dn_acc, g_all, False)
        slices_out(
            place, g_all.at[q], keep_ref, send_ref, pl.multiple_of(q * rows, rows), g_sem.at[q],
            slices, rows,
        )
        return 0

    lax.fori_loop(0, w_all.shape[0], quarter, 0)


def middle_next_kernel(place_ref, norm_ref, out_in, dn_in, dy_ref, bu_ref, *refs, slices, base):
    piece_refs = refs[:slices]
    out_ref, dn_ref, dbu_ref, keep_ref, send_ref, w_all, g_all, w_sem, g_sem = refs[slices:]
    out_ref[...] = out_in[...]
    dn_ref[...] = dn_in[...]
    other_quarters(
        place_ref[0], piece_refs, base, w_all, w_sem, norm_ref, dy_ref, bu_ref, dbu_ref, out_ref,
        dn_ref, g_all, g_sem, keep_ref, send_ref, slices,
    )
    rows = w_all.shape[1] // slices
    for q in range(w_all.shape[0]):
        slices_wait(g_all.at[q], keep_ref, g_sem.at[q], slices, rows)


def middle_next_call(place, norm, out, dn, dy, b_up, pieces, slices, base):
    own, width = norm.shape
    quarters, hidden = b_up.shape
    rows = width + hidden
    vmem = pl.BlockSpec(memory_space=pltpu.VMEM)
    sds = jax.ShapeDtypeStruct
    return pl.pallas_call(
        functools.partial(middle_next_kernel, slices=slices, base=base),
        in_specs=[SMEM] + [vmem] * 5 + [ANY] * len(pieces),
        out_specs=[vmem] * 3 + [ANY] * 2,
        out_shape=[sds((own, width), F32), sds((own, width), F32), sds((quarters, hidden), F32)]
        + [sds((slices // 2, quarters * rows // slices, width), BF)] * 2,
        scratch_shapes=[
            pltpu.VMEM((quarters, rows, width), BF),
            pltpu.VMEM((quarters, rows, width), BF),
            pltpu.SemaphoreType.DMA((quarters, slices)),
            pltpu.SemaphoreType.DMA((quarters, slices)),
        ],
        compiler_params=params(),
        cost_estimate=cost(8 * quarters),
        name="middle_next",
    )(place, norm, out, dn, dy, b_up, *pieces)


def middle_last_kernel(
    place_ref, hid_ref, norm_ref, out_in, dn_in, low_ref, mixed_ref, wo_ref, vec_ref, dy_ref,
    bu_ref, lse_ref, *refs, slices, base,
):
    piece_refs = refs[:slices]
    (
        act_ref, dh_ref, dheads_ref, head_ref, tail_ref, delta_ref, small_ref, dbu_ref,
        keep_ref, send_ref, w_all, g_all, go_all, out_acc, dn_acc, w_sem, g_sem,
    ) = refs[slices:]
    place = place_ref[0]
    own, width = norm_ref.shape
    quarters = w_all.shape[0]
    rows = w_all.shape[1] // slices
    out_acc[...] = out_in[...]
    dn_acc[...] = dn_in[...]
    other_quarters(
        place, piece_refs, base, w_all, w_sem, norm_ref, dy_ref, bu_ref, dbu_ref, out_acc, dn_acc,
        g_all, g_sem, keep_ref, send_ref, slices,
    )

    hidden_in = hid_ref[...]
    act_ref[...] = (hidden_in + out_acc[...] + vec_ref[B_DOWN]).astype(BF)
    xhat, inverse = norm_parts(hidden_in)
    dn = dn_acc[...]
    dy = dy_ref[...].astype(F32)
    d_hidden = dy + norm_back(dn, xhat, inverse, vec_ref[LN2_GAIN])
    dh_ref[...] = d_hidden
    d_att = d_hidden.astype(BF)
    small_ref[0:1, :] = columns_sum(dn * xhat)
    small_ref[1:2, :] = columns_sum(dn)
    small_ref[2:3, :] = columns_sum(dy)
    small_ref[3:4, :] = columns_sum(d_att.astype(F32))
    d_heads = dot_nt(d_att, wo_ref[...]).astype(BF)
    dheads_ref[:own, :] = d_heads
    spread = d_heads.astype(F32) * mixed_ref[...]
    pick = lax.broadcasted_iota(jnp.int32, (8, 256), 0)
    pick = (pick == lax.broadcasted_iota(jnp.int32, (8, 256), 1) // 64).astype(F32)
    for g in range(width // 256):
        for i in range(own // BLK):
            block = spread[BLK * i : BLK * i + BLK, 256 * g : 256 * g + 256]
            sums = lax.dot_general(
                pick, block, (((1,), (1,)), ((), ())),
                preferred_element_type=F32, precision=lax.Precision.HIGHEST,
            )
            delta = jnp.concatenate([sums[h : h + 1, :] for h in range(GROUP)], 1)
            delta_ref[g, i] = delta
            lse = lse_ref[g, i]
            left = jnp.concatenate(
                [lse[:, :256], lse[:, 256:], delta[:, :256], delta[:, 256:]], 0
            )
            parts = []
            for _ in range(3):
                parts.append(left.astype(BF))
                left = left - parts[-1].astype(F32)
            parts = jnp.concatenate(parts, 0)
            at = slice(256 * g, 256 * g + 256)
            lo = own + 2 * STAT_ROWS * i
            dheads_ref[lo : lo + 2 * STAT_ROWS, at] = parts
            for target, row in ((head_ref, 0), (tail_ref, own // BLK - 1)):
                if i == row:
                    target[REACH : REACH + 2 * STAT_ROWS, at] = parts
    blank = jnp.zeros((STAT_PAD - 2 * STAT_ROWS, width), BF)
    head_ref[REACH + 2 * STAT_ROWS :, :] = blank
    tail_ref[REACH + 2 * STAT_ROWS :, :] = blank
    head_ref[:REACH, :] = d_heads[:REACH, :]
    tail_ref[:REACH, :] = d_heads[own - REACH :, :]
    go_all[...] = dot_tn(low_ref[...], d_att).astype(BF)
    few = width // slices
    slices_out(place, go_all, keep_ref, send_ref, quarters * rows, g_sem.at[quarters], slices, few)
    for q in range(quarters):
        slices_wait(g_all.at[q], keep_ref, g_sem.at[q], slices, rows)
    slices_wait(go_all, keep_ref, g_sem.at[quarters], slices, few)


def middle_last_call(
    place, hidden_in, norm, out, dn, low, mixed, w_out, vectors, dy, b_up, lse, pieces, slices,
    base,
):
    own, width = norm.shape
    quarters, hidden = b_up.shape
    rows = width + hidden
    vmem = pl.BlockSpec(memory_space=pltpu.VMEM)
    sds = jax.ShapeDtypeStruct
    grads = sds((slices // 2, (quarters * rows + width) // slices, width), BF)
    return pl.pallas_call(
        functools.partial(middle_last_kernel, slices=slices, base=base),
        in_specs=[SMEM] + [vmem] * 11 + [ANY] * len(pieces),
        out_specs=[vmem] * 8 + [ANY] * 2,
        out_shape=[
            sds((own, width), BF),
            sds((own, width), F32),
            sds((own + own // BLK * 2 * STAT_ROWS, width), BF),
            sds((REACH + STAT_PAD, width), BF),
            sds((REACH + STAT_PAD, width), BF),
            sds((width // 256, own // BLK, 1, GROUP * BLK), F32),
            sds((4, width), F32),
            sds((quarters, hidden), F32),
            grads,
            grads,
        ],
        scratch_shapes=[
            pltpu.VMEM((quarters, rows, width), BF),
            pltpu.VMEM((quarters, rows, width), BF),
            pltpu.VMEM((width, width), BF),
            pltpu.VMEM((own, width), F32),
            pltpu.VMEM((own, width), F32),
            pltpu.SemaphoreType.DMA((quarters, slices)),
            pltpu.SemaphoreType.DMA((quarters + 1, slices)),
        ],
        compiler_params=params(),
        cost_estimate=cost(12),
        name="middle_last",
    )(place, hidden_in, norm, out, dn, low, mixed, w_out, vectors, dy, b_up, lse, *pieces)


def turn_back_kernel(
    place_ref, x_ref, vec_ref, dq_ref, dk_ref, dv_ref, q_ref, k_ref, hot_ref, table_ref, grid_ref,
    back_ref, d_ref, db_ref, freq_ref, keep_ref, send_ref, norm_ref, g_all, sem, *, slices,
):
    width = x_ref.shape[1]
    group = pl.program_id(0)

    @pl.when(group == 0)
    def _():
        norm_ref[...] = layer_norm_low(
            x_ref[...].astype(F32), vec_ref[LN1_GAIN], vec_ref[LN1_SHIFT]
        )

    c, s = cos_sin(hot_ref[...], table_ref[...])
    norm = norm_ref[...]

    def gradient(n, low):
        d_ref[n] = low
        db_ref[n : n + 1, :] = columns_sum(low.astype(F32))
        at = pl.ds(pl.multiple_of(n * width + group * 256, 256), 256)
        g_all[:, at] = dot_tn(norm, low).astype(BF)

    d_angle = 0.0
    for n, (grad, turned_ref) in enumerate(((dq_ref, q_ref), (dk_ref, k_ref))):
        g1, g2 = grad[:, :128], grad[:, 128:]
        d_angle = d_angle + (g2 * turned_ref[:, :128] - g1 * turned_ref[:, 128:])
        back = jnp.concatenate([g1 * c + g2 * s, g2 * c - g1 * s], 1).astype(BF)
        gradient(n, dot(back, back_ref[...]).astype(BF))
    freq_ref[...] = lax.dot_general(
        grid_ref[...], d_angle, (((1,), (0,)), ((), ())),
        preferred_element_type=F32, precision=lax.Precision.HIGHEST,
    )
    gradient(2, dv_ref[...].astype(BF))

    @pl.when(group == width // 256 - 1)
    def _():
        slices_out(place_ref[0], g_all, keep_ref, send_ref, 0, sem, slices, width // slices)
        slices_wait(g_all, keep_ref, sem, slices, width // slices)


def turn_back_call(
    place, x, vectors, dq, dk, dv, q_exact, k_exact, onehot, table, grid8, back, first, slices
):
    rows, width = dk.shape
    sds = jax.ShapeDtypeStruct
    part = pl.BlockSpec((rows, 256), lambda g: (0, g))
    hot = pl.BlockSpec(
        (pl.Element(rows), pl.Element(onehot.shape[1])),
        lambda g: (pl.multiple_of(first + 0 * g, BLK), 0),
    )
    return pl.pallas_call(
        functools.partial(turn_back_kernel, slices=slices),
        grid=(width // 256,),
        in_specs=[SMEM, whole(x.shape), whole(vectors.shape)]
        + [part] * 5
        + [
            hot,
            pl.BlockSpec((table.shape[0], 512), lambda g: (0, g)),
            whole(grid8.shape),
            whole(back.shape),
        ],
        out_specs=[
            pl.BlockSpec((3, rows, 256), lambda g: (0, 0, g)),
            pl.BlockSpec((3, 256), lambda g: (0, g)),
            pl.BlockSpec((8, 128), lambda g: (0, g)),
        ]
        + [ANY] * 2,
        out_shape=[
            sds((3, rows, width), BF),
            sds((3, width), F32),
            sds((8, width // 2), F32),
        ]
        + [sds((slices // 2, width // slices, 3 * width), BF)] * 2,
        scratch_shapes=[
            pltpu.VMEM((rows, width), BF),
            pltpu.VMEM((width, 3 * width), BF),
            pltpu.SemaphoreType.DMA((slices,)),
        ],
        compiler_params=params(),
        cost_estimate=cost(9),
        name="turn_back",
    )(place, x, vectors, dq, dk, dv, q_exact, k_exact, onehot, table, grid8, back)


def input_grad_kernel(x_ref, vec_ref, d_ref, w_ref, dh_ref, out_ref, small_ref):
    width = x_ref.shape[1]
    d_norm = sum(dot_nt(d_ref[n], w_ref[:, lanes_of(n, width)]) for n in range(3))
    xhat, inverse = norm_parts(x_ref[...].astype(F32))
    small_ref[0:1, :] = columns_sum(d_norm * xhat)
    small_ref[1:2, :] = columns_sum(d_norm)
    out_ref[...] = dh_ref[...] + norm_back(d_norm, xhat, inverse, vec_ref[LN1_GAIN])


def input_grad_call(x, vectors, d_qkv, weight, d_hidden):
    rows, width = x.shape
    return pl.pallas_call(
        input_grad_kernel,
        out_shape=[
            jax.ShapeDtypeStruct((rows, width), F32),
            jax.ShapeDtypeStruct((2, width), F32),
        ],
        compiler_params=params(),
        cost_estimate=cost(7),
        name="input_grad",
    )(x, vectors, d_qkv, weight, d_hidden)


def assemble_kernel(place_ref, *refs, split, outs):
    out_refs, (held, sem) = refs[4 : 4 + outs], refs[4 + outs :]
    pairs = refs[:4]
    piece_refs = [pairs[n // 2].at[n % 2] for n in range(8)]
    place, depth = place_ref[0], place_ref[1]
    slot = pl.program_id(0)

    def copy(ref, target):
        return pltpu.make_async_copy(ref, held.at[target], sem.at[target])

    @pl.when(slot == 0)
    def _():
        for ref, source in gathered(place, piece_refs):
            copy(ref, source).start()

    copy(piece_refs[0], slot).wait()
    rows = held.shape[-2]
    out_refs, squares = out_refs[:-1], out_refs[-1]

    @pl.when(slot == 0)
    def _():
        squares[...] = jnp.zeros_like(squares)

    def add_squares(block):
        total = fold8(block * block, jnp.sum)
        squares[...] += sum(total[:, lanes_of(n, 128)] for n in range(block.shape[1] // 128))

    if split:
        for n in range(split):
            block = held[slot, (depth - n + split) % split].astype(F32)
            add_squares(block)
            lo = 0
            for ref in out_refs:
                ref[n * rows : n * rows + rows, :] = block[:, lo : lo + ref.shape[1]]
                lo += ref.shape[1]
    else:
        block = held[slot].astype(F32)
        add_squares(block)
        each = held.shape[0] // len(out_refs)
        for n, ref in enumerate(out_refs):

            @pl.when(slot // each == n)
            def _():
                ref[...] = block


def assemble_call(place, arrays, shapes, split):
    pieces = 8
    rows = arrays[0].shape[-2] * max(split, 1)
    each = pieces if split else pieces // len(shapes)

    def spec(n, shape):
        lead = 0 if split else n * each
        return pl.BlockSpec((rows, shape[1]), lambda i: (jnp.clip(i - lead, 0, each - 1), 0))

    specs = [spec(n, shape) for n, shape in enumerate(shapes)] + [whole((8, 128))]
    shapes = shapes + [(8, 128)]
    return pl.pallas_call(
        functools.partial(assemble_kernel, split=split, outs=len(shapes)),
        grid=(pieces,),
        in_specs=[SMEM] + [ANY] * len(arrays),
        out_specs=specs,
        out_shape=[jax.ShapeDtypeStruct(s, F32) for s in shapes],
        scratch_shapes=[
            pltpu.VMEM((pieces,) + arrays[0].shape[1:], BF),
            pltpu.SemaphoreType.DMA((pieces,)),
        ],
        compiler_params=params(),
        cost_estimate=cost(6),
        name="assemble",
    )(place, *arrays)


def send(x, axis, pairs):
    return lax.ppermute(x, axis, pairs)


def plane_gather(piece):
    pair = jnp.stack([piece, send(piece, PLANE, FIRST)])
    return pair, send(pair, PLANE, SECOND)


def core_gather(pair, last):
    return [pair, last, send(pair, "c", SWAP), send(last, "c", SWAP)]


def wide_sum(x, extra):
    return lax.psum(x, "e") if extra > 1 else x


def sum_low(*terms):
    return functools.reduce(lambda x, y: x + y, [t.astype(F32) for t in terms])


def chip_sums(kept, far):
    total = [
        jnp.concatenate([sum_low(x[n], y[n]) for x, y in zip(kept, far)], 0).astype(BF)
        for n in range(4)
    ]
    return jnp.stack([total[1], total[3]]), (total[0], total[2])


def after(x, *others):
    return lax.optimization_barrier((x, others))[0]


def ring(size, step):
    return [(i, (i + step) % size) for i in range(size)]


def add_from(vector, axis, reach=0, size=2):
    return vector + send(vector, axis, [(i, i ^ (reach or 1)) for i in range(size)])


def on_device(
    tokens,
    segment,
    padding,
    coords,
    ln1_gain,
    ln1_shift,
    query_key_value_weight,
    b_qkv,
    output_weight,
    b_out,
    rope_freqs,
    ln2_gain,
    ln2_shift,
    w_up,
    b_up,
    w_down,
    b_down,
    cotangent,
    *,
    extra,
    depth,
):
    tokens, cotangent = tokens[0], cotangent[0]
    own, width = tokens.shape
    length = own * depth
    heads = rope_freqs.shape[1]
    half = width // heads // 2
    groups = heads // GROUP
    slices = 8
    outer = BLK
    side = own + outer
    win = own + 2 * side
    blocks = own // BLK
    z = lax.axis_index("n")
    plane = lax.axis_index("a") * 4 + lax.axis_index("b") * 2 + lax.axis_index("c")
    place = jnp.stack([plane, z]).astype(jnp.int32)
    up = [(i, i + 1) for i in range(depth - 1)]
    down = [(i + 1, i) for i in range(depth - 1)]
    up2 = [(i, i + 2) for i in range(depth - 2)]
    down2 = [(i + 2, i) for i in range(depth - 2)]

    def around(x, head, tail):
        before2 = send(tail, "n", up2)
        before = send(x, "n", up)
        after_ = send(x, "n", down)
        after2 = send(head, "n", down2)
        return [before2, before, after_, after2]

    position = jnp.arange(length, dtype=jnp.int32)
    ident = jnp.where(padding[0] == 0, segment[0], 1000 + position)
    ident = jnp.concatenate(
        [jnp.full((side,), -1, jnp.int32), ident, jnp.full((side,), 1 << 20, jnp.int32)]
    )
    ident_win = lax.dynamic_slice_in_dim(ident, z * own, win, 0)
    near = lax.broadcasted_iota(jnp.int32, (win,), 0)
    ident_win = jnp.where(near < outer - REACH, -1, ident_win)
    ident_win = jnp.where(near >= win - outer + REACH, 1 << 20, ident_win)
    idk = jnp.broadcast_to(ident_win[:, None], (win, BLK))
    idq = ident_win.reshape(win // BLK, BLK)

    lowest, highest = idq[:, 0], idq[:, BLK - 1]

    def bounds(queries, keys):
        before = highest[keys][None, :] < lowest[queries][:, None]
        reached = lowest[keys][None, :] <= highest[queries][:, None]
        return jnp.sum(before, 1), jnp.sum(reached, 1)

    def steps(blocks, span):
        return (jnp.maximum(blocks, 0) + span - 1) // span

    mid = slice(side // BLK, side // BLK + blocks)
    lo, hi = bounds(mid, slice(None))
    bounds_fwd = [
        lo, steps(hi - lo, SPAN), jnp.minimum(lo, mid.start), steps(mid.start - lo, SPAN_SIDE),
        steps(hi - mid.stop, SPAN_SIDE),
    ]
    bounds_fwd = jnp.stack(bounds_fwd, 1).astype(jnp.int32)
    lo, hi = bounds(slice(None), mid)
    bounds_bwd = jnp.stack([lo, steps(hi - lo, SPAN_BACK)], 1).astype(jnp.int32)

    grid = jnp.pad(coords[:, 0], ((0, 0), (side, side)))
    grid_win = lax.dynamic_slice_in_dim(grid, z * own, win, 1)
    grid_own = lax.dynamic_slice_in_dim(grid, z * own + side, own, 1)
    lane = jnp.arange(4 * SIDE)
    picked = jnp.where(lane[None, :] < 2 * SIDE, grid_win[0][:, None], grid_win[1][:, None])
    onehot = (picked == (lane % SIDE)[None, :]).astype(BF)
    table = turn_table(rope_freqs)

    local = np.arange(256)
    order = np.zeros((256, 256), np.float32)
    order[(local % 128) // 32 * 64 + local // 128 * 32 + local % 32, local] = 1.0
    order = jnp.asarray(order, BF)
    qk_bias = b_qkv[: 2 * width].reshape(2 * groups, GROUP, 2, half).swapaxes(1, 2)
    bias_turned = jnp.concatenate([qk_bias.reshape(-1), b_qkv[2 * width :]])

    x_parts = around(tokens, tokens[:REACH], tokens[own - REACH :])
    vectors = jnp.stack([ln1_gain, ln1_shift, b_out, ln2_gain, ln2_shift, b_down])
    rot_q, rot_k, values, q_exact, k_exact, weight_turned = qkv_own_call(
        tokens, onehot, vectors, query_key_value_weight, bias_turned, order, table, side
    )

    rows = (width + w_down.shape[0]) // slices
    eighth = jnp.where(
        plane < width // rows,
        lax.dynamic_slice_in_dim(w_up, jnp.minimum(plane * rows, width - rows), rows, 0),
        lax.dynamic_slice_in_dim(w_down, jnp.maximum(plane * rows - width, 0), rows, 0),
    )
    left, bias_rows = b_up, []
    for _ in range(3):
        bias_rows.append(left.astype(BF))
        left = left - rounded(left)
    bias_rows = jnp.pad(jnp.stack(bias_rows), ((0, 13), (0, 0)))
    eighth = jnp.concatenate([eighth, bias_rows], 0)
    others = [send(eighth, "n", ring(depth, k)) for k in range(1, depth)]
    x_parts, rot_q = lax.optimization_barrier((x_parts, rot_q))
    rot_q, rot_k, values = qkv_halo_call(
        x_parts, onehot, vectors, weight_turned, bias_turned, table, rot_q, rot_k, values, side
    )
    part = forward_call(bounds_fwd, rot_q, rot_k, values, idk, idq, side, own, 0, blocks // 2)
    others, part = lax.optimization_barrier((others, part))
    up_biases = jnp.concatenate(
        [jnp.sum(x[rows : rows + 3].astype(F32), 0, keepdims=True) for x in others]
    )
    own_w = jnp.stack([x[:rows] for x in others])
    over_1, over_2 = send(own_w, PLANE, FIRST), send(own_w, PLANE, SECOND)
    part, _ = lax.optimization_barrier((part, own_w))
    mixed, mixed_low, lse = forward_call(
        bounds_fwd, rot_q, rot_k, values, idk, idq, side, own, blocks // 2, blocks // 2, part
    )
    hidden_in, norm2, out0, dn0, up_sum0, kept_own, sent_own = middle_own_call(
        place, tokens, mixed_low, output_weight, vectors, cotangent, b_up[None],
        w_up, w_down, slices,
    )
    over_1, over_2, norm2 = lax.optimization_barrier((over_1, over_2, norm2))
    diagonal = send(over_1, PLANE, SECOND)
    far_own = send(after(sent_own, over_1, over_2), "c", SWAP)
    near = [own_w, over_1, over_2, diagonal]
    pieces = near + [send(x, "c", SWAP) for x in near]
    norm2 = after(norm2, far_own)
    split = depth - 2
    out1, dn1, up_sum1, kept_next, sent_next = middle_next_call(
        place, norm2, out0, dn0, cotangent, up_biases[:split], pieces, slices, 0
    )
    far_next = send(sent_next, "c", SWAP)
    (
        activations, d_hidden, d_heads, d_head, d_tail, delta, small_mid, up_sum2, kept_last,
        sent_last,
    ) = middle_last_call(
        place, hidden_in, norm2, out1, dn1, mixed_low, mixed, output_weight, vectors, cotangent,
        up_biases[split:], lse, pieces, slices, split,
    )
    up_sums = (up_sum0, up_sum1, up_sum2)
    far_next, d_heads = lax.optimization_barrier((far_next, d_heads))
    away_a, rest_a = chip_sums((kept_own, kept_next), (far_own, far_next))
    got_1a = send(away_a, PLANE, FIRST)
    far_last = send(sent_last, "c", SWAP)
    do_parts = around(d_heads, d_head, d_tail)

    dq, dk, dv = backward_own_call(
        bounds_fwd, rot_q, d_heads, rot_k, values, idk, idq, lse, delta, side, own
    )
    got_1a, far_last, dq = lax.optimization_barrier((got_1a, far_last, dq))
    away_a = sum_low(rest_a[1], got_1a[1]).astype(BF)
    got_2a = send(away_a, PLANE, SECOND)
    away_b, rest_b = chip_sums((kept_last,), (far_last,))
    got_1b = send(away_b, PLANE, FIRST)
    do_parts, dq, dk, _ = lax.optimization_barrier((do_parts, dq, dk, (away_a, away_b)))
    dk, dv = backward_halo_call(
        bounds_bwd, rot_q, do_parts, rot_k, values, idk, idq, dk, dv, side
    )
    got_1b, got_2a, dk = lax.optimization_barrier((got_1b, got_2a, dk))
    away_b = sum_low(rest_b[1], got_1b[1]).astype(BF)
    got_2b = send(away_b, PLANE, SECOND)

    def part_a(k):
        at = slice(k * rows, k * rows + rows)
        return wide_sum(sum_low(rest_a[0][at], got_1a[0, at], got_2a[at]), extra)

    ff_sent = [part_a(k).astype(BF) for k in range(1, depth - 1)]
    ff_got = [send(ff_sent[k - 1], "n", ring(depth, -k)) for k in range(1, depth - 1)]
    dk = after(dk, away_b, ff_sent)

    grid8 = jnp.pad(grid_own.astype(F32), ((0, 6), (0, 0)))
    d_qkv, grad_b_qkv, freqs8, kept_qkv, sent_qkv = turn_back_call(
        place, tokens, vectors, dq, dk, dv, q_exact, k_exact, onehot, table, grid8,
        order.T, side, slices,
    )
    far_qkv = send(sent_qkv, "c", SWAP)
    got_2b, far_qkv, d_qkv = lax.optimization_barrier((got_2b, far_qkv, d_qkv))
    away, rest_qkv = chip_sums((kept_qkv,), (far_qkv,))
    got_1_qkv = send(away, PLANE, FIRST)

    def part_b(lo, hi):
        at = slice(lo, hi)
        return wide_sum(sum_low(rest_b[0][at], got_1b[0, at], got_2b[at]), extra)

    got_2b = after(got_2b, away)
    ff_sent = part_b(0, rows).astype(BF)
    ff_got.append(send(ff_sent, "n", ring(depth, 1 - depth)))
    input_grad, small_in = input_grad_call(
        tokens, vectors, after(d_qkv, away, ff_sent), query_key_value_weight, d_hidden
    )
    got_1_qkv, small_in = lax.optimization_barrier((got_1_qkv, small_in))
    away = sum_low(rest_qkv[1], got_1_qkv[1]).astype(BF)
    got_2_qkv = send(away, PLANE, SECOND)
    ff_got, small_in, _ = lax.optimization_barrier((ff_got, small_in, away))
    ff_total = part_a(0) + sum_low(*ff_got)
    plane_qkv = wide_sum(sum_low(rest_qkv[0], got_1_qkv[0], got_2_qkv), extra)

    slot = (z - jnp.arange(depth)) % depth
    quarter_sums = jnp.take(jnp.concatenate(up_sums), slot, axis=0)
    named = [
        small_in[0], small_in[1], grad_b_qkv.reshape(-1), small_mid[3], freqs8[:2].reshape(-1),
        small_mid[0], small_mid[1], small_mid[2], quarter_sums.reshape(-1),
    ]
    small = add_from(jnp.concatenate(named).reshape(-1, 128), "c")

    part = jnp.concatenate([plane_qkv, part_b(rows, rows + width // slices)], 1).astype(BF)
    thin = part.shape[0] // depth
    cut = lambda k: lax.dynamic_slice_in_dim(part, ((z + k) % depth) * thin, thin, 0)
    got = [send(cut(k), "n", ring(depth, k)) for k in range(1, depth)]
    small = add_from(add_from(after(small, part), "b"), "a")
    if extra > 1:
        small = lax.psum(small, "e")
    got, small = lax.optimization_barrier((got, small))
    low = sum_low(cut(0), *got).astype(BF)
    strip = jnp.stack([low] + [send(low, "n", ring(depth, k)) for k in range(1, depth)])
    ff_pair, ff_last = plane_gather(after(ff_total, low).astype(BF))
    pair, last = plane_gather(strip)
    ff_pieces = [after(x, strip) for x in core_gather(ff_pair, ff_last)]
    total_w_up, total_w_down, ff_squares = assemble_call(
        place, ff_pieces, [w_up.shape, w_down.shape], 0
    )
    small = jnp.concatenate([small, ff_squares], 0)
    reach = 1
    while reach < depth:
        small = add_from(small, "n", reach, depth)
        reach *= 2
    last, small = lax.optimization_barrier((last, small))
    total_w_qkv, total_w_out, squares = assemble_call(
        place, core_gather(pair, last), [query_key_value_weight.shape, output_weight.shape], depth
    )
    small, large_sq = small[:-8].reshape(-1), jnp.sum(small[-8:] + squares)

    out, at = [], 0
    for vector in named:
        out.append(small[at : at + vector.size])
        at += vector.size
    t_gain1, t_shift1, t_b_qkv, t_b_out, t_freqs, t_gain2, t_shift2, t_b_down, t_up = out
    t_freqs = t_freqs.reshape(rope_freqs.shape)
    rot_sq = jnp.sum(t_freqs * t_freqs)
    skip = sum(v.size for v in named[:4])
    lane = jnp.arange(small.size)
    others = (lane < skip) | (lane >= skip + freqs8.shape[1] * 2)
    other_sq = large_sq + jnp.sum(jnp.where(others, small * small, 0.0))
    t_b_up = lax.dynamic_slice_in_dim(t_up, z * b_up.shape[0], b_up.shape[0], 0)
    return (
        activations[None],
        input_grad[None],
        t_gain1,
        t_shift1,
        total_w_qkv,
        t_b_qkv,
        total_w_out,
        t_b_out,
        t_freqs,
        t_gain2,
        t_shift2,
        total_w_up,
        t_b_up,
        total_w_down,
        t_b_down,
        rot_sq,
        other_sq,
    )


def solution(mesh):
    wide, depth = mesh.shape["wide"], mesh.shape["narrow"]
    extra = wide // 8
    fine = Mesh(mesh.devices.reshape(extra, 2, 2, 2, depth), ("e", "a", "b", "c", "n"))
    w, n = ("e", "a", "b", "c"), "n"
    return jax.shard_map(
        functools.partial(on_device, extra=extra, depth=depth),
        mesh=fine,
        in_specs=(
            P(w, n, None), P(w, None), P(w, None), P(None, w, None),
            P(), P(), P(), P(), P(), P(), P(), P(), P(),
            P(None, n), P(n), P(n, None), P(), P(w, n, None),
        ),
        out_specs=(
            P(w, n, None), P(w, n, None),
            P(), P(), P(), P(), P(), P(), P(), P(), P(),
            P(None, n), P(n), P(n, None), P(), P(), P(),
        ),
        check_vma=False,
    )
```

```python
import functools

import jax
import jax.numpy as jnp
import numpy as np
from jax import lax
from jax.experimental import pallas as pl
from jax.experimental.pallas import tpu as pltpu
from jax.sharding import Mesh, PartitionSpec as P

EPS = 1e-06
MASKED = -1e30
BLK = 128
SPAN = 6
SPAN_SIDE = 3
SPAN_BACK = 2
GROUP = 4
REACH = 64
STAT_ROWS = 6
STAT_PAD = 16
SIDE = 32
LN1_GAIN, LN1_SHIFT, B_OUT, LN2_GAIN, LN2_SHIFT, B_DOWN = (slice(n, n + 1) for n in range(6))
LOG2E = np.float32(1.4426950408889634)
BF = jnp.bfloat16
F32 = jnp.float32
PLANE = ("a", "b", "c")
SWAP = [(0, 1), (1, 0)]
FIRST = [(i, i ^ (4 if i % 2 else 2)) for i in range(8)]
SECOND = [(i, i ^ (2 if i % 2 else 4)) for i in range(8)]
VMEM_LIMIT = 56 * 1024 * 1024


def dot(left, right):
    return lax.dot_general(left, right, (((1,), (0,)), ((), ())), preferred_element_type=F32)


def dot_nt(left, right):
    return lax.dot_general(left, right, (((1,), (1,)), ((), ())), preferred_element_type=F32)


def dot_tn(left, right):
    return lax.dot_general(left, right, (((0,), (0,)), ((), ())), preferred_element_type=F32)


def params(**kw):
    return pltpu.CompilerParams(vmem_limit_bytes=VMEM_LIMIT, **kw)


def cost(us):
    return pl.CostEstimate(
        flops=int(us * 1.15e9), bytes_accessed=int(us * 3.0e6), transcendentals=0
    )


def whole(shape):
    return pl.BlockSpec(shape, lambda *_: (0,) * len(shape))


ANY = pl.BlockSpec(memory_space=pl.ANY)
SMEM = pl.BlockSpec(memory_space=pltpu.SMEM)


def rounded(x):
    return lax.reduce_precision(x, exponent_bits=8, mantissa_bits=7)


def turn_table(rope_freqs):
    lanes = rope_freqs.shape[1] * rope_freqs.shape[2]
    freq = rope_freqs.reshape(2, 1, lanes)
    angle = jnp.arange(SIDE, dtype=F32)[None, :, None] * freq
    cosine, sine = jnp.cos(angle), jnp.sin(angle)

    def halves(x):
        return jnp.concatenate([x.astype(BF), (x - rounded(x)).astype(BF)], 0)

    def grouped(x):
        return x.reshape(2 * SIDE, lanes // 128, 1, 128)

    zero = jnp.zeros((2 * SIDE, lanes // 128, 2, 128), BF)
    rows = jnp.concatenate([grouped(halves(cosine[0])), grouped(halves(sine[0])), zero], 2)
    cols = jnp.concatenate([zero, grouped(halves(cosine[1])), grouped(halves(sine[1]))], 2)
    return jnp.concatenate([rows, cols], 0).reshape(4 * SIDE, 4 * lanes)


def cos_sin(onehot, table):
    parts = dot(onehot, table)
    cr, sr, cc, sc = (parts[:, lanes_of(n, 128)] for n in range(4))
    return cr * cc - sr * sc, sr * cc + cr * sc


def layer_norm_low(x, gain, shift):
    centred = x - jnp.mean(x, -1, keepdims=True)
    var = jnp.mean(centred * centred, -1, keepdims=True)
    return (centred * lax.rsqrt(var + EPS) * gain + shift).astype(BF)


def project(norm, hot_ref, table_ref, weights, b_ref, outs, exact=()):
    width = norm.shape[1]
    for g in range(width // 256):
        c, s = cos_sin(hot_ref[...], table_ref[:, lanes_of(g, 512)])
        for n, out in outs:
            lo = n * width + 256 * g
            proj = dot(norm, weights[:, lo : lo + 256]) + b_ref[:, lo : lo + 256]
            if n == 2:
                out[:, lanes_of(g)] = proj.astype(BF)
                continue
            for half, turned in enumerate(
                (proj[:, :128] * c - proj[:, 128:] * s, proj[:, :128] * s + proj[:, 128:] * c)
            ):
                at = slice(256 * g + 128 * half, 256 * g + 128 * half + 128)
                out[:, at] = turned.astype(BF)
                if exact:
                    exact[n][:, at] = turned


def qkv_own_kernel(
    x_ref, hot_ref, vec_ref, w_ref, b_ref, order_ref, table_ref,
    q_ref, k_ref, v_ref, pq_ref, pk_ref, w_turned,
):
    width = x_ref.shape[1]

    @pl.when(pl.program_id(0) == 0)
    def _():
        for g in range(2 * width // 256):
            at = slice(256 * g, 256 * g + 256)
            w_turned[:, at] = dot(w_ref[:, at], order_ref[...]).astype(BF)
        w_turned[:, 2 * width :] = w_ref[:, 2 * width :]

    norm = layer_norm_low(x_ref[...].astype(F32), vec_ref[LN1_GAIN], vec_ref[LN1_SHIFT])
    outs = [(0, q_ref), (1, k_ref), (2, v_ref)]
    project(norm, hot_ref, table_ref, w_turned, b_ref, outs, (pq_ref, pk_ref))


def qkv_own_call(x, onehot, vectors, weight, bias, order, table, first):
    own, width = x.shape
    rows = onehot.shape[0]
    tile = 256
    shape = jax.ShapeDtypeStruct((rows, width), BF)
    exact = jax.ShapeDtypeStruct((own, width), F32)
    row = lambda w: pl.BlockSpec((tile, w), lambda i: (i, 0))
    inside = lambda w: pl.BlockSpec(
        (pl.Element(tile), pl.Element(w)), lambda i: (pl.multiple_of(first + tile * i, BLK), 0)
    )
    return pl.pallas_call(
        qkv_own_kernel,
        grid=(own // tile,),
        in_specs=[
            row(width),
            inside(onehot.shape[1]),
            whole(vectors.shape),
            whole(weight.shape),
            whole((1, 3 * width)),
            whole(order.shape),
            whole(table.shape),
        ],
        out_specs=[inside(width)] * 3 + [row(width)] * 2 + [whole(weight.shape)],
        out_shape=[shape] * 3 + [exact] * 2 + [jax.ShapeDtypeStruct(weight.shape, BF)],
        compiler_params=params(),
        cost_estimate=cost(8),
        name="qkv_own",
    )(x, onehot, vectors, weight, bias[None], order, table)


def halo_kernel(
    far_l, near_l, near_r, far_r, hot_ref, vec_ref, w_ref, b_ref, table_ref, *refs, which
):
    refs = refs[len(which) :]
    out_refs, (x_all, sem) = refs[: len(which)], refs[len(which) :]
    width = x_all.shape[1]
    step = pl.program_id(0)
    tile = out_refs[0].shape[0]

    @pl.when(step == 0)
    def _():
        own, reach = near_l.shape[0], far_l.shape[0]
        total = x_all.shape[0]
        blank = total // 2 - own - reach
        copies = []
        at = blank
        for n, ref in enumerate((far_l, near_l, near_r, far_r)):
            copies.append(
                pltpu.make_async_copy(ref, x_all.at[at : at + ref.shape[0], :], sem.at[n])
            )
            copies[-1].start()
            at += ref.shape[0]
        x_all[:blank, :] = jnp.zeros((blank, width), BF)
        x_all[total - blank :, :] = jnp.zeros((blank, width), BF)
        for copy in copies:
            copy.wait()

    x = x_all[pl.ds(pl.multiple_of(step * tile, tile), tile), :].astype(F32)
    norm = layer_norm_low(x, vec_ref[LN1_GAIN], vec_ref[LN1_SHIFT])
    project(norm, hot_ref, table_ref, w_ref, b_ref, list(zip(which, out_refs)))


def halo_call(pieces, onehot, vectors, weight, bias, table, arrays, which, first):
    rows, width = arrays[0].shape
    own = pieces[1].shape[0]
    tile = first // 2
    at = lambda w: pl.BlockSpec(
        (pl.Element(tile), pl.Element(w)),
        lambda i: (pl.multiple_of(tile * i + jnp.where(i >= 2, own, 0), 64), 0),
    )
    return pl.pallas_call(
        functools.partial(halo_kernel, which=which),
        grid=(4,),
        in_specs=[ANY] * 4
        + [
            at(onehot.shape[1]),
            whole(vectors.shape),
            whole(weight.shape),
            whole((1, 3 * width)),
            whole(table.shape),
        ]
        + [ANY] * len(which),
        out_specs=[at(width)] * len(which),
        out_shape=[jax.ShapeDtypeStruct((rows, width), BF)] * len(which),
        input_output_aliases={9 + n: n for n in range(len(which))},
        scratch_shapes=[pltpu.VMEM((2 * first, width), BF), pltpu.SemaphoreType.DMA((4,))],
        compiler_params=params(),
        cost_estimate=cost(4 * len(which)),
        name="halo",
    )(*pieces, onehot, vectors, weight, bias[None], table, *arrays)


def head_stack(block, turned, scale=None):
    lane = lax.broadcasted_iota(jnp.int32, block.shape, 1)
    head = (lane % 128) // 32 if turned else lane // 64
    if scale is not None:
        block = block * scale
    zero = jnp.zeros_like(block)
    return jnp.concatenate([jnp.where(head == h, block, zero) for h in range(GROUP)], 0)


def fold8(x, op):
    return op(x.reshape(x.shape[0] // 8, 8, x.shape[1]), axis=0)


def key_span(ident_ref, ident_q, start, c, span, end):
    block = jnp.minimum(start + c * span, end - span)
    lower = (start + c * span - block) * BLK
    at = pl.ds(pl.multiple_of(block * BLK, BLK), span * BLK)
    row = lax.broadcasted_iota(jnp.int32, (span * BLK, BLK), 0)
    return at, (ident_ref[at, :] == ident_q) & (row >= lower)


def lanes_of(g, size=256):
    return slice(size * g, size * g + size)


def forward_kernel(
    bound_ref, q_ref, k_ref, v_ref, idk_ref, idq_ref, *refs, first, base
):
    o_ref, low_ref, lse_ref, s_ref, acc_ref, q4_ref = refs[-6:]
    i = pl.program_id(0) + base
    groups = k_ref.shape[1] // 256
    lanes = GROUP * BLK
    window = k_ref.shape[0] // BLK
    start, count = bound_ref[i, 0], bound_ref[i, 1]
    for g in range(groups):
        q4_ref[g] = head_stack(q_ref[:, lanes_of(g)], True, jnp.asarray(0.125, BF))
    ident_q = idq_ref[pl.ds(first // BLK + i, 1), :]

    def scores(c, top):
        at, seen = key_span(idk_ref, ident_q, start, c, SPAN, window)
        here = pl.ds(pl.multiple_of(c * SPAN * BLK, BLK), SPAN * BLK)
        tops = []
        for g in range(groups):
            s = dot_nt(k_ref[at, lanes_of(g)], q4_ref[g]) * LOG2E
            for h in range(GROUP):
                masked = jnp.where(seen, s[:, lanes_of(h, BLK)], MASKED)
                s_ref[g, here, lanes_of(h, BLK)] = masked
                tops.append(fold8(masked, jnp.max))
        return jnp.maximum(top, jnp.concatenate(tops, 1))

    top = lax.fori_loop(0, count, scores, jnp.full((8, groups * lanes), -3e38, F32))
    top = jnp.max(top, 0, keepdims=True)
    acc_ref[...] = jnp.zeros_like(acc_ref)

    def mix(c, total):
        at, _ = key_span(idk_ref, ident_q, start, c, SPAN, window)
        here = pl.ds(pl.multiple_of(c * SPAN * BLK, BLK), SPAN * BLK)
        sums = []
        for g in range(groups):
            e = jnp.exp2(s_ref[g, here, :] - top[:, lanes_of(g, lanes)])
            sums.append(fold8(e, jnp.sum))
            acc_ref[g] += dot_tn(v_ref[at, lanes_of(g)], e.astype(BF))
        return total + jnp.concatenate(sums, 1)

    total = lax.fori_loop(0, count, mix, jnp.zeros((8, groups * lanes), F32))
    total = jnp.sum(total, 0, keepdims=True)
    lse = top + jnp.log(total) * LOG2E
    inverse = 1.0 / total
    for g in range(groups):
        lse_ref[g] = lse[:, lanes_of(g, lanes)]
        acc = acc_ref[g] * inverse[:, lanes_of(g, lanes)]
        out = jnp.concatenate(
            [acc[64 * h : 64 * h + 64, lanes_of(h, BLK)] for h in range(GROUP)], 0
        ).T
        o_ref[:, lanes_of(g)] = out
        low_ref[:, lanes_of(g)] = out.astype(BF)


def stat_spec(groups, base=0):
    return pl.BlockSpec((groups, None, 1, GROUP * BLK), lambda i: (0, i + base, 0, 0))


def query_rows(first, width):
    return pl.BlockSpec(
        (pl.Element(BLK), pl.Element(width)), lambda i: (pl.multiple_of(first + BLK * i, BLK), 0)
    )


def forward_call(bounds, q_win, k_win, v_win, idk, idq, first, own, base, count, earlier=()):
    win, width = k_win.shape
    groups, blocks = width // 256, own // BLK
    row = pl.BlockSpec((BLK, width), lambda i: (i + base, 0))
    steps = -(-win // (SPAN * BLK))
    return pl.pallas_call(
        functools.partial(forward_kernel, first=first, base=base),
        grid=(count,),
        in_specs=[SMEM, query_rows(first + base * BLK, width)]
        + [whole((win, width))] * 2
        + [whole(idk.shape), whole(idq.shape)]
        + [ANY] * len(earlier),
        out_specs=[row, row, stat_spec(groups, base)],
        input_output_aliases={6 + n: n for n in range(len(earlier))},
        out_shape=[
            jax.ShapeDtypeStruct((own, width), F32),
            jax.ShapeDtypeStruct((own, width), BF),
            jax.ShapeDtypeStruct((groups, blocks, 1, GROUP * BLK), F32),
        ],
        scratch_shapes=[
            pltpu.VMEM((groups, steps * SPAN * BLK, GROUP * BLK), F32),
            pltpu.VMEM((groups, 256, GROUP * BLK), F32),
            pltpu.VMEM((groups, GROUP * BLK, 256), BF),
        ],
        compiler_params=params(),
        cost_estimate=cost(4 * count),
        name="attention_forward",
    )(bounds, q_win, k_win, v_win, idk, idq, *earlier)


def score_gradients(s, dp, lse, delta, seen):
    low_p, low_ds = [], []
    for h in range(GROUP):
        at = lanes_of(h, BLK)
        p = jnp.exp2(jnp.where(seen, s[:, at] * LOG2E - lse[:, at], MASKED))
        low_p.append(p.astype(BF))
        low_ds.append((p * (dp[:, at] - delta[:, at])).astype(BF))
    return jnp.concatenate(low_p, 1), jnp.concatenate(low_ds, 1)


def backward_own_kernel(
    bound_ref, q_ref, do_ref, k_ref, v_ref, idk_ref, idq_ref, lse_ref, delta_ref,
    dq_ref, dk_ref, dv_ref, acc_ref, q4_ref, do4_ref, *, first,
):
    i = pl.program_id(0)
    groups = k_ref.shape[1] // 256
    own = dk_ref.shape[0]

    @pl.when(i == 0)
    def _():
        dk_ref[...] = jnp.zeros_like(dk_ref)
        dv_ref[...] = jnp.zeros_like(dv_ref)

    for g in range(groups):
        q4_ref[g] = head_stack(q_ref[:, lanes_of(g)], True, jnp.asarray(0.125, BF))
        do4_ref[g] = head_stack(do_ref[:, lanes_of(g)], False)
    ident_q = idq_ref[pl.ds(first // BLK + i, 1), :]

    def attend(at, seen, inside):
        for g in range(groups):
            keys = k_ref[at, lanes_of(g)]
            s = dot_nt(keys, q4_ref[g])
            dp = dot_nt(v_ref[at, lanes_of(g)], do4_ref[g])
            low_p, low_ds = score_gradients(s, dp, lse_ref[g], delta_ref[g], seen)
            if inside:
                acc_ref[g] = dot_tn(keys, low_ds)
                dk_ref[:, lanes_of(g)] += dot(low_ds, q4_ref[g])
                dv_ref[:, lanes_of(g)] += dot(low_p, do4_ref[g])
            else:
                acc_ref[g] += dot_tn(keys, low_ds)

    attend(slice(first, first + own), idk_ref[first : first + own, :] == ident_q, True)
    for start, count, end in (
        (bound_ref[i, 2], bound_ref[i, 3], first // BLK),
        ((first + own) // BLK, bound_ref[i, 4], k_ref.shape[0] // BLK),
    ):

        def step(c, _):
            attend(*key_span(idk_ref, ident_q, start, c, SPAN_SIDE, end), False)
            return 0

        lax.fori_loop(0, count, step, 0)
    for g in range(groups):
        acc = acc_ref[g]
        parts = [acc[32 * h : 32 * h + 32, lanes_of(h, BLK)] for h in range(GROUP)]
        parts += [acc[128 + 32 * h : 160 + 32 * h, lanes_of(h, BLK)] for h in range(GROUP)]
        dq_ref[:, lanes_of(g)] = (jnp.concatenate(parts, 0) * 0.125).T


def backward_own_call(bounds, q_win, do_own, k_win, v_win, idk, idq, lse, delta, first, own):
    win, width = k_win.shape
    groups = width // 256
    row = pl.BlockSpec((BLK, width), lambda i: (i, 0))
    return pl.pallas_call(
        functools.partial(backward_own_kernel, first=first),
        grid=(own // BLK,),
        in_specs=[SMEM, query_rows(first, width), row]
        + [whole((win, width))] * 2
        + [whole(idk.shape), whole(idq.shape), stat_spec(groups), stat_spec(groups)],
        out_specs=[row] + [whole((own, width))] * 2,
        out_shape=[jax.ShapeDtypeStruct((own, width), F32)] * 3,
        scratch_shapes=[pltpu.VMEM((groups, 256, GROUP * BLK), F32)]
        + [pltpu.VMEM((groups, GROUP * BLK, 256), BF)] * 2,
        compiler_params=params(),
        cost_estimate=cost(20),
        name="attention_backward_own",
    )(bounds, q_win, do_own, k_win, v_win, idk, idq, lse, delta)


def backward_halo_kernel(
    bound_ref, q_ref, far_l, near_l, near_r, far_r, k_ref, v_ref, idk_ref, idq_ref, dk_in, dv_in,
    dk_ref, dv_ref, q4_ref, do_all, do4_ref, stat_ref, *, first,
):
    groups = k_ref.shape[1] // 256
    own, reach = k_ref.shape[0], far_l.shape[0] - STAT_PAD
    blocks = own // BLK
    side = first // BLK
    step_id = pl.program_id(0)
    j = jnp.where(step_id < side, step_id, step_id + blocks)
    lanes = GROUP * BLK

    def stats(ref, row, slot):
        parts = ref[row : row + 2 * STAT_ROWS, :].astype(F32)
        sums = parts[0:4] + parts[4:8] + parts[8:12]
        for g in range(groups):
            for n in range(2):
                stat_ref[n, g, slot : slot + 1, :] = jnp.concatenate(
                    [sums[2 * n : 2 * n + 1, lanes_of(g)], sums[2 * n + 1 : 2 * n + 2, lanes_of(g)]],
                    1,
                )

    @pl.when(step_id == 0)
    def _():
        dk_ref[...] = dk_in[...]
        dv_ref[...] = dv_in[...]
        blank = jnp.zeros((BLK - reach, do_all.shape[1]), BF)
        do_all[0 : BLK - reach, :] = blank
        do_all[BLK - reach : BLK, :] = far_l[:reach, :]
        do_all[BLK : BLK + own, :] = near_l[:own, :]
        do_all[BLK + own : BLK + 2 * own, :] = near_r[:own, :]
        do_all[BLK + 2 * own : BLK + 2 * own + reach, :] = far_r[:reach, :]
        do_all[BLK + 2 * own + reach :, :] = blank
        stats(far_l, reach, 0)
        for i in range(blocks):
            stats(near_l, own + 2 * STAT_ROWS * i, 1 + i)
            stats(near_r, own + 2 * STAT_ROWS * i, 1 + blocks + i)
        stats(far_r, reach, 1 + 2 * blocks)

    start, count = bound_ref[j, 0], bound_ref[j, 1]

    @pl.when(count > 0)
    def _():
        here = pl.ds(pl.multiple_of(step_id * BLK, BLK), BLK)
        for g in range(groups):
            q4_ref[g] = head_stack(q_ref[:, lanes_of(g)], True, jnp.asarray(0.125, BF))
            do4_ref[g] = head_stack(do_all[here, lanes_of(g)], False)
        ident_q = idq_ref[pl.ds(j, 1), :]

        def step(c, _):
            at, seen = key_span(idk_ref, ident_q, start, c, SPAN_BACK, blocks)
            for g in range(groups):
                s = dot_nt(k_ref[at, lanes_of(g)], q4_ref[g])
                dp = dot_nt(v_ref[at, lanes_of(g)], do4_ref[g])
                lse = stat_ref[0, g, pl.ds(step_id, 1), :]
                delta = stat_ref[1, g, pl.ds(step_id, 1), :]
                low_p, low_ds = score_gradients(s, dp, lse, delta, seen)
                dk_ref[at, lanes_of(g)] += dot(low_ds, q4_ref[g])
                dv_ref[at, lanes_of(g)] += dot(low_p, do4_ref[g])
            return 0

        lax.fori_loop(0, count, step, 0)


def backward_halo_call(bounds, q_win, pieces, k_win, v_win, idk, idq, dk, dv, first):
    own, width = dk.shape
    groups = width // 256
    side, blocks = first // BLK, own // BLK
    inside = lambda w: pl.BlockSpec(
        (pl.Element(own), pl.Element(w)), lambda i: (pl.multiple_of(first + 0 * i, BLK), 0)
    )
    outside = pl.BlockSpec((BLK, width), lambda i: (jnp.where(i < side, i, i + blocks), 0))
    return pl.pallas_call(
        functools.partial(backward_halo_kernel, first=first),
        grid=(2 * side,),
        in_specs=[SMEM, outside]
        + [whole(p.shape) for p in pieces]
        + [inside(width)] * 2
        + [inside(idk.shape[1]), whole(idq.shape)]
        + [whole((own, width))] * 2,
        out_specs=[whole((own, width))] * 2,
        out_shape=[jax.ShapeDtypeStruct((own, width), F32)] * 2,
        scratch_shapes=[
            pltpu.VMEM((groups, GROUP * BLK, 256), BF),
            pltpu.VMEM((2 * first, width), BF),
            pltpu.VMEM((groups, GROUP * BLK, 256), BF),
            pltpu.VMEM((2, groups, 16, GROUP * BLK), F32),
        ],
        compiler_params=params(),
        cost_estimate=cost(11),
        name="attention_backward_halo",
    )(bounds, q_win, *pieces, k_win, v_win, idk, idq, dk, dv)


def norm_parts(x):
    centred = x - jnp.mean(x, -1, keepdims=True)
    inverse = lax.rsqrt(jnp.mean(centred * centred, -1, keepdims=True) + EPS)
    return centred * inverse, inverse


def norm_back(grad, xhat, inverse, gain):
    scaled = grad * gain
    return inverse * (
        scaled
        - jnp.mean(scaled, -1, keepdims=True)
        - xhat * jnp.mean(scaled * xhat, -1, keepdims=True)
    )


def columns_sum(x):
    return jnp.sum(x, 0, keepdims=True)


def chip_order(ab, core):
    return jnp.where(core == 0, ab, ab % 2 * 2 + ab // 2)


def slices_out(place, source, keep, away, lead, sem, slices, rows):
    for n in range(slices):
        rel = place ^ n
        for target, odd in ((keep, 0), (away, 1)):
            core = place % 2 ^ odd

            @pl.when(rel % 2 == odd)
            def _():
                pltpu.make_async_copy(
                    source.at[n * rows : (n + 1) * rows, :],
                    target.at[chip_order(rel // 2, core), pl.ds(lead, rows), :],
                    sem.at[n],
                ).start()


def gathered(place, refs):
    for far in range(2):
        for n in range(4):
            rel = 2 * chip_order(jnp.int32(n), place % 2 ^ far) + far
            yield refs[4 * far + n], place ^ rel


def slices_wait(source, keep, sem, slices, rows):
    for n in range(slices):
        pltpu.make_async_copy(
            source.at[n * rows : (n + 1) * rows, :], keep.at[0, 0:rows, :], sem.at[n]
        ).wait()


def one_quarter(q, w_all, norm_ref, dy_ref, bu_ref, dbu_ref, out_acc, dn_acc, g_all, fresh):
    own, width = norm_ref.shape
    tile = w_all.shape[1] - width
    for t in range((w_all.shape[1] - width) // tile):
        cols = slice(tile * t, tile * t + tile)
        down = slice(width + tile * t, width + tile * t + tile)
        norm, dy = norm_ref[...], dy_ref[...]
        up_w = w_all[q, :width, cols]
        down_w = w_all[q, down, :]
        pre = dot(norm, up_w) + bu_ref[pl.ds(q, 1), cols]
        cdf = 0.5 * (1.0 + lax.erf(pre * np.float32(0.7071067811865476)))
        density = jnp.exp(-0.5 * pre * pre) * np.float32(0.3989422804014327)
        act = (pre * cdf).astype(BF)
        d_pre = (dot_nt(dy, down_w) * (cdf + pre * density)).astype(BF)
        dbu_ref[pl.ds(q, 1), cols] = columns_sum(d_pre.astype(F32))
        if fresh and t == 0:
            out_acc[...] = dot(act, down_w)
            dn_acc[...] = dot_nt(d_pre, up_w)
        else:
            out_acc[...] += dot(act, down_w)
            dn_acc[...] += dot_nt(d_pre, up_w)
        g_all[q, :width, cols] = dot_tn(norm, d_pre).astype(BF)
        g_all[q, down, :] = dot_tn(act, dy).astype(BF)


def middle_own_kernel(
    place_ref, x_ref, low_ref, wo_ref, vec_ref, dy_ref, bu_ref, up_ref, down_ref,
    hid_ref, norm_ref, out_ref, dn_ref, dbu_ref, keep_ref, send_ref, w_all, g_all, w_sem, g_sem,
    *, slices,
):
    width = x_ref.shape[1]
    rows = w_all.shape[1] // slices
    copies = [
        pltpu.make_async_copy(up_ref, w_all.at[0, :width, :], w_sem.at[0]),
        pltpu.make_async_copy(down_ref, w_all.at[0, width:, :], w_sem.at[1]),
    ]
    for copy in copies:
        copy.start()
    hidden_in = x_ref[...].astype(F32) + dot(low_ref[...], wo_ref[...]) + vec_ref[B_OUT]
    hid_ref[...] = hidden_in
    norm_ref[...] = layer_norm_low(hidden_in, vec_ref[LN2_GAIN], vec_ref[LN2_SHIFT])
    for copy in copies:
        copy.wait()
    one_quarter(0, w_all, norm_ref, dy_ref, bu_ref, dbu_ref, out_ref, dn_ref, g_all, True)
    slices_out(place_ref[0], g_all.at[0], keep_ref, send_ref, 0, g_sem, slices, rows)
    slices_wait(g_all.at[0], keep_ref, g_sem, slices, rows)


def middle_own_call(place, x, low, w_out, vectors, dy, b_up, w_up, w_down, slices):
    own, width = x.shape
    hidden = b_up.shape[1]
    rows = width + hidden
    vmem = pl.BlockSpec(memory_space=pltpu.VMEM)
    sds = jax.ShapeDtypeStruct
    return pl.pallas_call(
        functools.partial(middle_own_kernel, slices=slices),
        in_specs=[SMEM] + [vmem] * 6 + [ANY] * 2,
        out_specs=[vmem] * 5 + [ANY] * 2,
        out_shape=[
            sds((own, width), F32),
            sds((own, width), BF),
            sds((own, width), F32),
            sds((own, width), F32),
            sds((1, hidden), F32),
        ]
        + [sds((slices // 2, rows // slices, width), BF)] * 2,
        scratch_shapes=[
            pltpu.VMEM((1, rows, width), BF),
            pltpu.VMEM((1, rows, width), BF),
            pltpu.SemaphoreType.DMA((2,)),
            pltpu.SemaphoreType.DMA((slices,)),
        ],
        compiler_params=params(),
        cost_estimate=cost(12),
        name="middle_own",
    )(place, x, low, w_out, vectors, dy, b_up, w_up, w_down)


def middle_kernel(
    place_ref, vec_ref, bu_ref, lse_ref, norm_in, dy_in, out_in, dn_in, hid_in, low_in, mixed_in,
    wo_in, keep_in, send_in, *refs, slices,
):
    piece_refs = refs[:slices]
    (
        act_out, dh_out, dheads_ref, head_ref, tail_ref, delta_ref, small_ref, dbu_ref, keep_ref,
        send_ref,
        w_all, g_all, go_all, norm_ref, dy_ref, out_acc, dn_acc, hid_ref, low_ref, mixed_ref,
        wo_ref, act_ref, dh_ref, own_grads, w_sem, g_sem, in_sem, out_sem,
    ) = refs[slices:]
    place = place_ref[0]
    own, width = norm_ref.shape
    quarters = w_all.shape[0]
    rows = w_all.shape[1] // slices

    def fetches(q):
        return [
            pltpu.make_async_copy(
                ref.at[q],
                w_all.at[q, pl.ds(pl.multiple_of(source * rows, rows), rows), :],
                w_sem.at[q, n],
            )
            for n, (ref, source) in enumerate(gathered(place, piece_refs))
        ]

    inputs = [
        pltpu.make_async_copy(source, target, in_sem.at[n])
        for n, (source, target) in enumerate(
            (
                (norm_in, norm_ref), (dy_in, dy_ref), (out_in, out_acc), (dn_in, dn_acc),
                (hid_in, hid_ref), (low_in, low_ref), (mixed_in, mixed_ref), (wo_in, wo_ref),
                (keep_in, own_grads.at[0]), (send_in, own_grads.at[1]),
            )
        )
    ]
    for copy in inputs[:2] + fetches(0) + inputs[2:4]:
        copy.start()
    for q in range(1, quarters):
        for copy in fetches(q):
            copy.start()
    for copy in inputs[4:]:
        copy.start()
    for copy in inputs[:2]:
        copy.wait()

    def quarter(q, _):
        for copy in fetches(q):
            copy.wait()

        @pl.when(q == 0)
        def _():
            for copy in inputs[2:4]:
                copy.wait()

        one_quarter(q, w_all, norm_ref, dy_ref, bu_ref, dbu_ref, out_acc, dn_acc, g_all, False)
        slices_out(
            place, g_all.at[q], keep_ref, send_ref, pl.multiple_of(q * rows + rows, rows),
            g_sem.at[q], slices, rows,
        )
        return 0

    lax.fori_loop(0, quarters, quarter, 0)

    for copy in inputs[4:]:
        copy.wait()
    hidden_in = hid_ref[...]
    xhat, inverse = norm_parts(hidden_in)
    dn = dn_acc[...]
    dy = dy_ref[...].astype(F32)
    d_hidden = dy + norm_back(dn, xhat, inverse, vec_ref[LN2_GAIN])
    dh_ref[...] = d_hidden
    d_att = d_hidden.astype(BF)
    d_heads = dot_nt(d_att, wo_ref[...]).astype(BF)
    dheads_ref[:own, :] = d_heads
    go_all[...] = dot_tn(low_ref[...], d_att).astype(BF)
    few = width // slices
    base = quarters * rows + rows
    slices_out(place, go_all, keep_ref, send_ref, base, g_sem.at[quarters], slices, few)
    act_ref[...] = (hidden_in + out_acc[...] + vec_ref[B_DOWN]).astype(BF)
    outputs = [
        pltpu.make_async_copy(source, target, out_sem.at[n])
        for n, (source, target) in enumerate(
            (
                (act_ref, act_out), (dh_ref, dh_out),
                (own_grads.at[0], keep_ref.at[:, 0:rows, :]),
                (own_grads.at[1], send_ref.at[:, 0:rows, :]),
            )
        )
    ]
    for copy in outputs:
        copy.start()
    small_ref[0:1, :] = columns_sum(dn * xhat)
    small_ref[1:2, :] = columns_sum(dn)
    small_ref[2:3, :] = columns_sum(dy)
    small_ref[3:4, :] = columns_sum(d_att.astype(F32))
    spread = d_heads.astype(F32) * mixed_ref[...]
    pick = lax.broadcasted_iota(jnp.int32, (8, 256), 0)
    pick = (pick == lax.broadcasted_iota(jnp.int32, (8, 256), 1) // 64).astype(F32)
    for g in range(width // 256):
        for i in range(own // BLK):
            block = spread[BLK * i : BLK * i + BLK, 256 * g : 256 * g + 256]
            sums = lax.dot_general(
                pick, block, (((1,), (1,)), ((), ())),
                preferred_element_type=F32, precision=lax.Precision.HIGHEST,
            )
            delta = jnp.concatenate([sums[h : h + 1, :] for h in range(GROUP)], 1)
            delta_ref[g, i] = delta
            lse = lse_ref[g, i]
            left = jnp.concatenate(
                [lse[:, :256], lse[:, 256:], delta[:, :256], delta[:, 256:]], 0
            )
            parts = []
            for _ in range(3):
                parts.append(left.astype(BF))
                left = left - parts[-1].astype(F32)
            parts = jnp.concatenate(parts, 0)
            at = slice(256 * g, 256 * g + 256)
            lo = own + 2 * STAT_ROWS * i
            dheads_ref[lo : lo + 2 * STAT_ROWS, at] = parts
            for target, row in ((head_ref, 0), (tail_ref, own // BLK - 1)):
                if i == row:
                    target[REACH : REACH + 2 * STAT_ROWS, at] = parts
    blank = jnp.zeros((STAT_PAD - 2 * STAT_ROWS, width), BF)
    head_ref[REACH + 2 * STAT_ROWS :, :] = blank
    tail_ref[REACH + 2 * STAT_ROWS :, :] = blank
    head_ref[:REACH, :] = d_heads[:REACH, :]
    tail_ref[:REACH, :] = d_heads[own - REACH :, :]
    for q in range(quarters):
        slices_wait(g_all.at[q], keep_ref, g_sem.at[q], slices, rows)
    slices_wait(go_all, keep_ref, g_sem.at[quarters], slices, few)
    for copy in outputs:
        copy.wait()


def middle_call(
    place, hidden_in, norm, out, dn, low, mixed, w_out, vectors, dy, b_up, lse, kept, sent, pieces,
    slices,
):
    own, width = norm.shape
    quarters, hidden = b_up.shape
    rows = width + hidden
    vmem = pl.BlockSpec(memory_space=pltpu.VMEM)
    sds = jax.ShapeDtypeStruct
    grads = sds((slices // 2, ((quarters + 1) * rows + width) // slices, width), BF)
    return pl.pallas_call(
        functools.partial(middle_kernel, slices=slices),
        in_specs=[SMEM] + [vmem] * 3 + [ANY] * (10 + len(pieces)),
        out_specs=[ANY] * 2 + [vmem] * 6 + [ANY] * 2,
        out_shape=[
            sds((own, width), BF),
            sds((own, width), F32),
            sds((own + own // BLK * 2 * STAT_ROWS, width), BF),
            sds((REACH + STAT_PAD, width), BF),
            sds((REACH + STAT_PAD, width), BF),
            sds((width // 256, own // BLK, 1, GROUP * BLK), F32),
            sds((4, width), F32),
            sds((quarters, hidden), F32),
            grads,
            grads,
        ],
        scratch_shapes=[
            pltpu.VMEM((quarters, rows, width), BF),
            pltpu.VMEM((quarters, rows, width), BF),
            pltpu.VMEM((width, width), BF),
            pltpu.VMEM((own, width), BF),
            pltpu.VMEM((own, width), BF),
            pltpu.VMEM((own, width), F32),
            pltpu.VMEM((own, width), F32),
            pltpu.VMEM((own, width), F32),
            pltpu.VMEM((own, width), BF),
            pltpu.VMEM((own, width), F32),
            pltpu.VMEM((width, width), BF),
            pltpu.VMEM((own, width), BF),
            pltpu.VMEM((own, width), F32),
            pltpu.VMEM((2,) + kept.shape, BF),
            pltpu.SemaphoreType.DMA((quarters, slices)),
            pltpu.SemaphoreType.DMA((quarters + 1, slices)),
            pltpu.SemaphoreType.DMA((10,)),
            pltpu.SemaphoreType.DMA((4,)),
        ],
        compiler_params=params(),
        cost_estimate=cost(20),
        name="middle",
    )(
        place, vectors, b_up, lse, norm, dy, out, dn, hidden_in, low, mixed, w_out, kept, sent,
        *pieces,
    )


def turn_back_kernel(
    place_ref, x_ref, vec_ref, dq_ref, dk_ref, dv_ref, q_ref, k_ref, hot_ref, table_ref, grid_ref,
    back_ref, d_ref, db_ref, freq_ref, keep_ref, send_ref, norm_ref, g_all, sem, *, slices,
):
    width = x_ref.shape[1]
    group = pl.program_id(0)

    @pl.when(group == 0)
    def _():
        norm_ref[...] = layer_norm_low(
            x_ref[...].astype(F32), vec_ref[LN1_GAIN], vec_ref[LN1_SHIFT]
        )

    c, s = cos_sin(hot_ref[...], table_ref[...])
    norm = norm_ref[...]

    def gradient(n, low):
        d_ref[n] = low
        db_ref[n : n + 1, :] = columns_sum(low.astype(F32))
        at = pl.ds(pl.multiple_of(n * width + group * 256, 256), 256)
        g_all[:, at] = dot_tn(norm, low).astype(BF)

    d_angle = 0.0
    for n, (grad, turned_ref) in enumerate(((dq_ref, q_ref), (dk_ref, k_ref))):
        g1, g2 = grad[:, :128], grad[:, 128:]
        d_angle = d_angle + (g2 * turned_ref[:, :128] - g1 * turned_ref[:, 128:])
        back = jnp.concatenate([g1 * c + g2 * s, g2 * c - g1 * s], 1).astype(BF)
        gradient(n, dot(back, back_ref[...]).astype(BF))
    freq_ref[...] = lax.dot_general(
        grid_ref[...], d_angle, (((1,), (0,)), ((), ())),
        preferred_element_type=F32, precision=lax.Precision.HIGHEST,
    )
    gradient(2, dv_ref[...].astype(BF))

    @pl.when(group == width // 256 - 1)
    def _():
        slices_out(place_ref[0], g_all, keep_ref, send_ref, 0, sem, slices, width // slices)
        slices_wait(g_all, keep_ref, sem, slices, width // slices)


def turn_back_call(
    place, x, vectors, dq, dk, dv, q_exact, k_exact, onehot, table, grid8, back, first, slices
):
    rows, width = dk.shape
    sds = jax.ShapeDtypeStruct
    part = pl.BlockSpec((rows, 256), lambda g: (0, g))
    hot = pl.BlockSpec(
        (pl.Element(rows), pl.Element(onehot.shape[1])),
        lambda g: (pl.multiple_of(first + 0 * g, BLK), 0),
    )
    return pl.pallas_call(
        functools.partial(turn_back_kernel, slices=slices),
        grid=(width // 256,),
        in_specs=[SMEM, whole(x.shape), whole(vectors.shape)]
        + [part] * 5
        + [
            hot,
            pl.BlockSpec((table.shape[0], 512), lambda g: (0, g)),
            whole(grid8.shape),
            whole(back.shape),
        ],
        out_specs=[
            pl.BlockSpec((3, rows, 256), lambda g: (0, 0, g)),
            pl.BlockSpec((3, 256), lambda g: (0, g)),
            pl.BlockSpec((8, 128), lambda g: (0, g)),
        ]
        + [ANY] * 2,
        out_shape=[
            sds((3, rows, width), BF),
            sds((3, width), F32),
            sds((8, width // 2), F32),
        ]
        + [sds((slices // 2, width // slices, 3 * width), BF)] * 2,
        scratch_shapes=[
            pltpu.VMEM((rows, width), BF),
            pltpu.VMEM((width, 3 * width), BF),
            pltpu.SemaphoreType.DMA((slices,)),
        ],
        compiler_params=params(),
        cost_estimate=cost(9),
        name="turn_back",
    )(place, x, vectors, dq, dk, dv, q_exact, k_exact, onehot, table, grid8, back)


def input_grad_kernel(
    place_ref, x_ref, vec_ref, d_ref, w_ref, dh_ref, db_ref, mid_ref, freq_ref, up0_ref, up_ref,
    out_ref, small_ref,
):
    width = x_ref.shape[1]
    d_norm = sum(dot_nt(d_ref[n], w_ref[:, lanes_of(n, width)]) for n in range(3))
    xhat, inverse = norm_parts(x_ref[...].astype(F32))
    out_ref[...] = dh_ref[...] + norm_back(d_norm, xhat, inverse, vec_ref[LN1_GAIN])
    row = 0
    for vector in (
        columns_sum(d_norm * xhat), columns_sum(d_norm), *(db_ref[n : n + 1, :] for n in range(3)),
        mid_ref[3:4, :], freq_ref[0:1, :], freq_ref[1:2, :], *(mid_ref[n : n + 1, :] for n in range(3)),
    ):
        for n in range(vector.shape[1] // 128):
            small_ref[row : row + 1, :] = vector[:, lanes_of(n, 128)]
            row += 1
    depth = 1 + up_ref.shape[0]
    hidden = up0_ref.shape[1] // 128
    for k in range(depth):
        quarter = (place_ref[1] - k + depth) % depth
        vector = up_ref[k - 1 : k, :] if k else up0_ref[...]
        for n in range(hidden):
            small_ref[pl.ds(row + quarter * hidden + n, 1), :] = vector[:, lanes_of(n, 128)]


def input_grad_call(place, x, vectors, d_qkv, weight, d_hidden, db_qkv, small_mid, freqs, up0, up):
    rows, width = x.shape
    short = 9 * width + freqs.shape[1] * 2 + up0.size * (1 + up.shape[0])
    return pl.pallas_call(
        input_grad_kernel,
        in_specs=[SMEM] + [pl.BlockSpec(memory_space=pltpu.VMEM)] * 10,
        out_shape=[
            jax.ShapeDtypeStruct((rows, width), F32),
            jax.ShapeDtypeStruct((short // 128, 128), F32),
        ],
        compiler_params=params(),
        cost_estimate=cost(7),
        name="input_grad",
    )(place, x, vectors, d_qkv, weight, d_hidden, db_qkv, small_mid, freqs, up0, up)


def assemble_kernel(place_ref, *refs, split, outs, skip):
    out_refs, (held, sem) = refs[-2 - outs : -2], refs[-2:]
    pairs = refs[:4]
    piece_refs = [pairs[n // 2].at[n % 2] for n in range(8)]
    place, depth = place_ref[0], place_ref[1]
    slot = pl.program_id(0)

    def copy(ref, target):
        return pltpu.make_async_copy(ref, held.at[target], sem.at[target])

    @pl.when(slot == 0)
    def _():
        for ref, source in gathered(place, piece_refs):
            copy(ref, source).start()

    copy(piece_refs[0], slot).wait()
    rows = held.shape[-2]
    total_ref = None
    if skip is not None:
        out_refs, total_ref = out_refs[:-1], out_refs[-1]
    out_refs, squares = out_refs[:-1], out_refs[-1]

    @pl.when(slot == 0)
    def _():
        squares[...] = jnp.zeros_like(squares)

    def add_squares(block):
        total = fold8(block * block, jnp.sum)
        squares[...] += sum(total[:, lanes_of(n, 128)] for n in range(block.shape[1] // 128))

    if split:
        for n in range(split):
            block = held[slot, (depth - n + split) % split].astype(F32)
            add_squares(block)
            lo = 0
            for ref in out_refs:
                ref[n * rows : n * rows + rows, :] = block[:, lo : lo + ref.shape[1]]
                lo += ref.shape[1]
    else:
        block = held[slot].astype(F32)
        add_squares(block)
        each = held.shape[0] // len(out_refs)
        for n, ref in enumerate(out_refs):

            @pl.when(slot // each == n)
            def _():
                ref[...] = block
    if skip is not None:
        small_ref = refs[4]

        @pl.when(slot == held.shape[0] - 1)
        def _():
            short = small_ref[...]
            row = lax.broadcasted_iota(jnp.int32, short.shape, 0)
            mine = (row >= skip[0]) & (row < skip[1])
            parts = row >= short.shape[0] - 8
            others = jnp.where(mine, 0.0, jnp.where(parts, short, short * short))
            turned = jnp.where(mine, short * short, 0.0)
            total_ref[0:1, :] = jnp.full((1, 128), jnp.sum(turned))
            total_ref[1:2, :] = jnp.full((1, 128), jnp.sum(others) + jnp.sum(squares[...]))


def assemble_call(place, arrays, shapes, split, small=None, skip=None):
    pieces = 8
    rows = arrays[0].shape[-2] * max(split, 1)
    each = pieces if split else pieces // len(shapes)

    def spec(n, shape):
        lead = 0 if split else n * each
        return pl.BlockSpec((rows, shape[1]), lambda i: (jnp.clip(i - lead, 0, each - 1), 0))

    specs = [spec(n, shape) for n, shape in enumerate(shapes)] + [whole((8, 128))]
    shapes = shapes + [(8, 128)]
    given = []
    if small is not None:
        given, specs, shapes = [small], specs + [whole((2, 128))], shapes + [(2, 128)]
    return pl.pallas_call(
        functools.partial(assemble_kernel, split=split, outs=len(shapes), skip=skip),
        grid=(pieces,),
        in_specs=[SMEM] + [ANY] * len(arrays) + [whole(x.shape) for x in given],
        out_specs=specs,
        out_shape=[jax.ShapeDtypeStruct(s, F32) for s in shapes],
        scratch_shapes=[
            pltpu.VMEM((pieces,) + arrays[0].shape[1:], BF),
            pltpu.SemaphoreType.DMA((pieces,)),
        ],
        compiler_params=params(),
        cost_estimate=cost(6),
        name="assemble",
    )(place, *arrays, *given)


def send(x, axis, pairs):
    return lax.ppermute(x, axis, pairs)


def plane_gather(piece):
    pair = jnp.stack([piece, send(piece, PLANE, FIRST)])
    return pair, send(pair, PLANE, SECOND)


def core_gather(pair, last):
    return [pair, last, send(pair, "c", SWAP), send(last, "c", SWAP)]


def wide_sum(x, extra):
    return lax.psum(x, "e") if extra > 1 else x


def sum_low(*terms):
    return functools.reduce(lambda x, y: x + y, [t.astype(F32) for t in terms])


def after(x, *others):
    return lax.optimization_barrier((x, others))[0]


def ring(size, step):
    return [(i, (i + step) % size) for i in range(size)]


def add_from(vector, axis, reach=0, size=2):
    return vector + send(vector, axis, [(i, i ^ (reach or 1)) for i in range(size)])


def on_device(
    tokens,
    segment,
    padding,
    coords,
    ln1_gain,
    ln1_shift,
    query_key_value_weight,
    b_qkv,
    output_weight,
    b_out,
    rope_freqs,
    ln2_gain,
    ln2_shift,
    w_up,
    b_up,
    w_down,
    b_down,
    cotangent,
    *,
    extra,
    depth,
):
    tokens, cotangent = tokens[0], cotangent[0]
    own, width = tokens.shape
    length = own * depth
    heads = rope_freqs.shape[1]
    half = width // heads // 2
    groups = heads // GROUP
    slices = 8
    outer = BLK
    side = own + outer
    win = own + 2 * side
    blocks = own // BLK
    z = lax.axis_index("n")
    plane = lax.axis_index("a") * 4 + lax.axis_index("b") * 2 + lax.axis_index("c")
    place = jnp.stack([plane, z]).astype(jnp.int32)
    up = [(i, i + 1) for i in range(depth - 1)]
    down = [(i + 1, i) for i in range(depth - 1)]
    up2 = [(i, i + 2) for i in range(depth - 2)]
    down2 = [(i + 2, i) for i in range(depth - 2)]

    def around(x, head, tail):
        before2 = send(tail, "n", up2)
        before = send(x, "n", up)
        after_ = send(x, "n", down)
        after2 = send(head, "n", down2)
        return [before2, before, after_, after2]

    position = jnp.arange(length, dtype=jnp.int32)
    ident = jnp.where(padding[0] == 0, segment[0], 1000 + position)
    ident = jnp.concatenate(
        [jnp.full((side,), -1, jnp.int32), ident, jnp.full((side,), 1 << 20, jnp.int32)]
    )
    ident_win = lax.dynamic_slice_in_dim(ident, z * own, win, 0)
    near = lax.broadcasted_iota(jnp.int32, (win,), 0)
    ident_win = jnp.where(near < outer - REACH, -1, ident_win)
    ident_win = jnp.where(near >= win - outer + REACH, 1 << 20, ident_win)
    idk = jnp.broadcast_to(ident_win[:, None], (win, BLK))
    idq = ident_win.reshape(win // BLK, BLK)

    lowest, highest = idq[:, 0], idq[:, BLK - 1]

    def bounds(queries, keys):
        before = highest[keys][None, :] < lowest[queries][:, None]
        reached = lowest[keys][None, :] <= highest[queries][:, None]
        return jnp.sum(before, 1), jnp.sum(reached, 1)

    def steps(blocks, span):
        return (jnp.maximum(blocks, 0) + span - 1) // span

    mid = slice(side // BLK, side // BLK + blocks)
    lo, hi = bounds(mid, slice(None))
    bounds_fwd = [
        lo, steps(hi - lo, SPAN), jnp.minimum(lo, mid.start), steps(mid.start - lo, SPAN_SIDE),
        steps(hi - mid.stop, SPAN_SIDE),
    ]
    bounds_fwd = jnp.stack(bounds_fwd, 1).astype(jnp.int32)
    lo, hi = bounds(slice(None), mid)
    bounds_bwd = jnp.stack([lo, steps(hi - lo, SPAN_BACK)], 1).astype(jnp.int32)

    grid = jnp.pad(coords[:, 0], ((0, 0), (side, side)))
    grid_win = lax.dynamic_slice_in_dim(grid, z * own, win, 1)
    grid_own = lax.dynamic_slice_in_dim(grid, z * own + side, own, 1)
    lane = jnp.arange(4 * SIDE)
    picked = jnp.where(lane[None, :] < 2 * SIDE, grid_win[0][:, None], grid_win[1][:, None])
    onehot = (picked == (lane % SIDE)[None, :]).astype(BF)
    table = turn_table(rope_freqs)

    local = np.arange(256)
    order = np.zeros((256, 256), np.float32)
    order[(local % 128) // 32 * 64 + local // 128 * 32 + local % 32, local] = 1.0
    order = jnp.asarray(order, BF)
    qk_bias = b_qkv[: 2 * width].reshape(2 * groups, GROUP, 2, half).swapaxes(1, 2)
    bias_turned = jnp.concatenate([qk_bias.reshape(-1), b_qkv[2 * width :]])

    x_parts = around(tokens, tokens[:REACH], tokens[own - REACH :])
    vectors = jnp.stack([ln1_gain, ln1_shift, b_out, ln2_gain, ln2_shift, b_down])
    rot_q, rot_k, values, q_exact, k_exact, weight_turned = qkv_own_call(
        tokens, onehot, vectors, query_key_value_weight, bias_turned, order, table, side
    )
    rows = (width + w_down.shape[0]) // slices
    eighth = jnp.where(
        plane < width // rows,
        lax.dynamic_slice_in_dim(w_up, jnp.minimum(plane * rows, width - rows), rows, 0),
        lax.dynamic_slice_in_dim(w_down, jnp.maximum(plane * rows - width, 0), rows, 0),
    )
    left, bias_rows = b_up, []
    for _ in range(3):
        bias_rows.append(left.astype(BF))
        left = left - rounded(left)
    bias_rows = jnp.pad(jnp.stack(bias_rows), ((0, 13), (0, 0)))
    eighth = jnp.concatenate([eighth, bias_rows], 0)
    others = [send(eighth, "n", ring(depth, k)) for k in range(1, depth)]
    x_parts, rot_q, idk = lax.optimization_barrier((x_parts, rot_q, idk))
    halo_args = (x_parts, onehot, vectors, weight_turned, bias_turned, table)
    rot_q, rot_k, values = halo_call(*halo_args, (rot_q, rot_k, values), (0, 1, 2), side)
    part = forward_call(bounds_fwd, rot_q, rot_k, values, idk, idq, side, own, 0, blocks // 2)
    others, part = lax.optimization_barrier((others, part))
    up_biases = jnp.concatenate(
        [jnp.sum(x[rows : rows + 3].astype(F32), 0, keepdims=True) for x in others]
    )
    own_w = jnp.stack([x[:rows] for x in others])
    over_1, over_2 = send(own_w, PLANE, FIRST), send(own_w, PLANE, SECOND)
    part, _ = lax.optimization_barrier((part, own_w))
    mixed, mixed_low, lse = forward_call(
        bounds_fwd, rot_q, rot_k, values, idk, idq, side, own, blocks // 2, blocks // 2, part
    )
    hidden_in, norm2, out0, dn0, up_sum0, kept_own, sent_own = middle_own_call(
        place, tokens, mixed_low, output_weight, vectors, cotangent, b_up[None],
        w_up, w_down, slices,
    )
    over_1, over_2, norm2 = lax.optimization_barrier((over_1, over_2, norm2))
    diagonal = send(over_1, PLANE, SECOND)
    near = [own_w, over_1, over_2, diagonal]
    pieces = near + [send(x, "c", SWAP) for x in near]
    grid8 = jnp.pad(grid_own.astype(F32), ((0, 6), (0, 0)))
    norm2, up_biases, bounds_bwd = lax.optimization_barrier((norm2, up_biases, bounds_bwd))
    (
        activations, d_hidden, d_heads, d_head, d_tail, delta, small_mid, up_sums, kept_mid,
        sent_mid,
    ) = middle_call(
        place, hidden_in, norm2, out0, dn0, mixed_low, mixed, output_weight, vectors, cotangent,
        up_biases, lse, kept_own, sent_own, pieces, slices,
    )
    far_mid = send(sent_mid, "c", SWAP)
    do_parts = around(d_heads, d_head, d_tail)

    early = (depth - 1) * rows
    lots = (slice(0, early), slice(early, depth * rows + width // slices))

    def chip_sum(lot, n):
        return sum_low(kept_mid[n, lots[lot]], far_mid[n, lots[lot]])

    def plane_part(lot, lo, hi):
        at, there = slice(lots[lot].start + lo, lots[lot].start + hi), slice(lo, hi)
        total = sum_low(kept_mid[0, at], far_mid[0, at], got_1[lot][0, there], got_2[lot][there])
        return wide_sum(total, extra)

    got_1, got_2 = [None, None], [None, None]
    away = chip_sum(0, slice(1, None, 2)).astype(BF)
    got_1[0] = send(away, PLANE, FIRST)
    dq, dk, dv = backward_own_call(
        bounds_fwd, rot_q, d_heads, rot_k, values, idk, idq, lse, after(delta, away), side, own
    )
    got_1[0], dq = lax.optimization_barrier((got_1[0], dq))
    away = (chip_sum(0, 2) + got_1[0][1].astype(F32)).astype(BF)
    got_2[0] = send(away, PLANE, SECOND)
    away_b = chip_sum(1, slice(1, None, 2)).astype(BF)
    got_1[1] = send(away_b, PLANE, FIRST)
    do_parts, dq, dk, _ = lax.optimization_barrier((do_parts, dq, dk, (away, away_b)))
    dk, dv = backward_halo_call(
        bounds_bwd, rot_q, do_parts, rot_k, values, idk, idq, dk, dv, side
    )
    got_1[1], got_2[0], dk = lax.optimization_barrier((got_1[1], got_2[0], dk))
    away = (chip_sum(1, 2) + got_1[1][1].astype(F32)).astype(BF)
    got_2[1] = send(away, PLANE, SECOND)
    ff_sent = [plane_part(0, k * rows, k * rows + rows).astype(BF) for k in range(1, depth - 1)]
    ff_got = [send(ff_sent[k - 1], "n", ring(depth, -k)) for k in range(1, depth - 1)]
    dk = after(dk, away, ff_sent)

    d_qkv, grad_b_qkv, freqs8, kept_qkv, sent_qkv = turn_back_call(
        place, tokens, vectors, dq, dk, dv, q_exact, k_exact, onehot, table, grid8,
        order.T, side, slices,
    )
    far_qkv = send(sent_qkv, "c", SWAP)
    away = sum_low(kept_qkv[1::2], far_qkv[1::2]).astype(BF)
    got_1_qkv = send(away, PLANE, FIRST)
    got_2[1] = after(got_2[1], away)
    ff_sent = plane_part(1, 0, rows).astype(BF)
    ff_got.append(send(ff_sent, "n", ring(depth, 1 - depth)))
    input_grad, small_in = input_grad_call(
        place, tokens, vectors, after(d_qkv, ff_sent), query_key_value_weight, d_hidden,
        grad_b_qkv, small_mid, freqs8, up_sum0, up_sums,
    )
    got_1_qkv, small_in = lax.optimization_barrier((got_1_qkv, small_in))
    away = sum_low(kept_qkv[2], far_qkv[2], got_1_qkv[1]).astype(BF)
    got_2_qkv = send(away, PLANE, SECOND)
    ff_got, small_in, _ = lax.optimization_barrier((ff_got, small_in, away))
    plane_qkv = wide_sum(sum_low(kept_qkv[0], far_qkv[0], got_1_qkv[0], got_2_qkv), extra)
    ff_total = plane_part(0, 0, rows) + sum_low(*ff_got)

    sizes = [width, width, 3 * width, width, rope_freqs.size] + [width] * 3 + [b_up.size * depth]
    small = add_from(small_in, "c")

    part = plane_part(1, rows, rows + width // slices)
    part = jnp.concatenate([plane_qkv, part], 1).astype(BF)
    thin = part.shape[0] // depth
    cut = lambda k: lax.dynamic_slice_in_dim(part, ((z + k) % depth) * thin, thin, 0)
    got = [send(cut(k), "n", ring(depth, k)) for k in range(1, depth)]
    small = add_from(add_from(after(small, part), "b"), "a")
    if extra > 1:
        small = lax.psum(small, "e")
    got, small = lax.optimization_barrier((got, small))
    low = sum_low(cut(0), *got).astype(BF)
    strip = jnp.stack([low] + [send(low, "n", ring(depth, k)) for k in range(1, depth)])
    ff_pair, ff_last = plane_gather(after(ff_total, low).astype(BF))
    pair, last = plane_gather(strip)
    ff_pieces = [after(x, strip) for x in core_gather(ff_pair, ff_last)]
    total_w_up, total_w_down, ff_squares = assemble_call(
        place, ff_pieces, [w_up.shape, w_down.shape], 0
    )
    small = jnp.concatenate([small, ff_squares], 0)
    reach = 1
    while reach < depth:
        small = add_from(small, "n", reach, depth)
        reach *= 2
    last, small = lax.optimization_barrier((last, small))
    turned = sum(sizes[:4]) // 128
    total_w_qkv, total_w_out, _, norms = assemble_call(
        place, core_gather(pair, last), [query_key_value_weight.shape, output_weight.shape], depth,
        small, (turned, turned + sizes[4] // 128),
    )
    small = small[:-8].reshape(-1)
    out, at = [], 0
    for size in sizes:
        out.append(small[at : at + size])
        at += size
    t_gain1, t_shift1, t_b_qkv, t_b_out, t_freqs, t_gain2, t_shift2, t_b_down, t_up = out
    t_freqs = t_freqs.reshape(rope_freqs.shape)
    rot_sq, other_sq = norms[0, 0], norms[1, 0]
    t_b_up = lax.dynamic_slice_in_dim(t_up, z * b_up.shape[0], b_up.shape[0], 0)
    return (
        activations[None],
        input_grad[None],
        t_gain1,
        t_shift1,
        total_w_qkv,
        t_b_qkv,
        total_w_out,
        t_b_out,
        t_freqs,
        t_gain2,
        t_shift2,
        total_w_up,
        t_b_up,
        total_w_down,
        t_b_down,
        rot_sq,
        other_sq,
    )


def solution(mesh):
    wide, depth = mesh.shape["wide"], mesh.shape["narrow"]
    extra = wide // 8
    fine = Mesh(mesh.devices.reshape(extra, 2, 2, 2, depth), ("e", "a", "b", "c", "n"))
    w, n = ("e", "a", "b", "c"), "n"
    return jax.shard_map(
        functools.partial(on_device, extra=extra, depth=depth),
        mesh=fine,
        in_specs=(
            P(w, n, None), P(w, None), P(w, None), P(None, w, None),
            P(), P(), P(), P(), P(), P(), P(), P(), P(),
            P(None, n), P(n), P(n, None), P(), P(w, n, None),
        ),
        out_specs=(
            P(w, n, None), P(w, n, None),
            P(), P(), P(), P(), P(), P(), P(), P(), P(),
            P(None, n), P(n), P(n, None), P(), P(), P(),
        ),
        check_vma=False,
    )
```

```python
import functools

import jax
import jax.numpy as jnp
import numpy as np
from jax import lax
from jax.experimental import pallas as pl
from jax.experimental.pallas import tpu as pltpu
from jax.sharding import Mesh, PartitionSpec as P

EPS = 1e-06
MASKED = -1e30
BLK = 128
SPAN = 6
SPAN_SIDE = 3
SPAN_BACK = 2
GROUP = 4
REACH = 64
STAT_ROWS = 6
STAT_PAD = 16
SIDE = 32
LN1_GAIN, LN1_SHIFT, B_OUT, LN2_GAIN, LN2_SHIFT, B_DOWN = (slice(n, n + 1) for n in range(6))
LOG2E = np.float32(1.4426950408889634)
BF = jnp.bfloat16
F32 = jnp.float32
PLANE = ("a", "b", "c")
SWAP = [(0, 1), (1, 0)]
FIRST = [(i, i ^ (4 if i % 2 else 2)) for i in range(8)]
SECOND = [(i, i ^ (2 if i % 2 else 4)) for i in range(8)]


def dot(left, right):
    return lax.dot_general(left, right, (((1,), (0,)), ((), ())), preferred_element_type=F32)


def dot_nt(left, right):
    return lax.dot_general(left, right, (((1,), (1,)), ((), ())), preferred_element_type=F32)


def dot_tn(left, right):
    return lax.dot_general(left, right, (((0,), (0,)), ((), ())), preferred_element_type=F32)


def params(mebibytes):
    return pltpu.CompilerParams(vmem_limit_bytes=mebibytes * 1024 * 1024)


def cost(us):
    return pl.CostEstimate(
        flops=int(us * 1.15e9), bytes_accessed=int(us * 3.0e6), transcendentals=0
    )


def whole(shape):
    return pl.BlockSpec(shape, lambda *_: (0,) * len(shape))


ANY = pl.BlockSpec(memory_space=pl.ANY)
SMEM = pl.BlockSpec(memory_space=pltpu.SMEM)


def rounded(x):
    return lax.reduce_precision(x, exponent_bits=8, mantissa_bits=7)


def turn_table(rope_freqs):
    lanes = rope_freqs.shape[1] * rope_freqs.shape[2]
    freq = rope_freqs.reshape(2, 1, lanes)
    angle = jnp.arange(SIDE, dtype=F32)[None, :, None] * freq
    cosine, sine = jnp.cos(angle), jnp.sin(angle)

    def halves(x):
        return jnp.concatenate([x.astype(BF), (x - rounded(x)).astype(BF)], 0)

    def grouped(x):
        return x.reshape(2 * SIDE, lanes // 128, 1, 128)

    zero = jnp.zeros((2 * SIDE, lanes // 128, 2, 128), BF)
    rows = jnp.concatenate([grouped(halves(cosine[0])), grouped(halves(sine[0])), zero], 2)
    cols = jnp.concatenate([zero, grouped(halves(cosine[1])), grouped(halves(sine[1]))], 2)
    return jnp.concatenate([rows, cols], 0).reshape(4 * SIDE, 4 * lanes)


def cos_sin(onehot, table):
    parts = dot(onehot, table)
    cr, sr, cc, sc = (parts[:, lanes_of(n, 128)] for n in range(4))
    return cr * cc - sr * sc, sr * cc + cr * sc


def layer_norm_low(x, gain, shift):
    centred = x - jnp.mean(x, -1, keepdims=True)
    var = jnp.mean(centred * centred, -1, keepdims=True)
    return (centred * lax.rsqrt(var + EPS) * gain + shift).astype(BF)


def project(norm, hot_ref, table_ref, weights, b_ref, outs, exact=()):
    width = norm.shape[1]
    for g in range(width // 256):
        c, s = cos_sin(hot_ref[...], table_ref[:, lanes_of(g, 512)])
        for n, out in outs:
            lo = n * width + 256 * g
            proj = dot(norm, weights[:, lo : lo + 256]) + b_ref[:, lo : lo + 256]
            if n == 2:
                out[:, lanes_of(g)] = proj.astype(BF)
                continue
            for half, turned in enumerate(
                (proj[:, :128] * c - proj[:, 128:] * s, proj[:, :128] * s + proj[:, 128:] * c)
            ):
                at = slice(256 * g + 128 * half, 256 * g + 128 * half + 128)
                out[:, at] = turned.astype(BF)
                if exact:
                    exact[n][:, at] = turned


def qkv_own_kernel(
    x_ref, hot_ref, vec_ref, w_ref, b_ref, order_ref, table_ref,
    q_ref, k_ref, v_ref, pq_ref, pk_ref, w_turned,
):
    width = x_ref.shape[1]

    @pl.when(pl.program_id(0) == 0)
    def _():
        for g in range(2 * width // 256):
            at = slice(256 * g, 256 * g + 256)
            w_turned[:, at] = dot(w_ref[:, at], order_ref[...]).astype(BF)
        w_turned[:, 2 * width :] = w_ref[:, 2 * width :]

    norm = layer_norm_low(x_ref[...].astype(F32), vec_ref[LN1_GAIN], vec_ref[LN1_SHIFT])
    outs = [(0, q_ref), (1, k_ref), (2, v_ref)]
    project(norm, hot_ref, table_ref, w_turned, b_ref, outs, (pq_ref, pk_ref))


def qkv_own_call(x, onehot, vectors, weight, bias, order, table, first):
    own, width = x.shape
    rows = onehot.shape[0]
    tile = 256
    shape = jax.ShapeDtypeStruct((rows, width), BF)
    exact = jax.ShapeDtypeStruct((own, width), F32)
    row = lambda w: pl.BlockSpec((tile, w), lambda i: (i, 0))
    inside = lambda w: pl.BlockSpec(
        (pl.Element(tile), pl.Element(w)), lambda i: (pl.multiple_of(first + tile * i, BLK), 0)
    )
    return pl.pallas_call(
        qkv_own_kernel,
        grid=(own // tile,),
        in_specs=[
            row(width),
            inside(onehot.shape[1]),
            whole(vectors.shape),
            whole(weight.shape),
            whole((1, 3 * width)),
            whole(order.shape),
            whole(table.shape),
        ],
        out_specs=[inside(width)] * 3 + [row(width)] * 2 + [whole(weight.shape)],
        out_shape=[shape] * 3 + [exact] * 2 + [jax.ShapeDtypeStruct(weight.shape, BF)],
        compiler_params=params(56),
        cost_estimate=cost(8),
        name="qkv_own",
    )(x, onehot, vectors, weight, bias[None], order, table)


def halo_kernel(
    far_l, near_l, near_r, far_r, hot_ref, vec_ref, w_ref, b_ref, table_ref, *refs, which
):
    refs = refs[len(which) :]
    out_refs, (x_all, sem) = refs[: len(which)], refs[len(which) :]
    width = x_all.shape[1]
    step = pl.program_id(0)
    tile = out_refs[0].shape[0]

    @pl.when(step == 0)
    def _():
        own, reach = near_l.shape[0], far_l.shape[0]
        total = x_all.shape[0]
        blank = total // 2 - own - reach
        copies = []
        at = blank
        for n, ref in enumerate((far_l, near_l, near_r, far_r)):
            copies.append(
                pltpu.make_async_copy(ref, x_all.at[at : at + ref.shape[0], :], sem.at[n])
            )
            copies[-1].start()
            at += ref.shape[0]
        x_all[:blank, :] = jnp.zeros((blank, width), BF)
        x_all[total - blank :, :] = jnp.zeros((blank, width), BF)
        for copy in copies:
            copy.wait()

    x = x_all[pl.ds(pl.multiple_of(step * tile, tile), tile), :].astype(F32)
    norm = layer_norm_low(x, vec_ref[LN1_GAIN], vec_ref[LN1_SHIFT])
    project(norm, hot_ref, table_ref, w_ref, b_ref, list(zip(which, out_refs)))


def halo_call(pieces, onehot, vectors, weight, bias, table, arrays, which, first):
    rows, width = arrays[0].shape
    own = pieces[1].shape[0]
    tile = first // 2
    at = lambda w: pl.BlockSpec(
        (pl.Element(tile), pl.Element(w)),
        lambda i: (pl.multiple_of(tile * i + jnp.where(i >= 2, own, 0), 64), 0),
    )
    return pl.pallas_call(
        functools.partial(halo_kernel, which=which),
        grid=(4,),
        in_specs=[ANY] * 4
        + [
            at(onehot.shape[1]),
            whole(vectors.shape),
            whole(weight.shape),
            whole((1, 3 * width)),
            whole(table.shape),
        ]
        + [ANY] * len(which),
        out_specs=[at(width)] * len(which),
        out_shape=[jax.ShapeDtypeStruct((rows, width), BF)] * len(which),
        input_output_aliases={9 + n: n for n in range(len(which))},
        scratch_shapes=[pltpu.VMEM((2 * first, width), BF), pltpu.SemaphoreType.DMA((4,))],
        compiler_params=params(56),
        cost_estimate=cost(4 * len(which)),
        name="halo",
    )(*pieces, onehot, vectors, weight, bias[None], table, *arrays)


def head_stack(block, turned, scale=None):
    lane = lax.broadcasted_iota(jnp.int32, block.shape, 1)
    head = (lane % 128) // 32 if turned else lane // 64
    if scale is not None:
        block = block * scale
    zero = jnp.zeros_like(block)
    return jnp.concatenate([jnp.where(head == h, block, zero) for h in range(GROUP)], 0)


def fold8(x, op):
    return op(x.reshape(x.shape[0] // 8, 8, x.shape[1]), axis=0)


def key_span(ident_ref, ident_q, start, c, span, end):
    block = jnp.minimum(start + c * span, end - span)
    lower = (start + c * span - block) * BLK
    at = pl.ds(pl.multiple_of(block * BLK, BLK), span * BLK)
    row = lax.broadcasted_iota(jnp.int32, (span * BLK, BLK), 0)
    return at, (ident_ref[at, :] == ident_q) & (row >= lower)


def lanes_of(g, size=256):
    return slice(size * g, size * g + size)


def forward_kernel(
    bound_ref, q_ref, k_ref, v_ref, idk_ref, idq_ref, *refs, first, base
):
    o_ref, low_ref, lse_ref, s_ref, acc_ref, q4_ref = refs[-6:]
    i = pl.program_id(0) + base
    groups = k_ref.shape[1] // 256
    lanes = GROUP * BLK
    window = k_ref.shape[0] // BLK
    start, count = bound_ref[i, 0], bound_ref[i, 1]
    for g in range(groups):
        q4_ref[g] = head_stack(q_ref[:, lanes_of(g)], True, jnp.asarray(0.125, BF))
    ident_q = idq_ref[pl.ds(first // BLK + i, 1), :]

    def scores(c, top):
        at, seen = key_span(idk_ref, ident_q, start, c, SPAN, window)
        here = pl.ds(pl.multiple_of(c * SPAN * BLK, BLK), SPAN * BLK)
        tops = []
        for g in range(groups):
            s = dot_nt(k_ref[at, lanes_of(g)], q4_ref[g]) * LOG2E
            for h in range(GROUP):
                masked = jnp.where(seen, s[:, lanes_of(h, BLK)], MASKED)
                s_ref[g, here, lanes_of(h, BLK)] = masked
                tops.append(fold8(masked, jnp.max))
        return jnp.maximum(top, jnp.concatenate(tops, 1))

    top = lax.fori_loop(0, count, scores, jnp.full((8, groups * lanes), -3e38, F32))
    top = jnp.max(top, 0, keepdims=True)
    acc_ref[...] = jnp.zeros_like(acc_ref)

    def mix(c, total):
        at, _ = key_span(idk_ref, ident_q, start, c, SPAN, window)
        here = pl.ds(pl.multiple_of(c * SPAN * BLK, BLK), SPAN * BLK)
        sums = []
        for g in range(groups):
            e = jnp.exp2(s_ref[g, here, :] - top[:, lanes_of(g, lanes)])
            sums.append(fold8(e, jnp.sum))
            acc_ref[g] += dot_tn(v_ref[at, lanes_of(g)], e.astype(BF))
        return total + jnp.concatenate(sums, 1)

    total = lax.fori_loop(0, count, mix, jnp.zeros((8, groups * lanes), F32))
    total = jnp.sum(total, 0, keepdims=True)
    lse = top + jnp.log(total) * LOG2E
    inverse = 1.0 / total
    for g in range(groups):
        lse_ref[g] = lse[:, lanes_of(g, lanes)]
        acc = acc_ref[g] * inverse[:, lanes_of(g, lanes)]
        out = jnp.concatenate(
            [acc[64 * h : 64 * h + 64, lanes_of(h, BLK)] for h in range(GROUP)], 0
        ).T
        o_ref[:, lanes_of(g)] = out
        low_ref[:, lanes_of(g)] = out.astype(BF)


def stat_spec(groups, base=0):
    return pl.BlockSpec((groups, None, 1, GROUP * BLK), lambda i: (0, i + base, 0, 0))


def query_rows(first, width):
    return pl.BlockSpec(
        (pl.Element(BLK), pl.Element(width)), lambda i: (pl.multiple_of(first + BLK * i, BLK), 0)
    )


def forward_call(bounds, q_win, k_win, v_win, idk, idq, first, own, base, count, earlier=()):
    win, width = k_win.shape
    groups, blocks = width // 256, own // BLK
    row = pl.BlockSpec((BLK, width), lambda i: (i + base, 0))
    steps = -(-win // (SPAN * BLK))
    return pl.pallas_call(
        functools.partial(forward_kernel, first=first, base=base),
        grid=(count,),
        in_specs=[SMEM, query_rows(first + base * BLK, width)]
        + [whole((win, width))] * 2
        + [whole(idk.shape), whole(idq.shape)]
        + [ANY] * len(earlier),
        out_specs=[row, row, stat_spec(groups, base)],
        input_output_aliases={6 + n: n for n in range(len(earlier))},
        out_shape=[
            jax.ShapeDtypeStruct((own, width), F32),
            jax.ShapeDtypeStruct((own, width), BF),
            jax.ShapeDtypeStruct((groups, blocks, 1, GROUP * BLK), F32),
        ],
        scratch_shapes=[
            pltpu.VMEM((groups, steps * SPAN * BLK, GROUP * BLK), F32),
            pltpu.VMEM((groups, 256, GROUP * BLK), F32),
            pltpu.VMEM((groups, GROUP * BLK, 256), BF),
        ],
        compiler_params=params(56),
        cost_estimate=cost(4 * count),
        name="attention_forward",
    )(bounds, q_win, k_win, v_win, idk, idq, *earlier)


def score_gradients(s, dp, lse, delta, seen):
    low_p, low_ds = [], []
    for h in range(GROUP):
        at = lanes_of(h, BLK)
        p = jnp.exp2(jnp.where(seen, s[:, at] * LOG2E - lse[:, at], MASKED))
        low_p.append(p.astype(BF))
        low_ds.append((p * (dp[:, at] - delta[:, at])).astype(BF))
    return jnp.concatenate(low_p, 1), jnp.concatenate(low_ds, 1)


def backward_own_kernel(
    bound_ref, q_ref, do_ref, k_ref, v_ref, idk_ref, idq_ref, lse_ref, delta_ref,
    dq_ref, dk_ref, dv_ref, acc_ref, q4_ref, do4_ref, *, first,
):
    i = pl.program_id(0)
    groups = k_ref.shape[1] // 256
    own = dk_ref.shape[0]

    @pl.when(i == 0)
    def _():
        dk_ref[...] = jnp.zeros_like(dk_ref)
        dv_ref[...] = jnp.zeros_like(dv_ref)

    for g in range(groups):
        q4_ref[g] = head_stack(q_ref[:, lanes_of(g)], True, jnp.asarray(0.125, BF))
        do4_ref[g] = head_stack(do_ref[:, lanes_of(g)], False)
    ident_q = idq_ref[pl.ds(first // BLK + i, 1), :]

    def attend(at, seen, inside):
        for g in range(groups):
            keys = k_ref[at, lanes_of(g)]
            s = dot_nt(keys, q4_ref[g])
            dp = dot_nt(v_ref[at, lanes_of(g)], do4_ref[g])
            low_p, low_ds = score_gradients(s, dp, lse_ref[g], delta_ref[g], seen)
            if inside:
                acc_ref[g] = dot_tn(keys, low_ds)
                dk_ref[:, lanes_of(g)] += dot(low_ds, q4_ref[g])
                dv_ref[:, lanes_of(g)] += dot(low_p, do4_ref[g])
            else:
                acc_ref[g] += dot_tn(keys, low_ds)

    attend(slice(first, first + own), idk_ref[first : first + own, :] == ident_q, True)
    for start, count, end in (
        (bound_ref[i, 2], bound_ref[i, 3], first // BLK),
        ((first + own) // BLK, bound_ref[i, 4], k_ref.shape[0] // BLK),
    ):

        def step(c, _):
            attend(*key_span(idk_ref, ident_q, start, c, SPAN_SIDE, end), False)
            return 0

        lax.fori_loop(0, count, step, 0)
    for g in range(groups):
        acc = acc_ref[g]
        parts = [acc[32 * h : 32 * h + 32, lanes_of(h, BLK)] for h in range(GROUP)]
        parts += [acc[128 + 32 * h : 160 + 32 * h, lanes_of(h, BLK)] for h in range(GROUP)]
        dq_ref[:, lanes_of(g)] = (jnp.concatenate(parts, 0) * 0.125).T


def backward_own_call(bounds, q_win, do_own, k_win, v_win, idk, idq, lse, delta, first, own):
    win, width = k_win.shape
    groups = width // 256
    row = pl.BlockSpec((BLK, width), lambda i: (i, 0))
    return pl.pallas_call(
        functools.partial(backward_own_kernel, first=first),
        grid=(own // BLK,),
        in_specs=[SMEM, query_rows(first, width), row]
        + [whole((win, width))] * 2
        + [whole(idk.shape), whole(idq.shape), stat_spec(groups), stat_spec(groups)],
        out_specs=[row] + [whole((own, width))] * 2,
        out_shape=[jax.ShapeDtypeStruct((own, width), F32)] * 3,
        scratch_shapes=[pltpu.VMEM((groups, 256, GROUP * BLK), F32)]
        + [pltpu.VMEM((groups, GROUP * BLK, 256), BF)] * 2,
        compiler_params=params(24),
        cost_estimate=cost(20),
        name="attention_backward_own",
    )(bounds, q_win, do_own, k_win, v_win, idk, idq, lse, delta)


def backward_halo_kernel(
    bound_ref, q_ref, far_l, near_l, near_r, far_r, k_ref, v_ref, idk_ref, idq_ref, dk_in, dv_in,
    dk_ref, dv_ref, q4_ref, do_all, do4_ref, stat_ref, *, first,
):
    groups = k_ref.shape[1] // 256
    own, reach = k_ref.shape[0], far_l.shape[0] - STAT_PAD
    blocks = own // BLK
    side = first // BLK
    step_id = pl.program_id(0)
    j = jnp.where(step_id < side, step_id, step_id + blocks)
    lanes = GROUP * BLK

    def stats(ref, row, slot):
        parts = ref[row : row + 2 * STAT_ROWS, :].astype(F32)
        sums = parts[0:4] + parts[4:8] + parts[8:12]
        for g in range(groups):
            for n in range(2):
                stat_ref[n, g, slot : slot + 1, :] = jnp.concatenate(
                    [sums[2 * n : 2 * n + 1, lanes_of(g)], sums[2 * n + 1 : 2 * n + 2, lanes_of(g)]],
                    1,
                )

    @pl.when(step_id == 0)
    def _():
        dk_ref[...] = dk_in[...]
        dv_ref[...] = dv_in[...]
        blank = jnp.zeros((BLK - reach, do_all.shape[1]), BF)
        do_all[0 : BLK - reach, :] = blank
        do_all[BLK - reach : BLK, :] = far_l[:reach, :]
        do_all[BLK : BLK + own, :] = near_l[:own, :]
        do_all[BLK + own : BLK + 2 * own, :] = near_r[:own, :]
        do_all[BLK + 2 * own : BLK + 2 * own + reach, :] = far_r[:reach, :]
        do_all[BLK + 2 * own + reach :, :] = blank
        stats(far_l, reach, 0)
        for i in range(blocks):
            stats(near_l, own + 2 * STAT_ROWS * i, 1 + i)
            stats(near_r, own + 2 * STAT_ROWS * i, 1 + blocks + i)
        stats(far_r, reach, 1 + 2 * blocks)

    start, count = bound_ref[j, 0], bound_ref[j, 1]

    @pl.when(count > 0)
    def _():
        here = pl.ds(pl.multiple_of(step_id * BLK, BLK), BLK)
        for g in range(groups):
            q4_ref[g] = head_stack(q_ref[:, lanes_of(g)], True, jnp.asarray(0.125, BF))
            do4_ref[g] = head_stack(do_all[here, lanes_of(g)], False)
        ident_q = idq_ref[pl.ds(j, 1), :]

        def step(c, _):
            at, seen = key_span(idk_ref, ident_q, start, c, SPAN_BACK, blocks)
            for g in range(groups):
                s = dot_nt(k_ref[at, lanes_of(g)], q4_ref[g])
                dp = dot_nt(v_ref[at, lanes_of(g)], do4_ref[g])
                lse = stat_ref[0, g, pl.ds(step_id, 1), :]
                delta = stat_ref[1, g, pl.ds(step_id, 1), :]
                low_p, low_ds = score_gradients(s, dp, lse, delta, seen)
                dk_ref[at, lanes_of(g)] += dot(low_ds, q4_ref[g])
                dv_ref[at, lanes_of(g)] += dot(low_p, do4_ref[g])
            return 0

        lax.fori_loop(0, count, step, 0)


def backward_halo_call(bounds, q_win, pieces, k_win, v_win, idk, idq, dk, dv, first):
    own, width = dk.shape
    groups = width // 256
    side, blocks = first // BLK, own // BLK
    inside = lambda w: pl.BlockSpec(
        (pl.Element(own), pl.Element(w)), lambda i: (pl.multiple_of(first + 0 * i, BLK), 0)
    )
    outside = pl.BlockSpec((BLK, width), lambda i: (jnp.where(i < side, i, i + blocks), 0))
    return pl.pallas_call(
        functools.partial(backward_halo_kernel, first=first),
        grid=(2 * side,),
        in_specs=[SMEM, outside]
        + [whole(p.shape) for p in pieces]
        + [inside(width)] * 2
        + [inside(idk.shape[1]), whole(idq.shape)]
        + [whole((own, width))] * 2,
        out_specs=[whole((own, width))] * 2,
        out_shape=[jax.ShapeDtypeStruct((own, width), F32)] * 2,
        scratch_shapes=[
            pltpu.VMEM((groups, GROUP * BLK, 256), BF),
            pltpu.VMEM((2 * first, width), BF),
            pltpu.VMEM((groups, GROUP * BLK, 256), BF),
            pltpu.VMEM((2, groups, 16, GROUP * BLK), F32),
        ],
        compiler_params=params(20),
        cost_estimate=cost(11),
        name="attention_backward_halo",
    )(bounds, q_win, *pieces, k_win, v_win, idk, idq, dk, dv)


def norm_parts(x):
    centred = x - jnp.mean(x, -1, keepdims=True)
    inverse = lax.rsqrt(jnp.mean(centred * centred, -1, keepdims=True) + EPS)
    return centred * inverse, inverse


def norm_back(grad, xhat, inverse, gain):
    scaled = grad * gain
    return inverse * (
        scaled
        - jnp.mean(scaled, -1, keepdims=True)
        - xhat * jnp.mean(scaled * xhat, -1, keepdims=True)
    )


def columns_sum(x):
    return jnp.sum(x, 0, keepdims=True)


def chip_order(ab, core):
    return jnp.where(core == 0, ab, ab % 2 * 2 + ab // 2)


def slices_out(place, source, keep, away, lead, sem, slices, rows):
    for n in range(slices):
        rel = place ^ n
        for target, odd in ((keep, 0), (away, 1)):
            core = place % 2 ^ odd

            @pl.when(rel % 2 == odd)
            def _():
                pltpu.make_async_copy(
                    source.at[n * rows : (n + 1) * rows, :],
                    target.at[chip_order(rel // 2, core), pl.ds(lead, rows), :],
                    sem.at[n],
                ).start()


def gathered(place, refs):
    for far in range(2):
        for n in range(4):
            rel = 2 * chip_order(jnp.int32(n), place % 2 ^ far) + far
            yield refs[4 * far + n], place ^ rel


def slices_wait(source, keep, sem, slices, rows):
    for n in range(slices):
        pltpu.make_async_copy(
            source.at[n * rows : (n + 1) * rows, :], keep.at[0, 0:rows, :], sem.at[n]
        ).wait()


def one_quarter(q, w_all, norm_ref, dy_ref, bu_ref, dbu_ref, out_acc, dn_acc, g_all, fresh):
    own, width = norm_ref.shape
    tile = w_all.shape[1] - width
    for t in range((w_all.shape[1] - width) // tile):
        cols = slice(tile * t, tile * t + tile)
        down = slice(width + tile * t, width + tile * t + tile)
        norm, dy = norm_ref[...], dy_ref[...]
        up_w = w_all[q, :width, cols]
        down_w = w_all[q, down, :]
        pre = dot(norm, up_w) + bu_ref[pl.ds(q, 1), cols]
        cdf = 0.5 * (1.0 + lax.erf(pre * np.float32(0.7071067811865476)))
        density = jnp.exp(-0.5 * pre * pre) * np.float32(0.3989422804014327)
        act = (pre * cdf).astype(BF)
        d_pre = (dot_nt(dy, down_w) * (cdf + pre * density)).astype(BF)
        dbu_ref[pl.ds(q, 1), cols] = columns_sum(d_pre.astype(F32))
        if fresh and t == 0:
            out_acc[...] = dot(act, down_w)
            dn_acc[...] = dot_nt(d_pre, up_w)
        else:
            out_acc[...] += dot(act, down_w)
            dn_acc[...] += dot_nt(d_pre, up_w)
        g_all[q, :width, cols] = dot_tn(norm, d_pre).astype(BF)
        g_all[q, down, :] = dot_tn(act, dy).astype(BF)


def middle_own_kernel(
    place_ref, x_ref, low_ref, wo_ref, vec_ref, dy_ref, bu_ref, up_ref, down_ref,
    hid_ref, norm_ref, out_ref, dn_ref, dbu_ref, keep_ref, send_ref, w_all, g_all, w_sem, g_sem,
    *, slices,
):
    width = x_ref.shape[1]
    rows = w_all.shape[1] // slices
    copies = [
        pltpu.make_async_copy(up_ref, w_all.at[0, :width, :], w_sem.at[0]),
        pltpu.make_async_copy(down_ref, w_all.at[0, width:, :], w_sem.at[1]),
    ]
    for copy in copies:
        copy.start()
    hidden_in = x_ref[...].astype(F32) + dot(low_ref[...], wo_ref[...]) + vec_ref[B_OUT]
    hid_ref[...] = hidden_in
    norm_ref[...] = layer_norm_low(hidden_in, vec_ref[LN2_GAIN], vec_ref[LN2_SHIFT])
    for copy in copies:
        copy.wait()
    one_quarter(0, w_all, norm_ref, dy_ref, bu_ref, dbu_ref, out_ref, dn_ref, g_all, True)
    slices_out(place_ref[0], g_all.at[0], keep_ref, send_ref, 0, g_sem, slices, rows)
    slices_wait(g_all.at[0], keep_ref, g_sem, slices, rows)


def middle_own_call(place, x, low, w_out, vectors, dy, b_up, w_up, w_down, slices):
    own, width = x.shape
    hidden = b_up.shape[1]
    rows = width + hidden
    vmem = pl.BlockSpec(memory_space=pltpu.VMEM)
    sds = jax.ShapeDtypeStruct
    return pl.pallas_call(
        functools.partial(middle_own_kernel, slices=slices),
        in_specs=[SMEM] + [vmem] * 6 + [ANY] * 2,
        out_specs=[vmem] * 5 + [ANY] * 2,
        out_shape=[
            sds((own, width), F32),
            sds((own, width), BF),
            sds((own, width), F32),
            sds((own, width), F32),
            sds((1, hidden), F32),
        ]
        + [sds((slices // 2, rows // slices, width), BF)] * 2,
        scratch_shapes=[
            pltpu.VMEM((1, rows, width), BF),
            pltpu.VMEM((1, rows, width), BF),
            pltpu.SemaphoreType.DMA((2,)),
            pltpu.SemaphoreType.DMA((slices,)),
        ],
        compiler_params=params(56),
        cost_estimate=cost(12),
        name="middle_own",
    )(place, x, low, w_out, vectors, dy, b_up, w_up, w_down)


def middle_kernel(
    place_ref, vec_ref, bu_ref, lse_ref, norm_in, dy_in, out_in, dn_in, hid_in, low_in, mixed_in,
    wo_in, keep_in, send_in, *refs, slices,
):
    piece_refs = refs[:slices]
    (
        act_out, dh_out, dheads_ref, head_ref, tail_ref, delta_ref, small_ref, dbu_ref, keep_ref,
        send_ref,
        w_all, g_all, go_all, norm_ref, dy_ref, out_acc, dn_acc, hid_ref, low_ref, mixed_ref,
        wo_ref, act_ref, dh_ref, own_grads, w_sem, g_sem, in_sem, out_sem,
    ) = refs[slices:]
    place = place_ref[0]
    own, width = norm_ref.shape
    quarters = w_all.shape[0]
    rows = w_all.shape[1] // slices

    def fetches(q):
        return [
            pltpu.make_async_copy(
                ref.at[q],
                w_all.at[q, pl.ds(pl.multiple_of(source * rows, rows), rows), :],
                w_sem.at[q, n],
            )
            for n, (ref, source) in enumerate(gathered(place, piece_refs))
        ]

    inputs = [
        pltpu.make_async_copy(source, target, in_sem.at[n])
        for n, (source, target) in enumerate(
            (
                (norm_in, norm_ref), (dy_in, dy_ref), (out_in, out_acc), (dn_in, dn_acc),
                (hid_in, hid_ref), (low_in, low_ref), (mixed_in, mixed_ref), (wo_in, wo_ref),
                (keep_in, own_grads.at[0]), (send_in, own_grads.at[1]),
            )
        )
    ]
    for copy in inputs[:2] + fetches(0) + inputs[2:4]:
        copy.start()
    for q in range(1, quarters):
        for copy in fetches(q):
            copy.start()
    for copy in inputs[4:]:
        copy.start()
    for copy in inputs[:2]:
        copy.wait()

    def quarter(q, _):
        for copy in fetches(q):
            copy.wait()

        @pl.when(q == 0)
        def _():
            for copy in inputs[2:4]:
                copy.wait()

        one_quarter(q, w_all, norm_ref, dy_ref, bu_ref, dbu_ref, out_acc, dn_acc, g_all, False)
        slices_out(
            place, g_all.at[q], keep_ref, send_ref, pl.multiple_of(q * rows + rows, rows),
            g_sem.at[q], slices, rows,
        )
        return 0

    lax.fori_loop(0, quarters, quarter, 0)

    for copy in inputs[4:]:
        copy.wait()
    hidden_in = hid_ref[...]
    xhat, inverse = norm_parts(hidden_in)
    dn = dn_acc[...]
    dy = dy_ref[...].astype(F32)
    d_hidden = dy + norm_back(dn, xhat, inverse, vec_ref[LN2_GAIN])
    dh_ref[...] = d_hidden
    d_att = d_hidden.astype(BF)
    d_heads = dot_nt(d_att, wo_ref[...]).astype(BF)
    dheads_ref[:own, :] = d_heads
    go_all[...] = dot_tn(low_ref[...], d_att).astype(BF)
    few = width // slices
    base = quarters * rows + rows
    slices_out(place, go_all, keep_ref, send_ref, base, g_sem.at[quarters], slices, few)
    act_ref[...] = (hidden_in + out_acc[...] + vec_ref[B_DOWN]).astype(BF)
    outputs = [
        pltpu.make_async_copy(source, target, out_sem.at[n])
        for n, (source, target) in enumerate(
            (
                (act_ref, act_out), (dh_ref, dh_out),
                (own_grads.at[0], keep_ref.at[:, 0:rows, :]),
                (own_grads.at[1], send_ref.at[:, 0:rows, :]),
            )
        )
    ]
    for copy in outputs:
        copy.start()
    small_ref[0:1, :] = columns_sum(dn * xhat)
    small_ref[1:2, :] = columns_sum(dn)
    small_ref[2:3, :] = columns_sum(dy)
    small_ref[3:4, :] = columns_sum(d_att.astype(F32))
    spread = d_heads.astype(F32) * mixed_ref[...]
    pick = lax.broadcasted_iota(jnp.int32, (8, 256), 0)
    pick = (pick == lax.broadcasted_iota(jnp.int32, (8, 256), 1) // 64).astype(F32)
    for g in range(width // 256):
        for i in range(own // BLK):
            block = spread[BLK * i : BLK * i + BLK, 256 * g : 256 * g + 256]
            sums = lax.dot_general(
                pick, block, (((1,), (1,)), ((), ())),
                preferred_element_type=F32, precision=lax.Precision.HIGHEST,
            )
            delta = jnp.concatenate([sums[h : h + 1, :] for h in range(GROUP)], 1)
            delta_ref[g, i] = delta
            lse = lse_ref[g, i]
            left = jnp.concatenate(
                [lse[:, :256], lse[:, 256:], delta[:, :256], delta[:, 256:]], 0
            )
            parts = []
            for _ in range(3):
                parts.append(left.astype(BF))
                left = left - parts[-1].astype(F32)
            parts = jnp.concatenate(parts, 0)
            at = slice(256 * g, 256 * g + 256)
            lo = own + 2 * STAT_ROWS * i
            dheads_ref[lo : lo + 2 * STAT_ROWS, at] = parts
            for target, row in ((head_ref, 0), (tail_ref, own // BLK - 1)):
                if i == row:
                    target[REACH : REACH + 2 * STAT_ROWS, at] = parts
    blank = jnp.zeros((STAT_PAD - 2 * STAT_ROWS, width), BF)
    head_ref[REACH + 2 * STAT_ROWS :, :] = blank
    tail_ref[REACH + 2 * STAT_ROWS :, :] = blank
    head_ref[:REACH, :] = d_heads[:REACH, :]
    tail_ref[:REACH, :] = d_heads[own - REACH :, :]
    for q in range(quarters):
        slices_wait(g_all.at[q], keep_ref, g_sem.at[q], slices, rows)
    slices_wait(go_all, keep_ref, g_sem.at[quarters], slices, few)
    for copy in outputs:
        copy.wait()


def middle_call(
    place, hidden_in, norm, out, dn, low, mixed, w_out, vectors, dy, b_up, lse, kept, sent, pieces,
    slices,
):
    own, width = norm.shape
    quarters, hidden = b_up.shape
    rows = width + hidden
    vmem = pl.BlockSpec(memory_space=pltpu.VMEM)
    sds = jax.ShapeDtypeStruct
    grads = sds((slices // 2, ((quarters + 1) * rows + width) // slices, width), BF)
    return pl.pallas_call(
        functools.partial(middle_kernel, slices=slices),
        in_specs=[SMEM] + [vmem] * 3 + [ANY] * (10 + len(pieces)),
        out_specs=[ANY] * 2 + [vmem] * 6 + [ANY] * 2,
        out_shape=[
            sds((own, width), BF),
            sds((own, width), F32),
            sds((own + own // BLK * 2 * STAT_ROWS, width), BF),
            sds((REACH + STAT_PAD, width), BF),
            sds((REACH + STAT_PAD, width), BF),
            sds((width // 256, own // BLK, 1, GROUP * BLK), F32),
            sds((4, width), F32),
            sds((quarters, hidden), F32),
            grads,
            grads,
        ],
        scratch_shapes=[
            pltpu.VMEM((quarters, rows, width), BF),
            pltpu.VMEM((quarters, rows, width), BF),
            pltpu.VMEM((width, width), BF),
            pltpu.VMEM((own, width), BF),
            pltpu.VMEM((own, width), BF),
            pltpu.VMEM((own, width), F32),
            pltpu.VMEM((own, width), F32),
            pltpu.VMEM((own, width), F32),
            pltpu.VMEM((own, width), BF),
            pltpu.VMEM((own, width), F32),
            pltpu.VMEM((width, width), BF),
            pltpu.VMEM((own, width), BF),
            pltpu.VMEM((own, width), F32),
            pltpu.VMEM((2,) + kept.shape, BF),
            pltpu.SemaphoreType.DMA((quarters, slices)),
            pltpu.SemaphoreType.DMA((quarters + 1, slices)),
            pltpu.SemaphoreType.DMA((10,)),
            pltpu.SemaphoreType.DMA((4,)),
        ],
        compiler_params=params(44),
        cost_estimate=cost(20),
        name="middle",
    )(
        place, vectors, b_up, lse, norm, dy, out, dn, hidden_in, low, mixed, w_out, kept, sent,
        *pieces,
    )


def turn_back_kernel(
    place_ref, x_ref, vec_ref, dq_ref, dk_ref, dv_ref, q_ref, k_ref, hot_ref, table_ref, grid_ref,
    back_ref, d_ref, db_ref, freq_ref, keep_ref, send_ref, norm_ref, g_all, sem, *, slices,
):
    width = x_ref.shape[1]
    group = pl.program_id(0)

    @pl.when(group == 0)
    def _():
        norm_ref[...] = layer_norm_low(
            x_ref[...].astype(F32), vec_ref[LN1_GAIN], vec_ref[LN1_SHIFT]
        )

    c, s = cos_sin(hot_ref[...], table_ref[...])
    norm = norm_ref[...]

    def gradient(n, low):
        d_ref[n] = low
        db_ref[n : n + 1, :] = columns_sum(low.astype(F32))
        at = pl.ds(pl.multiple_of(n * width + group * 256, 256), 256)
        g_all[:, at] = dot_tn(norm, low).astype(BF)

    d_angle = 0.0
    for n, (grad, turned_ref) in enumerate(((dq_ref, q_ref), (dk_ref, k_ref))):
        g1, g2 = grad[:, :128], grad[:, 128:]
        d_angle = d_angle + (g2 * turned_ref[:, :128] - g1 * turned_ref[:, 128:])
        back = jnp.concatenate([g1 * c + g2 * s, g2 * c - g1 * s], 1).astype(BF)
        gradient(n, dot(back, back_ref[...]).astype(BF))
    freq_ref[...] = lax.dot_general(
        grid_ref[...], d_angle, (((1,), (0,)), ((), ())),
        preferred_element_type=F32, precision=lax.Precision.HIGHEST,
    )
    gradient(2, dv_ref[...].astype(BF))

    @pl.when(group == width // 256 - 1)
    def _():
        slices_out(place_ref[0], g_all, keep_ref, send_ref, 0, sem, slices, width // slices)
        slices_wait(g_all, keep_ref, sem, slices, width // slices)


def turn_back_call(
    place, x, vectors, dq, dk, dv, q_exact, k_exact, onehot, table, grid8, back, first, slices
):
    rows, width = dk.shape
    sds = jax.ShapeDtypeStruct
    part = pl.BlockSpec((rows, 256), lambda g: (0, g))
    hot = pl.BlockSpec(
        (pl.Element(rows), pl.Element(onehot.shape[1])),
        lambda g: (pl.multiple_of(first + 0 * g, BLK), 0),
    )
    return pl.pallas_call(
        functools.partial(turn_back_kernel, slices=slices),
        grid=(width // 256,),
        in_specs=[SMEM, whole(x.shape), whole(vectors.shape)]
        + [part] * 5
        + [
            hot,
            pl.BlockSpec((table.shape[0], 512), lambda g: (0, g)),
            whole(grid8.shape),
            whole(back.shape),
        ],
        out_specs=[
            pl.BlockSpec((3, rows, 256), lambda g: (0, 0, g)),
            pl.BlockSpec((3, 256), lambda g: (0, g)),
            pl.BlockSpec((8, 128), lambda g: (0, g)),
        ]
        + [ANY] * 2,
        out_shape=[
            sds((3, rows, width), BF),
            sds((3, width), F32),
            sds((8, width // 2), F32),
        ]
        + [sds((slices // 2, width // slices, 3 * width), BF)] * 2,
        scratch_shapes=[
            pltpu.VMEM((rows, width), BF),
            pltpu.VMEM((width, 3 * width), BF),
            pltpu.SemaphoreType.DMA((slices,)),
        ],
        compiler_params=params(16),
        cost_estimate=cost(9),
        name="turn_back",
    )(place, x, vectors, dq, dk, dv, q_exact, k_exact, onehot, table, grid8, back)


def input_grad_kernel(
    place_ref, x_ref, vec_ref, d_ref, w_ref, dh_ref, db_ref, mid_ref, freq_ref, up0_ref, up_ref,
    out_ref, small_ref,
):
    width = x_ref.shape[1]
    d_norm = sum(dot_nt(d_ref[n], w_ref[:, lanes_of(n, width)]) for n in range(3))
    xhat, inverse = norm_parts(x_ref[...].astype(F32))
    out_ref[...] = dh_ref[...] + norm_back(d_norm, xhat, inverse, vec_ref[LN1_GAIN])
    row = 0
    for vector in (
        columns_sum(d_norm * xhat), columns_sum(d_norm), *(db_ref[n : n + 1, :] for n in range(3)),
        mid_ref[3:4, :], freq_ref[0:1, :], freq_ref[1:2, :], *(mid_ref[n : n + 1, :] for n in range(3)),
    ):
        for n in range(vector.shape[1] // 128):
            small_ref[row : row + 1, :] = vector[:, lanes_of(n, 128)]
            row += 1
    depth = 1 + up_ref.shape[0]
    hidden = up0_ref.shape[1] // 128
    for k in range(depth):
        quarter = (place_ref[1] - k + depth) % depth
        vector = up_ref[k - 1 : k, :] if k else up0_ref[...]
        for n in range(hidden):
            small_ref[pl.ds(row + quarter * hidden + n, 1), :] = vector[:, lanes_of(n, 128)]


def input_grad_call(place, x, vectors, d_qkv, weight, d_hidden, db_qkv, small_mid, freqs, up0, up):
    rows, width = x.shape
    short = 9 * width + freqs.shape[1] * 2 + up0.size * (1 + up.shape[0])
    return pl.pallas_call(
        input_grad_kernel,
        in_specs=[SMEM] + [pl.BlockSpec(memory_space=pltpu.VMEM)] * 10,
        out_shape=[
            jax.ShapeDtypeStruct((rows, width), F32),
            jax.ShapeDtypeStruct((short // 128, 128), F32),
        ],
        compiler_params=params(20),
        cost_estimate=cost(7),
        name="input_grad",
    )(place, x, vectors, d_qkv, weight, d_hidden, db_qkv, small_mid, freqs, up0, up)


def assemble_kernel(place_ref, *refs, split, outs, skip):
    out_refs, (held, sem) = refs[-2 - outs : -2], refs[-2:]
    pairs = refs[:4]
    piece_refs = [pairs[n // 2].at[n % 2] for n in range(8)]
    place, depth = place_ref[0], place_ref[1]
    slot = pl.program_id(0)

    def copy(ref, target):
        return pltpu.make_async_copy(ref, held.at[target], sem.at[target])

    @pl.when(slot == 0)
    def _():
        for ref, source in gathered(place, piece_refs):
            copy(ref, source).start()

    copy(piece_refs[0], slot).wait()
    rows = held.shape[-2]
    total_ref = None
    if skip is not None:
        out_refs, total_ref = out_refs[:-1], out_refs[-1]
    out_refs, squares = out_refs[:-1], out_refs[-1]

    @pl.when(slot == 0)
    def _():
        squares[...] = jnp.zeros_like(squares)

    def add_squares(block):
        total = fold8(block * block, jnp.sum)
        squares[...] += sum(total[:, lanes_of(n, 128)] for n in range(block.shape[1] // 128))

    if split:
        for n in range(split):
            block = held[slot, (depth - n + split) % split].astype(F32)
            add_squares(block)
            lo = 0
            for ref in out_refs:
                ref[n * rows : n * rows + rows, :] = block[:, lo : lo + ref.shape[1]]
                lo += ref.shape[1]
    else:
        block = held[slot].astype(F32)
        add_squares(block)
        each = held.shape[0] // len(out_refs)
        for n, ref in enumerate(out_refs):

            @pl.when(slot // each == n)
            def _():
                ref[...] = block
    if skip is not None:
        small_ref = refs[4]

        @pl.when(slot == held.shape[0] - 1)
        def _():
            short = small_ref[...]
            row = lax.broadcasted_iota(jnp.int32, short.shape, 0)
            mine = (row >= skip[0]) & (row < skip[1])
            parts = row >= short.shape[0] - 8
            others = jnp.where(mine, 0.0, jnp.where(parts, short, short * short))
            turned = jnp.where(mine, short * short, 0.0)
            total_ref[0:1, :] = jnp.full((1, 128), jnp.sum(turned))
            total_ref[1:2, :] = jnp.full((1, 128), jnp.sum(others) + jnp.sum(squares[...]))


def assemble_call(place, arrays, shapes, split, small=None, skip=None):
    pieces = 8
    rows = arrays[0].shape[-2] * max(split, 1)
    each = pieces if split else pieces // len(shapes)

    def spec(n, shape):
        lead = 0 if split else n * each
        return pl.BlockSpec((rows, shape[1]), lambda i: (jnp.clip(i - lead, 0, each - 1), 0))

    specs = [spec(n, shape) for n, shape in enumerate(shapes)] + [whole((8, 128))]
    shapes = shapes + [(8, 128)]
    given = []
    if small is not None:
        given, specs, shapes = [small], specs + [whole((2, 128))], shapes + [(2, 128)]
    return pl.pallas_call(
        functools.partial(assemble_kernel, split=split, outs=len(shapes), skip=skip),
        grid=(pieces,),
        in_specs=[SMEM] + [ANY] * len(arrays) + [whole(x.shape) for x in given],
        out_specs=specs,
        out_shape=[jax.ShapeDtypeStruct(s, F32) for s in shapes],
        scratch_shapes=[
            pltpu.VMEM((pieces,) + arrays[0].shape[1:], BF),
            pltpu.SemaphoreType.DMA((pieces,)),
        ],
        compiler_params=params(16),
        cost_estimate=cost(6),
        name="assemble",
    )(place, *arrays, *given)


def send(x, axis, pairs):
    return lax.ppermute(x, axis, pairs)


def plane_gather(piece):
    pair = jnp.stack([piece, send(piece, PLANE, FIRST)])
    return pair, send(pair, PLANE, SECOND)


def core_gather(pair, last):
    return [pair, last, send(pair, "c", SWAP), send(last, "c", SWAP)]


def wide_sum(x, extra):
    return lax.psum(x, "e") if extra > 1 else x


def sum_low(*terms):
    return functools.reduce(lambda x, y: x + y, [t.astype(F32) for t in terms])


def after(x, *others):
    return lax.optimization_barrier((x, others))[0]


def ring(size, step):
    return [(i, (i + step) % size) for i in range(size)]


def add_from(vector, axis, reach=0, size=2):
    return vector + send(vector, axis, [(i, i ^ (reach or 1)) for i in range(size)])


def on_device(
    tokens,
    segment,
    padding,
    coords,
    ln1_gain,
    ln1_shift,
    query_key_value_weight,
    b_qkv,
    output_weight,
    b_out,
    rope_freqs,
    ln2_gain,
    ln2_shift,
    w_up,
    b_up,
    w_down,
    b_down,
    cotangent,
    *,
    extra,
    depth,
):
    tokens, cotangent = tokens[0], cotangent[0]
    own, width = tokens.shape
    length = own * depth
    heads = rope_freqs.shape[1]
    half = width // heads // 2
    groups = heads // GROUP
    slices = 8
    outer = BLK
    side = own + outer
    win = own + 2 * side
    blocks = own // BLK
    z = lax.axis_index("n")
    plane = lax.axis_index("a") * 4 + lax.axis_index("b") * 2 + lax.axis_index("c")
    place = jnp.stack([plane, z]).astype(jnp.int32)
    up = [(i, i + 1) for i in range(depth - 1)]
    down = [(i + 1, i) for i in range(depth - 1)]
    up2 = [(i, i + 2) for i in range(depth - 2)]
    down2 = [(i + 2, i) for i in range(depth - 2)]

    def around(x, head, tail):
        before2 = send(tail, "n", up2)
        before = send(x, "n", up)
        after_ = send(x, "n", down)
        after2 = send(head, "n", down2)
        return [before2, before, after_, after2]

    position = jnp.arange(length, dtype=jnp.int32)
    ident = jnp.where(padding[0] == 0, segment[0], 1000 + position)
    ident = jnp.concatenate(
        [jnp.full((side,), -1, jnp.int32), ident, jnp.full((side,), 1 << 20, jnp.int32)]
    )
    ident_win = lax.dynamic_slice_in_dim(ident, z * own, win, 0)
    near = lax.broadcasted_iota(jnp.int32, (win,), 0)
    ident_win = jnp.where(near < outer - REACH, -1, ident_win)
    ident_win = jnp.where(near >= win - outer + REACH, 1 << 20, ident_win)
    idk = jnp.broadcast_to(ident_win[:, None], (win, BLK))
    idq = ident_win.reshape(win // BLK, BLK)

    lowest, highest = idq[:, 0], idq[:, BLK - 1]

    def bounds(queries, keys):
        before = highest[keys][None, :] < lowest[queries][:, None]
        reached = lowest[keys][None, :] <= highest[queries][:, None]
        return jnp.sum(before, 1), jnp.sum(reached, 1)

    def steps(blocks, span):
        return (jnp.maximum(blocks, 0) + span - 1) // span

    mid = slice(side // BLK, side // BLK + blocks)
    lo, hi = bounds(mid, slice(None))
    bounds_fwd = [
        lo, steps(hi - lo, SPAN), jnp.minimum(lo, mid.start), steps(mid.start - lo, SPAN_SIDE),
        steps(hi - mid.stop, SPAN_SIDE),
    ]
    bounds_fwd = jnp.stack(bounds_fwd, 1).astype(jnp.int32)
    lo, hi = bounds(slice(None), mid)
    bounds_bwd = jnp.stack([lo, steps(hi - lo, SPAN_BACK)], 1).astype(jnp.int32)

    grid = jnp.pad(coords[:, 0], ((0, 0), (side, side)))
    grid_win = lax.dynamic_slice_in_dim(grid, z * own, win, 1)
    grid_own = lax.dynamic_slice_in_dim(grid, z * own + side, own, 1)
    lane = jnp.arange(4 * SIDE)
    picked = jnp.where(lane[None, :] < 2 * SIDE, grid_win[0][:, None], grid_win[1][:, None])
    onehot = (picked == (lane % SIDE)[None, :]).astype(BF)
    table = turn_table(rope_freqs)

    local = np.arange(256)
    order = np.zeros((256, 256), np.float32)
    order[(local % 128) // 32 * 64 + local // 128 * 32 + local % 32, local] = 1.0
    order = jnp.asarray(order, BF)
    qk_bias = b_qkv[: 2 * width].reshape(2 * groups, GROUP, 2, half).swapaxes(1, 2)
    bias_turned = jnp.concatenate([qk_bias.reshape(-1), b_qkv[2 * width :]])

    x_parts = around(tokens, tokens[:REACH], tokens[own - REACH :])
    vectors = jnp.stack([ln1_gain, ln1_shift, b_out, ln2_gain, ln2_shift, b_down])
    rot_q, rot_k, values, q_exact, k_exact, weight_turned = qkv_own_call(
        tokens, onehot, vectors, query_key_value_weight, bias_turned, order, table, side
    )
    rows = (width + w_down.shape[0]) // slices
    eighth = jnp.where(
        plane < width // rows,
        lax.dynamic_slice_in_dim(w_up, jnp.minimum(plane * rows, width - rows), rows, 0),
        lax.dynamic_slice_in_dim(w_down, jnp.maximum(plane * rows - width, 0), rows, 0),
    )
    left, bias_rows = b_up, []
    for _ in range(3):
        bias_rows.append(left.astype(BF))
        left = left - rounded(left)
    bias_rows = jnp.pad(jnp.stack(bias_rows), ((0, 13), (0, 0)))
    eighth = jnp.concatenate([eighth, bias_rows], 0)
    others = [send(eighth, "n", ring(depth, k)) for k in range(1, depth)]
    x_parts, rot_q, idk = lax.optimization_barrier((x_parts, rot_q, idk))
    halo_args = (x_parts, onehot, vectors, weight_turned, bias_turned, table)
    rot_q, rot_k, values = halo_call(*halo_args, (rot_q, rot_k, values), (0, 1, 2), side)
    part = forward_call(bounds_fwd, rot_q, rot_k, values, idk, idq, side, own, 0, blocks // 2)
    others, part = lax.optimization_barrier((others, part))
    up_biases = jnp.concatenate(
        [jnp.sum(x[rows : rows + 3].astype(F32), 0, keepdims=True) for x in others]
    )
    own_w = jnp.stack([x[:rows] for x in others])
    over_1, over_2 = send(own_w, PLANE, FIRST), send(own_w, PLANE, SECOND)
    part, _ = lax.optimization_barrier((part, own_w))
    mixed, mixed_low, lse = forward_call(
        bounds_fwd, rot_q, rot_k, values, idk, idq, side, own, blocks // 2, blocks // 2, part
    )
    hidden_in, norm2, out0, dn0, up_sum0, kept_own, sent_own = middle_own_call(
        place, tokens, mixed_low, output_weight, vectors, cotangent, b_up[None],
        w_up, w_down, slices,
    )
    over_1, over_2, norm2 = lax.optimization_barrier((over_1, over_2, norm2))
    diagonal = send(over_1, PLANE, SECOND)
    near = [own_w, over_1, over_2, diagonal]
    pieces = near + [send(x, "c", SWAP) for x in near]
    grid8 = jnp.pad(grid_own.astype(F32), ((0, 6), (0, 0)))
    norm2, up_biases, bounds_bwd = lax.optimization_barrier((norm2, up_biases, bounds_bwd))
    (
        activations, d_hidden, d_heads, d_head, d_tail, delta, small_mid, up_sums, kept_mid,
        sent_mid,
    ) = middle_call(
        place, hidden_in, norm2, out0, dn0, mixed_low, mixed, output_weight, vectors, cotangent,
        up_biases, lse, kept_own, sent_own, pieces, slices,
    )
    far_mid = send(sent_mid, "c", SWAP)
    do_parts = around(d_heads, d_head, d_tail)

    early = (depth - 1) * rows
    lots = (slice(0, early), slice(early, depth * rows + width // slices))

    def chip_sum(lot, n):
        return sum_low(kept_mid[n, lots[lot]], far_mid[n, lots[lot]])

    def plane_part(lot, lo, hi):
        at, there = slice(lots[lot].start + lo, lots[lot].start + hi), slice(lo, hi)
        total = sum_low(kept_mid[0, at], far_mid[0, at], got_1[lot][0, there], got_2[lot][there])
        return wide_sum(total, extra)

    got_1, got_2 = [None, None], [None, None]
    away = chip_sum(0, slice(1, None, 2)).astype(BF)
    got_1[0] = send(away, PLANE, FIRST)
    dq, dk, dv = backward_own_call(
        bounds_fwd, rot_q, d_heads, rot_k, values, idk, idq, lse, after(delta, away), side, own
    )
    got_1[0], dq = lax.optimization_barrier((got_1[0], dq))
    away = (chip_sum(0, 2) + got_1[0][1].astype(F32)).astype(BF)
    got_2[0] = send(away, PLANE, SECOND)
    away_b = chip_sum(1, slice(1, None, 2)).astype(BF)
    got_1[1] = send(away_b, PLANE, FIRST)
    do_parts, dq, dk, _ = lax.optimization_barrier((do_parts, dq, dk, (away, away_b)))
    dk, dv = backward_halo_call(
        bounds_bwd, rot_q, do_parts, rot_k, values, idk, idq, dk, dv, side
    )
    got_1[1], got_2[0], dk = lax.optimization_barrier((got_1[1], got_2[0], dk))
    away = (chip_sum(1, 2) + got_1[1][1].astype(F32)).astype(BF)
    got_2[1] = send(away, PLANE, SECOND)
    ff_sent = [plane_part(0, k * rows, k * rows + rows).astype(BF) for k in range(1, depth - 1)]
    ff_got = [send(ff_sent[k - 1], "n", ring(depth, -k)) for k in range(1, depth - 1)]
    dk = after(dk, away, ff_sent)

    d_qkv, grad_b_qkv, freqs8, kept_qkv, sent_qkv = turn_back_call(
        place, tokens, vectors, dq, dk, dv, q_exact, k_exact, onehot, table, grid8,
        order.T, side, slices,
    )
    far_qkv = send(sent_qkv, "c", SWAP)
    away = sum_low(kept_qkv[1::2], far_qkv[1::2]).astype(BF)
    got_1_qkv = send(away, PLANE, FIRST)
    got_2[1] = after(got_2[1], away)
    ff_sent = plane_part(1, 0, rows).astype(BF)
    ff_got.append(send(ff_sent, "n", ring(depth, 1 - depth)))
    input_grad, small_in = input_grad_call(
        place, tokens, vectors, after(d_qkv, ff_sent), query_key_value_weight, d_hidden,
        grad_b_qkv, small_mid, freqs8, up_sum0, up_sums,
    )
    got_1_qkv, small_in = lax.optimization_barrier((got_1_qkv, small_in))
    away = sum_low(kept_qkv[2], far_qkv[2], got_1_qkv[1]).astype(BF)
    got_2_qkv = send(away, PLANE, SECOND)
    ff_got, small_in, _ = lax.optimization_barrier((ff_got, small_in, away))
    plane_qkv = wide_sum(sum_low(kept_qkv[0], far_qkv[0], got_1_qkv[0], got_2_qkv), extra)
    ff_total = plane_part(0, 0, rows) + sum_low(*ff_got)

    sizes = [width, width, 3 * width, width, rope_freqs.size] + [width] * 3 + [b_up.size * depth]
    small = add_from(small_in, "c")

    part = plane_part(1, rows, rows + width // slices)
    part = jnp.concatenate([plane_qkv, part], 1).astype(BF)
    thin = part.shape[0] // depth
    cut = lambda k: lax.dynamic_slice_in_dim(part, ((z + k) % depth) * thin, thin, 0)
    got = [send(cut(k), "n", ring(depth, k)) for k in range(1, depth)]
    small = add_from(add_from(after(small, part), "b"), "a")
    if extra > 1:
        small = lax.psum(small, "e")
    got, small = lax.optimization_barrier((got, small))
    low = sum_low(cut(0), *got).astype(BF)
    strip = jnp.stack([low] + [send(low, "n", ring(depth, k)) for k in range(1, depth)])
    ff_pair, ff_last = plane_gather(after(ff_total, low).astype(BF))
    pair, last = plane_gather(strip)
    ff_pieces = [after(x, strip) for x in core_gather(ff_pair, ff_last)]
    total_w_up, total_w_down, ff_squares = assemble_call(
        place, ff_pieces, [w_up.shape, w_down.shape], 0
    )
    small = jnp.concatenate([small, ff_squares], 0)
    reach = 1
    while reach < depth:
        small = add_from(small, "n", reach, depth)
        reach *= 2
    last, small = lax.optimization_barrier((last, small))
    turned = sum(sizes[:4]) // 128
    total_w_qkv, total_w_out, _, norms = assemble_call(
        place, core_gather(pair, last), [query_key_value_weight.shape, output_weight.shape], depth,
        small, (turned, turned + sizes[4] // 128),
    )
    small = small[:-8].reshape(-1)
    out, at = [], 0
    for size in sizes:
        out.append(small[at : at + size])
        at += size
    t_gain1, t_shift1, t_b_qkv, t_b_out, t_freqs, t_gain2, t_shift2, t_b_down, t_up = out
    t_freqs = t_freqs.reshape(rope_freqs.shape)
    rot_sq, other_sq = norms[0, 0], norms[1, 0]
    t_b_up = lax.dynamic_slice_in_dim(t_up, z * b_up.shape[0], b_up.shape[0], 0)
    return (
        activations[None],
        input_grad[None],
        t_gain1,
        t_shift1,
        total_w_qkv,
        t_b_qkv,
        total_w_out,
        t_b_out,
        t_freqs,
        t_gain2,
        t_shift2,
        total_w_up,
        t_b_up,
        total_w_down,
        t_b_down,
        rot_sq,
        other_sq,
    )


def solution(mesh):
    wide, depth = mesh.shape["wide"], mesh.shape["narrow"]
    extra = wide // 8
    fine = Mesh(mesh.devices.reshape(extra, 2, 2, 2, depth), ("e", "a", "b", "c", "n"))
    w, n = ("e", "a", "b", "c"), "n"
    return jax.shard_map(
        functools.partial(on_device, extra=extra, depth=depth),
        mesh=fine,
        in_specs=(
            P(w, n, None), P(w, None), P(w, None), P(None, w, None),
            P(), P(), P(), P(), P(), P(), P(), P(), P(),
            P(None, n), P(n), P(n, None), P(), P(w, n, None),
        ),
        out_specs=(
            P(w, n, None), P(w, n, None),
            P(), P(), P(), P(), P(), P(), P(), P(), P(),
            P(None, n), P(n), P(n, None), P(), P(), P(),
        ),
        check_vma=False,
    )
```

```python
import functools

import jax
import jax.numpy as jnp
import numpy as np
from jax import lax
from jax.experimental import pallas as pl
from jax.experimental.pallas import tpu as pltpu
from jax.sharding import Mesh, PartitionSpec as P

EPS = 1e-06
MASKED = -1e30
BLK = 128
SPAN = 6
SPAN_SIDE = 3
SPAN_BACK = 2
GROUP = 4
REACH = 64
STAT_ROWS = 6
STAT_PAD = 16
SIDE = 32
LN1_GAIN, LN1_SHIFT, B_OUT, LN2_GAIN, LN2_SHIFT, B_DOWN = (slice(n, n + 1) for n in range(6))
LOG2E = np.float32(1.4426950408889634)
BF = jnp.bfloat16
F32 = jnp.float32
PLANE = ("a", "b", "c")
SWAP = [(0, 1), (1, 0)]
FIRST = [(i, i ^ (4 if i % 2 else 2)) for i in range(8)]
SECOND = [(i, i ^ (2 if i % 2 else 4)) for i in range(8)]


def dot(left, right):
    return lax.dot_general(left, right, (((1,), (0,)), ((), ())), preferred_element_type=F32)


def dot_nt(left, right):
    return lax.dot_general(left, right, (((1,), (1,)), ((), ())), preferred_element_type=F32)


def dot_tn(left, right):
    return lax.dot_general(left, right, (((0,), (0,)), ((), ())), preferred_element_type=F32)


def params(mebibytes):
    return pltpu.CompilerParams(vmem_limit_bytes=mebibytes * 1024 * 1024)


def cost(us):
    return pl.CostEstimate(
        flops=int(us * 1.15e9), bytes_accessed=int(us * 3.0e6), transcendentals=0
    )


def whole(shape):
    return pl.BlockSpec(shape, lambda *_: (0,) * len(shape))


ANY = pl.BlockSpec(memory_space=pl.ANY)
SMEM = pl.BlockSpec(memory_space=pltpu.SMEM)


def rounded(x):
    return lax.reduce_precision(x, exponent_bits=8, mantissa_bits=7)


def turn_table(rope_freqs):
    lanes = rope_freqs.shape[1] * rope_freqs.shape[2]
    freq = rope_freqs.reshape(2, 1, lanes)
    angle = jnp.arange(SIDE, dtype=F32)[None, :, None] * freq
    cosine, sine = jnp.cos(angle), jnp.sin(angle)

    def halves(x):
        return jnp.concatenate([x.astype(BF), (x - rounded(x)).astype(BF)], 0)

    def grouped(x):
        return x.reshape(2 * SIDE, lanes // 128, 1, 128)

    zero = jnp.zeros((2 * SIDE, lanes // 128, 2, 128), BF)
    rows = jnp.concatenate([grouped(halves(cosine[0])), grouped(halves(sine[0])), zero], 2)
    cols = jnp.concatenate([zero, grouped(halves(cosine[1])), grouped(halves(sine[1]))], 2)
    return jnp.concatenate([rows, cols], 0).reshape(4 * SIDE, 4 * lanes)


def cos_sin(onehot, table):
    parts = dot(onehot, table)
    cr, sr, cc, sc = (parts[:, lanes_of(n, 128)] for n in range(4))
    return cr * cc - sr * sc, sr * cc + cr * sc


def layer_norm_low(x, gain, shift):
    centred = x - jnp.mean(x, -1, keepdims=True)
    var = jnp.mean(centred * centred, -1, keepdims=True)
    return (centred * lax.rsqrt(var + EPS) * gain + shift).astype(BF)


def project(norm, hot_ref, table_ref, weights, b_ref, outs, exact=()):
    width = norm.shape[1]
    for g in range(width // 256):
        c, s = cos_sin(hot_ref[...], table_ref[:, lanes_of(g, 512)])
        for n, out in outs:
            lo = n * width + 256 * g
            proj = dot(norm, weights[:, lo : lo + 256]) + b_ref[:, lo : lo + 256]
            if n == 2:
                out[:, lanes_of(g)] = proj.astype(BF)
                continue
            for half, turned in enumerate(
                (proj[:, :128] * c - proj[:, 128:] * s, proj[:, :128] * s + proj[:, 128:] * c)
            ):
                at = slice(256 * g + 128 * half, 256 * g + 128 * half + 128)
                out[:, at] = turned.astype(BF)
                if exact:
                    exact[n][:, at] = turned


def qkv_own_kernel(
    x_ref, hot_ref, vec_ref, w_ref, b_ref, order_ref, table_ref,
    q_ref, k_ref, v_ref, pq_ref, pk_ref, w_turned,
):
    width = x_ref.shape[1]

    @pl.when(pl.program_id(0) == 0)
    def _():
        for g in range(2 * width // 256):
            at = slice(256 * g, 256 * g + 256)
            w_turned[:, at] = dot(w_ref[:, at], order_ref[...]).astype(BF)
        w_turned[:, 2 * width :] = w_ref[:, 2 * width :]

    norm = layer_norm_low(x_ref[...].astype(F32), vec_ref[LN1_GAIN], vec_ref[LN1_SHIFT])
    outs = [(0, q_ref), (1, k_ref), (2, v_ref)]
    project(norm, hot_ref, table_ref, w_turned, b_ref, outs, (pq_ref, pk_ref))


def qkv_own_call(x, onehot, vectors, weight, bias, order, table, first):
    own, width = x.shape
    rows = onehot.shape[0]
    tile = 256
    shape = jax.ShapeDtypeStruct((rows, width), BF)
    exact = jax.ShapeDtypeStruct((own, width), F32)
    row = lambda w: pl.BlockSpec((tile, w), lambda i: (i, 0))
    inside = lambda w: pl.BlockSpec(
        (pl.Element(tile), pl.Element(w)), lambda i: (pl.multiple_of(first + tile * i, BLK), 0)
    )
    return pl.pallas_call(
        qkv_own_kernel,
        grid=(own // tile,),
        in_specs=[
            row(width),
            inside(onehot.shape[1]),
            whole(vectors.shape),
            whole(weight.shape),
            whole((1, 3 * width)),
            whole(order.shape),
            whole(table.shape),
        ],
        out_specs=[inside(width)] * 3 + [row(width)] * 2 + [whole(weight.shape)],
        out_shape=[shape] * 3 + [exact] * 2 + [jax.ShapeDtypeStruct(weight.shape, BF)],
        compiler_params=params(56),
        cost_estimate=cost(8),
        name="qkv_own",
    )(x, onehot, vectors, weight, bias[None], order, table)


def halo_kernel(
    far_l, near_l, near_r, far_r, hot_ref, vec_ref, w_ref, b_ref, table_ref, *refs, which
):
    refs = refs[len(which) :]
    out_refs, (x_all, sem) = refs[: len(which)], refs[len(which) :]
    width = x_all.shape[1]
    step = pl.program_id(0)
    tile = out_refs[0].shape[0]

    @pl.when(step == 0)
    def _():
        own, reach = near_l.shape[0], far_l.shape[0]
        total = x_all.shape[0]
        blank = total // 2 - own - reach
        copies = []
        at = blank
        for n, ref in enumerate((far_l, near_l, near_r, far_r)):
            copies.append(
                pltpu.make_async_copy(ref, x_all.at[at : at + ref.shape[0], :], sem.at[n])
            )
            copies[-1].start()
            at += ref.shape[0]
        x_all[:blank, :] = jnp.zeros((blank, width), BF)
        x_all[total - blank :, :] = jnp.zeros((blank, width), BF)
        for copy in copies:
            copy.wait()

    x = x_all[pl.ds(pl.multiple_of(step * tile, tile), tile), :].astype(F32)
    norm = layer_norm_low(x, vec_ref[LN1_GAIN], vec_ref[LN1_SHIFT])
    project(norm, hot_ref, table_ref, w_ref, b_ref, list(zip(which, out_refs)))


def halo_call(pieces, onehot, vectors, weight, bias, table, arrays, which, first):
    rows, width = arrays[0].shape
    own = pieces[1].shape[0]
    tile = first // 2
    at = lambda w: pl.BlockSpec(
        (pl.Element(tile), pl.Element(w)),
        lambda i: (pl.multiple_of(tile * i + jnp.where(i >= 2, own, 0), 64), 0),
    )
    return pl.pallas_call(
        functools.partial(halo_kernel, which=which),
        grid=(4,),
        in_specs=[ANY] * 4
        + [
            at(onehot.shape[1]),
            whole(vectors.shape),
            whole(weight.shape),
            whole((1, 3 * width)),
            whole(table.shape),
        ]
        + [ANY] * len(which),
        out_specs=[at(width)] * len(which),
        out_shape=[jax.ShapeDtypeStruct((rows, width), BF)] * len(which),
        input_output_aliases={9 + n: n for n in range(len(which))},
        scratch_shapes=[pltpu.VMEM((2 * first, width), BF), pltpu.SemaphoreType.DMA((4,))],
        compiler_params=params(56),
        cost_estimate=cost(4 * len(which)),
        name="halo",
    )(*pieces, onehot, vectors, weight, bias[None], table, *arrays)


def head_stack(block, turned, scale=None):
    lane = lax.broadcasted_iota(jnp.int32, block.shape, 1)
    head = (lane % 128) // 32 if turned else lane // 64
    if scale is not None:
        block = block * scale
    zero = jnp.zeros_like(block)
    return jnp.concatenate([jnp.where(head == h, block, zero) for h in range(GROUP)], 0)


def fold8(x, op):
    return op(x.reshape(x.shape[0] // 8, 8, x.shape[1]), axis=0)


def key_span(ident_ref, ident_q, start, c, span, end):
    block = jnp.minimum(start + c * span, end - span)
    lower = (start + c * span - block) * BLK
    at = pl.ds(pl.multiple_of(block * BLK, BLK), span * BLK)
    row = lax.broadcasted_iota(jnp.int32, (span * BLK, BLK), 0)
    return at, (ident_ref[at, :] == ident_q) & (row >= lower)


def lanes_of(g, size=256):
    return slice(size * g, size * g + size)


def forward_kernel(
    bound_ref, q_ref, k_ref, v_ref, idk_ref, idq_ref, *refs, first, base
):
    o_ref, low_ref, lse_ref, s_ref, acc_ref, q4_ref = refs[-6:]
    i = pl.program_id(0) + base
    groups = k_ref.shape[1] // 256
    lanes = GROUP * BLK
    window = k_ref.shape[0] // BLK
    start, count = bound_ref[i, 0], bound_ref[i, 1]
    for g in range(groups):
        q4_ref[g] = head_stack(q_ref[:, lanes_of(g)], True, jnp.asarray(0.125, BF))
    ident_q = idq_ref[pl.ds(first // BLK + i, 1), :]

    def scores(c, top):
        at, seen = key_span(idk_ref, ident_q, start, c, SPAN, window)
        here = pl.ds(pl.multiple_of(c * SPAN * BLK, BLK), SPAN * BLK)
        tops = []
        for g in range(groups):
            s = dot_nt(k_ref[at, lanes_of(g)], q4_ref[g]) * LOG2E
            for h in range(GROUP):
                masked = jnp.where(seen, s[:, lanes_of(h, BLK)], MASKED)
                s_ref[g, here, lanes_of(h, BLK)] = masked
                tops.append(fold8(masked, jnp.max))
        return jnp.maximum(top, jnp.concatenate(tops, 1))

    top = lax.fori_loop(0, count, scores, jnp.full((8, groups * lanes), -3e38, F32))
    top = jnp.max(top, 0, keepdims=True)
    acc_ref[...] = jnp.zeros_like(acc_ref)

    def mix(c, total):
        at, _ = key_span(idk_ref, ident_q, start, c, SPAN, window)
        here = pl.ds(pl.multiple_of(c * SPAN * BLK, BLK), SPAN * BLK)
        sums = []
        for g in range(groups):
            e = jnp.exp2(s_ref[g, here, :] - top[:, lanes_of(g, lanes)])
            sums.append(fold8(e, jnp.sum))
            acc_ref[g] += dot_tn(v_ref[at, lanes_of(g)], e.astype(BF))
        return total + jnp.concatenate(sums, 1)

    total = lax.fori_loop(0, count, mix, jnp.zeros((8, groups * lanes), F32))
    total = jnp.sum(total, 0, keepdims=True)
    lse = top + jnp.log(total) * LOG2E
    inverse = 1.0 / total
    for g in range(groups):
        lse_ref[g] = lse[:, lanes_of(g, lanes)]
        acc = acc_ref[g] * inverse[:, lanes_of(g, lanes)]
        out = jnp.concatenate(
            [acc[64 * h : 64 * h + 64, lanes_of(h, BLK)] for h in range(GROUP)], 0
        ).T
        o_ref[:, lanes_of(g)] = out
        low_ref[:, lanes_of(g)] = out.astype(BF)


def stat_spec(groups, base=0):
    return pl.BlockSpec((groups, None, 1, GROUP * BLK), lambda i: (0, i + base, 0, 0))


def query_rows(first, width):
    return pl.BlockSpec(
        (pl.Element(BLK), pl.Element(width)), lambda i: (pl.multiple_of(first + BLK * i, BLK), 0)
    )


def forward_call(bounds, q_win, k_win, v_win, idk, idq, first, own, base, count, earlier=()):
    win, width = k_win.shape
    groups, blocks = width // 256, own // BLK
    row = pl.BlockSpec((BLK, width), lambda i: (i + base, 0))
    steps = -(-win // (SPAN * BLK))
    return pl.pallas_call(
        functools.partial(forward_kernel, first=first, base=base),
        grid=(count,),
        in_specs=[SMEM, query_rows(first + base * BLK, width)]
        + [whole((win, width))] * 2
        + [whole(idk.shape), whole(idq.shape)]
        + [ANY] * len(earlier),
        out_specs=[row, row, stat_spec(groups, base)],
        input_output_aliases={6 + n: n for n in range(len(earlier))},
        out_shape=[
            jax.ShapeDtypeStruct((own, width), F32),
            jax.ShapeDtypeStruct((own, width), BF),
            jax.ShapeDtypeStruct((groups, blocks, 1, GROUP * BLK), F32),
        ],
        scratch_shapes=[
            pltpu.VMEM((groups, steps * SPAN * BLK, GROUP * BLK), F32),
            pltpu.VMEM((groups, 256, GROUP * BLK), F32),
            pltpu.VMEM((groups, GROUP * BLK, 256), BF),
        ],
        compiler_params=params(56),
        cost_estimate=cost(4 * count),
        name="attention_forward",
    )(bounds, q_win, k_win, v_win, idk, idq, *earlier)


def score_gradients(s, dp, lse, delta, seen):
    low_p, low_ds = [], []
    for h in range(GROUP):
        at = lanes_of(h, BLK)
        p = jnp.exp2(jnp.where(seen, s[:, at] * LOG2E - lse[:, at], MASKED))
        low_p.append(p.astype(BF))
        low_ds.append((p * (dp[:, at] - delta[:, at])).astype(BF))
    return jnp.concatenate(low_p, 1), jnp.concatenate(low_ds, 1)


def backward_own_kernel(
    bound_ref, q_ref, do_ref, k_ref, v_ref, idk_ref, idq_ref, lse_ref, delta_ref,
    dq_ref, dk_ref, dv_ref, acc_ref, q4_ref, do4_ref, *, first,
):
    i = pl.program_id(0)
    groups = k_ref.shape[1] // 256
    own = dk_ref.shape[0]

    @pl.when(i == 0)
    def _():
        dk_ref[...] = jnp.zeros_like(dk_ref)
        dv_ref[...] = jnp.zeros_like(dv_ref)

    for g in range(groups):
        q4_ref[g] = head_stack(q_ref[:, lanes_of(g)], True, jnp.asarray(0.125, BF))
        do4_ref[g] = head_stack(do_ref[:, lanes_of(g)], False)
    ident_q = idq_ref[pl.ds(first // BLK + i, 1), :]

    def attend(at, seen, inside):
        for g in range(groups):
            keys = k_ref[at, lanes_of(g)]
            s = dot_nt(keys, q4_ref[g])
            dp = dot_nt(v_ref[at, lanes_of(g)], do4_ref[g])
            low_p, low_ds = score_gradients(s, dp, lse_ref[g], delta_ref[g], seen)
            if inside:
                acc_ref[g] = dot_tn(keys, low_ds)
                dk_ref[:, lanes_of(g)] += dot(low_ds, q4_ref[g])
                dv_ref[:, lanes_of(g)] += dot(low_p, do4_ref[g])
            else:
                acc_ref[g] += dot_tn(keys, low_ds)

    attend(slice(first, first + own), idk_ref[first : first + own, :] == ident_q, True)
    for start, count, end in (
        (bound_ref[i, 2], bound_ref[i, 3], first // BLK),
        ((first + own) // BLK, bound_ref[i, 4], k_ref.shape[0] // BLK),
    ):

        def step(c, _):
            attend(*key_span(idk_ref, ident_q, start, c, SPAN_SIDE, end), False)
            return 0

        lax.fori_loop(0, count, step, 0)
    for g in range(groups):
        acc = acc_ref[g]
        parts = [acc[32 * h : 32 * h + 32, lanes_of(h, BLK)] for h in range(GROUP)]
        parts += [acc[128 + 32 * h : 160 + 32 * h, lanes_of(h, BLK)] for h in range(GROUP)]
        dq_ref[:, lanes_of(g)] = (jnp.concatenate(parts, 0) * 0.125).T


def backward_own_call(bounds, q_win, do_own, k_win, v_win, idk, idq, lse, delta, first, own):
    win, width = k_win.shape
    groups = width // 256
    row = pl.BlockSpec((BLK, width), lambda i: (i, 0))
    return pl.pallas_call(
        functools.partial(backward_own_kernel, first=first),
        grid=(own // BLK,),
        in_specs=[SMEM, query_rows(first, width), row]
        + [whole((win, width))] * 2
        + [whole(idk.shape), whole(idq.shape), stat_spec(groups), stat_spec(groups)],
        out_specs=[row] + [whole((own, width))] * 2,
        out_shape=[jax.ShapeDtypeStruct((own, width), F32)] * 3,
        scratch_shapes=[pltpu.VMEM((groups, 256, GROUP * BLK), F32)]
        + [pltpu.VMEM((groups, GROUP * BLK, 256), BF)] * 2,
        compiler_params=params(24),
        cost_estimate=cost(20),
        name="attention_backward_own",
    )(bounds, q_win, do_own, k_win, v_win, idk, idq, lse, delta)


def backward_halo_kernel(
    bound_ref, q_ref, far_l, near_l, near_r, far_r, k_ref, v_ref, idk_ref, idq_ref, dk_in, dv_in,
    dk_ref, dv_ref, q4_ref, do_all, do4_ref, stat_ref, *, first,
):
    groups = k_ref.shape[1] // 256
    own, reach = k_ref.shape[0], far_l.shape[0] - STAT_PAD
    blocks = own // BLK
    side = first // BLK
    step_id = pl.program_id(0)
    j = jnp.where(step_id < side, step_id, step_id + blocks)
    lanes = GROUP * BLK

    def stats(ref, row, slot):
        parts = ref[row : row + 2 * STAT_ROWS, :].astype(F32)
        sums = parts[0:4] + parts[4:8] + parts[8:12]
        for g in range(groups):
            for n in range(2):
                stat_ref[n, g, slot : slot + 1, :] = jnp.concatenate(
                    [sums[2 * n : 2 * n + 1, lanes_of(g)], sums[2 * n + 1 : 2 * n + 2, lanes_of(g)]],
                    1,
                )

    @pl.when(step_id == 0)
    def _():
        dk_ref[...] = dk_in[...]
        dv_ref[...] = dv_in[...]
        blank = jnp.zeros((BLK - reach, do_all.shape[1]), BF)
        do_all[0 : BLK - reach, :] = blank
        do_all[BLK - reach : BLK, :] = far_l[:reach, :]
        do_all[BLK : BLK + own, :] = near_l[:own, :]
        do_all[BLK + own : BLK + 2 * own, :] = near_r[:own, :]
        do_all[BLK + 2 * own : BLK + 2 * own + reach, :] = far_r[:reach, :]
        do_all[BLK + 2 * own + reach :, :] = blank
        stats(far_l, reach, 0)
        for i in range(blocks):
            stats(near_l, own + 2 * STAT_ROWS * i, 1 + i)
            stats(near_r, own + 2 * STAT_ROWS * i, 1 + blocks + i)
        stats(far_r, reach, 1 + 2 * blocks)

    start, count = bound_ref[j, 0], bound_ref[j, 1]

    @pl.when(count > 0)
    def _():
        here = pl.ds(pl.multiple_of(step_id * BLK, BLK), BLK)
        for g in range(groups):
            q4_ref[g] = head_stack(q_ref[:, lanes_of(g)], True, jnp.asarray(0.125, BF))
            do4_ref[g] = head_stack(do_all[here, lanes_of(g)], False)
        ident_q = idq_ref[pl.ds(j, 1), :]

        def step(c, _):
            at, seen = key_span(idk_ref, ident_q, start, c, SPAN_BACK, blocks)
            for g in range(groups):
                s = dot_nt(k_ref[at, lanes_of(g)], q4_ref[g])
                dp = dot_nt(v_ref[at, lanes_of(g)], do4_ref[g])
                lse = stat_ref[0, g, pl.ds(step_id, 1), :]
                delta = stat_ref[1, g, pl.ds(step_id, 1), :]
                low_p, low_ds = score_gradients(s, dp, lse, delta, seen)
                dk_ref[at, lanes_of(g)] += dot(low_ds, q4_ref[g])
                dv_ref[at, lanes_of(g)] += dot(low_p, do4_ref[g])
            return 0

        lax.fori_loop(0, count, step, 0)


def backward_halo_call(bounds, q_win, pieces, k_win, v_win, idk, idq, dk, dv, first):
    own, width = dk.shape
    groups = width // 256
    side, blocks = first // BLK, own // BLK
    inside = lambda w: pl.BlockSpec(
        (pl.Element(own), pl.Element(w)), lambda i: (pl.multiple_of(first + 0 * i, BLK), 0)
    )
    outside = pl.BlockSpec((BLK, width), lambda i: (jnp.where(i < side, i, i + blocks), 0))
    return pl.pallas_call(
        functools.partial(backward_halo_kernel, first=first),
        grid=(2 * side,),
        in_specs=[SMEM, outside]
        + [whole(p.shape) for p in pieces]
        + [inside(width)] * 2
        + [inside(idk.shape[1]), whole(idq.shape)]
        + [whole((own, width))] * 2,
        out_specs=[whole((own, width))] * 2,
        out_shape=[jax.ShapeDtypeStruct((own, width), F32)] * 2,
        scratch_shapes=[
            pltpu.VMEM((groups, GROUP * BLK, 256), BF),
            pltpu.VMEM((2 * first, width), BF),
            pltpu.VMEM((groups, GROUP * BLK, 256), BF),
            pltpu.VMEM((2, groups, 16, GROUP * BLK), F32),
        ],
        compiler_params=params(20),
        cost_estimate=cost(11),
        name="attention_backward_halo",
    )(bounds, q_win, *pieces, k_win, v_win, idk, idq, dk, dv)


def norm_parts(x):
    centred = x - jnp.mean(x, -1, keepdims=True)
    inverse = lax.rsqrt(jnp.mean(centred * centred, -1, keepdims=True) + EPS)
    return centred * inverse, inverse


def norm_back(grad, xhat, inverse, gain):
    scaled = grad * gain
    return inverse * (
        scaled
        - jnp.mean(scaled, -1, keepdims=True)
        - xhat * jnp.mean(scaled * xhat, -1, keepdims=True)
    )


def columns_sum(x):
    return jnp.sum(x, 0, keepdims=True)


def chip_order(ab, core):
    return jnp.where(core == 0, ab, ab % 2 * 2 + ab // 2)


def slices_out(place, source, keep, away, lead, sem, slices, rows):
    for n in range(slices):
        rel = place ^ n
        for target, odd in ((keep, 0), (away, 1)):
            core = place % 2 ^ odd

            @pl.when(rel % 2 == odd)
            def _():
                pltpu.make_async_copy(
                    source.at[n * rows : (n + 1) * rows, :],
                    target.at[chip_order(rel // 2, core), pl.ds(lead, rows), :],
                    sem.at[n],
                ).start()


def gathered(place, refs):
    for far in range(2):
        for n in range(4):
            rel = 2 * chip_order(jnp.int32(n), place % 2 ^ far) + far
            yield refs[4 * far + n], place ^ rel


def slices_wait(source, keep, sem, slices, rows):
    for n in range(slices):
        pltpu.make_async_copy(
            source.at[n * rows : (n + 1) * rows, :], keep.at[0, 0:rows, :], sem.at[n]
        ).wait()


def one_quarter(q, w_all, norm_ref, dy_ref, bu_ref, dbu_ref, out_acc, dn_acc, g_all, fresh):
    own, width = norm_ref.shape
    tile = w_all.shape[1] - width
    for t in range((w_all.shape[1] - width) // tile):
        cols = slice(tile * t, tile * t + tile)
        down = slice(width + tile * t, width + tile * t + tile)
        norm, dy = norm_ref[...], dy_ref[...]
        up_w = w_all[q, :width, cols]
        down_w = w_all[q, down, :]
        pre = dot(norm, up_w) + bu_ref[pl.ds(q, 1), cols]
        cdf = 0.5 * (1.0 + lax.erf(pre * np.float32(0.7071067811865476)))
        density = jnp.exp(-0.5 * pre * pre) * np.float32(0.3989422804014327)
        act = (pre * cdf).astype(BF)
        d_pre = (dot_nt(dy, down_w) * (cdf + pre * density)).astype(BF)
        dbu_ref[pl.ds(q, 1), cols] = columns_sum(d_pre.astype(F32))
        if fresh and t == 0:
            out_acc[...] = dot(act, down_w)
            dn_acc[...] = dot_nt(d_pre, up_w)
        else:
            out_acc[...] += dot(act, down_w)
            dn_acc[...] += dot_nt(d_pre, up_w)
        g_all[q, :width, cols] = dot_tn(norm, d_pre).astype(BF)
        g_all[q, down, :] = dot_tn(act, dy).astype(BF)


def middle_own_kernel(
    place_ref, x_ref, low_ref, wo_ref, vec_ref, dy_ref, bu_ref, up_ref, down_ref,
    hid_ref, norm_ref, out_ref, dn_ref, dbu_ref, keep_ref, send_ref, w_all, g_all, w_sem, g_sem,
    *, slices,
):
    width = x_ref.shape[1]
    rows = w_all.shape[1] // slices
    copies = [
        pltpu.make_async_copy(up_ref, w_all.at[0, :width, :], w_sem.at[0]),
        pltpu.make_async_copy(down_ref, w_all.at[0, width:, :], w_sem.at[1]),
    ]
    for copy in copies:
        copy.start()
    hidden_in = x_ref[...].astype(F32) + dot(low_ref[...], wo_ref[...]) + vec_ref[B_OUT]
    hid_ref[...] = hidden_in
    norm_ref[...] = layer_norm_low(hidden_in, vec_ref[LN2_GAIN], vec_ref[LN2_SHIFT])
    for copy in copies:
        copy.wait()
    one_quarter(0, w_all, norm_ref, dy_ref, bu_ref, dbu_ref, out_ref, dn_ref, g_all, True)
    slices_out(place_ref[0], g_all.at[0], keep_ref, send_ref, 0, g_sem, slices, rows)
    slices_wait(g_all.at[0], keep_ref, g_sem, slices, rows)


def middle_own_call(place, x, low, w_out, vectors, dy, b_up, w_up, w_down, slices):
    own, width = x.shape
    hidden = b_up.shape[1]
    rows = width + hidden
    vmem = pl.BlockSpec(memory_space=pltpu.VMEM)
    sds = jax.ShapeDtypeStruct
    return pl.pallas_call(
        functools.partial(middle_own_kernel, slices=slices),
        in_specs=[SMEM] + [vmem] * 6 + [ANY] * 2,
        out_specs=[vmem] * 5 + [ANY] * 2,
        out_shape=[
            sds((own, width), F32),
            sds((own, width), BF),
            sds((own, width), F32),
            sds((own, width), F32),
            sds((1, hidden), F32),
        ]
        + [sds((slices // 2, rows // slices, width), BF)] * 2,
        scratch_shapes=[
            pltpu.VMEM((1, rows, width), BF),
            pltpu.VMEM((1, rows, width), BF),
            pltpu.SemaphoreType.DMA((2,)),
            pltpu.SemaphoreType.DMA((slices,)),
        ],
        compiler_params=params(56),
        cost_estimate=cost(12),
        name="middle_own",
    )(place, x, low, w_out, vectors, dy, b_up, w_up, w_down)


def middle_kernel(
    place_ref, vec_ref, bu_ref, lse_ref, norm_in, dy_in, out_in, dn_in, hid_in, low_in, mixed_in,
    wo_in, *refs, slices,
):
    piece_refs = refs[:slices]
    (
        act_out, dh_out, dheads_ref, head_ref, tail_ref, delta_ref, small_ref, dbu_ref, keep_ref,
        send_ref,
        w_all, g_all, go_all, norm_ref, dy_ref, out_acc, dn_acc, hid_ref, low_ref, mixed_ref,
        wo_ref, act_ref, dh_ref, w_sem, g_sem, in_sem, out_sem,
    ) = refs[slices:]
    place = place_ref[0]
    own, width = norm_ref.shape
    quarters = w_all.shape[0]
    rows = w_all.shape[1] // slices

    def fetches(q):
        return [
            pltpu.make_async_copy(
                ref.at[q],
                w_all.at[q, pl.ds(pl.multiple_of(source * rows, rows), rows), :],
                w_sem.at[q, n],
            )
            for n, (ref, source) in enumerate(gathered(place, piece_refs))
        ]

    inputs = [
        pltpu.make_async_copy(source, target, in_sem.at[n])
        for n, (source, target) in enumerate(
            (
                (norm_in, norm_ref), (dy_in, dy_ref), (out_in, out_acc), (dn_in, dn_acc),
                (hid_in, hid_ref), (low_in, low_ref), (mixed_in, mixed_ref), (wo_in, wo_ref),
            )
        )
    ]
    for copy in inputs[:2] + fetches(0) + inputs[2:4]:
        copy.start()
    for q in range(1, quarters):
        for copy in fetches(q):
            copy.start()
    for copy in inputs[4:]:
        copy.start()
    for copy in inputs[:2]:
        copy.wait()

    def quarter(q, _):
        for copy in fetches(q):
            copy.wait()

        @pl.when(q == 0)
        def _():
            for copy in inputs[2:4]:
                copy.wait()

        one_quarter(q, w_all, norm_ref, dy_ref, bu_ref, dbu_ref, out_acc, dn_acc, g_all, False)
        slices_out(
            place, g_all.at[q], keep_ref, send_ref, pl.multiple_of(q * rows, rows),
            g_sem.at[q], slices, rows,
        )
        return 0

    lax.fori_loop(0, quarters, quarter, 0)

    for copy in inputs[4:]:
        copy.wait()
    hidden_in = hid_ref[...]
    xhat, inverse = norm_parts(hidden_in)
    dn = dn_acc[...]
    dy = dy_ref[...].astype(F32)
    d_hidden = dy + norm_back(dn, xhat, inverse, vec_ref[LN2_GAIN])
    dh_ref[...] = d_hidden
    d_att = d_hidden.astype(BF)
    d_heads = dot_nt(d_att, wo_ref[...]).astype(BF)
    dheads_ref[:own, :] = d_heads
    go_all[...] = dot_tn(low_ref[...], d_att).astype(BF)
    few = width // slices
    base = quarters * rows
    slices_out(place, go_all, keep_ref, send_ref, base, g_sem.at[quarters], slices, few)
    act_ref[...] = (hidden_in + out_acc[...] + vec_ref[B_DOWN]).astype(BF)
    outputs = [
        pltpu.make_async_copy(source, target, out_sem.at[n])
        for n, (source, target) in enumerate(
            (
                (act_ref, act_out), (dh_ref, dh_out),
            )
        )
    ]
    for copy in outputs:
        copy.start()
    small_ref[0:1, :] = columns_sum(dn * xhat)
    small_ref[1:2, :] = columns_sum(dn)
    small_ref[2:3, :] = columns_sum(dy)
    small_ref[3:4, :] = columns_sum(d_att.astype(F32))
    spread = d_heads.astype(F32) * mixed_ref[...]
    pick = lax.broadcasted_iota(jnp.int32, (8, 256), 0)
    pick = (pick == lax.broadcasted_iota(jnp.int32, (8, 256), 1) // 64).astype(F32)
    for g in range(width // 256):
        for i in range(own // BLK):
            block = spread[BLK * i : BLK * i + BLK, 256 * g : 256 * g + 256]
            sums = lax.dot_general(
                pick, block, (((1,), (1,)), ((), ())),
                preferred_element_type=F32, precision=lax.Precision.HIGHEST,
            )
            delta = jnp.concatenate([sums[h : h + 1, :] for h in range(GROUP)], 1)
            delta_ref[g, i] = delta
            lse = lse_ref[g, i]
            left = jnp.concatenate(
                [lse[:, :256], lse[:, 256:], delta[:, :256], delta[:, 256:]], 0
            )
            parts = []
            for _ in range(3):
                parts.append(left.astype(BF))
                left = left - parts[-1].astype(F32)
            parts = jnp.concatenate(parts, 0)
            at = slice(256 * g, 256 * g + 256)
            lo = own + 2 * STAT_ROWS * i
            dheads_ref[lo : lo + 2 * STAT_ROWS, at] = parts
            for target, row in ((head_ref, 0), (tail_ref, own // BLK - 1)):
                if i == row:
                    target[REACH : REACH + 2 * STAT_ROWS, at] = parts
    blank = jnp.zeros((STAT_PAD - 2 * STAT_ROWS, width), BF)
    head_ref[REACH + 2 * STAT_ROWS :, :] = blank
    tail_ref[REACH + 2 * STAT_ROWS :, :] = blank
    head_ref[:REACH, :] = d_heads[:REACH, :]
    tail_ref[:REACH, :] = d_heads[own - REACH :, :]
    for q in range(quarters):
        slices_wait(g_all.at[q], keep_ref, g_sem.at[q], slices, rows)
    slices_wait(go_all, keep_ref, g_sem.at[quarters], slices, few)
    for copy in outputs:
        copy.wait()


def middle_call(
    place, hidden_in, norm, out, dn, low, mixed, w_out, vectors, dy, b_up, lse, pieces, slices,
):
    own, width = norm.shape
    quarters, hidden = b_up.shape
    rows = width + hidden
    vmem = pl.BlockSpec(memory_space=pltpu.VMEM)
    sds = jax.ShapeDtypeStruct
    grads = sds((slices // 2, (quarters * rows + width) // slices, width), BF)
    return pl.pallas_call(
        functools.partial(middle_kernel, slices=slices),
        in_specs=[SMEM] + [vmem] * 3 + [ANY] * (8 + len(pieces)),
        out_specs=[ANY] * 2 + [vmem] * 6 + [ANY] * 2,
        out_shape=[
            sds((own, width), BF),
            sds((own, width), F32),
            sds((own + own // BLK * 2 * STAT_ROWS, width), BF),
            sds((REACH + STAT_PAD, width), BF),
            sds((REACH + STAT_PAD, width), BF),
            sds((width // 256, own // BLK, 1, GROUP * BLK), F32),
            sds((4, width), F32),
            sds((quarters, hidden), F32),
            grads,
            grads,
        ],
        scratch_shapes=[
            pltpu.VMEM((quarters, rows, width), BF),
            pltpu.VMEM((quarters, rows, width), BF),
            pltpu.VMEM((width, width), BF),
            pltpu.VMEM((own, width), BF),
            pltpu.VMEM((own, width), BF),
            pltpu.VMEM((own, width), F32),
            pltpu.VMEM((own, width), F32),
            pltpu.VMEM((own, width), F32),
            pltpu.VMEM((own, width), BF),
            pltpu.VMEM((own, width), F32),
            pltpu.VMEM((width, width), BF),
            pltpu.VMEM((own, width), BF),
            pltpu.VMEM((own, width), F32),
            pltpu.SemaphoreType.DMA((quarters, slices)),
            pltpu.SemaphoreType.DMA((quarters + 1, slices)),
            pltpu.SemaphoreType.DMA((10,)),
            pltpu.SemaphoreType.DMA((4,)),
        ],
        compiler_params=params(44),
        cost_estimate=cost(20),
        name="middle",
    )(
        place, vectors, b_up, lse, norm, dy, out, dn, hidden_in, low, mixed, w_out, *pieces,
    )


def turn_back_kernel(
    place_ref, x_ref, vec_ref, dq_ref, dk_ref, dv_ref, q_ref, k_ref, hot_ref, table_ref, grid_ref,
    back_ref, d_ref, db_ref, freq_ref, keep_ref, send_ref, norm_ref, g_all, sem, *, slices,
):
    width = x_ref.shape[1]
    group = pl.program_id(0)

    @pl.when(group == 0)
    def _():
        norm_ref[...] = layer_norm_low(
            x_ref[...].astype(F32), vec_ref[LN1_GAIN], vec_ref[LN1_SHIFT]
        )

    c, s = cos_sin(hot_ref[...], table_ref[...])
    norm = norm_ref[...]

    def gradient(n, low):
        d_ref[n] = low
        db_ref[n : n + 1, :] = columns_sum(low.astype(F32))
        at = pl.ds(pl.multiple_of(n * width + group * 256, 256), 256)
        g_all[:, at] = dot_tn(norm, low).astype(BF)

    d_angle = 0.0
    for n, (grad, turned_ref) in enumerate(((dq_ref, q_ref), (dk_ref, k_ref))):
        g1, g2 = grad[:, :128], grad[:, 128:]
        d_angle = d_angle + (g2 * turned_ref[:, :128] - g1 * turned_ref[:, 128:])
        back = jnp.concatenate([g1 * c + g2 * s, g2 * c - g1 * s], 1).astype(BF)
        gradient(n, dot(back, back_ref[...]).astype(BF))
    freq_ref[...] = lax.dot_general(
        grid_ref[...], d_angle, (((1,), (0,)), ((), ())),
        preferred_element_type=F32, precision=lax.Precision.HIGHEST,
    )
    gradient(2, dv_ref[...].astype(BF))

    @pl.when(group == width // 256 - 1)
    def _():
        slices_out(place_ref[0], g_all, keep_ref, send_ref, 0, sem, slices, width // slices)
        slices_wait(g_all, keep_ref, sem, slices, width // slices)


def turn_back_call(
    place, x, vectors, dq, dk, dv, q_exact, k_exact, onehot, table, grid8, back, first, slices
):
    rows, width = dk.shape
    sds = jax.ShapeDtypeStruct
    part = pl.BlockSpec((rows, 256), lambda g: (0, g))
    hot = pl.BlockSpec(
        (pl.Element(rows), pl.Element(onehot.shape[1])),
        lambda g: (pl.multiple_of(first + 0 * g, BLK), 0),
    )
    return pl.pallas_call(
        functools.partial(turn_back_kernel, slices=slices),
        grid=(width // 256,),
        in_specs=[SMEM, whole(x.shape), whole(vectors.shape)]
        + [part] * 5
        + [
            hot,
            pl.BlockSpec((table.shape[0], 512), lambda g: (0, g)),
            whole(grid8.shape),
            whole(back.shape),
        ],
        out_specs=[
            pl.BlockSpec((3, rows, 256), lambda g: (0, 0, g)),
            pl.BlockSpec((3, 256), lambda g: (0, g)),
            pl.BlockSpec((8, 128), lambda g: (0, g)),
        ]
        + [ANY] * 2,
        out_shape=[
            sds((3, rows, width), BF),
            sds((3, width), F32),
            sds((8, width // 2), F32),
        ]
        + [sds((slices // 2, width // slices, 3 * width), BF)] * 2,
        scratch_shapes=[
            pltpu.VMEM((rows, width), BF),
            pltpu.VMEM((width, 3 * width), BF),
            pltpu.SemaphoreType.DMA((slices,)),
        ],
        compiler_params=params(16),
        cost_estimate=cost(9),
        name="turn_back",
    )(place, x, vectors, dq, dk, dv, q_exact, k_exact, onehot, table, grid8, back)


def input_grad_kernel(
    place_ref, x_ref, vec_ref, d_ref, w_ref, dh_ref, db_ref, mid_ref, freq_ref, up0_ref, up_ref,
    out_ref, small_ref,
):
    width = x_ref.shape[1]
    d_norm = sum(dot_nt(d_ref[n], w_ref[:, lanes_of(n, width)]) for n in range(3))
    xhat, inverse = norm_parts(x_ref[...].astype(F32))
    out_ref[...] = dh_ref[...] + norm_back(d_norm, xhat, inverse, vec_ref[LN1_GAIN])
    row = 0
    for vector in (
        columns_sum(d_norm * xhat), columns_sum(d_norm), *(db_ref[n : n + 1, :] for n in range(3)),
        mid_ref[3:4, :], freq_ref[0:1, :], freq_ref[1:2, :], *(mid_ref[n : n + 1, :] for n in range(3)),
    ):
        for n in range(vector.shape[1] // 128):
            small_ref[row : row + 1, :] = vector[:, lanes_of(n, 128)]
            row += 1
    depth = 1 + up_ref.shape[0]
    hidden = up0_ref.shape[1] // 128
    for k in range(depth):
        quarter = (place_ref[1] - k + depth) % depth
        vector = up_ref[k - 1 : k, :] if k else up0_ref[...]
        for n in range(hidden):
            small_ref[pl.ds(row + quarter * hidden + n, 1), :] = vector[:, lanes_of(n, 128)]


def input_grad_call(place, x, vectors, d_qkv, weight, d_hidden, db_qkv, small_mid, freqs, up0, up):
    rows, width = x.shape
    short = 9 * width + freqs.shape[1] * 2 + up0.size * (1 + up.shape[0])
    return pl.pallas_call(
        input_grad_kernel,
        in_specs=[SMEM] + [pl.BlockSpec(memory_space=pltpu.VMEM)] * 10,
        out_shape=[
            jax.ShapeDtypeStruct((rows, width), F32),
            jax.ShapeDtypeStruct((short // 128, 128), F32),
        ],
        compiler_params=params(20),
        cost_estimate=cost(7),
        name="input_grad",
    )(place, x, vectors, d_qkv, weight, d_hidden, db_qkv, small_mid, freqs, up0, up)


def assemble_kernel(place_ref, *refs, split, outs, skip):
    out_refs, (held, sem) = refs[-2 - outs : -2], refs[-2:]
    pairs = refs[:4]
    piece_refs = [pairs[n // 2].at[n % 2] for n in range(8)]
    place, depth = place_ref[0], place_ref[1]
    slot = pl.program_id(0)

    def copy(ref, target):
        return pltpu.make_async_copy(ref, held.at[target], sem.at[target])

    @pl.when(slot == 0)
    def _():
        for ref, source in gathered(place, piece_refs):
            copy(ref, source).start()

    copy(piece_refs[0], slot).wait()
    rows = held.shape[-2]
    total_ref = None
    if skip is not None:
        out_refs, total_ref = out_refs[:-1], out_refs[-1]
    out_refs, squares = out_refs[:-1], out_refs[-1]

    @pl.when(slot == 0)
    def _():
        squares[...] = jnp.zeros_like(squares)

    def add_squares(block):
        total = fold8(block * block, jnp.sum)
        squares[...] += sum(total[:, lanes_of(n, 128)] for n in range(block.shape[1] // 128))

    if split:
        for n in range(split):
            block = held[slot, (depth - n + split) % split].astype(F32)
            add_squares(block)
            lo = 0
            for ref in out_refs:
                ref[n * rows : n * rows + rows, :] = block[:, lo : lo + ref.shape[1]]
                lo += ref.shape[1]
    else:
        block = held[slot].astype(F32)
        add_squares(block)
        each = held.shape[0] // len(out_refs)
        for n, ref in enumerate(out_refs):

            @pl.when(slot // each == n)
            def _():
                ref[...] = block
    if skip is not None:
        small_ref = refs[4]

        @pl.when(slot == held.shape[0] - 1)
        def _():
            short = small_ref[...]
            row = lax.broadcasted_iota(jnp.int32, short.shape, 0)
            mine = (row >= skip[0]) & (row < skip[1])
            parts = row >= short.shape[0] - 8
            others = jnp.where(mine, 0.0, jnp.where(parts, short, short * short))
            turned = jnp.where(mine, short * short, 0.0)
            total_ref[0:1, :] = jnp.full((1, 128), jnp.sum(turned))
            total_ref[1:2, :] = jnp.full((1, 128), jnp.sum(others) + jnp.sum(squares[...]))


def assemble_call(place, arrays, shapes, split, small=None, skip=None):
    pieces = 8
    rows = arrays[0].shape[-2] * max(split, 1)
    each = pieces if split else pieces // len(shapes)

    def spec(n, shape):
        lead = 0 if split else n * each
        return pl.BlockSpec((rows, shape[1]), lambda i: (jnp.clip(i - lead, 0, each - 1), 0))

    specs = [spec(n, shape) for n, shape in enumerate(shapes)] + [whole((8, 128))]
    shapes = shapes + [(8, 128)]
    given = []
    if small is not None:
        given, specs, shapes = [small], specs + [whole((2, 128))], shapes + [(2, 128)]
    return pl.pallas_call(
        functools.partial(assemble_kernel, split=split, outs=len(shapes), skip=skip),
        grid=(pieces,),
        in_specs=[SMEM] + [ANY] * len(arrays) + [whole(x.shape) for x in given],
        out_specs=specs,
        out_shape=[jax.ShapeDtypeStruct(s, F32) for s in shapes],
        scratch_shapes=[
            pltpu.VMEM((pieces,) + arrays[0].shape[1:], BF),
            pltpu.SemaphoreType.DMA((pieces,)),
        ],
        compiler_params=params(16),
        cost_estimate=cost(6),
        name="assemble",
    )(place, *arrays, *given)


def send(x, axis, pairs):
    return lax.ppermute(x, axis, pairs)


def plane_gather(piece):
    pair = jnp.stack([piece, send(piece, PLANE, FIRST)])
    return pair, send(pair, PLANE, SECOND)


def core_gather(pair, last):
    return [pair, last, send(pair, "c", SWAP), send(last, "c", SWAP)]


def wide_sum(x, extra):
    return lax.psum(x, "e") if extra > 1 else x


def sum_low(*terms):
    return functools.reduce(lambda x, y: x + y, [t.astype(F32) for t in terms])


def after(x, *others):
    return lax.optimization_barrier((x, others))[0]


def ring(size, step):
    return [(i, (i + step) % size) for i in range(size)]


def add_from(vector, axis, reach=0, size=2):
    return vector + send(vector, axis, [(i, i ^ (reach or 1)) for i in range(size)])


def on_device(
    tokens,
    segment,
    padding,
    coords,
    ln1_gain,
    ln1_shift,
    query_key_value_weight,
    b_qkv,
    output_weight,
    b_out,
    rope_freqs,
    ln2_gain,
    ln2_shift,
    w_up,
    b_up,
    w_down,
    b_down,
    cotangent,
    *,
    extra,
    depth,
):
    tokens, cotangent = tokens[0], cotangent[0]
    own, width = tokens.shape
    length = own * depth
    heads = rope_freqs.shape[1]
    half = width // heads // 2
    groups = heads // GROUP
    slices = 8
    outer = BLK
    side = own + outer
    win = own + 2 * side
    blocks = own // BLK
    z = lax.axis_index("n")
    plane = lax.axis_index("a") * 4 + lax.axis_index("b") * 2 + lax.axis_index("c")
    place = jnp.stack([plane, z]).astype(jnp.int32)
    up = [(i, i + 1) for i in range(depth - 1)]
    down = [(i + 1, i) for i in range(depth - 1)]
    up2 = [(i, i + 2) for i in range(depth - 2)]
    down2 = [(i + 2, i) for i in range(depth - 2)]

    def around(x, head, tail):
        before2 = send(tail, "n", up2)
        before = send(x, "n", up)
        after_ = send(x, "n", down)
        after2 = send(head, "n", down2)
        return [before2, before, after_, after2]

    position = jnp.arange(length, dtype=jnp.int32)
    ident = jnp.where(padding[0] == 0, segment[0], 1000 + position)
    ident = jnp.concatenate(
        [jnp.full((side,), -1, jnp.int32), ident, jnp.full((side,), 1 << 20, jnp.int32)]
    )
    ident_win = lax.dynamic_slice_in_dim(ident, z * own, win, 0)
    near = lax.broadcasted_iota(jnp.int32, (win,), 0)
    ident_win = jnp.where(near < outer - REACH, -1, ident_win)
    ident_win = jnp.where(near >= win - outer + REACH, 1 << 20, ident_win)
    idk = jnp.broadcast_to(ident_win[:, None], (win, BLK))
    idq = ident_win.reshape(win // BLK, BLK)

    lowest, highest = idq[:, 0], idq[:, BLK - 1]

    def bounds(queries, keys):
        before = highest[keys][None, :] < lowest[queries][:, None]
        reached = lowest[keys][None, :] <= highest[queries][:, None]
        return jnp.sum(before, 1), jnp.sum(reached, 1)

    def steps(blocks, span):
        return (jnp.maximum(blocks, 0) + span - 1) // span

    mid = slice(side // BLK, side // BLK + blocks)
    lo, hi = bounds(mid, slice(None))
    bounds_fwd = [
        lo, steps(hi - lo, SPAN), jnp.minimum(lo, mid.start), steps(mid.start - lo, SPAN_SIDE),
        steps(hi - mid.stop, SPAN_SIDE),
    ]
    bounds_fwd = jnp.stack(bounds_fwd, 1).astype(jnp.int32)
    lo, hi = bounds(slice(None), mid)
    bounds_bwd = jnp.stack([lo, steps(hi - lo, SPAN_BACK)], 1).astype(jnp.int32)

    grid = jnp.pad(coords[:, 0], ((0, 0), (side, side)))
    grid_win = lax.dynamic_slice_in_dim(grid, z * own, win, 1)
    grid_own = lax.dynamic_slice_in_dim(grid, z * own + side, own, 1)
    lane = jnp.arange(4 * SIDE)
    picked = jnp.where(lane[None, :] < 2 * SIDE, grid_win[0][:, None], grid_win[1][:, None])
    onehot = (picked == (lane % SIDE)[None, :]).astype(BF)
    table = turn_table(rope_freqs)

    local = np.arange(256)
    order = np.zeros((256, 256), np.float32)
    order[(local % 128) // 32 * 64 + local // 128 * 32 + local % 32, local] = 1.0
    order = jnp.asarray(order, BF)
    qk_bias = b_qkv[: 2 * width].reshape(2 * groups, GROUP, 2, half).swapaxes(1, 2)
    bias_turned = jnp.concatenate([qk_bias.reshape(-1), b_qkv[2 * width :]])

    x_parts = around(tokens, tokens[:REACH], tokens[own - REACH :])
    vectors = jnp.stack([ln1_gain, ln1_shift, b_out, ln2_gain, ln2_shift, b_down])
    rot_q, rot_k, values, q_exact, k_exact, weight_turned = qkv_own_call(
        tokens, onehot, vectors, query_key_value_weight, bias_turned, order, table, side
    )
    rows = (width + w_down.shape[0]) // slices
    eighth = jnp.where(
        plane < width // rows,
        lax.dynamic_slice_in_dim(w_up, jnp.minimum(plane * rows, width - rows), rows, 0),
        lax.dynamic_slice_in_dim(w_down, jnp.maximum(plane * rows - width, 0), rows, 0),
    )
    left, bias_rows = b_up, []
    for _ in range(3):
        bias_rows.append(left.astype(BF))
        left = left - rounded(left)
    bias_rows = jnp.pad(jnp.stack(bias_rows), ((0, 13), (0, 0)))
    eighth = jnp.concatenate([eighth, bias_rows], 0)
    others = [send(eighth, "n", ring(depth, k)) for k in range(1, depth)]
    x_parts, rot_q, idk = lax.optimization_barrier((x_parts, rot_q, idk))
    halo_args = (x_parts, onehot, vectors, weight_turned, bias_turned, table)
    rot_q, rot_k, values = halo_call(*halo_args, (rot_q, rot_k, values), (0, 1, 2), side)
    part = forward_call(bounds_fwd, rot_q, rot_k, values, idk, idq, side, own, 0, blocks // 2)
    others, part = lax.optimization_barrier((others, part))
    up_biases = jnp.concatenate(
        [jnp.sum(x[rows : rows + 3].astype(F32), 0, keepdims=True) for x in others]
    )
    own_w = jnp.stack([x[:rows] for x in others])
    over_1, over_2 = send(own_w, PLANE, FIRST), send(own_w, PLANE, SECOND)
    part, _ = lax.optimization_barrier((part, own_w))
    mixed, mixed_low, lse = forward_call(
        bounds_fwd, rot_q, rot_k, values, idk, idq, side, own, blocks // 2, blocks // 2, part
    )
    hidden_in, norm2, out0, dn0, up_sum0, kept_own, sent_own = middle_own_call(
        place, tokens, mixed_low, output_weight, vectors, cotangent, b_up[None],
        w_up, w_down, slices,
    )
    over_1, over_2, norm2 = lax.optimization_barrier((over_1, over_2, norm2))
    diagonal = send(over_1, PLANE, SECOND)
    near = [own_w, over_1, over_2, diagonal]
    pieces = near + [send(x, "c", SWAP) for x in near]
    grid8 = jnp.pad(grid_own.astype(F32), ((0, 6), (0, 0)))
    far_own = send(after(sent_own, over_1, over_2), "c", SWAP)
    away_own = sum_low(kept_own[1::2], far_own[1::2]).astype(BF)
    got_own = [send(away_own, PLANE, FIRST)]
    norm2, up_biases, bounds_bwd, _ = lax.optimization_barrier(
        (norm2, up_biases, bounds_bwd, away_own)
    )
    (
        activations, d_hidden, d_heads, d_head, d_tail, delta, small_mid, up_sums, kept_mid,
        sent_mid,
    ) = middle_call(
        place, hidden_in, norm2, out0, dn0, mixed_low, mixed, output_weight, vectors, cotangent,
        up_biases, lse, pieces, slices,
    )
    far_mid = send(sent_mid, "c", SWAP)
    do_parts = around(d_heads, d_head, d_tail)

    got_own[0], far_mid = lax.optimization_barrier((got_own[0], far_mid))
    away_own = sum_low(kept_own[2], far_own[2], got_own[0][1]).astype(BF)
    got_own.append(send(away_own, PLANE, SECOND))
    away = sum_low(kept_mid[1::2], far_mid[1::2]).astype(BF)
    got_1 = send(away, PLANE, FIRST)
    dq, dk, dv = backward_own_call(
        bounds_fwd, rot_q, d_heads, rot_k, values, idk, idq, lse, after(delta, away, away_own),
        side, own,
    )
    got_1, got_own[1], dq = lax.optimization_barrier((got_1, got_own[1], dq))
    away = sum_low(kept_mid[2], far_mid[2], got_1[1]).astype(BF)
    got_2 = send(away, PLANE, SECOND)
    do_parts, dq, dk, _ = lax.optimization_barrier((do_parts, dq, dk, away))
    dk, dv = backward_halo_call(
        bounds_bwd, rot_q, do_parts, rot_k, values, idk, idq, dk, dv, side
    )
    got_2, dk = lax.optimization_barrier((got_2, dk))

    def plane_part(lo, hi):
        at = slice(lo, hi)
        total = sum_low(kept_mid[0, at], far_mid[0, at], got_1[0, at], got_2[at])
        return wide_sum(total, extra)

    ff_sent = [plane_part(k * rows - rows, k * rows).astype(BF) for k in range(1, depth)]
    ff_got = [send(x, "n", ring(depth, -1 - k)) for k, x in enumerate(ff_sent)]
    dk = after(dk, ff_sent)

    d_qkv, grad_b_qkv, freqs8, kept_qkv, sent_qkv = turn_back_call(
        place, tokens, vectors, dq, dk, dv, q_exact, k_exact, onehot, table, grid8,
        order.T, side, slices,
    )
    far_qkv = send(sent_qkv, "c", SWAP)
    away = sum_low(kept_qkv[1::2], far_qkv[1::2]).astype(BF)
    got_1_qkv = send(away, PLANE, FIRST)
    input_grad, small_in = input_grad_call(
        place, tokens, vectors, after(d_qkv, away), query_key_value_weight, d_hidden,
        grad_b_qkv, small_mid, freqs8, up_sum0, up_sums,
    )
    got_1_qkv, small_in = lax.optimization_barrier((got_1_qkv, small_in))
    away = sum_low(kept_qkv[2], far_qkv[2], got_1_qkv[1]).astype(BF)
    got_2_qkv = send(away, PLANE, SECOND)
    ff_got, small_in, _ = lax.optimization_barrier((ff_got, small_in, away))
    plane_qkv = wide_sum(sum_low(kept_qkv[0], far_qkv[0], got_1_qkv[0], got_2_qkv), extra)
    ff_total = wide_sum(sum_low(kept_own[0], far_own[0], got_own[0][0], got_own[1]), extra)
    ff_total = ff_total + sum_low(*ff_got)

    sizes = [width, width, 3 * width, width, rope_freqs.size] + [width] * 3 + [b_up.size * depth]
    small = add_from(small_in, "c")

    part = plane_part((depth - 1) * rows, (depth - 1) * rows + width // slices)
    part = jnp.concatenate([plane_qkv, part], 1).astype(BF)
    thin = part.shape[0] // depth
    cut = lambda k: lax.dynamic_slice_in_dim(part, ((z + k) % depth) * thin, thin, 0)
    got = [send(cut(k), "n", ring(depth, k)) for k in range(1, depth)]
    small = add_from(add_from(after(small, part), "b"), "a")
    if extra > 1:
        small = lax.psum(small, "e")
    got, small = lax.optimization_barrier((got, small))
    low = sum_low(cut(0), *got).astype(BF)
    strip = jnp.stack([low] + [send(low, "n", ring(depth, k)) for k in range(1, depth)])
    ff_pair, ff_last = plane_gather(after(ff_total, low).astype(BF))
    pair, last = plane_gather(strip)
    ff_pieces = [after(x, strip) for x in core_gather(ff_pair, ff_last)]
    total_w_up, total_w_down, ff_squares = assemble_call(
        place, ff_pieces, [w_up.shape, w_down.shape], 0
    )
    small = jnp.concatenate([small, ff_squares], 0)
    reach = 1
    while reach < depth:
        small = add_from(small, "n", reach, depth)
        reach *= 2
    last, small = lax.optimization_barrier((last, small))
    turned = sum(sizes[:4]) // 128
    total_w_qkv, total_w_out, _, norms = assemble_call(
        place, core_gather(pair, last), [query_key_value_weight.shape, output_weight.shape], depth,
        small, (turned, turned + sizes[4] // 128),
    )
    small = small[:-8].reshape(-1)
    out, at = [], 0
    for size in sizes:
        out.append(small[at : at + size])
        at += size
    t_gain1, t_shift1, t_b_qkv, t_b_out, t_freqs, t_gain2, t_shift2, t_b_down, t_up = out
    t_freqs = t_freqs.reshape(rope_freqs.shape)
    rot_sq, other_sq = norms[0, 0], norms[1, 0]
    t_b_up = lax.dynamic_slice_in_dim(t_up, z * b_up.shape[0], b_up.shape[0], 0)
    return (
        activations[None],
        input_grad[None],
        t_gain1,
        t_shift1,
        total_w_qkv,
        t_b_qkv,
        total_w_out,
        t_b_out,
        t_freqs,
        t_gain2,
        t_shift2,
        total_w_up,
        t_b_up,
        total_w_down,
        t_b_down,
        rot_sq,
        other_sq,
    )


def solution(mesh):
    wide, depth = mesh.shape["wide"], mesh.shape["narrow"]
    extra = wide // 8
    fine = Mesh(mesh.devices.reshape(extra, 2, 2, 2, depth), ("e", "a", "b", "c", "n"))
    w, n = ("e", "a", "b", "c"), "n"
    return jax.shard_map(
        functools.partial(on_device, extra=extra, depth=depth),
        mesh=fine,
        in_specs=(
            P(w, n, None), P(w, None), P(w, None), P(None, w, None),
            P(), P(), P(), P(), P(), P(), P(), P(), P(),
            P(None, n), P(n), P(n, None), P(), P(w, n, None),
        ),
        out_specs=(
            P(w, n, None), P(w, n, None),
            P(), P(), P(), P(), P(), P(), P(), P(), P(),
            P(None, n), P(n), P(n, None), P(), P(), P(),
        ),
        check_vma=False,
    )
```

```python
import functools

import jax
import jax.numpy as jnp
import numpy as np
from jax import lax
from jax.experimental import pallas as pl
from jax.experimental.pallas import tpu as pltpu
from jax.sharding import Mesh, PartitionSpec as P

EPS = 1e-06
MASKED = -1e30
BLK = 128
SPAN = 6
SPAN_SIDE = 3
SPAN_BACK = 2
GROUP = 4
REACH = 64
STAT_ROWS = 6
STAT_PAD = 16
SIDE = 32
LN1_GAIN, LN1_SHIFT, B_OUT, LN2_GAIN, LN2_SHIFT, B_DOWN = (slice(n, n + 1) for n in range(6))
LOG2E = np.float32(1.4426950408889634)
BF = jnp.bfloat16
F32 = jnp.float32
PLANE = ("a", "b", "c")
SWAP = [(0, 1), (1, 0)]
FIRST = [(i, i ^ (4 if i % 2 else 2)) for i in range(8)]
SECOND = [(i, i ^ (2 if i % 2 else 4)) for i in range(8)]


def dot(left, right):
    return lax.dot_general(left, right, (((1,), (0,)), ((), ())), preferred_element_type=F32)


def dot_nt(left, right):
    return lax.dot_general(left, right, (((1,), (1,)), ((), ())), preferred_element_type=F32)


def dot_tn(left, right):
    return lax.dot_general(left, right, (((0,), (0,)), ((), ())), preferred_element_type=F32)


def params(mebibytes):
    return pltpu.CompilerParams(vmem_limit_bytes=mebibytes * 1024 * 1024)


def cost(us):
    return pl.CostEstimate(
        flops=int(us * 1.15e9), bytes_accessed=int(us * 3.0e6), transcendentals=0
    )


def whole(shape):
    return pl.BlockSpec(shape, lambda *_: (0,) * len(shape))


ANY = pl.BlockSpec(memory_space=pl.ANY)
SMEM = pl.BlockSpec(memory_space=pltpu.SMEM)


def rounded(x):
    return lax.reduce_precision(x, exponent_bits=8, mantissa_bits=7)


def turn_table(rope_freqs):
    lanes = rope_freqs.shape[1] * rope_freqs.shape[2]
    freq = rope_freqs.reshape(2, 1, lanes)
    angle = jnp.arange(SIDE, dtype=F32)[None, :, None] * freq
    cosine, sine = jnp.cos(angle), jnp.sin(angle)

    def halves(x):
        return jnp.concatenate([x.astype(BF), (x - rounded(x)).astype(BF)], 0)

    def grouped(x):
        return x.reshape(2 * SIDE, lanes // 128, 1, 128)

    zero = jnp.zeros((2 * SIDE, lanes // 128, 2, 128), BF)
    rows = jnp.concatenate([grouped(halves(cosine[0])), grouped(halves(sine[0])), zero], 2)
    cols = jnp.concatenate([zero, grouped(halves(cosine[1])), grouped(halves(sine[1]))], 2)
    return jnp.concatenate([rows, cols], 0).reshape(4 * SIDE, 4 * lanes)


def cos_sin(onehot, table):
    parts = dot(onehot, table)
    cr, sr, cc, sc = (parts[:, lanes_of(n, 128)] for n in range(4))
    return cr * cc - sr * sc, sr * cc + cr * sc


def layer_norm_low(x, gain, shift):
    centred = x - jnp.mean(x, -1, keepdims=True)
    var = jnp.mean(centred * centred, -1, keepdims=True)
    return (centred * lax.rsqrt(var + EPS) * gain + shift).astype(BF)


def project(norm, hot_ref, table_ref, weights, b_ref, outs, exact=()):
    width = norm.shape[1]
    for g in range(width // 256):
        c, s = cos_sin(hot_ref[...], table_ref[:, lanes_of(g, 512)])
        for n, out in outs:
            lo = n * width + 256 * g
            proj = dot(norm, weights[:, lo : lo + 256]) + b_ref[:, lo : lo + 256]
            if n == 2:
                out[:, lanes_of(g)] = proj.astype(BF)
                continue
            for half, turned in enumerate(
                (proj[:, :128] * c - proj[:, 128:] * s, proj[:, :128] * s + proj[:, 128:] * c)
            ):
                at = slice(256 * g + 128 * half, 256 * g + 128 * half + 128)
                out[:, at] = turned.astype(BF)
                if exact:
                    exact[n][:, at] = turned


def qkv_own_kernel(
    x_ref, hot_ref, vec_ref, w_ref, b_ref, order_ref, table_ref,
    q_ref, k_ref, v_ref, pq_ref, pk_ref, w_turned,
):
    width = x_ref.shape[1]

    @pl.when(pl.program_id(0) == 0)
    def _():
        for g in range(2 * width // 256):
            at = slice(256 * g, 256 * g + 256)
            w_turned[:, at] = dot(w_ref[:, at], order_ref[...]).astype(BF)
        w_turned[:, 2 * width :] = w_ref[:, 2 * width :]

    norm = layer_norm_low(x_ref[...].astype(F32), vec_ref[LN1_GAIN], vec_ref[LN1_SHIFT])
    outs = [(0, q_ref), (1, k_ref), (2, v_ref)]
    project(norm, hot_ref, table_ref, w_turned, b_ref, outs, (pq_ref, pk_ref))


def qkv_own_call(x, onehot, vectors, weight, bias, order, table, first):
    own, width = x.shape
    rows = onehot.shape[0]
    tile = 256
    shape = jax.ShapeDtypeStruct((rows, width), BF)
    exact = jax.ShapeDtypeStruct((own, width), F32)
    row = lambda w: pl.BlockSpec((tile, w), lambda i: (i, 0))
    inside = lambda w: pl.BlockSpec(
        (pl.Element(tile), pl.Element(w)), lambda i: (pl.multiple_of(first + tile * i, BLK), 0)
    )
    return pl.pallas_call(
        qkv_own_kernel,
        grid=(own // tile,),
        in_specs=[
            row(width),
            inside(onehot.shape[1]),
            whole(vectors.shape),
            whole(weight.shape),
            whole((1, 3 * width)),
            whole(order.shape),
            whole(table.shape),
        ],
        out_specs=[inside(width)] * 3 + [row(width)] * 2 + [whole(weight.shape)],
        out_shape=[shape] * 3 + [exact] * 2 + [jax.ShapeDtypeStruct(weight.shape, BF)],
        compiler_params=params(56),
        cost_estimate=cost(8),
        name="qkv_own",
    )(x, onehot, vectors, weight, bias[None], order, table)


def halo_kernel(
    far_l, near_l, near_r, far_r, hot_ref, vec_ref, w_ref, b_ref, table_ref, *refs, which
):
    refs = refs[len(which) :]
    out_refs, (x_all, sem) = refs[: len(which)], refs[len(which) :]
    width = x_all.shape[1]
    step = pl.program_id(0)
    tile = out_refs[0].shape[0]

    @pl.when(step == 0)
    def _():
        own, reach = near_l.shape[0], far_l.shape[0]
        total = x_all.shape[0]
        blank = total // 2 - own - reach
        copies = []
        at = blank
        for n, ref in enumerate((far_l, near_l, near_r, far_r)):
            copies.append(
                pltpu.make_async_copy(ref, x_all.at[at : at + ref.shape[0], :], sem.at[n])
            )
            copies[-1].start()
            at += ref.shape[0]
        x_all[:blank, :] = jnp.zeros((blank, width), BF)
        x_all[total - blank :, :] = jnp.zeros((blank, width), BF)
        for copy in copies:
            copy.wait()

    x = x_all[pl.ds(pl.multiple_of(step * tile, tile), tile), :].astype(F32)
    norm = layer_norm_low(x, vec_ref[LN1_GAIN], vec_ref[LN1_SHIFT])
    project(norm, hot_ref, table_ref, w_ref, b_ref, list(zip(which, out_refs)))


def halo_call(pieces, onehot, vectors, weight, bias, table, arrays, which, first):
    rows, width = arrays[0].shape
    own = pieces[1].shape[0]
    tile = first // 2
    at = lambda w: pl.BlockSpec(
        (pl.Element(tile), pl.Element(w)),
        lambda i: (pl.multiple_of(tile * i + jnp.where(i >= 2, own, 0), 64), 0),
    )
    return pl.pallas_call(
        functools.partial(halo_kernel, which=which),
        grid=(4,),
        in_specs=[ANY] * 4
        + [
            at(onehot.shape[1]),
            whole(vectors.shape),
            whole(weight.shape),
            whole((1, 3 * width)),
            whole(table.shape),
        ]
        + [ANY] * len(which),
        out_specs=[at(width)] * len(which),
        out_shape=[jax.ShapeDtypeStruct((rows, width), BF)] * len(which),
        input_output_aliases={9 + n: n for n in range(len(which))},
        scratch_shapes=[pltpu.VMEM((2 * first, width), BF), pltpu.SemaphoreType.DMA((4,))],
        compiler_params=params(56),
        cost_estimate=cost(4 * len(which)),
        name="halo",
    )(*pieces, onehot, vectors, weight, bias[None], table, *arrays)


def head_stack(block, turned, scale=None):
    lane = lax.broadcasted_iota(jnp.int32, block.shape, 1)
    head = (lane % 128) // 32 if turned else lane // 64
    if scale is not None:
        block = block * scale
    zero = jnp.zeros_like(block)
    return jnp.concatenate([jnp.where(head == h, block, zero) for h in range(GROUP)], 0)


def fold8(x, op):
    return op(x.reshape(x.shape[0] // 8, 8, x.shape[1]), axis=0)


def key_span(ident_ref, ident_q, start, c, span, end):
    block = jnp.minimum(start + c * span, end - span)
    lower = (start + c * span - block) * BLK
    at = pl.ds(pl.multiple_of(block * BLK, BLK), span * BLK)
    row = lax.broadcasted_iota(jnp.int32, (span * BLK, BLK), 0)
    return at, (ident_ref[at, :] == ident_q) & (row >= lower)


def lanes_of(g, size=256):
    return slice(size * g, size * g + size)


def forward_kernel(
    bound_ref, q_ref, k_ref, v_ref, idk_ref, idq_ref, *refs, first, base
):
    o_ref, low_ref, lse_ref, s_ref, acc_ref, q4_ref = refs[-6:]
    i = pl.program_id(0) + base
    groups = k_ref.shape[1] // 256
    lanes = GROUP * BLK
    window = k_ref.shape[0] // BLK
    start, count = bound_ref[i, 0], bound_ref[i, 1]
    for g in range(groups):
        q4_ref[g] = head_stack(q_ref[:, lanes_of(g)], True, jnp.asarray(0.125, BF))
    ident_q = idq_ref[pl.ds(first // BLK + i, 1), :]

    def scores(c, top):
        at, seen = key_span(idk_ref, ident_q, start, c, SPAN, window)
        here = pl.ds(pl.multiple_of(c * SPAN * BLK, BLK), SPAN * BLK)
        tops = []
        for g in range(groups):
            s = dot_nt(k_ref[at, lanes_of(g)], q4_ref[g]) * LOG2E
            for h in range(GROUP):
                masked = jnp.where(seen, s[:, lanes_of(h, BLK)], MASKED)
                s_ref[g, here, lanes_of(h, BLK)] = masked
                tops.append(fold8(masked, jnp.max))
        return jnp.maximum(top, jnp.concatenate(tops, 1))

    top = lax.fori_loop(0, count, scores, jnp.full((8, groups * lanes), -3e38, F32))
    top = jnp.max(top, 0, keepdims=True)
    acc_ref[...] = jnp.zeros_like(acc_ref)

    def mix(c, total):
        at, _ = key_span(idk_ref, ident_q, start, c, SPAN, window)
        here = pl.ds(pl.multiple_of(c * SPAN * BLK, BLK), SPAN * BLK)
        sums = []
        for g in range(groups):
            e = jnp.exp2(s_ref[g, here, :] - top[:, lanes_of(g, lanes)])
            sums.append(fold8(e, jnp.sum))
            acc_ref[g] += dot_tn(v_ref[at, lanes_of(g)], e.astype(BF))
        return total + jnp.concatenate(sums, 1)

    total = lax.fori_loop(0, count, mix, jnp.zeros((8, groups * lanes), F32))
    total = jnp.sum(total, 0, keepdims=True)
    lse = top + jnp.log(total) * LOG2E
    inverse = 1.0 / total
    for g in range(groups):
        lse_ref[g] = lse[:, lanes_of(g, lanes)]
        acc = acc_ref[g] * inverse[:, lanes_of(g, lanes)]
        out = jnp.concatenate(
            [acc[64 * h : 64 * h + 64, lanes_of(h, BLK)] for h in range(GROUP)], 0
        ).T
        o_ref[:, lanes_of(g)] = out
        low_ref[:, lanes_of(g)] = out.astype(BF)


def stat_spec(groups, base=0):
    return pl.BlockSpec((groups, None, 1, GROUP * BLK), lambda i: (0, i + base, 0, 0))


def query_rows(first, width):
    return pl.BlockSpec(
        (pl.Element(BLK), pl.Element(width)), lambda i: (pl.multiple_of(first + BLK * i, BLK), 0)
    )


def forward_call(bounds, q_win, k_win, v_win, idk, idq, first, own, base, count, earlier=()):
    win, width = k_win.shape
    groups, blocks = width // 256, own // BLK
    row = pl.BlockSpec((BLK, width), lambda i: (i + base, 0))
    steps = -(-win // (SPAN * BLK))
    return pl.pallas_call(
        functools.partial(forward_kernel, first=first, base=base),
        grid=(count,),
        in_specs=[SMEM, query_rows(first + base * BLK, width)]
        + [whole((win, width))] * 2
        + [whole(idk.shape), whole(idq.shape)]
        + [ANY] * len(earlier),
        out_specs=[row, row, stat_spec(groups, base)],
        input_output_aliases={6 + n: n for n in range(len(earlier))},
        out_shape=[
            jax.ShapeDtypeStruct((own, width), F32),
            jax.ShapeDtypeStruct((own, width), BF),
            jax.ShapeDtypeStruct((groups, blocks, 1, GROUP * BLK), F32),
        ],
        scratch_shapes=[
            pltpu.VMEM((groups, steps * SPAN * BLK, GROUP * BLK), F32),
            pltpu.VMEM((groups, 256, GROUP * BLK), F32),
            pltpu.VMEM((groups, GROUP * BLK, 256), BF),
        ],
        compiler_params=params(56),
        cost_estimate=cost(4 * count),
        name="attention_forward",
    )(bounds, q_win, k_win, v_win, idk, idq, *earlier)


def score_gradients(s, dp, lse, delta, seen):
    low_p, low_ds = [], []
    for h in range(GROUP):
        at = lanes_of(h, BLK)
        p = jnp.exp2(jnp.where(seen, s[:, at] * LOG2E - lse[:, at], MASKED))
        low_p.append(p.astype(BF))
        low_ds.append((p * (dp[:, at] - delta[:, at])).astype(BF))
    return jnp.concatenate(low_p, 1), jnp.concatenate(low_ds, 1)


def backward_own_kernel(
    bound_ref, q_ref, do_ref, k_ref, v_ref, idk_ref, idq_ref, lse_ref, delta_ref,
    dq_ref, dk_ref, dv_ref, acc_ref, q4_ref, do4_ref, *, first,
):
    i = pl.program_id(0)
    groups = k_ref.shape[1] // 256
    own = dk_ref.shape[0]

    @pl.when(i == 0)
    def _():
        dk_ref[...] = jnp.zeros_like(dk_ref)
        dv_ref[...] = jnp.zeros_like(dv_ref)

    for g in range(groups):
        q4_ref[g] = head_stack(q_ref[:, lanes_of(g)], True, jnp.asarray(0.125, BF))
        do4_ref[g] = head_stack(do_ref[:, lanes_of(g)], False)
    ident_q = idq_ref[pl.ds(first // BLK + i, 1), :]

    def attend(at, seen, inside):
        for g in range(groups):
            keys = k_ref[at, lanes_of(g)]
            s = dot_nt(keys, q4_ref[g])
            dp = dot_nt(v_ref[at, lanes_of(g)], do4_ref[g])
            low_p, low_ds = score_gradients(s, dp, lse_ref[g], delta_ref[g], seen)
            if inside:
                acc_ref[g] = dot_tn(keys, low_ds)
                dk_ref[:, lanes_of(g)] += dot(low_ds, q4_ref[g])
                dv_ref[:, lanes_of(g)] += dot(low_p, do4_ref[g])
            else:
                acc_ref[g] += dot_tn(keys, low_ds)

    attend(slice(first, first + own), idk_ref[first : first + own, :] == ident_q, True)
    for start, count, end in (
        (bound_ref[i, 2], bound_ref[i, 3], first // BLK),
        ((first + own) // BLK, bound_ref[i, 4], k_ref.shape[0] // BLK),
    ):

        def step(c, _):
            attend(*key_span(idk_ref, ident_q, start, c, SPAN_SIDE, end), False)
            return 0

        lax.fori_loop(0, count, step, 0)
    for g in range(groups):
        acc = acc_ref[g]
        parts = [acc[32 * h : 32 * h + 32, lanes_of(h, BLK)] for h in range(GROUP)]
        parts += [acc[128 + 32 * h : 160 + 32 * h, lanes_of(h, BLK)] for h in range(GROUP)]
        dq_ref[:, lanes_of(g)] = (jnp.concatenate(parts, 0) * 0.125).T


def backward_own_call(bounds, q_win, do_own, k_win, v_win, idk, idq, lse, delta, first, own):
    win, width = k_win.shape
    groups = width // 256
    row = pl.BlockSpec((BLK, width), lambda i: (i, 0))
    return pl.pallas_call(
        functools.partial(backward_own_kernel, first=first),
        grid=(own // BLK,),
        in_specs=[SMEM, query_rows(first, width), row]
        + [whole((win, width))] * 2
        + [whole(idk.shape), whole(idq.shape), stat_spec(groups), stat_spec(groups)],
        out_specs=[row] + [whole((own, width))] * 2,
        out_shape=[jax.ShapeDtypeStruct((own, width), F32)] * 3,
        scratch_shapes=[pltpu.VMEM((groups, 256, GROUP * BLK), F32)]
        + [pltpu.VMEM((groups, GROUP * BLK, 256), BF)] * 2,
        compiler_params=params(24),
        cost_estimate=cost(20),
        name="attention_backward_own",
    )(bounds, q_win, do_own, k_win, v_win, idk, idq, lse, delta)


def backward_halo_kernel(
    bound_ref, q_ref, far_l, near_l, near_r, far_r, k_ref, v_ref, idk_ref, idq_ref, dk_in, dv_in,
    dk_ref, dv_ref, q4_ref, do_all, do4_ref, stat_ref, *, first,
):
    groups = k_ref.shape[1] // 256
    own, reach = k_ref.shape[0], far_l.shape[0] - STAT_PAD
    blocks = own // BLK
    side = first // BLK
    step_id = pl.program_id(0)
    j = jnp.where(step_id < side, step_id, step_id + blocks)
    lanes = GROUP * BLK

    def stats(ref, row, slot):
        parts = ref[row : row + 2 * STAT_ROWS, :].astype(F32)
        sums = parts[0:4] + parts[4:8] + parts[8:12]
        for g in range(groups):
            for n in range(2):
                stat_ref[n, g, slot : slot + 1, :] = jnp.concatenate(
                    [sums[2 * n : 2 * n + 1, lanes_of(g)], sums[2 * n + 1 : 2 * n + 2, lanes_of(g)]],
                    1,
                )

    @pl.when(step_id == 0)
    def _():
        dk_ref[...] = dk_in[...]
        dv_ref[...] = dv_in[...]
        blank = jnp.zeros((BLK - reach, do_all.shape[1]), BF)
        do_all[0 : BLK - reach, :] = blank
        do_all[BLK - reach : BLK, :] = far_l[:reach, :]
        do_all[BLK : BLK + own, :] = near_l[:own, :]
        do_all[BLK + own : BLK + 2 * own, :] = near_r[:own, :]
        do_all[BLK + 2 * own : BLK + 2 * own + reach, :] = far_r[:reach, :]
        do_all[BLK + 2 * own + reach :, :] = blank
        stats(far_l, reach, 0)
        for i in range(blocks):
            stats(near_l, own + 2 * STAT_ROWS * i, 1 + i)
            stats(near_r, own + 2 * STAT_ROWS * i, 1 + blocks + i)
        stats(far_r, reach, 1 + 2 * blocks)

    start, count = bound_ref[j, 0], bound_ref[j, 1]

    @pl.when(count > 0)
    def _():
        here = pl.ds(pl.multiple_of(step_id * BLK, BLK), BLK)
        for g in range(groups):
            q4_ref[g] = head_stack(q_ref[:, lanes_of(g)], True, jnp.asarray(0.125, BF))
            do4_ref[g] = head_stack(do_all[here, lanes_of(g)], False)
        ident_q = idq_ref[pl.ds(j, 1), :]

        def step(c, _):
            at, seen = key_span(idk_ref, ident_q, start, c, SPAN_BACK, blocks)
            for g in range(groups):
                s = dot_nt(k_ref[at, lanes_of(g)], q4_ref[g])
                dp = dot_nt(v_ref[at, lanes_of(g)], do4_ref[g])
                lse = stat_ref[0, g, pl.ds(step_id, 1), :]
                delta = stat_ref[1, g, pl.ds(step_id, 1), :]
                low_p, low_ds = score_gradients(s, dp, lse, delta, seen)
                dk_ref[at, lanes_of(g)] += dot(low_ds, q4_ref[g])
                dv_ref[at, lanes_of(g)] += dot(low_p, do4_ref[g])
            return 0

        lax.fori_loop(0, count, step, 0)


def backward_halo_call(bounds, q_win, pieces, k_win, v_win, idk, idq, dk, dv, first):
    own, width = dk.shape
    groups = width // 256
    side, blocks = first // BLK, own // BLK
    inside = lambda w: pl.BlockSpec(
        (pl.Element(own), pl.Element(w)), lambda i: (pl.multiple_of(first + 0 * i, BLK), 0)
    )
    outside = pl.BlockSpec((BLK, width), lambda i: (jnp.where(i < side, i, i + blocks), 0))
    return pl.pallas_call(
        functools.partial(backward_halo_kernel, first=first),
        grid=(2 * side,),
        in_specs=[SMEM, outside]
        + [whole(p.shape) for p in pieces]
        + [inside(width)] * 2
        + [inside(idk.shape[1]), whole(idq.shape)]
        + [whole((own, width))] * 2,
        out_specs=[whole((own, width))] * 2,
        out_shape=[jax.ShapeDtypeStruct((own, width), F32)] * 2,
        scratch_shapes=[
            pltpu.VMEM((groups, GROUP * BLK, 256), BF),
            pltpu.VMEM((2 * first, width), BF),
            pltpu.VMEM((groups, GROUP * BLK, 256), BF),
            pltpu.VMEM((2, groups, 16, GROUP * BLK), F32),
        ],
        compiler_params=params(20),
        cost_estimate=cost(11),
        name="attention_backward_halo",
    )(bounds, q_win, *pieces, k_win, v_win, idk, idq, dk, dv)


def norm_parts(x):
    centred = x - jnp.mean(x, -1, keepdims=True)
    inverse = lax.rsqrt(jnp.mean(centred * centred, -1, keepdims=True) + EPS)
    return centred * inverse, inverse


def norm_back(grad, xhat, inverse, gain):
    scaled = grad * gain
    return inverse * (
        scaled
        - jnp.mean(scaled, -1, keepdims=True)
        - xhat * jnp.mean(scaled * xhat, -1, keepdims=True)
    )


def columns_sum(x):
    return jnp.sum(x, 0, keepdims=True)


def chip_order(ab, core):
    return jnp.where(core == 0, ab, ab % 2 * 2 + ab // 2)


def slices_out(place, source, keep, away, lead, sem, slices, rows):
    for n in range(slices):
        rel = place ^ n
        for target, odd in ((keep, 0), (away, 1)):
            core = place % 2 ^ odd

            @pl.when(rel % 2 == odd)
            def _():
                pltpu.make_async_copy(
                    source.at[n * rows : (n + 1) * rows, :],
                    target.at[chip_order(rel // 2, core), pl.ds(lead, rows), :],
                    sem.at[n],
                ).start()


def gathered(place, refs):
    for far in range(2):
        for n in range(4):
            rel = 2 * chip_order(jnp.int32(n), place % 2 ^ far) + far
            yield refs[4 * far + n], place ^ rel


def slices_wait(source, keep, sem, slices, rows):
    for n in range(slices):
        pltpu.make_async_copy(
            source.at[n * rows : (n + 1) * rows, :], keep.at[0, 0:rows, :], sem.at[n]
        ).wait()


def one_quarter(q, w_all, norm_ref, dy_ref, bu_ref, dbu_ref, out_acc, dn_acc, g_all, fresh):
    own, width = norm_ref.shape
    tile = w_all.shape[1] - width
    for t in range((w_all.shape[1] - width) // tile):
        cols = slice(tile * t, tile * t + tile)
        down = slice(width + tile * t, width + tile * t + tile)
        norm, dy = norm_ref[...], dy_ref[...]
        up_w = w_all[q, :width, cols]
        down_w = w_all[q, down, :]
        pre = dot(norm, up_w) + bu_ref[pl.ds(q, 1), cols]
        cdf = 0.5 * (1.0 + lax.erf(pre * np.float32(0.7071067811865476)))
        density = jnp.exp(-0.5 * pre * pre) * np.float32(0.3989422804014327)
        act = (pre * cdf).astype(BF)
        d_pre = (dot_nt(dy, down_w) * (cdf + pre * density)).astype(BF)
        dbu_ref[pl.ds(q, 1), cols] = columns_sum(d_pre.astype(F32))
        if fresh and t == 0:
            out_acc[...] = dot(act, down_w)
            dn_acc[...] = dot_nt(d_pre, up_w)
        else:
            out_acc[...] += dot(act, down_w)
            dn_acc[...] += dot_nt(d_pre, up_w)
        g_all[q, :width, cols] = dot_tn(norm, d_pre).astype(BF)
        g_all[q, down, :] = dot_tn(act, dy).astype(BF)


def middle_own_kernel(
    place_ref, x_ref, low_ref, wo_ref, vec_ref, dy_ref, bu_ref, up_ref, down_ref,
    hid_ref, norm_ref, out_ref, dn_ref, dbu_ref, keep_ref, send_ref, w_all, g_all, w_sem, g_sem,
    *, slices,
):
    width = x_ref.shape[1]
    rows = w_all.shape[1] // slices
    copies = [
        pltpu.make_async_copy(up_ref, w_all.at[0, :width, :], w_sem.at[0]),
        pltpu.make_async_copy(down_ref, w_all.at[0, width:, :], w_sem.at[1]),
    ]
    for copy in copies:
        copy.start()
    hidden_in = x_ref[...].astype(F32) + dot(low_ref[...], wo_ref[...]) + vec_ref[B_OUT]
    hid_ref[...] = hidden_in
    norm_ref[...] = layer_norm_low(hidden_in, vec_ref[LN2_GAIN], vec_ref[LN2_SHIFT])
    for copy in copies:
        copy.wait()
    one_quarter(0, w_all, norm_ref, dy_ref, bu_ref, dbu_ref, out_ref, dn_ref, g_all, True)
    slices_out(place_ref[0], g_all.at[0], keep_ref, send_ref, 0, g_sem, slices, rows)
    slices_wait(g_all.at[0], keep_ref, g_sem, slices, rows)


def middle_own_call(place, x, low, w_out, vectors, dy, b_up, w_up, w_down, slices):
    own, width = x.shape
    hidden = b_up.shape[1]
    rows = width + hidden
    vmem = pl.BlockSpec(memory_space=pltpu.VMEM)
    sds = jax.ShapeDtypeStruct
    return pl.pallas_call(
        functools.partial(middle_own_kernel, slices=slices),
        in_specs=[SMEM] + [vmem] * 6 + [ANY] * 2,
        out_specs=[vmem] * 5 + [ANY] * 2,
        out_shape=[
            sds((own, width), F32),
            sds((own, width), BF),
            sds((own, width), F32),
            sds((own, width), F32),
            sds((1, hidden), F32),
        ]
        + [sds((slices // 2, rows // slices, width), BF)] * 2,
        scratch_shapes=[
            pltpu.VMEM((1, rows, width), BF),
            pltpu.VMEM((1, rows, width), BF),
            pltpu.SemaphoreType.DMA((2,)),
            pltpu.SemaphoreType.DMA((slices,)),
        ],
        compiler_params=params(56),
        cost_estimate=cost(12),
        name="middle_own",
    )(place, x, low, w_out, vectors, dy, b_up, w_up, w_down)


def middle_kernel(
    place_ref, vec_ref, bu_ref, lse_ref, norm_in, dy_in, out_in, dn_in, hid_in, low_in, mixed_in,
    wo_in, *refs, slices,
):
    piece_refs = refs[:slices]
    (
        act_out, dh_out, dheads_ref, head_ref, tail_ref, delta_ref, small_ref, dbu_ref, keep_ref,
        send_ref,
        w_all, g_all, go_all, norm_ref, dy_ref, out_acc, dn_acc, hid_ref, low_ref, mixed_ref,
        wo_ref, act_ref, dh_ref, w_sem, g_sem, in_sem, out_sem,
    ) = refs[slices:]
    place = place_ref[0]
    own, width = norm_ref.shape
    quarters = w_all.shape[0]
    rows = w_all.shape[1] // slices

    def fetches(q):
        return [
            pltpu.make_async_copy(
                ref.at[q],
                w_all.at[q, pl.ds(pl.multiple_of(source * rows, rows), rows), :],
                w_sem.at[q, n],
            )
            for n, (ref, source) in enumerate(gathered(place, piece_refs))
        ]

    inputs = [
        pltpu.make_async_copy(source, target, in_sem.at[n])
        for n, (source, target) in enumerate(
            (
                (norm_in, norm_ref), (dy_in, dy_ref), (out_in, out_acc), (dn_in, dn_acc),
                (hid_in, hid_ref), (low_in, low_ref), (mixed_in, mixed_ref), (wo_in, wo_ref),
            )
        )
    ]
    for copy in inputs[:2] + fetches(0) + inputs[2:4]:
        copy.start()
    for q in range(1, quarters):
        for copy in fetches(q):
            copy.start()
    for copy in inputs[4:]:
        copy.start()
    for copy in inputs[:2]:
        copy.wait()

    def quarter(q, _):
        for copy in fetches(q):
            copy.wait()

        @pl.when(q == 0)
        def _():
            for copy in inputs[2:4]:
                copy.wait()

        one_quarter(q, w_all, norm_ref, dy_ref, bu_ref, dbu_ref, out_acc, dn_acc, g_all, False)
        slices_out(
            place, g_all.at[q], keep_ref, send_ref, pl.multiple_of(q * rows, rows),
            g_sem.at[q], slices, rows,
        )
        return 0

    lax.fori_loop(0, quarters, quarter, 0)

    for copy in inputs[4:]:
        copy.wait()
    hidden_in = hid_ref[...]
    xhat, inverse = norm_parts(hidden_in)
    dn = dn_acc[...]
    dy = dy_ref[...].astype(F32)
    d_hidden = dy + norm_back(dn, xhat, inverse, vec_ref[LN2_GAIN])
    dh_ref[...] = d_hidden
    d_att = d_hidden.astype(BF)
    d_heads = dot_nt(d_att, wo_ref[...]).astype(BF)
    dheads_ref[:own, :] = d_heads
    go_all[...] = dot_tn(low_ref[...], d_att).astype(BF)
    few = width // slices
    base = quarters * rows
    slices_out(place, go_all, keep_ref, send_ref, base, g_sem.at[quarters], slices, few)
    act_ref[...] = (hidden_in + out_acc[...] + vec_ref[B_DOWN]).astype(BF)
    outputs = [
        pltpu.make_async_copy(source, target, out_sem.at[n])
        for n, (source, target) in enumerate(
            (
                (act_ref, act_out), (dh_ref, dh_out),
            )
        )
    ]
    for copy in outputs:
        copy.start()
    small_ref[0:1, :] = columns_sum(dn * xhat)
    small_ref[1:2, :] = columns_sum(dn)
    small_ref[2:3, :] = columns_sum(dy)
    small_ref[3:4, :] = columns_sum(d_att.astype(F32))
    spread = d_heads.astype(F32) * mixed_ref[...]
    pick = lax.broadcasted_iota(jnp.int32, (8, 256), 0)
    pick = (pick == lax.broadcasted_iota(jnp.int32, (8, 256), 1) // 64).astype(F32)
    for g in range(width // 256):
        for i in range(own // BLK):
            block = spread[BLK * i : BLK * i + BLK, 256 * g : 256 * g + 256]
            sums = lax.dot_general(
                pick, block, (((1,), (1,)), ((), ())),
                preferred_element_type=F32, precision=lax.Precision.HIGHEST,
            )
            delta = jnp.concatenate([sums[h : h + 1, :] for h in range(GROUP)], 1)
            delta_ref[g, i] = delta
            lse = lse_ref[g, i]
            left = jnp.concatenate(
                [lse[:, :256], lse[:, 256:], delta[:, :256], delta[:, 256:]], 0
            )
            parts = []
            for _ in range(3):
                parts.append(left.astype(BF))
                left = left - parts[-1].astype(F32)
            parts = jnp.concatenate(parts, 0)
            at = slice(256 * g, 256 * g + 256)
            lo = own + 2 * STAT_ROWS * i
            dheads_ref[lo : lo + 2 * STAT_ROWS, at] = parts
            for target, row in ((head_ref, 0), (tail_ref, own // BLK - 1)):
                if i == row:
                    target[REACH : REACH + 2 * STAT_ROWS, at] = parts
    blank = jnp.zeros((STAT_PAD - 2 * STAT_ROWS, width), BF)
    head_ref[REACH + 2 * STAT_ROWS :, :] = blank
    tail_ref[REACH + 2 * STAT_ROWS :, :] = blank
    head_ref[:REACH, :] = d_heads[:REACH, :]
    tail_ref[:REACH, :] = d_heads[own - REACH :, :]
    for q in range(quarters):
        slices_wait(g_all.at[q], keep_ref, g_sem.at[q], slices, rows)
    slices_wait(go_all, keep_ref, g_sem.at[quarters], slices, few)
    for copy in outputs:
        copy.wait()


def middle_call(
    place, hidden_in, norm, out, dn, low, mixed, w_out, vectors, dy, b_up, lse, pieces, slices,
):
    own, width = norm.shape
    quarters, hidden = b_up.shape
    rows = width + hidden
    vmem = pl.BlockSpec(memory_space=pltpu.VMEM)
    sds = jax.ShapeDtypeStruct
    grads = sds((slices // 2, (quarters * rows + width) // slices, width), BF)
    return pl.pallas_call(
        functools.partial(middle_kernel, slices=slices),
        in_specs=[SMEM] + [vmem] * 3 + [ANY] * (8 + len(pieces)),
        out_specs=[ANY] * 2 + [vmem] * 6 + [ANY] * 2,
        out_shape=[
            sds((own, width), BF),
            sds((own, width), F32),
            sds((own + own // BLK * 2 * STAT_ROWS, width), BF),
            sds((REACH + STAT_PAD, width), BF),
            sds((REACH + STAT_PAD, width), BF),
            sds((width // 256, own // BLK, 1, GROUP * BLK), F32),
            sds((4, width), F32),
            sds((quarters, hidden), F32),
            grads,
            grads,
        ],
        scratch_shapes=[
            pltpu.VMEM((quarters, rows, width), BF),
            pltpu.VMEM((quarters, rows, width), BF),
            pltpu.VMEM((width, width), BF),
            pltpu.VMEM((own, width), BF),
            pltpu.VMEM((own, width), BF),
            pltpu.VMEM((own, width), F32),
            pltpu.VMEM((own, width), F32),
            pltpu.VMEM((own, width), F32),
            pltpu.VMEM((own, width), BF),
            pltpu.VMEM((own, width), F32),
            pltpu.VMEM((width, width), BF),
            pltpu.VMEM((own, width), BF),
            pltpu.VMEM((own, width), F32),
            pltpu.SemaphoreType.DMA((quarters, slices)),
            pltpu.SemaphoreType.DMA((quarters + 1, slices)),
            pltpu.SemaphoreType.DMA((10,)),
            pltpu.SemaphoreType.DMA((4,)),
        ],
        compiler_params=params(44),
        cost_estimate=cost(20),
        name="middle",
    )(
        place, vectors, b_up, lse, norm, dy, out, dn, hidden_in, low, mixed, w_out, *pieces,
    )


def turn_back_kernel(
    place_ref, x_ref, vec_ref, dq_ref, dk_ref, dv_ref, q_ref, k_ref, hot_ref, table_ref, grid_ref,
    back_ref, d_ref, db_ref, freq_ref, keep_ref, send_ref, norm_ref, g_all, sem, *, slices,
):
    width = x_ref.shape[1]
    group = pl.program_id(0)

    @pl.when(group == 0)
    def _():
        norm_ref[...] = layer_norm_low(
            x_ref[...].astype(F32), vec_ref[LN1_GAIN], vec_ref[LN1_SHIFT]
        )

    c, s = cos_sin(hot_ref[...], table_ref[...])
    norm = norm_ref[...]

    def gradient(n, low):
        d_ref[n] = low
        db_ref[n : n + 1, :] = columns_sum(low.astype(F32))
        at = pl.ds(pl.multiple_of(n * width + group * 256, 256), 256)
        g_all[:, at] = dot_tn(norm, low).astype(BF)

    d_angle = 0.0
    for n, (grad, turned_ref) in enumerate(((dq_ref, q_ref), (dk_ref, k_ref))):
        g1, g2 = grad[:, :128], grad[:, 128:]
        d_angle = d_angle + (g2 * turned_ref[:, :128] - g1 * turned_ref[:, 128:])
        back = jnp.concatenate([g1 * c + g2 * s, g2 * c - g1 * s], 1).astype(BF)
        gradient(n, dot(back, back_ref[...]).astype(BF))
    freq_ref[...] = lax.dot_general(
        grid_ref[...], d_angle, (((1,), (0,)), ((), ())),
        preferred_element_type=F32, precision=lax.Precision.HIGHEST,
    )
    gradient(2, dv_ref[...].astype(BF))

    @pl.when(group == width // 256 - 1)
    def _():
        slices_out(place_ref[0], g_all, keep_ref, send_ref, 0, sem, slices, width // slices)
        slices_wait(g_all, keep_ref, sem, slices, width // slices)


def turn_back_call(
    place, x, vectors, dq, dk, dv, q_exact, k_exact, onehot, table, grid8, back, first, slices
):
    rows, width = dk.shape
    sds = jax.ShapeDtypeStruct
    part = pl.BlockSpec((rows, 256), lambda g: (0, g))
    hot = pl.BlockSpec(
        (pl.Element(rows), pl.Element(onehot.shape[1])),
        lambda g: (pl.multiple_of(first + 0 * g, BLK), 0),
    )
    return pl.pallas_call(
        functools.partial(turn_back_kernel, slices=slices),
        grid=(width // 256,),
        in_specs=[SMEM, whole(x.shape), whole(vectors.shape)]
        + [part] * 5
        + [
            hot,
            pl.BlockSpec((table.shape[0], 512), lambda g: (0, g)),
            whole(grid8.shape),
            whole(back.shape),
        ],
        out_specs=[
            pl.BlockSpec((3, rows, 256), lambda g: (0, 0, g)),
            pl.BlockSpec((3, 256), lambda g: (0, g)),
            pl.BlockSpec((8, 128), lambda g: (0, g)),
        ]
        + [ANY] * 2,
        out_shape=[
            sds((3, rows, width), BF),
            sds((3, width), F32),
            sds((8, width // 2), F32),
        ]
        + [sds((slices // 2, width // slices, 3 * width), BF)] * 2,
        scratch_shapes=[
            pltpu.VMEM((rows, width), BF),
            pltpu.VMEM((width, 3 * width), BF),
            pltpu.SemaphoreType.DMA((slices,)),
        ],
        compiler_params=params(16),
        cost_estimate=cost(9),
        name="turn_back",
    )(place, x, vectors, dq, dk, dv, q_exact, k_exact, onehot, table, grid8, back)


def input_grad_kernel(
    place_ref, x_ref, vec_ref, d_ref, w_ref, dh_ref, db_ref, mid_ref, freq_ref, up0_ref, up_ref,
    out_ref, small_ref,
):
    width = x_ref.shape[1]
    d_norm = sum(dot_nt(d_ref[n], w_ref[:, lanes_of(n, width)]) for n in range(3))
    xhat, inverse = norm_parts(x_ref[...].astype(F32))
    out_ref[...] = dh_ref[...] + norm_back(d_norm, xhat, inverse, vec_ref[LN1_GAIN])
    row = 0
    for vector in (
        columns_sum(d_norm * xhat), columns_sum(d_norm), *(db_ref[n : n + 1, :] for n in range(3)),
        mid_ref[3:4, :], freq_ref[0:1, :], freq_ref[1:2, :], *(mid_ref[n : n + 1, :] for n in range(3)),
    ):
        for n in range(vector.shape[1] // 128):
            small_ref[row : row + 1, :] = vector[:, lanes_of(n, 128)]
            row += 1
    depth = 1 + up_ref.shape[0]
    hidden = up0_ref.shape[1] // 128
    for k in range(depth):
        quarter = (place_ref[1] - k + depth) % depth
        vector = up_ref[k - 1 : k, :] if k else up0_ref[...]
        for n in range(hidden):
            small_ref[pl.ds(row + quarter * hidden + n, 1), :] = vector[:, lanes_of(n, 128)]


def input_grad_call(place, x, vectors, d_qkv, weight, d_hidden, db_qkv, small_mid, freqs, up0, up):
    rows, width = x.shape
    short = 9 * width + freqs.shape[1] * 2 + up0.size * (1 + up.shape[0])
    return pl.pallas_call(
        input_grad_kernel,
        in_specs=[SMEM] + [pl.BlockSpec(memory_space=pltpu.VMEM)] * 10,
        out_shape=[
            jax.ShapeDtypeStruct((rows, width), F32),
            jax.ShapeDtypeStruct((short // 128, 128), F32),
        ],
        compiler_params=params(20),
        cost_estimate=cost(7),
        name="input_grad",
    )(place, x, vectors, d_qkv, weight, d_hidden, db_qkv, small_mid, freqs, up0, up)


def assemble_kernel(place_ref, *refs, split, outs, skip):
    out_refs, (held, sem) = refs[-2 - outs : -2], refs[-2:]
    pairs = refs[:4]
    piece_refs = [pairs[n // 2].at[n % 2] for n in range(8)]
    place, depth = place_ref[0], place_ref[1]
    slot = pl.program_id(0)

    def copy(ref, target):
        return pltpu.make_async_copy(ref, held.at[target], sem.at[target])

    @pl.when(slot == 0)
    def _():
        for ref, source in gathered(place, piece_refs):
            copy(ref, source).start()

    copy(piece_refs[0], slot).wait()
    rows = held.shape[-2]
    total_ref = None
    if skip is not None:
        out_refs, total_ref = out_refs[:-1], out_refs[-1]
    out_refs, squares = out_refs[:-1], out_refs[-1]

    @pl.when(slot == 0)
    def _():
        squares[...] = jnp.zeros_like(squares)

    def add_squares(block):
        total = fold8(block * block, jnp.sum)
        squares[...] += sum(total[:, lanes_of(n, 128)] for n in range(block.shape[1] // 128))

    if split:
        for n in range(split):
            block = held[slot, (depth - n + split) % split].astype(F32)
            add_squares(block)
            lo = 0
            for ref in out_refs:
                ref[n * rows : n * rows + rows, :] = block[:, lo : lo + ref.shape[1]]
                lo += ref.shape[1]
    else:
        block = held[slot].astype(F32)
        add_squares(block)
        each = held.shape[0] // len(out_refs)
        for n, ref in enumerate(out_refs):

            @pl.when(slot // each == n)
            def _():
                ref[...] = block
    if skip is not None:
        small_ref = refs[4]

        @pl.when(slot == held.shape[0] - 1)
        def _():
            short = small_ref[...]
            row = lax.broadcasted_iota(jnp.int32, short.shape, 0)
            mine = (row >= skip[0]) & (row < skip[1])
            parts = row >= short.shape[0] - 8
            others = jnp.where(mine, 0.0, jnp.where(parts, short, short * short))
            turned = jnp.where(mine, short * short, 0.0)
            total_ref[0:1, :] = jnp.full((1, 128), jnp.sum(turned))
            total_ref[1:2, :] = jnp.full((1, 128), jnp.sum(others) + jnp.sum(squares[...]))


def assemble_call(place, arrays, shapes, split, small=None, skip=None):
    pieces = 8
    rows = arrays[0].shape[-2] * max(split, 1)
    each = pieces if split else pieces // len(shapes)

    def spec(n, shape):
        lead = 0 if split else n * each
        return pl.BlockSpec((rows, shape[1]), lambda i: (jnp.clip(i - lead, 0, each - 1), 0))

    specs = [spec(n, shape) for n, shape in enumerate(shapes)] + [whole((8, 128))]
    shapes = shapes + [(8, 128)]
    given = []
    if small is not None:
        given, specs, shapes = [small], specs + [whole((2, 128))], shapes + [(2, 128)]
    return pl.pallas_call(
        functools.partial(assemble_kernel, split=split, outs=len(shapes), skip=skip),
        grid=(pieces,),
        in_specs=[SMEM] + [ANY] * len(arrays) + [whole(x.shape) for x in given],
        out_specs=specs,
        out_shape=[jax.ShapeDtypeStruct(s, F32) for s in shapes],
        scratch_shapes=[
            pltpu.VMEM((pieces,) + arrays[0].shape[1:], BF),
            pltpu.SemaphoreType.DMA((pieces,)),
        ],
        compiler_params=params(16),
        cost_estimate=cost(6),
        name="assemble",
    )(place, *arrays, *given)


def send(x, axis, pairs):
    return lax.ppermute(x, axis, pairs)


def plane_gather(piece):
    pair = jnp.stack([piece, send(piece, PLANE, FIRST)])
    return pair, send(pair, PLANE, SECOND)


def core_gather(pair, last):
    return [pair, last, send(pair, "c", SWAP), send(last, "c", SWAP)]


def wide_sum(x, extra):
    return lax.psum(x, "e") if extra > 1 else x


def sum_low(*terms):
    return functools.reduce(lambda x, y: x + y, [t.astype(F32) for t in terms])


def after(x, *others):
    return lax.optimization_barrier((x, others))[0]


def ring(size, step):
    return [(i, (i + step) % size) for i in range(size)]


def add_from(vector, axis, reach=0, size=2):
    return vector + send(vector, axis, [(i, i ^ (reach or 1)) for i in range(size)])


def on_device(
    tokens,
    segment,
    padding,
    coords,
    ln1_gain,
    ln1_shift,
    query_key_value_weight,
    b_qkv,
    output_weight,
    b_out,
    rope_freqs,
    ln2_gain,
    ln2_shift,
    w_up,
    b_up,
    w_down,
    b_down,
    cotangent,
    *,
    extra,
    depth,
):
    tokens, cotangent = tokens[0], cotangent[0]
    own, width = tokens.shape
    length = own * depth
    heads = rope_freqs.shape[1]
    half = width // heads // 2
    groups = heads // GROUP
    slices = 8
    outer = BLK
    side = own + outer
    win = own + 2 * side
    blocks = own // BLK
    z = lax.axis_index("n")
    plane = lax.axis_index("a") * 4 + lax.axis_index("b") * 2 + lax.axis_index("c")
    place = jnp.stack([plane, z]).astype(jnp.int32)
    up = [(i, i + 1) for i in range(depth - 1)]
    down = [(i + 1, i) for i in range(depth - 1)]
    up2 = [(i, i + 2) for i in range(depth - 2)]
    down2 = [(i + 2, i) for i in range(depth - 2)]

    def around(x, head, tail):
        before2 = send(tail, "n", up2)
        before = send(x, "n", up)
        after_ = send(x, "n", down)
        after2 = send(head, "n", down2)
        return [before2, before, after_, after2]

    position = jnp.arange(length, dtype=jnp.int32)
    ident = jnp.where(padding[0] == 0, segment[0], 1000 + position)
    ident = jnp.concatenate(
        [jnp.full((side,), -1, jnp.int32), ident, jnp.full((side,), 1 << 20, jnp.int32)]
    )
    ident_win = lax.dynamic_slice_in_dim(ident, z * own, win, 0)
    near = lax.broadcasted_iota(jnp.int32, (win,), 0)
    ident_win = jnp.where(near < outer - REACH, -1, ident_win)
    ident_win = jnp.where(near >= win - outer + REACH, 1 << 20, ident_win)
    idk = jnp.broadcast_to(ident_win[:, None], (win, BLK))
    idq = ident_win.reshape(win // BLK, BLK)

    lowest, highest = idq[:, 0], idq[:, BLK - 1]

    def bounds(queries, keys):
        before = highest[keys][None, :] < lowest[queries][:, None]
        reached = lowest[keys][None, :] <= highest[queries][:, None]
        return jnp.sum(before, 1), jnp.sum(reached, 1)

    def steps(blocks, span):
        return (jnp.maximum(blocks, 0) + span - 1) // span

    mid = slice(side // BLK, side // BLK + blocks)
    lo, hi = bounds(mid, slice(None))
    bounds_fwd = [
        lo, steps(hi - lo, SPAN), jnp.minimum(lo, mid.start), steps(mid.start - lo, SPAN_SIDE),
        steps(hi - mid.stop, SPAN_SIDE),
    ]
    bounds_fwd = jnp.stack(bounds_fwd, 1).astype(jnp.int32)
    lo, hi = bounds(slice(None), mid)
    bounds_bwd = jnp.stack([lo, steps(hi - lo, SPAN_BACK)], 1).astype(jnp.int32)

    grid = jnp.pad(coords[:, 0], ((0, 0), (side, side)))
    grid_win = lax.dynamic_slice_in_dim(grid, z * own, win, 1)
    grid_own = lax.dynamic_slice_in_dim(grid, z * own + side, own, 1)
    lane = jnp.arange(4 * SIDE)
    picked = jnp.where(lane[None, :] < 2 * SIDE, grid_win[0][:, None], grid_win[1][:, None])
    onehot = (picked == (lane % SIDE)[None, :]).astype(BF)
    table = turn_table(rope_freqs)

    local = np.arange(256)
    order = np.zeros((256, 256), np.float32)
    order[(local % 128) // 32 * 64 + local // 128 * 32 + local % 32, local] = 1.0
    order = jnp.asarray(order, BF)
    qk_bias = b_qkv[: 2 * width].reshape(2 * groups, GROUP, 2, half).swapaxes(1, 2)
    bias_turned = jnp.concatenate([qk_bias.reshape(-1), b_qkv[2 * width :]])

    x_parts = around(tokens, tokens[:REACH], tokens[own - REACH :])
    vectors = jnp.stack([ln1_gain, ln1_shift, b_out, ln2_gain, ln2_shift, b_down])
    rot_q, rot_k, values, q_exact, k_exact, weight_turned = qkv_own_call(
        tokens, onehot, vectors, query_key_value_weight, bias_turned, order, table, side
    )
    rows = (width + w_down.shape[0]) // slices
    eighth = jnp.where(
        plane < width // rows,
        lax.dynamic_slice_in_dim(w_up, jnp.minimum(plane * rows, width - rows), rows, 0),
        lax.dynamic_slice_in_dim(w_down, jnp.maximum(plane * rows - width, 0), rows, 0),
    )
    left, bias_rows = b_up, []
    for _ in range(3):
        bias_rows.append(left.astype(BF))
        left = left - rounded(left)
    bias_rows = jnp.pad(jnp.stack(bias_rows), ((0, 13), (0, 0)))
    eighth = jnp.concatenate([eighth, bias_rows], 0)
    others = [send(eighth, "n", ring(depth, k)) for k in range(1, depth)]
    x_parts, rot_q, idk = lax.optimization_barrier((x_parts, rot_q, idk))
    halo_args = (x_parts, onehot, vectors, weight_turned, bias_turned, table)
    rot_q, rot_k, values = halo_call(*halo_args, (rot_q, rot_k, values), (0, 1, 2), side)
    part = forward_call(bounds_fwd, rot_q, rot_k, values, idk, idq, side, own, 0, blocks // 2)
    others, part = lax.optimization_barrier((others, part))
    up_biases = jnp.concatenate(
        [jnp.sum(x[rows : rows + 3].astype(F32), 0, keepdims=True) for x in others]
    )
    own_w = jnp.stack([x[:rows] for x in others])
    over_1, over_2 = send(own_w, PLANE, FIRST), send(own_w, PLANE, SECOND)
    part, _ = lax.optimization_barrier((part, own_w))
    mixed, mixed_low, lse = forward_call(
        bounds_fwd, rot_q, rot_k, values, idk, idq, side, own, blocks // 2, blocks // 2, part
    )
    hidden_in, norm2, out0, dn0, up_sum0, kept_own, sent_own = middle_own_call(
        place, tokens, mixed_low, output_weight, vectors, cotangent, b_up[None],
        w_up, w_down, slices,
    )
    over_1, over_2, norm2 = lax.optimization_barrier((over_1, over_2, norm2))
    diagonal = send(over_1, PLANE, SECOND)
    near = [own_w, over_1, over_2, diagonal]
    pieces = near + [send(x, "c", SWAP) for x in near]
    grid8 = jnp.pad(grid_own.astype(F32), ((0, 6), (0, 0)))
    far_own = send(after(sent_own, over_1, over_2), "c", SWAP)
    away_own = sum_low(kept_own[1::2], far_own[1::2]).astype(BF)
    got_own = [send(away_own, PLANE, FIRST)]
    norm2, up_biases, bounds_bwd, _ = lax.optimization_barrier(
        (norm2, up_biases, bounds_bwd, away_own)
    )
    (
        activations, d_hidden, d_heads, d_head, d_tail, delta, small_mid, up_sums, kept_mid,
        sent_mid,
    ) = middle_call(
        place, hidden_in, norm2, out0, dn0, mixed_low, mixed, output_weight, vectors, cotangent,
        up_biases, lse, pieces, slices,
    )
    far_mid = send(sent_mid, "c", SWAP)
    do_parts = around(d_heads, d_head, d_tail)

    got_own[0], far_mid = lax.optimization_barrier((got_own[0], far_mid))
    away_own = sum_low(kept_own[2], far_own[2], got_own[0][1]).astype(BF)
    got_own.append(send(away_own, PLANE, SECOND))
    away = sum_low(kept_mid[1::2], far_mid[1::2]).astype(BF)
    got_1 = send(away, PLANE, FIRST)
    dq, dk, dv = backward_own_call(
        bounds_fwd, rot_q, d_heads, rot_k, values, idk, idq, lse, after(delta, away, away_own),
        side, own,
    )
    got_1, got_own[1], dq = lax.optimization_barrier((got_1, got_own[1], dq))
    away = sum_low(kept_mid[2], far_mid[2], got_1[1]).astype(BF)
    got_2 = send(away, PLANE, SECOND)
    do_parts, dq, dk, _ = lax.optimization_barrier((do_parts, dq, dk, away))
    dk, dv = backward_halo_call(
        bounds_bwd, rot_q, do_parts, rot_k, values, idk, idq, dk, dv, side
    )
    got_2, dk = lax.optimization_barrier((got_2, dk))

    def plane_part(lo, hi):
        at = slice(lo, hi)
        total = sum_low(kept_mid[0, at], far_mid[0, at], got_1[0, at], got_2[at])
        return wide_sum(total, extra)

    ff_sent = [plane_part(k * rows - rows, k * rows).astype(BF) for k in range(1, depth)]
    ff_got = [send(x, "n", ring(depth, -1 - k)) for k, x in enumerate(ff_sent)]
    dk = after(dk, ff_sent)

    d_qkv, grad_b_qkv, freqs8, kept_qkv, sent_qkv = turn_back_call(
        place, tokens, vectors, dq, dk, dv, q_exact, k_exact, onehot, table, grid8,
        order.T, side, slices,
    )
    far_qkv = send(sent_qkv, "c", SWAP)
    away = sum_low(kept_qkv[1::2], far_qkv[1::2]).astype(BF)
    got_1_qkv = send(away, PLANE, FIRST)
    input_grad, small_in = input_grad_call(
        place, tokens, vectors, after(d_qkv, away), query_key_value_weight, d_hidden,
        grad_b_qkv, small_mid, freqs8, up_sum0, up_sums,
    )
    away = sum_low(kept_qkv[2], far_qkv[2], got_1_qkv[1]).astype(BF)
    got_2_qkv = send(away, PLANE, SECOND)
    plane_qkv = wide_sum(sum_low(kept_qkv[0], far_qkv[0], got_1_qkv[0], got_2_qkv), extra)

    sizes = [width, width, 3 * width, width, rope_freqs.size] + [width] * 3 + [b_up.size * depth]

    part = plane_part((depth - 1) * rows, (depth - 1) * rows + width // slices)
    part = jnp.concatenate([plane_qkv, part], 1).astype(BF)
    part, ff_got = lax.optimization_barrier((part, ff_got))
    thin = part.shape[0] // depth
    cut = lambda k: lax.dynamic_slice_in_dim(part, ((z + k) % depth) * thin, thin, 0)
    got = [send(cut(k), "n", ring(depth, k)) for k in range(1, depth)]
    small = add_from(add_from(add_from(after(small_in, part), "c"), "b"), "a")
    if extra > 1:
        small = lax.psum(small, "e")
    got, small = lax.optimization_barrier((got, small))
    low = sum_low(cut(0), *got).astype(BF)
    strip = jnp.stack([low] + [send(low, "n", ring(depth, k)) for k in range(1, depth)])
    ff_total = wide_sum(sum_low(kept_own[0], far_own[0], got_own[0][0], got_own[1]), extra)
    ff_total = ff_total + sum_low(*ff_got)
    ff_pair, ff_last = plane_gather(after(ff_total, low).astype(BF))
    pair, last = plane_gather(strip)
    ff_pieces = [after(x, strip) for x in core_gather(ff_pair, ff_last)]
    total_w_up, total_w_down, ff_squares = assemble_call(
        place, ff_pieces, [w_up.shape, w_down.shape], 0
    )
    small = jnp.concatenate([small, ff_squares], 0)
    reach = 1
    while reach < depth:
        small = add_from(small, "n", reach, depth)
        reach *= 2
    last, small = lax.optimization_barrier((last, small))
    turned = sum(sizes[:4]) // 128
    total_w_qkv, total_w_out, _, norms = assemble_call(
        place, core_gather(pair, last), [query_key_value_weight.shape, output_weight.shape], depth,
        small, (turned, turned + sizes[4] // 128),
    )
    small = small[:-8].reshape(-1)
    out, at = [], 0
    for size in sizes:
        out.append(small[at : at + size])
        at += size
    t_gain1, t_shift1, t_b_qkv, t_b_out, t_freqs, t_gain2, t_shift2, t_b_down, t_up = out
    t_freqs = t_freqs.reshape(rope_freqs.shape)
    rot_sq, other_sq = norms[0, 0], norms[1, 0]
    t_b_up = lax.dynamic_slice_in_dim(t_up, z * b_up.shape[0], b_up.shape[0], 0)
    return (
        activations[None],
        input_grad[None],
        t_gain1,
        t_shift1,
        total_w_qkv,
        t_b_qkv,
        total_w_out,
        t_b_out,
        t_freqs,
        t_gain2,
        t_shift2,
        total_w_up,
        t_b_up,
        total_w_down,
        t_b_down,
        rot_sq,
        other_sq,
    )


def solution(mesh):
    wide, depth = mesh.shape["wide"], mesh.shape["narrow"]
    extra = wide // 8
    fine = Mesh(mesh.devices.reshape(extra, 2, 2, 2, depth), ("e", "a", "b", "c", "n"))
    w, n = ("e", "a", "b", "c"), "n"
    return jax.shard_map(
        functools.partial(on_device, extra=extra, depth=depth),
        mesh=fine,
        in_specs=(
            P(w, n, None), P(w, None), P(w, None), P(None, w, None),
            P(), P(), P(), P(), P(), P(), P(), P(), P(),
            P(None, n), P(n), P(n, None), P(), P(w, n, None),
        ),
        out_specs=(
            P(w, n, None), P(w, n, None),
            P(), P(), P(), P(), P(), P(), P(), P(), P(),
            P(None, n), P(n), P(n, None), P(), P(), P(),
        ),
        check_vma=False,
    )
```

```python
import functools

import jax
import jax.numpy as jnp
import numpy as np
from jax import lax
from jax.experimental import pallas as pl
from jax.experimental.pallas import tpu as pltpu
from jax.sharding import Mesh, PartitionSpec as P

EPS = 1e-06
MASKED = -1e30
BLK = 128
SPAN = 6
SPAN_SIDE = 3
SPAN_BACK = 2
GROUP = 4
REACH = 64
STAT_ROWS = 6
STAT_PAD = 16
SIDE = 32
LN1_GAIN, LN1_SHIFT, B_OUT, LN2_GAIN, LN2_SHIFT, B_DOWN = (slice(n, n + 1) for n in range(6))
LOG2E = np.float32(1.4426950408889634)
BF = jnp.bfloat16
F32 = jnp.float32
PLANE = ("a", "b", "c")
SWAP = [(0, 1), (1, 0)]
FIRST = [(i, i ^ (4 if i % 2 else 2)) for i in range(8)]
SECOND = [(i, i ^ (2 if i % 2 else 4)) for i in range(8)]


def dot(left, right):
    return lax.dot_general(left, right, (((1,), (0,)), ((), ())), preferred_element_type=F32)


def dot_nt(left, right):
    return lax.dot_general(left, right, (((1,), (1,)), ((), ())), preferred_element_type=F32)


def dot_tn(left, right):
    return lax.dot_general(left, right, (((0,), (0,)), ((), ())), preferred_element_type=F32)


def params(mebibytes):
    return pltpu.CompilerParams(vmem_limit_bytes=mebibytes * 1024 * 1024)


def cost(us):
    return pl.CostEstimate(
        flops=int(us * 1.15e9), bytes_accessed=int(us * 3.0e6), transcendentals=0
    )


def whole(shape):
    return pl.BlockSpec(shape, lambda *_: (0,) * len(shape))


ANY = pl.BlockSpec(memory_space=pl.ANY)
SMEM = pl.BlockSpec(memory_space=pltpu.SMEM)


def rounded(x):
    return lax.reduce_precision(x, exponent_bits=8, mantissa_bits=7)


def turn_table(rope_freqs):
    lanes = rope_freqs.shape[1] * rope_freqs.shape[2]
    freq = rope_freqs.reshape(2, 1, lanes)
    angle = jnp.arange(SIDE, dtype=F32)[None, :, None] * freq
    cosine, sine = jnp.cos(angle), jnp.sin(angle)

    def halves(x):
        return jnp.concatenate([x.astype(BF), (x - rounded(x)).astype(BF)], 0)

    def grouped(x):
        return x.reshape(2 * SIDE, lanes // 128, 1, 128)

    zero = jnp.zeros((2 * SIDE, lanes // 128, 2, 128), BF)
    rows = jnp.concatenate([grouped(halves(cosine[0])), grouped(halves(sine[0])), zero], 2)
    cols = jnp.concatenate([zero, grouped(halves(cosine[1])), grouped(halves(sine[1]))], 2)
    return jnp.concatenate([rows, cols], 0).reshape(4 * SIDE, 4 * lanes)


def cos_sin(onehot, table):
    parts = dot(onehot, table)
    cr, sr, cc, sc = (parts[:, lanes_of(n, 128)] for n in range(4))
    return cr * cc - sr * sc, sr * cc + cr * sc


def layer_norm_low(x, gain, shift):
    centred = x - jnp.mean(x, -1, keepdims=True)
    var = jnp.mean(centred * centred, -1, keepdims=True)
    return (centred * lax.rsqrt(var + EPS) * gain + shift).astype(BF)


def project(norm, hot_ref, table_ref, weights, b_ref, outs, exact=()):
    width = norm.shape[1]
    for g in range(width // 256):
        c, s = cos_sin(hot_ref[...], table_ref[:, lanes_of(g, 512)])
        for n, out in outs:
            lo = n * width + 256 * g
            proj = dot(norm, weights[:, lo : lo + 256]) + b_ref[:, lo : lo + 256]
            if n == 2:
                out[:, lanes_of(g)] = proj.astype(BF)
                continue
            for half, turned in enumerate(
                (proj[:, :128] * c - proj[:, 128:] * s, proj[:, :128] * s + proj[:, 128:] * c)
            ):
                at = slice(256 * g + 128 * half, 256 * g + 128 * half + 128)
                out[:, at] = turned.astype(BF)
                if exact:
                    exact[n][:, at] = turned


def qkv_own_kernel(
    x_ref, hot_ref, vec_ref, w_ref, b_ref, order_ref, table_ref,
    q_ref, k_ref, v_ref, pq_ref, pk_ref, w_turned,
):
    width = x_ref.shape[1]

    @pl.when(pl.program_id(0) == 0)
    def _():
        for g in range(2 * width // 256):
            at = slice(256 * g, 256 * g + 256)
            w_turned[:, at] = dot(w_ref[:, at], order_ref[...]).astype(BF)
        w_turned[:, 2 * width :] = w_ref[:, 2 * width :]

    norm = layer_norm_low(x_ref[...].astype(F32), vec_ref[LN1_GAIN], vec_ref[LN1_SHIFT])
    outs = [(0, q_ref), (1, k_ref), (2, v_ref)]
    project(norm, hot_ref, table_ref, w_turned, b_ref, outs, (pq_ref, pk_ref))


def qkv_own_call(x, onehot, vectors, weight, bias, order, table, first):
    own, width = x.shape
    rows = onehot.shape[0]
    tile = 256
    shape = jax.ShapeDtypeStruct((rows, width), BF)
    exact = jax.ShapeDtypeStruct((own, width), F32)
    row = lambda w: pl.BlockSpec((tile, w), lambda i: (i, 0))
    inside = lambda w: pl.BlockSpec(
        (pl.Element(tile), pl.Element(w)), lambda i: (pl.multiple_of(first + tile * i, BLK), 0)
    )
    return pl.pallas_call(
        qkv_own_kernel,
        grid=(own // tile,),
        in_specs=[
            row(width),
            inside(onehot.shape[1]),
            whole(vectors.shape),
            whole(weight.shape),
            whole((1, 3 * width)),
            whole(order.shape),
            whole(table.shape),
        ],
        out_specs=[inside(width)] * 3 + [row(width)] * 2 + [whole(weight.shape)],
        out_shape=[shape] * 3 + [exact] * 2 + [jax.ShapeDtypeStruct(weight.shape, BF)],
        compiler_params=params(56),
        cost_estimate=cost(8),
        name="qkv_own",
    )(x, onehot, vectors, weight, bias[None], order, table)


def halo_kernel(
    far_l, near_l, near_r, far_r, hot_ref, vec_ref, w_ref, b_ref, table_ref, *refs, which
):
    refs = refs[len(which) :]
    out_refs, (x_all, sem) = refs[: len(which)], refs[len(which) :]
    width = x_all.shape[1]
    step = pl.program_id(0)
    tile = out_refs[0].shape[0]

    @pl.when(step == 0)
    def _():
        own, reach = near_l.shape[0], far_l.shape[0]
        total = x_all.shape[0]
        blank = total // 2 - own - reach
        copies = []
        at = blank
        for n, ref in enumerate((far_l, near_l, near_r, far_r)):
            copies.append(
                pltpu.make_async_copy(ref, x_all.at[at : at + ref.shape[0], :], sem.at[n])
            )
            copies[-1].start()
            at += ref.shape[0]
        x_all[:blank, :] = jnp.zeros((blank, width), BF)
        x_all[total - blank :, :] = jnp.zeros((blank, width), BF)
        for copy in copies:
            copy.wait()

    x = x_all[pl.ds(pl.multiple_of(step * tile, tile), tile), :].astype(F32)
    norm = layer_norm_low(x, vec_ref[LN1_GAIN], vec_ref[LN1_SHIFT])
    project(norm, hot_ref, table_ref, w_ref, b_ref, list(zip(which, out_refs)))


def halo_call(pieces, onehot, vectors, weight, bias, table, arrays, which, first):
    rows, width = arrays[0].shape
    own = pieces[1].shape[0]
    tile = first // 2
    at = lambda w: pl.BlockSpec(
        (pl.Element(tile), pl.Element(w)),
        lambda i: (pl.multiple_of(tile * i + jnp.where(i >= 2, own, 0), 64), 0),
    )
    return pl.pallas_call(
        functools.partial(halo_kernel, which=which),
        grid=(4,),
        in_specs=[ANY] * 4
        + [
            at(onehot.shape[1]),
            whole(vectors.shape),
            whole(weight.shape),
            whole((1, 3 * width)),
            whole(table.shape),
        ]
        + [ANY] * len(which),
        out_specs=[at(width)] * len(which),
        out_shape=[jax.ShapeDtypeStruct((rows, width), BF)] * len(which),
        input_output_aliases={9 + n: n for n in range(len(which))},
        scratch_shapes=[pltpu.VMEM((2 * first, width), BF), pltpu.SemaphoreType.DMA((4,))],
        compiler_params=params(56),
        cost_estimate=cost(4 * len(which)),
        name="halo",
    )(*pieces, onehot, vectors, weight, bias[None], table, *arrays)


def head_stack(block, turned, scale=None):
    lane = lax.broadcasted_iota(jnp.int32, block.shape, 1)
    head = (lane % 128) // 32 if turned else lane // 64
    if scale is not None:
        block = block * scale
    zero = jnp.zeros_like(block)
    return jnp.concatenate([jnp.where(head == h, block, zero) for h in range(GROUP)], 0)


def fold8(x, op):
    return op(x.reshape(x.shape[0] // 8, 8, x.shape[1]), axis=0)


def key_span(ident_ref, ident_q, start, c, span, end):
    block = jnp.minimum(start + c * span, end - span)
    lower = (start + c * span - block) * BLK
    at = pl.ds(pl.multiple_of(block * BLK, BLK), span * BLK)
    row = lax.broadcasted_iota(jnp.int32, (span * BLK, BLK), 0)
    return at, (ident_ref[at, :] == ident_q) & (row >= lower)


def lanes_of(g, size=256):
    return slice(size * g, size * g + size)


def forward_kernel(
    bound_ref, q_ref, k_ref, v_ref, idk_ref, idq_ref, *refs, first, base
):
    o_ref, low_ref, lse_ref, s_ref, acc_ref, q4_ref = refs[-6:]
    i = pl.program_id(0) + base
    groups = k_ref.shape[1] // 256
    lanes = GROUP * BLK
    window = k_ref.shape[0] // BLK
    start, count = bound_ref[i, 0], bound_ref[i, 1]
    for g in range(groups):
        q4_ref[g] = head_stack(q_ref[:, lanes_of(g)], True, jnp.asarray(0.125, BF))
    ident_q = idq_ref[pl.ds(first // BLK + i, 1), :]

    def scores(c, top):
        at, seen = key_span(idk_ref, ident_q, start, c, SPAN, window)
        here = pl.ds(pl.multiple_of(c * SPAN * BLK, BLK), SPAN * BLK)
        tops = []
        for g in range(groups):
            s = dot_nt(k_ref[at, lanes_of(g)], q4_ref[g]) * LOG2E
            for h in range(GROUP):
                masked = jnp.where(seen, s[:, lanes_of(h, BLK)], MASKED)
                s_ref[g, here, lanes_of(h, BLK)] = masked
                tops.append(fold8(masked, jnp.max))
        return jnp.maximum(top, jnp.concatenate(tops, 1))

    top = lax.fori_loop(0, count, scores, jnp.full((8, groups * lanes), -3e38, F32))
    top = jnp.max(top, 0, keepdims=True)
    acc_ref[...] = jnp.zeros_like(acc_ref)

    def mix(c, total):
        at, _ = key_span(idk_ref, ident_q, start, c, SPAN, window)
        here = pl.ds(pl.multiple_of(c * SPAN * BLK, BLK), SPAN * BLK)
        sums = []
        for g in range(groups):
            e = jnp.exp2(s_ref[g, here, :] - top[:, lanes_of(g, lanes)])
            sums.append(fold8(e, jnp.sum))
            acc_ref[g] += dot_tn(v_ref[at, lanes_of(g)], e.astype(BF))
        return total + jnp.concatenate(sums, 1)

    total = lax.fori_loop(0, count, mix, jnp.zeros((8, groups * lanes), F32))
    total = jnp.sum(total, 0, keepdims=True)
    lse = top + jnp.log(total) * LOG2E
    inverse = 1.0 / total
    for g in range(groups):
        lse_ref[g] = lse[:, lanes_of(g, lanes)]
        acc = acc_ref[g] * inverse[:, lanes_of(g, lanes)]
        out = jnp.concatenate(
            [acc[64 * h : 64 * h + 64, lanes_of(h, BLK)] for h in range(GROUP)], 0
        ).T
        o_ref[:, lanes_of(g)] = out
        low_ref[:, lanes_of(g)] = out.astype(BF)


def stat_spec(groups, base=0):
    return pl.BlockSpec((groups, None, 1, GROUP * BLK), lambda i: (0, i + base, 0, 0))


def query_rows(first, width):
    return pl.BlockSpec(
        (pl.Element(BLK), pl.Element(width)), lambda i: (pl.multiple_of(first + BLK * i, BLK), 0)
    )


def forward_call(bounds, q_win, k_win, v_win, idk, idq, first, own, base, count, earlier=()):
    win, width = k_win.shape
    groups, blocks = width // 256, own // BLK
    row = pl.BlockSpec((BLK, width), lambda i: (i + base, 0))
    steps = -(-win // (SPAN * BLK))
    return pl.pallas_call(
        functools.partial(forward_kernel, first=first, base=base),
        grid=(count,),
        in_specs=[SMEM, query_rows(first + base * BLK, width)]
        + [whole((win, width))] * 2
        + [whole(idk.shape), whole(idq.shape)]
        + [ANY] * len(earlier),
        out_specs=[row, row, stat_spec(groups, base)],
        input_output_aliases={6 + n: n for n in range(len(earlier))},
        out_shape=[
            jax.ShapeDtypeStruct((own, width), F32),
            jax.ShapeDtypeStruct((own, width), BF),
            jax.ShapeDtypeStruct((groups, blocks, 1, GROUP * BLK), F32),
        ],
        scratch_shapes=[
            pltpu.VMEM((groups, steps * SPAN * BLK, GROUP * BLK), F32),
            pltpu.VMEM((groups, 256, GROUP * BLK), F32),
            pltpu.VMEM((groups, GROUP * BLK, 256), BF),
        ],
        compiler_params=params(56),
        cost_estimate=cost(4 * count),
        name="attention_forward",
    )(bounds, q_win, k_win, v_win, idk, idq, *earlier)


def score_gradients(s, dp, lse, delta, seen):
    low_p, low_ds = [], []
    for h in range(GROUP):
        at = lanes_of(h, BLK)
        p = jnp.exp2(jnp.where(seen, s[:, at] * LOG2E - lse[:, at], MASKED))
        low_p.append(p.astype(BF))
        low_ds.append((p * (dp[:, at] - delta[:, at])).astype(BF))
    return jnp.concatenate(low_p, 1), jnp.concatenate(low_ds, 1)


def backward_own_kernel(
    bound_ref, q_ref, do_ref, k_ref, v_ref, idk_ref, idq_ref, lse_ref, delta_ref,
    dq_ref, dk_ref, dv_ref, acc_ref, q4_ref, do4_ref, *, first,
):
    i = pl.program_id(0)
    groups = k_ref.shape[1] // 256
    own = dk_ref.shape[0]

    @pl.when(i == 0)
    def _():
        dk_ref[...] = jnp.zeros_like(dk_ref)
        dv_ref[...] = jnp.zeros_like(dv_ref)

    for g in range(groups):
        q4_ref[g] = head_stack(q_ref[:, lanes_of(g)], True, jnp.asarray(0.125, BF))
        do4_ref[g] = head_stack(do_ref[:, lanes_of(g)], False)
    ident_q = idq_ref[pl.ds(first // BLK + i, 1), :]

    def attend(at, seen, inside):
        for g in range(groups):
            keys = k_ref[at, lanes_of(g)]
            s = dot_nt(keys, q4_ref[g])
            dp = dot_nt(v_ref[at, lanes_of(g)], do4_ref[g])
            low_p, low_ds = score_gradients(s, dp, lse_ref[g], delta_ref[g], seen)
            if inside:
                acc_ref[g] = dot_tn(keys, low_ds)
                dk_ref[:, lanes_of(g)] += dot(low_ds, q4_ref[g])
                dv_ref[:, lanes_of(g)] += dot(low_p, do4_ref[g])
            else:
                acc_ref[g] += dot_tn(keys, low_ds)

    attend(slice(first, first + own), idk_ref[first : first + own, :] == ident_q, True)
    for start, count, end in (
        (bound_ref[i, 2], bound_ref[i, 3], first // BLK),
        ((first + own) // BLK, bound_ref[i, 4], k_ref.shape[0] // BLK),
    ):

        def step(c, _):
            attend(*key_span(idk_ref, ident_q, start, c, SPAN_SIDE, end), False)
            return 0

        lax.fori_loop(0, count, step, 0)
    for g in range(groups):
        acc = acc_ref[g]
        parts = [acc[32 * h : 32 * h + 32, lanes_of(h, BLK)] for h in range(GROUP)]
        parts += [acc[128 + 32 * h : 160 + 32 * h, lanes_of(h, BLK)] for h in range(GROUP)]
        dq_ref[:, lanes_of(g)] = (jnp.concatenate(parts, 0) * 0.125).T


def backward_own_call(bounds, q_win, do_own, k_win, v_win, idk, idq, lse, delta, first, own):
    win, width = k_win.shape
    groups = width // 256
    row = pl.BlockSpec((BLK, width), lambda i: (i, 0))
    return pl.pallas_call(
        functools.partial(backward_own_kernel, first=first),
        grid=(own // BLK,),
        in_specs=[SMEM, query_rows(first, width), row]
        + [whole((win, width))] * 2
        + [whole(idk.shape), whole(idq.shape), stat_spec(groups), stat_spec(groups)],
        out_specs=[row] + [whole((own, width))] * 2,
        out_shape=[jax.ShapeDtypeStruct((own, width), F32)] * 3,
        scratch_shapes=[pltpu.VMEM((groups, 256, GROUP * BLK), F32)]
        + [pltpu.VMEM((groups, GROUP * BLK, 256), BF)] * 2,
        compiler_params=params(24),
        cost_estimate=cost(20),
        name="attention_backward_own",
    )(bounds, q_win, do_own, k_win, v_win, idk, idq, lse, delta)


def backward_halo_kernel(
    bound_ref, q_ref, far_l, near_l, near_r, far_r, k_ref, v_ref, idk_ref, idq_ref, dk_in, dv_in,
    dk_ref, dv_ref, q4_ref, do_all, do4_ref, stat_ref, *, first,
):
    groups = k_ref.shape[1] // 256
    own, reach = k_ref.shape[0], far_l.shape[0] - STAT_PAD
    blocks = own // BLK
    side = first // BLK
    step_id = pl.program_id(0)
    j = jnp.where(step_id < side, step_id, step_id + blocks)
    lanes = GROUP * BLK

    def stats(ref, row, slot):
        parts = ref[row : row + 2 * STAT_ROWS, :].astype(F32)
        sums = parts[0:4] + parts[4:8] + parts[8:12]
        for g in range(groups):
            for n in range(2):
                stat_ref[n, g, slot : slot + 1, :] = jnp.concatenate(
                    [sums[2 * n : 2 * n + 1, lanes_of(g)], sums[2 * n + 1 : 2 * n + 2, lanes_of(g)]],
                    1,
                )

    @pl.when(step_id == 0)
    def _():
        dk_ref[...] = dk_in[...]
        dv_ref[...] = dv_in[...]
        blank = jnp.zeros((BLK - reach, do_all.shape[1]), BF)
        do_all[0 : BLK - reach, :] = blank
        do_all[BLK - reach : BLK, :] = far_l[:reach, :]
        do_all[BLK : BLK + own, :] = near_l[:own, :]
        do_all[BLK + own : BLK + 2 * own, :] = near_r[:own, :]
        do_all[BLK + 2 * own : BLK + 2 * own + reach, :] = far_r[:reach, :]
        do_all[BLK + 2 * own + reach :, :] = blank
        stats(far_l, reach, 0)
        for i in range(blocks):
            stats(near_l, own + 2 * STAT_ROWS * i, 1 + i)
            stats(near_r, own + 2 * STAT_ROWS * i, 1 + blocks + i)
        stats(far_r, reach, 1 + 2 * blocks)

    start, count = bound_ref[j, 0], bound_ref[j, 1]

    @pl.when(count > 0)
    def _():
        here = pl.ds(pl.multiple_of(step_id * BLK, BLK), BLK)
        for g in range(groups):
            q4_ref[g] = head_stack(q_ref[:, lanes_of(g)], True, jnp.asarray(0.125, BF))
            do4_ref[g] = head_stack(do_all[here, lanes_of(g)], False)
        ident_q = idq_ref[pl.ds(j, 1), :]

        def step(c, _):
            at, seen = key_span(idk_ref, ident_q, start, c, SPAN_BACK, blocks)
            for g in range(groups):
                s = dot_nt(k_ref[at, lanes_of(g)], q4_ref[g])
                dp = dot_nt(v_ref[at, lanes_of(g)], do4_ref[g])
                lse = stat_ref[0, g, pl.ds(step_id, 1), :]
                delta = stat_ref[1, g, pl.ds(step_id, 1), :]
                low_p, low_ds = score_gradients(s, dp, lse, delta, seen)
                dk_ref[at, lanes_of(g)] += dot(low_ds, q4_ref[g])
                dv_ref[at, lanes_of(g)] += dot(low_p, do4_ref[g])
            return 0

        lax.fori_loop(0, count, step, 0)


def backward_halo_call(bounds, q_win, pieces, k_win, v_win, idk, idq, dk, dv, first):
    own, width = dk.shape
    groups = width // 256
    side, blocks = first // BLK, own // BLK
    inside = lambda w: pl.BlockSpec(
        (pl.Element(own), pl.Element(w)), lambda i: (pl.multiple_of(first + 0 * i, BLK), 0)
    )
    outside = pl.BlockSpec((BLK, width), lambda i: (jnp.where(i < side, i, i + blocks), 0))
    return pl.pallas_call(
        functools.partial(backward_halo_kernel, first=first),
        grid=(2 * side,),
        in_specs=[SMEM, outside]
        + [whole(p.shape) for p in pieces]
        + [inside(width)] * 2
        + [inside(idk.shape[1]), whole(idq.shape)]
        + [whole((own, width))] * 2,
        out_specs=[whole((own, width))] * 2,
        out_shape=[jax.ShapeDtypeStruct((own, width), F32)] * 2,
        scratch_shapes=[
            pltpu.VMEM((groups, GROUP * BLK, 256), BF),
            pltpu.VMEM((2 * first, width), BF),
            pltpu.VMEM((groups, GROUP * BLK, 256), BF),
            pltpu.VMEM((2, groups, 16, GROUP * BLK), F32),
        ],
        compiler_params=params(20),
        cost_estimate=cost(11),
        name="attention_backward_halo",
    )(bounds, q_win, *pieces, k_win, v_win, idk, idq, dk, dv)


def norm_parts(x):
    centred = x - jnp.mean(x, -1, keepdims=True)
    inverse = lax.rsqrt(jnp.mean(centred * centred, -1, keepdims=True) + EPS)
    return centred * inverse, inverse


def norm_back(grad, xhat, inverse, gain):
    scaled = grad * gain
    return inverse * (
        scaled
        - jnp.mean(scaled, -1, keepdims=True)
        - xhat * jnp.mean(scaled * xhat, -1, keepdims=True)
    )


def columns_sum(x):
    return jnp.sum(x, 0, keepdims=True)


def chip_order(ab, core):
    return jnp.where(core == 0, ab, ab % 2 * 2 + ab // 2)


def slices_out(place, source, keep, away, lead, sem, slices, rows):
    for n in range(slices):
        rel = place ^ n
        for target, odd in ((keep, 0), (away, 1)):
            core = place % 2 ^ odd

            @pl.when(rel % 2 == odd)
            def _():
                pltpu.make_async_copy(
                    source.at[n * rows : (n + 1) * rows, :],
                    target.at[chip_order(rel // 2, 1 - core), pl.ds(lead, rows), :],
                    sem.at[n],
                ).start()


def gathered(place, refs):
    for far in range(2):
        for n in range(4):
            rel = 2 * chip_order(jnp.int32(n), place % 2 ^ far) + far
            yield refs[4 * far + n], place ^ rel


def slices_wait(source, keep, sem, slices, rows):
    for n in range(slices):
        pltpu.make_async_copy(
            source.at[n * rows : (n + 1) * rows, :], keep.at[0, 0:rows, :], sem.at[n]
        ).wait()


def one_quarter(q, w_all, norm_ref, dy_ref, bu_ref, dbu_ref, out_acc, dn_acc, g_all, fresh):
    own, width = norm_ref.shape
    tile = w_all.shape[1] - width
    for t in range((w_all.shape[1] - width) // tile):
        cols = slice(tile * t, tile * t + tile)
        down = slice(width + tile * t, width + tile * t + tile)
        norm, dy = norm_ref[...], dy_ref[...]
        up_w = w_all[q, :width, cols]
        down_w = w_all[q, down, :]
        pre = dot(norm, up_w) + bu_ref[pl.ds(q, 1), cols]
        cdf = 0.5 * (1.0 + lax.erf(pre * np.float32(0.7071067811865476)))
        density = jnp.exp(-0.5 * pre * pre) * np.float32(0.3989422804014327)
        act = (pre * cdf).astype(BF)
        d_pre = (dot_nt(dy, down_w) * (cdf + pre * density)).astype(BF)
        dbu_ref[pl.ds(q, 1), cols] = columns_sum(d_pre.astype(F32))
        if fresh and t == 0:
            out_acc[...] = dot(act, down_w)
            dn_acc[...] = dot_nt(d_pre, up_w)
        else:
            out_acc[...] += dot(act, down_w)
            dn_acc[...] += dot_nt(d_pre, up_w)
        g_all[q, :width, cols] = dot_tn(norm, d_pre).astype(BF)
        g_all[q, down, :] = dot_tn(act, dy).astype(BF)


def middle_own_kernel(
    place_ref, x_ref, low_ref, wo_ref, vec_ref, dy_ref, bu_ref, up_ref, down_ref,
    hid_ref, norm_ref, out_ref, dn_ref, dbu_ref, keep_ref, send_ref, w_all, g_all, w_sem, g_sem,
    *, slices,
):
    width = x_ref.shape[1]
    rows = w_all.shape[1] // slices
    copies = [
        pltpu.make_async_copy(up_ref, w_all.at[0, :width, :], w_sem.at[0]),
        pltpu.make_async_copy(down_ref, w_all.at[0, width:, :], w_sem.at[1]),
    ]
    for copy in copies:
        copy.start()
    hidden_in = x_ref[...].astype(F32) + dot(low_ref[...], wo_ref[...]) + vec_ref[B_OUT]
    hid_ref[...] = hidden_in
    norm_ref[...] = layer_norm_low(hidden_in, vec_ref[LN2_GAIN], vec_ref[LN2_SHIFT])
    for copy in copies:
        copy.wait()
    one_quarter(0, w_all, norm_ref, dy_ref, bu_ref, dbu_ref, out_ref, dn_ref, g_all, True)
    slices_out(place_ref[0], g_all.at[0], keep_ref, send_ref, 0, g_sem, slices, rows)
    slices_wait(g_all.at[0], keep_ref, g_sem, slices, rows)


def middle_own_call(place, x, low, w_out, vectors, dy, b_up, w_up, w_down, slices):
    own, width = x.shape
    hidden = b_up.shape[1]
    rows = width + hidden
    vmem = pl.BlockSpec(memory_space=pltpu.VMEM)
    sds = jax.ShapeDtypeStruct
    return pl.pallas_call(
        functools.partial(middle_own_kernel, slices=slices),
        in_specs=[SMEM] + [vmem] * 6 + [ANY] * 2,
        out_specs=[vmem] * 5 + [ANY] * 2,
        out_shape=[
            sds((own, width), F32),
            sds((own, width), BF),
            sds((own, width), F32),
            sds((own, width), F32),
            sds((1, hidden), F32),
        ]
        + [sds((slices // 2, rows // slices, width), BF)] * 2,
        scratch_shapes=[
            pltpu.VMEM((1, rows, width), BF),
            pltpu.VMEM((1, rows, width), BF),
            pltpu.SemaphoreType.DMA((2,)),
            pltpu.SemaphoreType.DMA((slices,)),
        ],
        compiler_params=params(56),
        cost_estimate=cost(12),
        name="middle_own",
    )(place, x, low, w_out, vectors, dy, b_up, w_up, w_down)


def middle_kernel(
    place_ref, vec_ref, bu_ref, lse_ref, norm_in, dy_in, out_in, dn_in, hid_in, low_in, mixed_in,
    wo_in, *refs, slices,
):
    piece_refs = refs[:slices]
    (
        act_out, dh_out, dheads_ref, head_ref, tail_ref, delta_ref, small_ref, dbu_ref, keep_ref,
        send_ref,
        w_all, g_all, go_all, norm_ref, dy_ref, out_acc, dn_acc, hid_ref, low_ref, mixed_ref,
        wo_ref, act_ref, dh_ref, w_sem, g_sem, in_sem, out_sem,
    ) = refs[slices:]
    place = place_ref[0]
    own, width = norm_ref.shape
    quarters = w_all.shape[0]
    rows = w_all.shape[1] // slices

    def fetches(q):
        return [
            pltpu.make_async_copy(
                ref.at[q],
                w_all.at[q, pl.ds(pl.multiple_of(source * rows, rows), rows), :],
                w_sem.at[q, n],
            )
            for n, (ref, source) in enumerate(gathered(place, piece_refs))
        ]

    inputs = [
        pltpu.make_async_copy(source, target, in_sem.at[n])
        for n, (source, target) in enumerate(
            (
                (norm_in, norm_ref), (dy_in, dy_ref), (out_in, out_acc), (dn_in, dn_acc),
                (hid_in, hid_ref), (low_in, low_ref), (mixed_in, mixed_ref), (wo_in, wo_ref),
            )
        )
    ]
    for copy in inputs[:2] + fetches(0) + inputs[2:4]:
        copy.start()
    for q in range(1, quarters):
        for copy in fetches(q):
            copy.start()
    for copy in inputs[4:]:
        copy.start()
    for copy in inputs[:2]:
        copy.wait()

    def quarter(q, _):
        for copy in fetches(q):
            copy.wait()

        @pl.when(q == 0)
        def _():
            for copy in inputs[2:4]:
                copy.wait()

        one_quarter(q, w_all, norm_ref, dy_ref, bu_ref, dbu_ref, out_acc, dn_acc, g_all, False)
        slices_out(
            place, g_all.at[q], keep_ref, send_ref, pl.multiple_of(q * rows, rows),
            g_sem.at[q], slices, rows,
        )
        return 0

    lax.fori_loop(0, quarters, quarter, 0)

    for copy in inputs[4:]:
        copy.wait()
    hidden_in = hid_ref[...]
    xhat, inverse = norm_parts(hidden_in)
    dn = dn_acc[...]
    dy = dy_ref[...].astype(F32)
    d_hidden = dy + norm_back(dn, xhat, inverse, vec_ref[LN2_GAIN])
    dh_ref[...] = d_hidden
    d_att = d_hidden.astype(BF)
    d_heads = dot_nt(d_att, wo_ref[...]).astype(BF)
    dheads_ref[:own, :] = d_heads
    go_all[...] = dot_tn(low_ref[...], d_att).astype(BF)
    few = width // slices
    base = quarters * rows
    slices_out(place, go_all, keep_ref, send_ref, base, g_sem.at[quarters], slices, few)
    act_ref[...] = (hidden_in + out_acc[...] + vec_ref[B_DOWN]).astype(BF)
    outputs = [
        pltpu.make_async_copy(source, target, out_sem.at[n])
        for n, (source, target) in enumerate(
            (
                (act_ref, act_out), (dh_ref, dh_out),
            )
        )
    ]
    for copy in outputs:
        copy.start()
    small_ref[0:1, :] = columns_sum(dn * xhat)
    small_ref[1:2, :] = columns_sum(dn)
    small_ref[2:3, :] = columns_sum(dy)
    small_ref[3:4, :] = columns_sum(d_att.astype(F32))
    spread = d_heads.astype(F32) * mixed_ref[...]
    pick = lax.broadcasted_iota(jnp.int32, (8, 256), 0)
    pick = (pick == lax.broadcasted_iota(jnp.int32, (8, 256), 1) // 64).astype(F32)
    for g in range(width // 256):
        for i in range(own // BLK):
            block = spread[BLK * i : BLK * i + BLK, 256 * g : 256 * g + 256]
            sums = lax.dot_general(
                pick, block, (((1,), (1,)), ((), ())),
                preferred_element_type=F32, precision=lax.Precision.HIGHEST,
            )
            delta = jnp.concatenate([sums[h : h + 1, :] for h in range(GROUP)], 1)
            delta_ref[g, i] = delta
            lse = lse_ref[g, i]
            left = jnp.concatenate(
                [lse[:, :256], lse[:, 256:], delta[:, :256], delta[:, 256:]], 0
            )
            parts = []
            for _ in range(3):
                parts.append(left.astype(BF))
                left = left - parts[-1].astype(F32)
            parts = jnp.concatenate(parts, 0)
            at = slice(256 * g, 256 * g + 256)
            lo = own + 2 * STAT_ROWS * i
            dheads_ref[lo : lo + 2 * STAT_ROWS, at] = parts
            for target, row in ((head_ref, 0), (tail_ref, own // BLK - 1)):
                if i == row:
                    target[REACH : REACH + 2 * STAT_ROWS, at] = parts
    blank = jnp.zeros((STAT_PAD - 2 * STAT_ROWS, width), BF)
    head_ref[REACH + 2 * STAT_ROWS :, :] = blank
    tail_ref[REACH + 2 * STAT_ROWS :, :] = blank
    head_ref[:REACH, :] = d_heads[:REACH, :]
    tail_ref[:REACH, :] = d_heads[own - REACH :, :]
    for q in range(quarters):
        slices_wait(g_all.at[q], keep_ref, g_sem.at[q], slices, rows)
    slices_wait(go_all, keep_ref, g_sem.at[quarters], slices, few)
    for copy in outputs:
        copy.wait()


def middle_call(
    place, hidden_in, norm, out, dn, low, mixed, w_out, vectors, dy, b_up, lse, pieces, slices,
):
    own, width = norm.shape
    quarters, hidden = b_up.shape
    rows = width + hidden
    vmem = pl.BlockSpec(memory_space=pltpu.VMEM)
    sds = jax.ShapeDtypeStruct
    grads = sds((slices // 2, (quarters * rows + width) // slices, width), BF)
    return pl.pallas_call(
        functools.partial(middle_kernel, slices=slices),
        in_specs=[SMEM] + [vmem] * 3 + [ANY] * (8 + len(pieces)),
        out_specs=[ANY] * 2 + [vmem] * 6 + [ANY] * 2,
        out_shape=[
            sds((own, width), BF),
            sds((own, width), F32),
            sds((own + own // BLK * 2 * STAT_ROWS, width), BF),
            sds((REACH + STAT_PAD, width), BF),
            sds((REACH + STAT_PAD, width), BF),
            sds((width // 256, own // BLK, 1, GROUP * BLK), F32),
            sds((4, width), F32),
            sds((quarters, hidden), F32),
            grads,
            grads,
        ],
        scratch_shapes=[
            pltpu.VMEM((quarters, rows, width), BF),
            pltpu.VMEM((quarters, rows, width), BF),
            pltpu.VMEM((width, width), BF),
            pltpu.VMEM((own, width), BF),
            pltpu.VMEM((own, width), BF),
            pltpu.VMEM((own, width), F32),
            pltpu.VMEM((own, width), F32),
            pltpu.VMEM((own, width), F32),
            pltpu.VMEM((own, width), BF),
            pltpu.VMEM((own, width), F32),
            pltpu.VMEM((width, width), BF),
            pltpu.VMEM((own, width), BF),
            pltpu.VMEM((own, width), F32),
            pltpu.SemaphoreType.DMA((quarters, slices)),
            pltpu.SemaphoreType.DMA((quarters + 1, slices)),
            pltpu.SemaphoreType.DMA((10,)),
            pltpu.SemaphoreType.DMA((4,)),
        ],
        compiler_params=params(44),
        cost_estimate=cost(20),
        name="middle",
    )(
        place, vectors, b_up, lse, norm, dy, out, dn, hidden_in, low, mixed, w_out, *pieces,
    )


def turn_back_kernel(
    place_ref, x_ref, vec_ref, dq_ref, dk_ref, dv_ref, q_ref, k_ref, hot_ref, table_ref, grid_ref,
    back_ref, d_ref, db_ref, freq_ref, keep_ref, send_ref, norm_ref, g_all, sem, *, slices,
):
    width = x_ref.shape[1]
    group = pl.program_id(0)

    @pl.when(group == 0)
    def _():
        norm_ref[...] = layer_norm_low(
            x_ref[...].astype(F32), vec_ref[LN1_GAIN], vec_ref[LN1_SHIFT]
        )

    c, s = cos_sin(hot_ref[...], table_ref[...])
    norm = norm_ref[...]

    def gradient(n, low):
        d_ref[n] = low
        db_ref[n : n + 1, :] = columns_sum(low.astype(F32))
        at = pl.ds(pl.multiple_of(n * width + group * 256, 256), 256)
        g_all[:, at] = dot_tn(norm, low).astype(BF)

    d_angle = 0.0
    for n, (grad, turned_ref) in enumerate(((dq_ref, q_ref), (dk_ref, k_ref))):
        g1, g2 = grad[:, :128], grad[:, 128:]
        d_angle = d_angle + (g2 * turned_ref[:, :128] - g1 * turned_ref[:, 128:])
        back = jnp.concatenate([g1 * c + g2 * s, g2 * c - g1 * s], 1).astype(BF)
        gradient(n, dot(back, back_ref[...]).astype(BF))
    freq_ref[...] = lax.dot_general(
        grid_ref[...], d_angle, (((1,), (0,)), ((), ())),
        preferred_element_type=F32, precision=lax.Precision.HIGHEST,
    )
    gradient(2, dv_ref[...].astype(BF))

    @pl.when(group == width // 256 - 1)
    def _():
        slices_out(place_ref[0], g_all, keep_ref, send_ref, 0, sem, slices, width // slices)
        slices_wait(g_all, keep_ref, sem, slices, width // slices)


def turn_back_call(
    place, x, vectors, dq, dk, dv, q_exact, k_exact, onehot, table, grid8, back, first, slices
):
    rows, width = dk.shape
    sds = jax.ShapeDtypeStruct
    part = pl.BlockSpec((rows, 256), lambda g: (0, g))
    hot = pl.BlockSpec(
        (pl.Element(rows), pl.Element(onehot.shape[1])),
        lambda g: (pl.multiple_of(first + 0 * g, BLK), 0),
    )
    return pl.pallas_call(
        functools.partial(turn_back_kernel, slices=slices),
        grid=(width // 256,),
        in_specs=[SMEM, whole(x.shape), whole(vectors.shape)]
        + [part] * 5
        + [
            hot,
            pl.BlockSpec((table.shape[0], 512), lambda g: (0, g)),
            whole(grid8.shape),
            whole(back.shape),
        ],
        out_specs=[
            pl.BlockSpec((3, rows, 256), lambda g: (0, 0, g)),
            pl.BlockSpec((3, 256), lambda g: (0, g)),
            pl.BlockSpec((8, 128), lambda g: (0, g)),
        ]
        + [ANY] * 2,
        out_shape=[
            sds((3, rows, width), BF),
            sds((3, width), F32),
            sds((8, width // 2), F32),
        ]
        + [sds((slices // 2, width // slices, 3 * width), BF)] * 2,
        scratch_shapes=[
            pltpu.VMEM((rows, width), BF),
            pltpu.VMEM((width, 3 * width), BF),
            pltpu.SemaphoreType.DMA((slices,)),
        ],
        compiler_params=params(16),
        cost_estimate=cost(9),
        name="turn_back",
    )(place, x, vectors, dq, dk, dv, q_exact, k_exact, onehot, table, grid8, back)


def input_grad_kernel(
    place_ref, x_ref, vec_ref, d_ref, w_ref, dh_ref, db_ref, mid_ref, freq_ref, up0_ref, up_ref,
    out_ref, small_ref,
):
    width = x_ref.shape[1]
    d_norm = sum(dot_nt(d_ref[n], w_ref[:, lanes_of(n, width)]) for n in range(3))
    xhat, inverse = norm_parts(x_ref[...].astype(F32))
    out_ref[...] = dh_ref[...] + norm_back(d_norm, xhat, inverse, vec_ref[LN1_GAIN])
    row = 0
    for vector in (
        columns_sum(d_norm * xhat), columns_sum(d_norm), *(db_ref[n : n + 1, :] for n in range(3)),
        mid_ref[3:4, :], freq_ref[0:1, :], freq_ref[1:2, :], *(mid_ref[n : n + 1, :] for n in range(3)),
    ):
        for n in range(vector.shape[1] // 128):
            small_ref[row : row + 1, :] = vector[:, lanes_of(n, 128)]
            row += 1
    depth = 1 + up_ref.shape[0]
    hidden = up0_ref.shape[1] // 128
    for k in range(depth):
        quarter = (place_ref[1] - k + depth) % depth
        vector = up_ref[k - 1 : k, :] if k else up0_ref[...]
        for n in range(hidden):
            small_ref[pl.ds(row + quarter * hidden + n, 1), :] = vector[:, lanes_of(n, 128)]


def input_grad_call(place, x, vectors, d_qkv, weight, d_hidden, db_qkv, small_mid, freqs, up0, up):
    rows, width = x.shape
    short = 9 * width + freqs.shape[1] * 2 + up0.size * (1 + up.shape[0])
    return pl.pallas_call(
        input_grad_kernel,
        in_specs=[SMEM] + [pl.BlockSpec(memory_space=pltpu.VMEM)] * 10,
        out_shape=[
            jax.ShapeDtypeStruct((rows, width), F32),
            jax.ShapeDtypeStruct((short // 128, 128), F32),
        ],
        compiler_params=params(20),
        cost_estimate=cost(7),
        name="input_grad",
    )(place, x, vectors, d_qkv, weight, d_hidden, db_qkv, small_mid, freqs, up0, up)


def assemble_kernel(place_ref, *refs, split, outs, skip):
    out_refs, (held, sem) = refs[-2 - outs : -2], refs[-2:]
    pairs = refs[:4]
    piece_refs = [pairs[n // 2].at[n % 2] for n in range(8)]
    place, depth = place_ref[0], place_ref[1]
    slot = pl.program_id(0)

    def copy(ref, target):
        return pltpu.make_async_copy(ref, held.at[target], sem.at[target])

    @pl.when(slot == 0)
    def _():
        for ref, source in gathered(place, piece_refs):
            copy(ref, source).start()

    copy(piece_refs[0], slot).wait()
    rows = held.shape[-2]
    total_ref = None
    if skip is not None:
        out_refs, total_ref = out_refs[:-1], out_refs[-1]
    out_refs, squares = out_refs[:-1], out_refs[-1]

    @pl.when(slot == 0)
    def _():
        squares[...] = jnp.zeros_like(squares)

    def add_squares(block):
        total = fold8(block * block, jnp.sum)
        squares[...] += sum(total[:, lanes_of(n, 128)] for n in range(block.shape[1] // 128))

    if split:
        for n in range(split):
            block = held[slot, (depth - n + split) % split].astype(F32)
            add_squares(block)
            lo = 0
            for ref in out_refs:
                ref[n * rows : n * rows + rows, :] = block[:, lo : lo + ref.shape[1]]
                lo += ref.shape[1]
    else:
        block = held[slot].astype(F32)
        add_squares(block)
        each = held.shape[0] // len(out_refs)
        for n, ref in enumerate(out_refs):

            @pl.when(slot // each == n)
            def _():
                ref[...] = block
    if skip is not None:
        small_ref = refs[4]

        @pl.when(slot == held.shape[0] - 1)
        def _():
            short = small_ref[...]
            row = lax.broadcasted_iota(jnp.int32, short.shape, 0)
            mine = (row >= skip[0]) & (row < skip[1])
            parts = row >= short.shape[0] - 8
            others = jnp.where(mine, 0.0, jnp.where(parts, short, short * short))
            turned = jnp.where(mine, short * short, 0.0)
            total_ref[0:1, :] = jnp.full((1, 128), jnp.sum(turned))
            total_ref[1:2, :] = jnp.full((1, 128), jnp.sum(others) + jnp.sum(squares[...]))


def assemble_call(place, arrays, shapes, split, small=None, skip=None):
    pieces = 8
    rows = arrays[0].shape[-2] * max(split, 1)
    each = pieces if split else pieces // len(shapes)

    def spec(n, shape):
        lead = 0 if split else n * each
        return pl.BlockSpec((rows, shape[1]), lambda i: (jnp.clip(i - lead, 0, each - 1), 0))

    specs = [spec(n, shape) for n, shape in enumerate(shapes)] + [whole((8, 128))]
    shapes = shapes + [(8, 128)]
    given = []
    if small is not None:
        given, specs, shapes = [small], specs + [whole((2, 128))], shapes + [(2, 128)]
    return pl.pallas_call(
        functools.partial(assemble_kernel, split=split, outs=len(shapes), skip=skip),
        grid=(pieces,),
        in_specs=[SMEM] + [ANY] * len(arrays) + [whole(x.shape) for x in given],
        out_specs=specs,
        out_shape=[jax.ShapeDtypeStruct(s, F32) for s in shapes],
        scratch_shapes=[
            pltpu.VMEM((pieces,) + arrays[0].shape[1:], BF),
            pltpu.SemaphoreType.DMA((pieces,)),
        ],
        compiler_params=params(16),
        cost_estimate=cost(6),
        name="assemble",
    )(place, *arrays, *given)


def send(x, axis, pairs):
    return lax.ppermute(x, axis, pairs)


def plane_gather(piece):
    pair = jnp.stack([piece, send(piece, PLANE, FIRST)])
    return pair, send(pair, PLANE, SECOND)


def core_gather(pair, last):
    return [pair, last, send(pair, "c", SWAP), send(last, "c", SWAP)]


def wide_sum(x, extra):
    return lax.psum(x, "e") if extra > 1 else x


def sum_low(*terms):
    return functools.reduce(lambda x, y: x + y, [t.astype(F32) for t in terms])


def after(x, *others):
    return lax.optimization_barrier((x, others))[0]


def ring(size, step):
    return [(i, (i + step) % size) for i in range(size)]


def add_from(vector, axis, reach=0, size=2):
    return vector + send(vector, axis, [(i, i ^ (reach or 1)) for i in range(size)])


def on_device(
    tokens,
    segment,
    padding,
    coords,
    ln1_gain,
    ln1_shift,
    query_key_value_weight,
    b_qkv,
    output_weight,
    b_out,
    rope_freqs,
    ln2_gain,
    ln2_shift,
    w_up,
    b_up,
    w_down,
    b_down,
    cotangent,
    *,
    extra,
    depth,
):
    tokens, cotangent = tokens[0], cotangent[0]
    own, width = tokens.shape
    length = own * depth
    heads = rope_freqs.shape[1]
    half = width // heads // 2
    groups = heads // GROUP
    slices = 8
    outer = BLK
    side = own + outer
    win = own + 2 * side
    blocks = own // BLK
    z = lax.axis_index("n")
    plane = lax.axis_index("a") * 4 + lax.axis_index("b") * 2 + lax.axis_index("c")
    place = jnp.stack([plane, z]).astype(jnp.int32)
    up = [(i, i + 1) for i in range(depth - 1)]
    down = [(i + 1, i) for i in range(depth - 1)]
    up2 = [(i, i + 2) for i in range(depth - 2)]
    down2 = [(i + 2, i) for i in range(depth - 2)]

    def around(x, head, tail):
        before2 = send(tail, "n", up2)
        before = send(x, "n", up)
        after_ = send(x, "n", down)
        after2 = send(head, "n", down2)
        return [before2, before, after_, after2]

    position = jnp.arange(length, dtype=jnp.int32)
    ident = jnp.where(padding[0] == 0, segment[0], 1000 + position)
    ident = jnp.concatenate(
        [jnp.full((side,), -1, jnp.int32), ident, jnp.full((side,), 1 << 20, jnp.int32)]
    )
    ident_win = lax.dynamic_slice_in_dim(ident, z * own, win, 0)
    near = lax.broadcasted_iota(jnp.int32, (win,), 0)
    ident_win = jnp.where(near < outer - REACH, -1, ident_win)
    ident_win = jnp.where(near >= win - outer + REACH, 1 << 20, ident_win)
    idk = jnp.broadcast_to(ident_win[:, None], (win, BLK))
    idq = ident_win.reshape(win // BLK, BLK)

    lowest, highest = idq[:, 0], idq[:, BLK - 1]

    def bounds(queries, keys):
        before = highest[keys][None, :] < lowest[queries][:, None]
        reached = lowest[keys][None, :] <= highest[queries][:, None]
        return jnp.sum(before, 1), jnp.sum(reached, 1)

    def steps(blocks, span):
        return (jnp.maximum(blocks, 0) + span - 1) // span

    mid = slice(side // BLK, side // BLK + blocks)
    lo, hi = bounds(mid, slice(None))
    bounds_fwd = [
        lo, steps(hi - lo, SPAN), jnp.minimum(lo, mid.start), steps(mid.start - lo, SPAN_SIDE),
        steps(hi - mid.stop, SPAN_SIDE),
    ]
    bounds_fwd = jnp.stack(bounds_fwd, 1).astype(jnp.int32)
    lo, hi = bounds(slice(None), mid)
    bounds_bwd = jnp.stack([lo, steps(hi - lo, SPAN_BACK)], 1).astype(jnp.int32)

    grid = jnp.pad(coords[:, 0], ((0, 0), (side, side)))
    grid_win = lax.dynamic_slice_in_dim(grid, z * own, win, 1)
    grid_own = lax.dynamic_slice_in_dim(grid, z * own + side, own, 1)
    lane = jnp.arange(4 * SIDE)
    picked = jnp.where(lane[None, :] < 2 * SIDE, grid_win[0][:, None], grid_win[1][:, None])
    onehot = (picked == (lane % SIDE)[None, :]).astype(BF)
    table = turn_table(rope_freqs)

    local = np.arange(256)
    order = np.zeros((256, 256), np.float32)
    order[(local % 128) // 32 * 64 + local // 128 * 32 + local % 32, local] = 1.0
    order = jnp.asarray(order, BF)
    qk_bias = b_qkv[: 2 * width].reshape(2 * groups, GROUP, 2, half).swapaxes(1, 2)
    bias_turned = jnp.concatenate([qk_bias.reshape(-1), b_qkv[2 * width :]])

    x_parts = around(tokens, tokens[:REACH], tokens[own - REACH :])
    vectors = jnp.stack([ln1_gain, ln1_shift, b_out, ln2_gain, ln2_shift, b_down])
    rot_q, rot_k, values, q_exact, k_exact, weight_turned = qkv_own_call(
        tokens, onehot, vectors, query_key_value_weight, bias_turned, order, table, side
    )
    rows = (width + w_down.shape[0]) // slices
    eighth = jnp.where(
        plane < width // rows,
        lax.dynamic_slice_in_dim(w_up, jnp.minimum(plane * rows, width - rows), rows, 0),
        lax.dynamic_slice_in_dim(w_down, jnp.maximum(plane * rows - width, 0), rows, 0),
    )
    left, bias_rows = b_up, []
    for _ in range(3):
        bias_rows.append(left.astype(BF))
        left = left - rounded(left)
    bias_rows = jnp.pad(jnp.stack(bias_rows), ((0, 13), (0, 0)))
    eighth = jnp.concatenate([eighth, bias_rows], 0)
    others = [send(eighth, "n", ring(depth, k)) for k in range(1, depth)]
    x_parts, rot_q, idk = lax.optimization_barrier((x_parts, rot_q, idk))
    halo_args = (x_parts, onehot, vectors, weight_turned, bias_turned, table)
    rot_q, rot_k, values = halo_call(*halo_args, (rot_q, rot_k, values), (0, 1, 2), side)
    part = forward_call(bounds_fwd, rot_q, rot_k, values, idk, idq, side, own, 0, blocks // 2)
    others, part = lax.optimization_barrier((others, part))
    up_biases = jnp.concatenate(
        [jnp.sum(x[rows : rows + 3].astype(F32), 0, keepdims=True) for x in others]
    )
    own_w = jnp.stack([x[:rows] for x in others])
    over_1, over_2 = send(own_w, PLANE, FIRST), send(own_w, PLANE, SECOND)
    part, _ = lax.optimization_barrier((part, own_w))
    mixed, mixed_low, lse = forward_call(
        bounds_fwd, rot_q, rot_k, values, idk, idq, side, own, blocks // 2, blocks // 2, part
    )
    hidden_in, norm2, out0, dn0, up_sum0, kept_own, sent_own = middle_own_call(
        place, tokens, mixed_low, output_weight, vectors, cotangent, b_up[None],
        w_up, w_down, slices,
    )
    over_1, over_2, norm2 = lax.optimization_barrier((over_1, over_2, norm2))
    diagonal = send(over_1, PLANE, SECOND)
    near = [own_w, over_1, over_2, diagonal]
    pieces = near + [send(x, "c", SWAP) for x in near]
    grid8 = jnp.pad(grid_own.astype(F32), ((0, 6), (0, 0)))
    far_own = send(after(sent_own, over_1, over_2), "c", SWAP)
    away_own = sum_low(kept_own[2:], far_own[2:]).astype(BF)
    got_own = [send(away_own, PLANE, FIRST)]
    norm2, up_biases, bounds_bwd, _ = lax.optimization_barrier(
        (norm2, up_biases, bounds_bwd, away_own)
    )
    (
        activations, d_hidden, d_heads, d_head, d_tail, delta, small_mid, up_sums, kept_mid,
        sent_mid,
    ) = middle_call(
        place, hidden_in, norm2, out0, dn0, mixed_low, mixed, output_weight, vectors, cotangent,
        up_biases, lse, pieces, slices,
    )
    far_mid = send(sent_mid, "c", SWAP)
    do_parts = around(d_heads, d_head, d_tail)

    got_own[0], far_mid = lax.optimization_barrier((got_own[0], far_mid))
    away_own = sum_low(kept_own[1], far_own[1], got_own[0][1]).astype(BF)
    got_own.append(send(away_own, PLANE, SECOND))
    away = sum_low(kept_mid[2:], far_mid[2:]).astype(BF)
    got_1 = send(away, PLANE, FIRST)
    dq, dk, dv = backward_own_call(
        bounds_fwd, rot_q, d_heads, rot_k, values, idk, idq, lse, after(delta, away, away_own),
        side, own,
    )
    got_1, got_own[1], dq = lax.optimization_barrier((got_1, got_own[1], dq))
    away = sum_low(kept_mid[1], far_mid[1], got_1[1]).astype(BF)
    got_2 = send(away, PLANE, SECOND)
    do_parts, dq, dk, _ = lax.optimization_barrier((do_parts, dq, dk, away))
    dk, dv = backward_halo_call(
        bounds_bwd, rot_q, do_parts, rot_k, values, idk, idq, dk, dv, side
    )
    got_2, dk = lax.optimization_barrier((got_2, dk))

    def plane_part(lo, hi):
        at = slice(lo, hi)
        total = sum_low(kept_mid[0, at], far_mid[0, at], got_1[0, at], got_2[at])
        return wide_sum(total, extra)

    ff_sent = [plane_part(k * rows - rows, k * rows).astype(BF) for k in range(1, depth)]
    ff_got = [send(x, "n", ring(depth, -1 - k)) for k, x in enumerate(ff_sent)]

    d_qkv, grad_b_qkv, freqs8, kept_qkv, sent_qkv = turn_back_call(
        place, tokens, vectors, dq, dk, dv, q_exact, k_exact, onehot, table, grid8,
        order.T, side, slices,
    )
    far_qkv = send(sent_qkv, "c", SWAP)
    away = sum_low(kept_qkv[2:], far_qkv[2:]).astype(BF)
    got_1_qkv = send(away, PLANE, FIRST)
    input_grad, small_in = input_grad_call(
        place, tokens, vectors, after(d_qkv, away), query_key_value_weight, d_hidden,
        grad_b_qkv, small_mid, freqs8, up_sum0, up_sums,
    )
    away = sum_low(kept_qkv[1], far_qkv[1], got_1_qkv[1]).astype(BF)
    got_2_qkv = send(away, PLANE, SECOND)
    plane_qkv = wide_sum(sum_low(kept_qkv[0], far_qkv[0], got_1_qkv[0], got_2_qkv), extra)

    sizes = [width, width, 3 * width, width, rope_freqs.size] + [width] * 3 + [b_up.size * depth]

    part = plane_part((depth - 1) * rows, (depth - 1) * rows + width // slices)
    part = jnp.concatenate([plane_qkv, part], 1).astype(BF)
    part, ff_got = lax.optimization_barrier((part, ff_got))
    thin = part.shape[0] // depth
    cut = lambda k: lax.dynamic_slice_in_dim(part, ((z + k) % depth) * thin, thin, 0)
    got = [send(cut(k), "n", ring(depth, k)) for k in range(1, depth)]
    small = add_from(add_from(add_from(after(small_in, part), "c"), "b"), "a")
    if extra > 1:
        small = lax.psum(small, "e")
    got, small = lax.optimization_barrier((got, small))
    low = sum_low(cut(0), *got).astype(BF)
    strip = jnp.stack([low] + [send(low, "n", ring(depth, k)) for k in range(1, depth)])
    ff_total = wide_sum(sum_low(kept_own[0], far_own[0], got_own[0][0], got_own[1]), extra)
    ff_total = ff_total + sum_low(*ff_got)
    ff_pair, ff_last = plane_gather(after(ff_total, low).astype(BF))
    pair, last = plane_gather(strip)
    ff_pieces = [after(x, strip) for x in core_gather(ff_pair, ff_last)]
    total_w_up, total_w_down, ff_squares = assemble_call(
        place, ff_pieces, [w_up.shape, w_down.shape], 0
    )
    small = jnp.concatenate([small, ff_squares], 0)
    reach = 1
    while reach < depth:
        small = add_from(small, "n", reach, depth)
        reach *= 2
    last, small = lax.optimization_barrier((last, small))
    turned = sum(sizes[:4]) // 128
    total_w_qkv, total_w_out, _, norms = assemble_call(
        place, core_gather(pair, last), [query_key_value_weight.shape, output_weight.shape], depth,
        small, (turned, turned + sizes[4] // 128),
    )
    small = small[:-8].reshape(-1)
    out, at = [], 0
    for size in sizes:
        out.append(small[at : at + size])
        at += size
    t_gain1, t_shift1, t_b_qkv, t_b_out, t_freqs, t_gain2, t_shift2, t_b_down, t_up = out
    t_freqs = t_freqs.reshape(rope_freqs.shape)
    rot_sq, other_sq = norms[0, 0], norms[1, 0]
    t_b_up = lax.dynamic_slice_in_dim(t_up, z * b_up.shape[0], b_up.shape[0], 0)
    return (
        activations[None],
        input_grad[None],
        t_gain1,
        t_shift1,
        total_w_qkv,
        t_b_qkv,
        total_w_out,
        t_b_out,
        t_freqs,
        t_gain2,
        t_shift2,
        total_w_up,
        t_b_up,
        total_w_down,
        t_b_down,
        rot_sq,
        other_sq,
    )


def solution(mesh):
    wide, depth = mesh.shape["wide"], mesh.shape["narrow"]
    extra = wide // 8
    fine = Mesh(mesh.devices.reshape(extra, 2, 2, 2, depth), ("e", "a", "b", "c", "n"))
    w, n = ("e", "a", "b", "c"), "n"
    return jax.shard_map(
        functools.partial(on_device, extra=extra, depth=depth),
        mesh=fine,
        in_specs=(
            P(w, n, None), P(w, None), P(w, None), P(None, w, None),
            P(), P(), P(), P(), P(), P(), P(), P(), P(),
            P(None, n), P(n), P(n, None), P(), P(w, n, None),
        ),
        out_specs=(
            P(w, n, None), P(w, n, None),
            P(), P(), P(), P(), P(), P(), P(), P(), P(),
            P(None, n), P(n), P(n, None), P(), P(), P(),
        ),
        check_vma=False,
    )
```
